32 devices in a mesh: dp: 4 (over x, core), sol: 4 (over z), tensor: 2 (over y).
Axes of the slice: x: 2, y: 2, z: 4, core: 2. Of those that a mesh axis runs over, the one named last changes fastest.
Arguments:
- inputs: bfloat16 [8192, 2048], P(('dp', 'sol')), may hold values from -6 to 6
- cotangent: bfloat16 [8192, 2048], P(('dp', 'sol')), may hold values from -6 to 6
- attn_gain: float32 [2048], replicated, may hold values from 0.25 to 1.75
- attn_shift: float32 [2048], replicated, may hold values from -3 to 3
- query_weight: bfloat16 [2048, 2048], P(('dp', 'sol'), 'tensor'), may hold values from -0.25 to 0.25
- key_weight: bfloat16 [2048, 2048], P(('dp', 'sol'), 'tensor'), may hold values from -0.125 to 0.125
- value_weight: bfloat16 [2048, 2048], P(('dp', 'sol'), 'tensor'), may hold values from -0.125 to 0.125
- out_weight: bfloat16 [2048, 2048], P(('dp', 'sol'), 'tensor'), may hold values from -0.5 to 0.5
- mlp_gain: float32 [2048], replicated, may hold values from 0.25 to 1.75
- mlp_shift: float32 [2048], replicated, may hold values from -3 to 3
- up_weight: bfloat16 [2048, 8192], P(('dp', 'sol'), 'tensor'), may hold values from -0.125 to 0.125
- up_bias: float32 [8192], P('tensor'), may hold values from -3 to 3
- down_weight: bfloat16 [2048, 8192], P(('dp', 'sol'), 'tensor'), may hold values from -0.0625 to 0.0625
- down_bias: float32 [2048], replicated, may hold values from -3 to 3
- live_rows: int32 [16], replicated, may hold values from 128 to 512, as said below
Outputs:
- outputs: bfloat16 [8192, 2048], P(('dp', 'sol'))
- input_grad: bfloat16 [8192, 2048], P(('dp', 'sol'))
- attn_gain_grad: float32 [2048], replicated
- attn_shift_grad: float32 [2048], replicated
- query_grad: float32 [2048, 2048], P(('dp', 'sol'), 'tensor')
- key_grad: float32 [2048, 2048], P(('dp', 'sol'), 'tensor')
- value_grad: float32 [2048, 2048], P(('dp', 'sol'), 'tensor')
- out_grad: float32 [2048, 2048], P(('dp', 'sol'), 'tensor')
- mlp_gain_grad: float32 [2048], replicated
- mlp_shift_grad: float32 [2048], replicated
- up_grad: float32 [2048, 8192], P(('dp', 'sol'), 'tensor')
- up_bias_grad: float32 [8192], P('tensor')
- down_grad: float32 [2048, 8192], P(('dp', 'sol'), 'tensor')
- down_bias_grad: float32 [2048], replicated
The draws below stay inside these ranges and needn't reach their ends.
Inputs may be any that keep to these rules, and one draw needn't show every extreme that they name: Entry g * 4 of live_rows is the length of problem g's prefix; entry g * 4 + s for s > 0 the length of the solution in that block. Some entry equals 512 and some other entry equals 128.
All inputs are finite; a program needn't handle non-finite values.
Results may differ from the reference program's by a relative error of at most 0.014.
Values may be sent and summed in bfloat16 or wider, within the bound.
A program may use at most 448 MiB of HBM per device.

```python
import math
import jax
import jax.numpy as jnp
from jax import lax

D = 2048
HEADS = 16
HEAD_DIM = 128
FF = 8192
TOK_DEV = 512
GROUP = 4
BLOCKS = 16
TOKENS = 8192


def draw_live_rows(key, part):
    key = jax.random.fold_in(key, 11)
    key_lengths, key_high, key_low = jax.random.split(key, 3)
    lengths_all = jax.random.randint(key_lengths, (BLOCKS,), TOK_DEV // 4, TOK_DEV + 1)
    high_pick = jax.random.randint(key_high, (), 0, BLOCKS)
    low_pick = (high_pick + 1 + jax.random.randint(key_low, (), 0, BLOCKS - 1)) % BLOCKS
    places = jnp.arange(BLOCKS)
    lengths_all = jnp.where(places == high_pick, TOK_DEV, lengths_all)
    lengths_all = jnp.where(places == low_pick, TOK_DEV // 4, lengths_all)
    return lengths_all.astype(jnp.int32)


def with_spikes(drawn, own_key, source, target, blocks, factor):
    owner, partner = [(jnp.arange(drawn.shape[position]) // (drawn.shape[position] // blocks)).reshape([-1 if axis == position else 1 for axis in range(drawn.ndim)]) for position in (source, target)]
    chosen = jax.random.permutation(own_key, blocks)[partner]
    strong = (owner == chosen) | (owner == (partner + blocks // 2) % blocks)
    return jnp.where(strong, factor * drawn, drawn)


def steps_of(own_key, extent, shards, least, largest):
    def one(position, shards_of):
        draws = jax.random.uniform(jax.random.fold_in(jax.random.fold_in(own_key, 6), position), (shards_of,), jnp.float32, least / len(shards), largest / len(shards))
        return jnp.repeat(jnp.exp(draws), extent[position] // shards_of).reshape((-1,) + (1,) * (len(extent) - position - 1))

    gain = one(*shards[0])
    for cut in shards[1:]:
        gain = gain * one(*cut)
    return gain


def gaussian(key, extent, deviation, most, cuts=(), dtype=jnp.bfloat16):
    loudness = steps_of(key, extent, cuts, -0.22, 0.18) if cuts else 1.0
    values = jax.random.normal(key, extent, jnp.float32) * deviation * loudness
    return jnp.minimum(jnp.maximum(values, -most), most).astype(dtype)


def heavy_noise(key, shape, spread, limit, shards, heavy, dtype=jnp.bfloat16):
    entries = spread * jax.random.normal(key, shape, jnp.float32)
    if shards:
        entries = entries * steps_of(key, shape, shards, -0.22, 0.18)
    return jnp.clip(with_spikes(entries, jax.random.fold_in(key, 3), *heavy), -limit, limit).astype(dtype)


def setup_inputs(seed: int = 0) -> dict:
    splits = jax.random.split(jax.random.key(seed), 16)
    inputs = gaussian(splits[0], (TOKENS, D), 1.0, 6.0, ((0, 16),))
    cotangent = heavy_noise(splits[1], (TOKENS, D), 1.0, 6.0, ((0, 16),), (0, 1, 16, 2.0))
    attn_gain = jnp.clip(1.0 + 0.15 * jax.random.normal(splits[2], (D,), jnp.float32), 0.25, 1.75)
    attn_shift = gaussian(splits[3], (D,), 0.3, 3.0, (), jnp.float32)
    query_weight = gaussian(splits[4], (D, D), (D // 4) ** -0.5, 0.25, ((0, 16), (1, 2)))
    key_weight = gaussian(splits[5], (D, D), D ** -0.5, 0.125, ((0, 16), (1, 2)))
    value_weight = gaussian(splits[6], (D, D), D ** -0.5, 0.125, ((0, 16), (1, 2)))
    out_weight = gaussian(splits[7], (D, D), (D // 16) ** -0.5, 0.5, ((0, 16), (1, 2)))
    mlp_gain = jnp.clip(1.0 + 0.15 * jax.random.normal(splits[8], (D,), jnp.float32), 0.25, 1.75)
    mlp_shift = gaussian(splits[9], (D,), 0.3, 3.0, (), jnp.float32)
    up_weight = gaussian(splits[10], (D, FF), D ** -0.5, 0.125, ((0, 16), (1, 2)))
    up_bias = gaussian(splits[11], (FF,), 0.3, 3.0, ((0, 2),), jnp.float32)
    down_weight = gaussian(splits[12], (D, FF), FF ** -0.5, 0.0625, ((0, 16), (1, 2)))
    down_bias = gaussian(splits[13], (D,), 0.3, 3.0, (), jnp.float32)
    live_rows = draw_live_rows(jax.random.fold_in(splits[15], 71), 0)
    return dict(inputs=inputs, cotangent=cotangent, attn_gain=attn_gain, attn_shift=attn_shift, query_weight=query_weight, key_weight=key_weight, value_weight=value_weight, out_weight=out_weight, mlp_gain=mlp_gain, mlp_shift=mlp_shift, up_weight=up_weight, up_bias=up_bias, down_weight=down_weight, down_bias=down_bias, live_rows=live_rows)


EPSILON = 1e-05
NEG_FILL = -1e+30

@jax.custom_vjp
def low(v):
    return lax.optimization_barrier(v.astype(jnp.bfloat16)).astype(jnp.float32)

@jax.custom_vjp
def low_back(v):
    return v

def low_keep(v):
    return (low(v), None)

def low_pass(kept, grad):
    return (grad,)

def back_keep(v):
    return (v, None)

def back_low(kept, grad):
    return (low(grad),)
low.defvjp(low_keep, low_pass)
low_back.defvjp(back_keep, back_low)

def layer_norm(features, norm_gain, norm_shift):
    row_mean = lax.optimization_barrier(jnp.mean(features, axis=-1, keepdims=True))
    centered = features - row_mean
    variance = lax.optimization_barrier(jnp.mean(centered * centered, axis=-1, keepdims=True))
    return centered * lax.rsqrt(variance + EPSILON) * norm_gain + norm_shift

def matmul_plain(left_side, right_side):
    return jnp.dot(left_side, right_side, precision=lax.Precision.HIGHEST, preferred_element_type=jnp.float32)

def matmul_right_t(left_side, right_side):
    return lax.dot_general(left_side, right_side, (((1,), (1,)), ((), ())), precision=lax.Precision.HIGHEST, preferred_element_type=jnp.float32)

def attend_block(packed):
    queries, prefix_keys, prefix_values, own_keys, own_values, own_live, prefix_live, is_first = packed
    row_ids = jnp.arange(TOK_DEV)[:, None]
    col_ids = jnp.arange(TOK_DEV)[None, :]
    prefix_ok = jnp.logical_and(col_ids < prefix_live, jnp.logical_not(is_first))
    own_ok = jnp.logical_and(col_ids <= row_ids, col_ids < own_live)
    allowed = jnp.concatenate([jnp.broadcast_to(prefix_ok, (TOK_DEV, TOK_DEV)), own_ok], axis=1)[None]
    all_keys = jnp.concatenate([prefix_keys, own_keys], 0).reshape(2 * TOK_DEV, HEADS, HEAD_DIM)
    all_values = jnp.concatenate([prefix_values, own_values], 0).reshape(2 * TOK_DEV, HEADS, HEAD_DIM)
    head_queries = queries.reshape(TOK_DEV, HEADS, HEAD_DIM)
    scores = jnp.einsum('qhd,khd->hqk', head_queries, all_keys, precision=lax.Precision.HIGHEST) * (1.0 / math.sqrt(HEAD_DIM))
    scores = jnp.where(allowed, low_back(scores), NEG_FILL)
    row_peak = lax.optimization_barrier(jnp.max(scores, axis=-1, keepdims=True))
    exp_scores = jnp.exp(scores - row_peak)
    attn_probs = exp_scores / lax.optimization_barrier(jnp.sum(exp_scores, axis=-1, keepdims=True))
    mixed = jnp.einsum('hqk,khd->qhd', low(attn_probs), all_values, precision=lax.Precision.HIGHEST)
    return mixed.reshape(TOK_DEV, D)

def first_of_group(array_in):
    blocked = array_in.reshape(BLOCKS // GROUP, GROUP, TOK_DEV, D)
    return jnp.broadcast_to(blocked[:, :1], blocked.shape).reshape(BLOCKS, TOK_DEV, D)

def forward(inputs, attn_gain, attn_shift, query_weight, key_weight, value_weight, out_weight, mlp_gain, mlp_shift, up_weight, up_bias, down_weight, down_bias, live_rows):
    normed = low(layer_norm(inputs, attn_gain, attn_shift))
    queries = low(low_back(matmul_plain(normed, query_weight)))
    keys_all = low(low_back(matmul_plain(normed, key_weight)))
    values_all = low(low_back(matmul_plain(normed, value_weight)))
    live_grid = live_rows.reshape(BLOCKS // GROUP, GROUP)
    prefix_live = jnp.broadcast_to(live_grid[:, :1], (BLOCKS // GROUP, GROUP)).reshape(BLOCKS)
    is_first = jnp.arange(BLOCKS) % GROUP == 0
    packed = (queries.reshape(BLOCKS, TOK_DEV, D), first_of_group(keys_all), first_of_group(values_all), keys_all.reshape(BLOCKS, TOK_DEV, D), values_all.reshape(BLOCKS, TOK_DEV, D), live_rows, prefix_live, is_first)
    mixed = lax.map(jax.checkpoint(attend_block), packed).reshape(TOKENS, D)
    mixed = low(low_back(mixed))
    hidden = inputs + low_back(matmul_right_t(mixed, out_weight))
    normed_two = low(layer_norm(hidden, mlp_gain, mlp_shift))
    upward = low_back(matmul_plain(normed_two, up_weight) + up_bias)
    active = low(jax.nn.gelu(upward, approximate=True))
    return hidden + matmul_right_t(active, down_weight) + down_bias

def reference(inputs, cotangent, attn_gain, attn_shift, query_weight, key_weight, value_weight, out_weight, mlp_gain, mlp_shift, up_weight, up_bias, down_weight, down_bias, live_rows):

    def whole_layer(*arguments):
        return forward(*arguments, live_rows)
    arguments = tuple((argument.astype(jnp.float32) for argument in (inputs, attn_gain, attn_shift, query_weight, key_weight, value_weight, out_weight, mlp_gain, mlp_shift, up_weight, up_bias, down_weight, down_bias)))
    result, pullback = jax.vjp(whole_layer, *arguments)
    gradients = pullback(cotangent.astype(jnp.float32))
    return (result.astype(jnp.bfloat16), gradients[0].astype(jnp.bfloat16), gradients[1], gradients[2], gradients[3], gradients[4], gradients[5], gradients[6], gradients[7], gradients[8], gradients[9], gradients[10], gradients[11], gradients[12])
```

```python
import math

import jax
import jax.numpy as jnp
from jax import lax
from jax.experimental import pallas as pl
from jax.experimental.pallas import tpu as pltpu
from jax.sharding import PartitionSpec as P

HEAD_DIM = 128
EPSILON = 1e-05
NEG_FILL = -1e30
ROWS_AXES = ("dp", "sol")
LOW = jnp.bfloat16
WIDE = jnp.float32


def ring_place(position, sol_size):
    x, along = position // sol_size, position % sol_size
    return x, (along if x % 2 == 0 else sol_size - 1 - along)


def ring_pairs(dp_size, sol_size):
    count = dp_size // 2 * sol_size

    def flat(position, core):
        x, z = ring_place(position % count, sol_size)
        return (x * 2 + core) * sol_size + z

    places = [(q, c) for q in range(count) for c in range(2)]
    ahead = [(flat(q, c), flat(q + 1, c)) for q, c in places]
    back = [(b, a) for a, b in ahead]
    cores = [(flat(q, c), flat(q, 1 - c)) for q, c in places]
    return count, ahead, back, cores


def dot_plain(left_side, right_side):
    return jnp.dot(left_side, right_side, preferred_element_type=WIDE)


def dot_right_t(left_side, right_side):
    return lax.dot_general(
        left_side, right_side, (((1,), (1,)), ((), ())), preferred_element_type=WIDE
    )


def dot_left_t(left_side, right_side):
    return lax.dot_general(
        left_side, right_side, (((0,), (0,)), ((), ())), preferred_element_type=WIDE
    )


def norm_stats(features):
    row_mean = jnp.mean(features, axis=-1, keepdims=True)
    centered = features - row_mean
    variance = jnp.mean(centered * centered, axis=-1, keepdims=True)
    return row_mean, lax.rsqrt(variance + EPSILON)


def layer_norm(features, norm_gain, norm_shift):
    row_mean, inverse = norm_stats(features)
    return (features - row_mean) * inverse * norm_gain + norm_shift


def layer_norm_back(features, norm_gain, grad):
    row_mean, inverse = norm_stats(features)
    unit = (features - row_mean) * inverse
    scaled = grad * norm_gain
    along = jnp.mean(scaled * unit, axis=-1, keepdims=True)
    level = jnp.mean(scaled, axis=-1, keepdims=True)
    grad_features = (scaled - level - unit * along) * inverse
    return grad_features, jnp.sum(grad * unit, axis=0), jnp.sum(grad, axis=0)


def gelu_tanh(upward):
    return jax.nn.gelu(upward, approximate=True)


def copy_block(order_ref, in_ref, out_ref):
    out_ref[...] = in_ref[...]


def reorder(rows, order):
    blocks = order.shape[0]
    height, width = rows.shape
    part = width // blocks
    if part % 128:
        return jnp.take(rows.reshape(height, blocks, part), order, axis=1).reshape(height, width)
    return pl.pallas_call(
        copy_block,
        grid_spec=pltpu.PrefetchScalarGridSpec(
            num_scalar_prefetch=1,
            grid=(blocks,),
            in_specs=[pl.BlockSpec((height, part), lambda j, order_ref: (0, order_ref[j]))],
            out_specs=pl.BlockSpec((height, part), lambda j, order_ref: (0, j)),
        ),
        out_shape=jax.ShapeDtypeStruct(rows.shape, rows.dtype),
        cost_estimate=pl.CostEstimate(
            flops=0, bytes_accessed=4 * height * width, transcendentals=0
        ),
    )(order, rows)


def per_device(
    inputs,
    cotangent,
    attn_gain,
    attn_shift,
    query_weight,
    key_weight,
    value_weight,
    out_weight,
    mlp_gain,
    mlp_shift,
    up_weight,
    up_bias,
    down_weight,
    down_bias,
    live_rows,
):
    block_rows, width = inputs.shape
    shard_rows = query_weight.shape[0]
    head_cols = query_weight.shape[1] // 2
    ff_cols = up_weight.shape[1] // 2
    ff_part = ff_cols // 2
    local_heads = head_cols // HEAD_DIM
    score_scale = 1.0 / math.sqrt(HEAD_DIM)
    dp_size, sol_size = lax.axis_size("dp"), lax.axis_size("sol")
    count, ahead, back, cores = ring_pairs(dp_size, sol_size)
    dp_place, sol_place = lax.axis_index("dp"), lax.axis_index("sol")
    x_place, core = dp_place // 2, dp_place % 2
    first_core = core == 0
    along = jnp.where(x_place % 2 == 0, sol_place, sol_size - 1 - sol_place)
    ring_here = x_place * sol_size + along

    order_list = []
    for j in range(count):
        q = (ring_here + j) % count
        qx, qa = q // sol_size, q % sol_size
        qz = jnp.where(qx % 2 == 0, qa, sol_size - 1 - qa)
        order_list += [(qx * 2) * sol_size + qz, (qx * 2 + 1) * sol_size + qz]
    order = jnp.stack(order_list).astype(jnp.int32)
    back_order = jnp.argsort(order).astype(jnp.int32)

    def to_core(value):
        return lax.ppermute(value, ROWS_AXES, cores)

    def to_tensor(value):
        return lax.ppermute(value, "tensor", [(0, 1), (1, 0)])

    def reorder_vector(vector, by):
        return jnp.take(vector.reshape(by.shape[0], -1), by, axis=0).reshape(vector.shape)

    def gather_ring(piece, flip):
        hops_ahead = count // 2 - (1 if flip else 0)
        hops_back = count - 1 - hops_ahead
        got = {0: piece}
        moving_a, moving_b = piece, piece
        for k in range(1, count // 2 + 1):
            if k <= hops_ahead:
                moving_a = lax.ppermute(moving_a, ROWS_AXES, ahead)
                got[count - k] = moving_a
            if k <= hops_back:
                moving_b = lax.ppermute(moving_b, ROWS_AXES, back)
                got[k] = moving_b
        return jnp.concatenate([got[j] for j in range(count)], axis=0)

    def scatter_ring(chunk, flip):
        hops_ahead = count // 2 - (1 if flip else 0)
        hops_back = count - 1 - hops_ahead
        carried_a = carried_b = None
        for k in range(count // 2, 0, -1):
            if k <= hops_ahead:
                value = chunk(k)
                if carried_a is not None:
                    value = value + carried_a.astype(WIDE)
                carried_a = lax.ppermute(value.astype(LOW), ROWS_AXES, ahead)
            if k <= hops_back:
                value = chunk(count - k)
                if carried_b is not None:
                    value = value + carried_b.astype(WIDE)
                carried_b = lax.ppermute(value.astype(LOW), ROWS_AXES, back)
        return chunk(0) + carried_a.astype(WIDE) + carried_b.astype(WIDE)

    def own_part(shards):
        firsts, seconds = [], []
        for shard, start, size in shards:
            half = shard.shape[1] // 2
            firsts.append(shard[:, start : start + size])
            seconds.append(shard[:, half + start : half + start + size])
        low_half = jnp.concatenate(firsts, axis=1) if len(firsts) > 1 else firsts[0]
        high_half = jnp.concatenate(seconds, axis=1) if len(seconds) > 1 else seconds[0]
        mine = jnp.where(first_core, low_half, high_half)
        other = to_core(jnp.where(first_core, high_half, low_half))
        return jnp.concatenate(
            [jnp.where(first_core, mine, other), jnp.where(first_core, other, mine)], axis=0
        )

    def split_rows(full):
        upper, lower = full[:shard_rows], full[shard_rows:]
        mine = jnp.where(first_core, upper, lower)
        other = to_core(jnp.where(first_core, lower, upper))
        return jnp.where(first_core, mine, other), jnp.where(first_core, other, mine)

    def sum_partials(partial):
        mine = partial[:block_rows] + to_core(partial[block_rows:].astype(LOW)).astype(WIDE)
        low = mine.astype(LOW)
        return low.astype(WIDE) + to_tensor(low).astype(WIDE)

    def pair_rows(own):
        return jnp.concatenate([own, to_core(own)], axis=0)

    qk_piece = own_part([(query_weight, 0, head_cols), (key_weight, 0, head_cols)])
    vo_piece = own_part([(value_weight, 0, head_cols), (out_weight, 0, head_cols)])
    up_pieces = [own_part([(up_weight, s, ff_part)]) for s in (0, ff_part)]
    down_pieces = [own_part([(down_weight, s, ff_part)]) for s in (0, ff_part)]
    qk_full = gather_ring(qk_piece, False)
    vo_full = gather_ring(vo_piece, True)
    up_full = [gather_ring(up_pieces[0], False), gather_ring(up_pieces[1], True)]
    down_full = [gather_ring(down_pieces[0], False), gather_ring(down_pieces[1], True)]
    query_full, key_full = qk_full[:, :head_cols], qk_full[:, head_cols:]
    value_full, out_full = vo_full[:, :head_cols], vo_full[:, head_cols:]

    tensor_place = lax.axis_index("tensor")
    half_rows = block_rows // 2
    half = jnp.where(tensor_place == 0, inputs[:half_rows], inputs[half_rows:])
    prefix_half = half
    hop = half
    for k in range(1, sol_size):
        hop = lax.ppermute(hop, "sol", [(k - 1, k)])
        prefix_half = jnp.where(sol_place == k, hop, prefix_half)
    other_half = to_tensor(prefix_half)
    prefix_inputs = jnp.concatenate(
        [
            jnp.where(tensor_place == 0, prefix_half, other_half),
            jnp.where(tensor_place == 0, other_half, prefix_half),
        ],
        axis=0,
    )

    own_low = reorder(inputs, order)
    prefix_low = reorder(prefix_inputs, order)
    cot_low = reorder(cotangent, order)
    attn_gain_o, attn_shift_o, mlp_gain_o, mlp_shift_o, down_bias_o = [
        reorder_vector(v, order) for v in (attn_gain, attn_shift, mlp_gain, mlp_shift, down_bias)
    ]
    up_bias_c = jnp.where(first_core, up_bias[:ff_cols], up_bias[ff_cols:])
    up_bias_parts = [up_bias_c[:ff_part], up_bias_c[ff_part:]]

    features = own_low.astype(WIDE)
    normed = pair_rows(layer_norm(features, attn_gain_o, attn_shift_o).astype(LOW))
    normed_prefix = pair_rows(
        layer_norm(prefix_low.astype(WIDE), attn_gain_o, attn_shift_o).astype(LOW)
    )
    cot_pair = pair_rows(cot_low)

    query_rows = dot_plain(normed, query_full).astype(LOW)
    key_rows = dot_plain(normed, key_full).astype(LOW)
    value_rows = dot_plain(normed, value_full).astype(LOW)
    key_prefix = dot_plain(normed_prefix, key_full).astype(LOW)
    value_prefix = dot_plain(normed_prefix, value_full).astype(LOW)

    def heads_of(rows):
        return rows.reshape(2, -1, local_heads, HEAD_DIM)

    head_queries = heads_of(query_rows)
    all_keys = jnp.concatenate([heads_of(key_prefix), heads_of(key_rows)], axis=1)
    all_values = jnp.concatenate([heads_of(value_prefix), heads_of(value_rows)], axis=1)

    row_ids = jnp.arange(block_rows)[:, None]
    col_ids = jnp.arange(block_rows)[None, :]
    masks = []
    for place in (dp_place, dp_place + 1 - 2 * core):
        own_live = live_rows[place * sol_size + sol_place]
        prefix_live = live_rows[place * sol_size]
        prefix_ok = jnp.logical_and(col_ids < prefix_live, sol_place != 0)
        own_ok = jnp.logical_and(col_ids <= row_ids, col_ids < own_live)
        masks.append(
            jnp.concatenate(
                [jnp.broadcast_to(prefix_ok, (block_rows, block_rows)), own_ok], axis=1
            )
        )
    allowed = jnp.stack(masks)[:, None]

    def masked_scores():
        raw = jnp.einsum("bqhd,bkhd->bhqk", head_queries, all_keys, preferred_element_type=WIDE)
        return jnp.where(allowed, raw * score_scale, NEG_FILL)

    scores = masked_scores()
    row_peak = jnp.max(scores, axis=-1, keepdims=True)
    exp_scores = jnp.exp(scores - row_peak)
    totals = jnp.sum(exp_scores, axis=-1, keepdims=True)
    attn_probs = exp_scores / totals
    log_total = row_peak + jnp.log(totals)
    mixed = jnp.einsum(
        "bhqk,bkhd->bqhd", attn_probs.astype(LOW), all_values, preferred_element_type=WIDE
    )
    mixed_low = mixed.reshape(2 * block_rows, head_cols).astype(LOW)

    hidden = features + sum_partials(dot_right_t(mixed_low, out_full))
    normed_two = pair_rows(layer_norm(hidden, mlp_gain_o, mlp_shift_o).astype(LOW))
    upward = [dot_plain(normed_two, up_full[i]) + up_bias_parts[i] for i in range(2)]
    active = [gelu_tanh(u).astype(LOW) for u in upward]
    down_grads = [
        scatter_ring(
            lambda j, i=i: dot_left_t(
                cot_pair[:, j * 2 * shard_rows : (j + 1) * 2 * shard_rows], active[i]
            ),
            i == 1,
        )
        for i in range(2)
    ]
    grad_up = []
    for i in range(2):
        grad_active = dot_plain(cot_pair, down_full[i])
        unused_gelu, gelu_pull = jax.vjp(gelu_tanh, upward[i])
        grad_up.append(gelu_pull(grad_active)[0].astype(LOW))
    grad_normed_two = sum_partials(
        dot_right_t(grad_up[0], up_full[0]) + dot_right_t(grad_up[1], up_full[1])
    )
    up_grads = [
        scatter_ring(
            lambda j, i=i: dot_left_t(
                normed_two[:, j * 2 * shard_rows : (j + 1) * 2 * shard_rows], grad_up[i]
            ),
            i == 1,
        )
        for i in range(2)
    ]
    mlp_total = sum_partials(
        dot_right_t(active[0], down_full[0]) + dot_right_t(active[1], down_full[1])
    )
    outputs = reorder((hidden + mlp_total + down_bias_o).astype(LOW), back_order)

    grad_out = cot_low.astype(WIDE)
    down_bias_grad = jnp.sum(grad_out, axis=0)
    grad_hidden_norm, mlp_gain_grad, mlp_shift_grad = layer_norm_back(
        hidden, mlp_gain_o, grad_normed_two
    )
    grad_hidden = grad_out + grad_hidden_norm
    grad_branch = pair_rows(grad_hidden.astype(LOW))
    grad_mixed_low = dot_plain(grad_branch, out_full).astype(LOW)

    grad_head_mixed = heads_of(grad_mixed_low)
    attn_probs = jnp.exp(masked_scores() - log_total)
    grad_probs = jnp.einsum(
        "bqhd,bkhd->bhqk", grad_head_mixed, all_values, preferred_element_type=WIDE
    )
    row_delta = jnp.sum(attn_probs * grad_probs, axis=-1, keepdims=True)
    grad_scores = (attn_probs * (grad_probs - row_delta)).astype(LOW)
    grad_queries = (
        jnp.einsum("bhqk,bkhd->bqhd", grad_scores, all_keys, preferred_element_type=WIDE)
        * score_scale
    )
    grad_keys = (
        jnp.einsum("bhqk,bqhd->bkhd", grad_scores, head_queries, preferred_element_type=WIDE)
        * score_scale
    )
    grad_values = jnp.einsum(
        "bhqk,bqhd->bkhd", attn_probs.astype(LOW), grad_head_mixed, preferred_element_type=WIDE
    )

    def rows_of(heads):
        return heads.reshape(2 * block_rows, head_cols).astype(LOW)

    query_grad_low = rows_of(grad_queries)
    key_own = rows_of(grad_keys[:, block_rows:])
    value_own = rows_of(grad_values[:, block_rows:])
    key_pre = rows_of(grad_keys[:, :block_rows])
    value_pre = rows_of(grad_values[:, :block_rows])

    kv_pre = jnp.concatenate([key_pre, value_pre], axis=1)
    carried = kv_pre
    for k in range(sol_size - 1, 0, -1):
        came = lax.ppermute(carried, "sol", [(k, k - 1)])
        if k > 1:
            carried = (kv_pre.astype(WIDE) + came.astype(WIDE)).astype(LOW)
    key_all = (key_own.astype(WIDE) + came[:, :head_cols].astype(WIDE)).astype(LOW)
    value_all = (value_own.astype(WIDE) + came[:, head_cols:].astype(WIDE)).astype(LOW)

    normed_all = jnp.concatenate([normed, normed_prefix], axis=0)
    key_rows_grad = jnp.concatenate([key_own, key_pre], axis=0)
    value_rows_grad = jnp.concatenate([value_own, value_pre], axis=0)

    def qk_chunk(j):
        at = slice(j * 2 * shard_rows, (j + 1) * 2 * shard_rows)
        return jnp.concatenate(
            [
                dot_left_t(normed[:, at], query_grad_low),
                dot_left_t(normed_all[:, at], key_rows_grad),
            ],
            axis=1,
        )

    def vo_chunk(j):
        at = slice(j * 2 * shard_rows, (j + 1) * 2 * shard_rows)
        return jnp.concatenate(
            [
                dot_left_t(normed_all[:, at], value_rows_grad),
                dot_left_t(grad_branch[:, at], mixed_low),
            ],
            axis=1,
        )

    qk_grad = scatter_ring(qk_chunk, False)
    vo_grad = scatter_ring(vo_chunk, True)

    grad_normed = sum_partials(
        dot_right_t(query_grad_low, query_full)
        + dot_right_t(key_all, key_full)
        + dot_right_t(value_all, value_full)
    )
    grad_features, attn_gain_grad, attn_shift_grad = layer_norm_back(
        features, attn_gain_o, grad_normed
    )
    input_grad = reorder((grad_hidden + grad_features).astype(LOW), back_order)

    up_bias_grad = jnp.concatenate([jnp.sum(g.astype(WIDE), axis=0) for g in grad_up])
    up_bias_both = jnp.concatenate(
        [
            jnp.where(first_core, up_bias_grad, 0.0),
            jnp.where(first_core, 0.0, up_bias_grad),
        ]
    )

    def sum_rows_axes(vector):
        vector = vector + to_core(vector)
        step = 1
        while step < sol_size:
            vector = vector + lax.ppermute(vector, "sol", [(i, i ^ step) for i in range(sol_size)])
            step *= 2
        step = 2
        while step < dp_size:
            vector = vector + lax.ppermute(vector, "dp", [(i, i ^ step) for i in range(dp_size)])
            step *= 2
        return vector

    early = sum_rows_axes(
        jnp.concatenate(
            [reorder_vector(v, back_order) for v in (mlp_gain_grad, mlp_shift_grad, down_bias_grad)]
            + [up_bias_both]
        )
    )
    late = sum_rows_axes(
        jnp.concatenate([reorder_vector(v, back_order) for v in (attn_gain_grad, attn_shift_grad)])
    )

    qk_low, qk_high = split_rows(qk_grad)
    vo_low, vo_high = split_rows(vo_grad)
    up_low, up_high = zip(*[split_rows(g) for g in up_grads])
    down_low, down_high = zip(*[split_rows(g) for g in down_grads])

    def both(low_cols, high_cols):
        return jnp.concatenate([low_cols, high_cols], axis=1)

    return (
        outputs,
        input_grad,
        late[:width],
        late[width:],
        both(qk_low[:, :head_cols], qk_high[:, :head_cols]),
        both(qk_low[:, head_cols:], qk_high[:, head_cols:]),
        both(vo_low[:, :head_cols], vo_high[:, :head_cols]),
        both(vo_low[:, head_cols:], vo_high[:, head_cols:]),
        early[:width],
        early[width : 2 * width],
        jnp.concatenate(up_low + up_high, axis=1),
        early[3 * width :],
        jnp.concatenate(down_low + down_high, axis=1),
        early[2 * width : 3 * width],
    )


def solution(mesh):
    rows = P(("dp", "sol"), None)
    matrix = P(("dp", "sol"), "tensor")
    return jax.shard_map(
        per_device,
        mesh=mesh,
        in_specs=(
            rows,
            rows,
            P(),
            P(),
            matrix,
            matrix,
            matrix,
            matrix,
            P(),
            P(),
            matrix,
            P("tensor"),
            matrix,
            P(),
            P(),
        ),
        out_specs=(
            rows,
            rows,
            P(),
            P(),
            matrix,
            matrix,
            matrix,
            matrix,
            P(),
            P(),
            matrix,
            P("tensor"),
            matrix,
            P(),
        ),
        check_vma=False,
    )
```

```python
import functools
import math

import jax
import jax.numpy as jnp
from jax import lax
from jax.experimental import pallas as pl
from jax.experimental.pallas import tpu as pltpu
from jax.sharding import PartitionSpec as P

HEAD_DIM = 128
EPSILON = 1e-05
NEG_FILL = -1e30
ROWS_AXES = ("dp", "sol")
LOW = jnp.bfloat16
WIDE = jnp.float32


def ring_place(position, sol_size):
    x, along = position // sol_size, position % sol_size
    return x, (along if x % 2 == 0 else sol_size - 1 - along)


def ring_pairs(dp_size, sol_size):
    count = dp_size // 2 * sol_size

    def flat(position, core):
        x, z = ring_place(position % count, sol_size)
        return (x * 2 + core) * sol_size + z

    places = [(q, c) for q in range(count) for c in range(2)]
    ahead = [(flat(q, c), flat(q + 1, c)) for q, c in places]
    back = [(b, a) for a, b in ahead]
    cores = [(flat(q, c), flat(q, 1 - c)) for q, c in places]
    return count, ahead, back, cores


def dot_plain(left_side, right_side):
    return jnp.dot(left_side, right_side, preferred_element_type=WIDE)


def dot_right_t(left_side, right_side):
    return lax.dot_general(
        left_side, right_side, (((1,), (1,)), ((), ())), preferred_element_type=WIDE
    )


def dot_left_t(left_side, right_side):
    return lax.dot_general(
        left_side, right_side, (((0,), (0,)), ((), ())), preferred_element_type=WIDE
    )


def norm_stats(features):
    row_mean = jnp.mean(features, axis=-1, keepdims=True)
    centered = features - row_mean
    variance = jnp.mean(centered * centered, axis=-1, keepdims=True)
    return row_mean, lax.rsqrt(variance + EPSILON)


def layer_norm(features, norm_gain, norm_shift):
    row_mean, inverse = norm_stats(features)
    return (features - row_mean) * inverse * norm_gain + norm_shift


def layer_norm_back(features, norm_gain, grad):
    row_mean, inverse = norm_stats(features)
    unit = (features - row_mean) * inverse
    scaled = grad * norm_gain
    along = jnp.mean(scaled * unit, axis=-1, keepdims=True)
    level = jnp.mean(scaled, axis=-1, keepdims=True)
    grad_features = (scaled - level - unit * along) * inverse
    return grad_features, jnp.sum(grad * unit, axis=0), jnp.sum(grad, axis=0)


def gelu_tanh(upward):
    return jax.nn.gelu(upward, approximate=True)


def copy_block(order_ref, in_ref, out_ref):
    out_ref[...] = in_ref[...]


def reorder(rows, order):
    blocks = order.shape[0]
    height, width = rows.shape
    part = width // blocks
    if part % 128:
        return jnp.take(rows.reshape(height, blocks, part), order, axis=1).reshape(height, width)
    return pl.pallas_call(
        copy_block,
        grid_spec=pltpu.PrefetchScalarGridSpec(
            num_scalar_prefetch=1,
            grid=(blocks,),
            in_specs=[pl.BlockSpec((height, part), lambda j, order_ref: (0, order_ref[j]))],
            out_specs=pl.BlockSpec((height, part), lambda j, order_ref: (0, j)),
        ),
        out_shape=jax.ShapeDtypeStruct(rows.shape, rows.dtype),
        cost_estimate=pl.CostEstimate(
            flops=0, bytes_accessed=4 * height * width, transcendentals=0
        ),
    )(order, rows)


MESH = pl.DeviceIdType.MESH
CHUNK = 256


def any_spec():
    return pl.BlockSpec(memory_space=pl.ANY)


def vmem_spec():
    return pl.BlockSpec(memory_space=pltpu.VMEM)


class Place:
    def __init__(self, dp_size, sol_size):
        self.sol_size = sol_size
        self.count = dp_size // 2 * sol_size
        dp, self.z = lax.axis_index("dp"), lax.axis_index("sol")
        self.y = lax.axis_index("tensor")
        self.x, self.core = dp // 2, dp % 2
        self.dp = dp
        turned = jnp.where(self.x % 2 == 0, self.z, sol_size - 1 - self.z)
        self.at = self.x * sol_size + turned
        self.next = self._chip((self.at + 1) % self.count)
        self.prev = self._chip((self.at + self.count - 1) % self.count)
        self.sibling = (dp + 1 - 2 * self.core, self.z, self.y)
        self.across = (dp, self.z, 1 - self.y)

    def _coords(self, position):
        x, turned = position // self.sol_size, position % self.sol_size
        return x, jnp.where(x % 2 == 0, turned, self.sol_size - 1 - turned)

    def _chip(self, position):
        x, z = self._coords(position)
        return (x * 2 + self.core, z, self.y)

    def along(self, step):
        return (self.dp, self.z + step, self.y)

    def blocks(self):
        result = []
        for j in range(self.count):
            x, z = self._coords((self.at + j) % self.count)
            result += [(x * 2) * self.sol_size + z, (x * 2 + 1) * self.sol_size + z]
        return result

    def greet(self):
        barrier = pltpu.get_barrier_semaphore()
        peers = (self.next, self.prev, self.sibling, self.across)
        for peer in peers:
            pl.semaphore_signal(barrier, inc=1, device_id=peer, device_id_type=MESH)
        pl.semaphore_wait(barrier, len(peers))


def remote(src, dst, send_sem, recv_sem, device):
    return pltpu.make_async_remote_copy(
        src_ref=src,
        dst_ref=dst,
        send_sem=send_sem,
        recv_sem=recv_sem,
        device_id=device,
        device_id_type=MESH,
    )


def norm_rows(values, gain, shift):
    row_mean = jnp.mean(values, axis=-1, keepdims=True)
    centered = values - row_mean
    variance = jnp.mean(centered * centered, axis=-1, keepdims=True)
    return centered * lax.rsqrt(variance + EPSILON) * gain + shift


def forward_kernel(
    dp_size,
    sol_size,
    x_ref,
    vectors_ref,
    up_bias_ref,
    live_ref,
    cot_hbm,
    query_ref,
    key_ref,
    value_ref,
    out_ref,
    up_ref,
    down_ref,
    weights,
    normed_out,
    cot_out,
    query_out,
    key_out,
    value_out,
    probs_out,
    mixed_out,
    hidden_out,
    normed_two_out,
    slope_out,
    active_out,
    w_v,
    normed_v,
    query_v,
    key_v,
    value_v,
    probs_v,
    mixed_v,
    hidden_v,
    normed_two_v,
    slope_v,
    active_v,
    core_send_v,
    core_recv_v,
    cross_send_v,
    cross_recv_v,
    ring_send,
    ring_recv,
    swap_local,
    swap_send,
    swap_recv,
    prefix_send,
    prefix_recv,
    pair_send,
    pair_recv,
    sum_send,
    sum_recv,
    cot_sem,
    load_sem,
    probs_sem,
    store_sem,
):
    here = Place(dp_size, sol_size)
    count, core = here.count, here.core
    rows, width = x_ref.shape
    prefix_v = slope_v
    shard = query_ref.shape[0]
    head_cols = query_ref.shape[1] // 2
    ff = up_ref.shape[1] // 2
    half = width // 2
    local_heads = head_cols // HEAD_DIM
    scale = 1.0 / math.sqrt(HEAD_DIM)
    blocks = here.blocks()
    far = count // 2
    own_class, other_class = core, 1 - core

    here.greet()

    def slot(j, which):
        return pl.ds(pl.multiple_of((2 * j + which) * shard, shard), shard)

    shards = (
        (0, 0, query_ref, head_cols),
        (0, head_cols, key_ref, head_cols),
        (0, 2 * head_cols, value_ref, head_cols),
        (0, 3 * head_cols, out_ref, head_cols),
        (1, 0, up_ref, ff),
        (2, 0, down_ref, ff),
    )

    def swap_copies(i):
        matrix, start, source, size = shards[i]
        target = weights.at[matrix, slot(0, own_class), pl.ds(start, size)]

        def columns(which):
            return source.at[:, pl.ds(pl.multiple_of(which * size, size), size)]

        return (
            pltpu.make_async_copy(columns(core), target, swap_local.at[i]),
            remote(columns(1 - core), target, swap_send.at[i], swap_recv.at[i], here.sibling),
        )

    def start_swap(matrix):
        for i in range(len(shards)):
            if shards[i][0] == matrix:
                for copy in swap_copies(i):
                    copy.start()

    def hops(matrix, k, sub):
        which = own_class if sub == 0 else other_class
        ahead_cols = pl.ds(0, half if k == far else width)
        back_cols = pl.ds(half if k == far else 0, half if k == far else width)
        return (
            remote(
                weights.at[matrix, slot((count - k + 1) % count, which), ahead_cols],
                weights.at[matrix, slot(count - k, which), ahead_cols],
                ring_send.at[matrix, 0, k - 1, sub],
                ring_recv.at[matrix, 0, k - 1, sub],
                here.next,
            ),
            remote(
                weights.at[matrix, slot(k - 1, which), back_cols],
                weights.at[matrix, slot(k, which), back_cols],
                ring_send.at[matrix, 1, k - 1, sub],
                ring_recv.at[matrix, 1, k - 1, sub],
                here.prev,
            ),
        )

    def start_ring(matrix, sub):
        for i in range(len(shards)):
            if shards[i][0] == matrix:
                if sub == 0:
                    swap_copies(i)[0].wait()
                else:
                    swap_copies(i)[1].wait_recv()
        for copy in hops(matrix, 1, sub):
            copy.start()

    def pump(matrix, k, sub):
        came = hops(matrix, k, sub)
        if k < far:
            further = hops(matrix, k + 1, sub)
        for i in range(2):
            came[i].wait_recv()
            if k < far:
                further[i].start()
        if k == far - 1 and matrix < 2:
            start_ring(matrix + 1, sub)

    steps = [
        (matrix, k, sub) for matrix in range(3) for k in range(1, far + 1) for sub in range(2)
    ]
    done = [0]

    def pump_to(number):
        while done[0] < min(number, len(steps)):
            pump(*steps[done[0]])
            done[0] += 1

    y_rows = rows // 2
    part = y_rows // 2

    def prefix_rows(which_half, i):
        return pl.ds(pl.multiple_of(which_half * y_rows + i * part, part), part)

    def prefix_hop(i, from_input):
        at = prefix_rows(here.y, i)
        return remote(
            x_ref.at[at] if from_input else prefix_v.at[at],
            prefix_v.at[at],
            prefix_send.at[0, i],
            prefix_recv.at[0, i],
            here.along(1),
        )

    def prefix_cross(i, from_input):
        at = prefix_rows(here.y, i)
        return remote(
            x_ref.at[at] if from_input else prefix_v.at[at],
            prefix_v.at[at],
            prefix_send.at[1, i],
            prefix_recv.at[1, i],
            here.across,
        )

    def prefix_stage(stage, i):
        @pl.when(here.z == stage)
        def _():
            if stage == 0:
                prefix_hop(i, True).start()
                prefix_cross(i, True).start()
            else:
                prefix_hop(i, False).wait_recv()
                if stage < sol_size - 1:
                    prefix_hop(i, False).start()
                prefix_cross(i, False).start()

    def prefix_finish():
        for i in range(2):
            prefix_cross(i, False).wait_recv()

        @pl.when(here.z == 0)
        def _():
            for i in range(2):
                at = prefix_rows(here.y, i)
                prefix_v[at, :] = x_ref[at, :]

    cot_load = pltpu.make_async_copy(cot_hbm, active_v.at[pl.ds(0, rows)], cot_sem.at[1])
    start_swap(0)
    for i in range(2):
        prefix_stage(0, i)
    start_swap(1)
    start_swap(2)
    cot_load.start()

    start_ring(0, 0)
    start_ring(0, 1)

    def ordered(ref, at):
        return jnp.concatenate(
            [ref[at, pl.ds(pl.multiple_of(b * shard, shard), shard)] for b in blocks], axis=1
        ).astype(WIDE)

    gain, shift = vectors_ref[0:1, :], vectors_ref[1:2, :]
    gain_two, shift_two = vectors_ref[2:3, :], vectors_ref[3:4, :]

    def norm_into(ref, start):
        @pl.loop(0, rows // 128)
        def _(t):
            at = pl.ds(pl.multiple_of(t * 128, 128), 128)
            to = pl.ds(pl.multiple_of(start + t * 128, 128), 128)
            normed_v[to, :] = norm_rows(ordered(ref, at), gain, shift).astype(LOW)

    normed_pair = remote(
        normed_v.at[pl.ds(0, rows)],
        normed_v.at[pl.ds(rows, rows)],
        pair_send.at[1],
        pair_recv.at[1],
        here.sibling,
    )
    prefix_pair = remote(
        normed_v.at[pl.ds(2 * rows, rows)],
        normed_v.at[pl.ds(3 * rows, rows)],
        pair_send.at[2],
        pair_recv.at[2],
        here.sibling,
    )
    norm_into(x_ref, 0)
    normed_pair.start()
    pump_to(1)
    for stage in range(1, sol_size + 1):
        if stage < sol_size:
            prefix_stage(stage, 0)
        if stage > 1:
            prefix_stage(stage - 1, 1)
        pump_to(1 + stage)
    pump_to(2 * far)

    cot_pair = remote(
        core_send_v,
        cot_out.at[pl.ds(rows, rows)],
        pair_send.at[0],
        pair_recv.at[0],
        here.sibling,
    )
    cot_own = pltpu.make_async_copy(core_send_v, cot_out.at[pl.ds(0, rows)], cot_sem.at[0])

    cot_load.wait()

    @pl.loop(0, rows // 128)
    def _(t):
        at = pl.ds(pl.multiple_of(t * 128, 128), 128)
        core_send_v[at, :] = ordered(active_v, at).astype(LOW)

    cot_pair.start()
    cot_own.start()

    load_first = pltpu.make_async_copy(weights.at[0], w_v, load_sem.at[0])
    load_first.start()
    normed_pair.wait_recv()
    load_first.wait()

    def row_tile(t):
        return pl.ds(pl.multiple_of(t * CHUNK, CHUNK), CHUNK)

    def project(first, last, with_queries):
        @pl.loop(first, last)
        def _(t):
            at = row_tile(t)
            tile = normed_v[at, :]
            kv = dot_plain(tile, w_v[:, head_cols : 3 * head_cols])
            key_v[at, :] = kv[:, :head_cols].astype(LOW)
            value_v[at, :] = kv[:, head_cols:].astype(LOW)
            if with_queries:
                query_v[at, :] = dot_plain(tile, w_v[:, :head_cols]).astype(LOW)

    tiles = rows // CHUNK
    project(0, 2 * tiles, True)
    pump_to(2 * far + 1)
    prefix_finish()
    norm_into(prefix_v, 2 * rows)
    prefix_pair.start()
    pump_to(2 * far + 2)
    prefix_pair.wait_recv()
    project(2 * tiles, 4 * tiles, False)
    pump_to(2 * far + 3)

    stores = []

    def store(src, dst):
        copy = pltpu.make_async_copy(src, dst, store_sem.at[len(stores)])
        copy.start()
        stores.append(copy)

    store(normed_v, normed_out)
    store(query_v, query_out)
    store(key_v, key_out)
    store(value_v, value_out)

    def probs_copy(unit):
        return pltpu.make_async_copy(
            probs_v.at[unit % 2], probs_out.at[unit], probs_sem.at[unit % 2]
        )

    def attend(unit):
        block, head = unit // local_heads, unit % local_heads
        cols = pl.ds(pl.multiple_of(head * HEAD_DIM, HEAD_DIM), HEAD_DIM)
        place = jnp.where(block == 0, here.dp, here.dp + 1 - 2 * core)
        own_live = live_ref[place * sol_size + here.z]
        prefix_live = jnp.where(here.z == 0, 0, live_ref[place * sol_size])
        own_at = pl.ds(pl.multiple_of(block * rows, rows), rows)
        prefix_at = pl.ds(pl.multiple_of((2 + block) * rows, rows), rows)

        @pl.when(unit >= 2)
        def _():
            probs_copy(unit - 2).wait()

        for t in range(tiles):
            at = pl.ds(pl.multiple_of(block * rows + t * CHUNK, CHUNK), CHUNK)
            queries = query_v[at, cols]
            col = lax.broadcasted_iota(jnp.int32, (CHUNK, rows), 1)
            row = lax.broadcasted_iota(jnp.int32, (CHUNK, rows), 0) + t * CHUNK
            first = dot_right_t(queries, key_v[prefix_at, cols]) * scale
            second = dot_right_t(queries, key_v[own_at, cols]) * scale
            first = jnp.where(col < prefix_live, first, NEG_FILL)
            second = jnp.where(
                jnp.logical_and(col <= row, col < own_live), second, NEG_FILL
            )
            peak = jnp.maximum(
                jnp.max(first, axis=-1, keepdims=True), jnp.max(second, axis=-1, keepdims=True)
            )
            first = jnp.exp(first - peak)
            second = jnp.exp(second - peak)
            total = jnp.sum(first, axis=-1, keepdims=True) + jnp.sum(
                second, axis=-1, keepdims=True
            )
            inverse = 1.0 / total
            first = (first * inverse).astype(LOW)
            second = (second * inverse).astype(LOW)
            probs_v[unit % 2, pl.ds(t * CHUNK, CHUNK), pl.ds(0, rows)] = first
            probs_v[unit % 2, pl.ds(t * CHUNK, CHUNK), pl.ds(rows, rows)] = second
            mixed_v[at, cols] = (
                dot_plain(first, value_v[prefix_at, cols])
                + dot_plain(second, value_v[own_at, cols])
            ).astype(LOW)
        probs_copy(unit).start()

    units = 2 * local_heads
    for quarter in range(4):
        pl.loop(quarter * units // 4, (quarter + 1) * units // 4)(attend)
        pump_to(2 * far + 4 + quarter)
    for unit in (units - 2, units - 1):
        probs_copy(unit).wait()
    store(mixed_v, mixed_out)

    out_cols = slice(3 * head_cols, 4 * head_cols)

    def core_copy(t):
        at = pl.ds(t * CHUNK, CHUNK)
        return remote(
            core_send_v.at[at], core_recv_v.at[at], sum_send.at[0, t], sum_recv.at[0, t], here.sibling
        )

    def cross_copy(t):
        at = pl.ds(t * CHUNK, CHUNK)
        return remote(
            cross_send_v.at[at], cross_recv_v.at[at], sum_send.at[1, t], sum_recv.at[1, t], here.across
        )

    def two_copy(t):
        return remote(
            normed_two_v.at[pl.ds(t * CHUNK, CHUNK)],
            normed_two_v.at[pl.ds(rows + t * CHUNK, CHUNK)],
            sum_send.at[2, t],
            sum_recv.at[2, t],
            here.sibling,
        )

    def hidden_store(t):
        return pltpu.make_async_copy(
            hidden_v, hidden_out.at[pl.ds(t * CHUNK, CHUNK)], load_sem.at[1]
        )

    cot_own.wait()
    cot_pair.wait_send()
    for t in range(tiles):
        core_send_v[pl.ds(t * CHUNK, CHUNK), :] = dot_right_t(
            mixed_v[pl.ds(rows + t * CHUNK, CHUNK), :], w_v[:, out_cols]
        ).astype(LOW)
        core_copy(t).start()
    for t in range(tiles):
        at = pl.ds(t * CHUNK, CHUNK)
        partial = dot_right_t(mixed_v[at, :], w_v[:, out_cols])
        core_copy(t).wait_recv()
        cross_send_v[at, :] = (partial + core_recv_v[at, :].astype(WIDE)).astype(LOW)
        cross_copy(t).start()
    pump_to(4 * far)
    load_second = pltpu.make_async_copy(weights.at[1], w_v, load_sem.at[0])
    load_second.start()
    for t in range(tiles):
        at = pl.ds(t * CHUNK, CHUNK)
        cross_copy(t).wait_recv()
        hidden = (
            ordered(x_ref, at)
            + cross_send_v[at, :].astype(WIDE)
            + cross_recv_v[at, :].astype(WIDE)
        )
        if t > 0:
            hidden_store(t - 1).wait()
        hidden_v[...] = hidden
        hidden_store(t).start()
        normed_two_v[at, :] = norm_rows(hidden, gain_two, shift_two).astype(LOW)
        two_copy(t).start()
    hidden_store(tiles - 1).wait()
    load_second.wait()
    for t in range(tiles):
        two_copy(t).wait_recv()
    pump_to(4 * far + 1)
    store(normed_two_v, normed_two_out)

    bend = math.sqrt(2.0 / math.pi)
    spans = ff // half

    def feed(i):
        at = row_tile(i // spans)
        cols = pl.ds(pl.multiple_of((i % spans) * half, half), half)
        upward = dot_plain(normed_two_v[at, :], w_v[:, cols]) + up_bias_ref[:, cols]
        square = upward * upward
        curve = jnp.tanh(bend * (upward + 0.044715 * (upward * square)))
        active_v[at, cols] = (0.5 * upward * (1.0 + curve)).astype(LOW)
        slope_v[at, cols] = (
            0.5 * (1.0 + curve)
            + 0.5 * upward * (1.0 - curve * curve) * (bend + (3.0 * 0.044715 * bend) * square)
        ).astype(LOW)

    for i in range(2):

        @pl.when(here.z < sol_size - 1)
        def _():
            prefix_hop(i, False).wait_send()

        prefix_cross(i, False).wait_send()

    feeds = 2 * tiles * spans
    for quarter in range(4):
        pl.loop(quarter * feeds // 4, (quarter + 1) * feeds // 4)(feed)
        pump_to(4 * far + 2 + quarter)
    store(active_v, active_out)
    store(slope_v, slope_out)

    pump_to(len(steps))
    cot_pair.wait_recv()
    normed_pair.wait_send()
    prefix_pair.wait_send()
    for i in range(len(shards)):
        swap_copies(i)[1].wait_send()
    for step in steps:
        for copy in hops(*step):
            copy.wait_send()
    for t in range(tiles):
        core_copy(t).wait_send()
        cross_copy(t).wait_send()
        two_copy(t).wait_send()
    for copy in stores:
        copy.wait()


def run_forward(dp_size, sol_size, x, vectors, up_bias, live_rows, cot, matrices):
    rows, width = x.shape
    head_cols = matrices[0].shape[1] // 2
    ff = matrices[4].shape[1] // 2
    heads = head_cols // HEAD_DIM
    count = dp_size // 2 * sol_size
    far = count // 2

    def shape(*dims, dtype=LOW):
        return jax.ShapeDtypeStruct(dims, dtype)

    outs = [
        shape(3, width, width),
        shape(4 * rows, width),
        shape(2 * rows, width),
        shape(2 * rows, head_cols),
        shape(4 * rows, head_cols),
        shape(4 * rows, head_cols),
        shape(2 * heads, rows, 2 * rows),
        shape(2 * rows, head_cols),
        shape(rows, width, dtype=WIDE),
        shape(2 * rows, width),
        shape(2 * rows, ff),
        shape(2 * rows, ff),
    ]
    dma = pltpu.SemaphoreType.DMA
    return pl.pallas_call(
        functools.partial(forward_kernel, dp_size, sol_size),
        out_shape=outs,
        in_specs=[
            vmem_spec(),
            vmem_spec(),
            vmem_spec(),
            pl.BlockSpec(memory_space=pltpu.SMEM),
        ]
        + [any_spec()]
        + [vmem_spec()] * 6,
        out_specs=[any_spec()] * len(outs),
        scratch_shapes=[
            pltpu.VMEM((width, width), LOW),
            pltpu.VMEM((4 * rows, width), LOW),
            pltpu.VMEM((2 * rows, head_cols), LOW),
            pltpu.VMEM((4 * rows, head_cols), LOW),
            pltpu.VMEM((4 * rows, head_cols), LOW),
            pltpu.VMEM((2, rows, 2 * rows), LOW),
            pltpu.VMEM((2 * rows, head_cols), LOW),
            pltpu.VMEM((CHUNK, width), WIDE),
            pltpu.VMEM((2 * rows, width), LOW),
            pltpu.VMEM((2 * rows, ff), LOW),
            pltpu.VMEM((2 * rows, ff), LOW),
        ]
        + [pltpu.VMEM((rows, width), LOW)] * 4
        + [
            dma((3, 2, far, 2)),
            dma((3, 2, far, 2)),
            dma((6,)),
            dma((6,)),
            dma((6,)),
            dma((2, 2)),
            dma((2, 2)),
            dma((3,)),
            dma((3,)),
            dma((3, rows // CHUNK)),
            dma((3, rows // CHUNK)),
            dma((2,)),
            dma((2,)),
            dma((2,)),
            dma((16,)),
        ],
        compiler_params=pltpu.CompilerParams(
            collective_id=0, has_side_effects=True, vmem_limit_bytes=60 * 2**20
        ),
    )(x, vectors, up_bias, live_rows, cot, *matrices)


class RingSum:
    def __init__(self, here, chunk, send_v, recv_v, stage_v, sems, target):
        self.here, self.chunk = here, chunk
        self.send_v, self.recv_v, self.stage_v = send_v, recv_v, stage_v
        self.send_sem, self.recv_sem, self.end_sem = sems
        self.target = target
        self.far = here.count // 2
        self.cols = stage_v.shape[2]
        self.steps = [(t, sub) for t in range(1, self.far + 1) for sub in range(2)]
        self.done = 0

    def _class(self, sub):
        return self.here.core if sub == 0 else 1 - self.here.core

    def _columns(self, t, way):
        if t > 1:
            return pl.ds(0, self.cols)
        return pl.ds(way * (self.cols // 2), self.cols // 2)

    def _copy(self, t, way, sub):
        at = self._columns(t, way)
        return remote(
            self.send_v.at[way, sub, :, at],
            self.recv_v.at[(t - 1) % 3, way, sub, :, at],
            self.send_sem.at[t - 1, way, sub],
            self.recv_sem.at[t - 1, way, sub],
            self.here.prev if way else self.here.next,
        )

    def _event(self, t, sub):
        far, count = self.far, self.here.count
        half = self.cols // 2
        if t == 1:
            value = self.chunk(far, self._class(sub))
            self.send_v[0, sub, :, :half] = value[:, :half].astype(LOW)
            self.send_v[1, sub, :, half:] = value[:, half:].astype(LOW)
            for way in range(2):
                self._copy(1, way, sub).start()
            return
        for way in range(2):
            j = far + 1 - t if way == 0 else count - (far + 1 - t)
            value = self.chunk(j, self._class(sub))
            self._copy(t - 1, way, sub).wait()
            if t == 2:
                near = slice(0, half) if way == 0 else slice(half, 2 * half)
                rest = slice(half, 2 * half) if way == 0 else slice(0, half)
                self.send_v[way, sub, :, near] = (
                    value[:, near] + self.recv_v[0, way, sub, :, near].astype(WIDE)
                ).astype(LOW)
                self.send_v[way, sub, :, rest] = value[:, rest].astype(LOW)
            else:
                self.send_v[way, sub] = (
                    value + self.recv_v[(t - 2) % 3, way, sub].astype(WIDE)
                ).astype(LOW)
            self._copy(t, way, sub).start()

    def _last(self, sub):
        value = self.chunk(0, self._class(sub))
        for way in range(2):
            self._copy(self.far, way, sub).wait()
        value = value + self.recv_v[(self.far - 1) % 3, 0, sub].astype(WIDE)
        self.stage_v[sub] = value + self.recv_v[(self.far - 1) % 3, 1, sub].astype(WIDE)
        for copy in self._results(sub):
            copy.start()

    def _results(self, sub):
        copies = []
        core = self.here.core
        for i, (ref, start, size) in enumerate(self.target):
            to = ref.at[:, pl.ds(pl.multiple_of(core * size, size), size)]
            source = self.stage_v.at[sub, :, pl.ds(start, size)]
            if sub == 0:
                copies.append(pltpu.make_async_copy(source, to, self.end_sem.at[0, i]))
            else:
                copies.append(
                    remote(
                        source, to, self.end_sem.at[1, i], self.end_sem.at[2, i], self.here.sibling
                    )
                )
        return copies

    def to(self, number):
        while self.done < min(number, len(self.steps) + 2):
            if self.done < len(self.steps):
                self._event(*self.steps[self.done])
            else:
                self._last(self.done - len(self.steps))
            self.done += 1

    def finish(self):
        self.to(len(self.steps) + 2)
        for sub in range(2):
            for copy in self._results(sub):
                copy.wait()


def ring_sum_scratch(far, shard, cols, results):
    dma = pltpu.SemaphoreType.DMA
    return [
        pltpu.VMEM((2, 2, shard, cols), LOW),
        pltpu.VMEM((3, 2, 2, shard, cols), LOW),
        pltpu.VMEM((2, shard, cols), WIDE),
        dma((far, 2, 2)),
        dma((far, 2, 2)),
        dma((3, results)),
    ]


def norm_back(values, gain, grad):
    row_mean = jnp.mean(values, axis=-1, keepdims=True)
    centered = values - row_mean
    variance = jnp.mean(centered * centered, axis=-1, keepdims=True)
    inverse = lax.rsqrt(variance + EPSILON)
    unit = centered * inverse
    scaled = grad * gain
    terms = grad * unit
    along = jnp.mean(scaled * unit, axis=-1, keepdims=True)
    level = jnp.mean(scaled, axis=-1, keepdims=True)
    return (
        (scaled - level - unit * along) * inverse,
        jnp.sum(terms, axis=0, keepdims=True),
        jnp.sum(grad, axis=0, keepdims=True),
    )


def tile_rows(t):
    return pl.ds(t * CHUNK, CHUNK)


def down_kernel(
    dp_size,
    sol_size,
    vectors_ref,
    weights,
    cot_hbm,
    active_hbm,
    slope_hbm,
    hidden_hbm,
    grad_up_out,
    branch_out,
    grad_hidden_out,
    mlp_low_out,
    down_grad_out,
    sums_ref,
    cot_v,
    active_v,
    slope_v,
    down_v,
    up_v,
    hidden_v,
    core_send_v,
    core_recv_v,
    second_recv_v,
    cross_send_v,
    cross_recv_v,
    ring_send_v,
    ring_recv_v,
    stage_v,
    ring_send,
    ring_recv,
    ring_end,
    load_sem,
    store_sem,
    sum_send,
    sum_recv,
):
    here = Place(dp_size, sol_size)
    rows, width = core_send_v.shape
    shard = stage_v.shape[1]
    ff = active_v.shape[1]
    tiles = rows // CHUNK
    halves = (pl.ds(0, width // 2), pl.ds(width // 2, width // 2))
    loads = [
        pltpu.make_async_copy(src, dst, load_sem.at[i])
        for i, (src, dst) in enumerate(
            (
                (cot_hbm, cot_v),
                (active_hbm, active_v),
                (weights.at[2], down_v),
                (slope_hbm, slope_v),
                (weights.at[1], up_v),
            )
        )
    ]
    for copy in loads:
        copy.start()
    here.greet()

    def chunk(j, which):
        at = pl.ds(pl.multiple_of((2 * j + which) * shard, shard), shard)
        return dot_left_t(cot_v[:, at], active_v[...])

    ring = RingSum(
        here,
        chunk,
        ring_send_v,
        ring_recv_v,
        stage_v,
        (ring_send, ring_recv, ring_end),
        ((down_grad_out, 0, ff),),
    )
    loads[0].wait()
    loads[1].wait()
    ring.to(2)
    loads[2].wait()
    loads[3].wait()

    sums_ref[...] = jnp.zeros_like(sums_ref)
    spans = 2

    def back_feed(i):
        at = pl.ds(pl.multiple_of(i // spans * CHUNK, CHUNK), CHUNK)
        cols = pl.ds(pl.multiple_of(i % spans * (ff // spans), ff // spans), ff // spans)
        grad = dot_plain(cot_v[at, :], down_v[:, cols]) * slope_v[at, cols].astype(WIDE)
        low = grad.astype(LOW)
        slope_v[at, cols] = low
        sums_ref[3:4, cols] += jnp.sum(low.astype(WIDE), axis=0, keepdims=True)

    pl.loop(0, tiles * spans)(back_feed)
    ring.to(3)
    pl.loop(tiles * spans, 2 * tiles * spans)(back_feed)
    ring.to(4)
    loads[4].wait()
    stores = [pltpu.make_async_copy(slope_v, grad_up_out, store_sem.at[0])]
    stores[0].start()

    def core_copy(t):
        return remote(
            core_send_v.at[tile_rows(t)],
            core_recv_v.at[tile_rows(t)],
            sum_send.at[0, t],
            sum_recv.at[0, t],
            here.sibling,
        )

    def cross_copy(t):
        return remote(
            cross_send_v.at[tile_rows(t)],
            cross_recv_v.at[tile_rows(t)],
            sum_send.at[1, t],
            sum_recv.at[1, t],
            here.across,
        )

    def second_copy(t):
        return remote(
            core_send_v.at[tile_rows(t)],
            second_recv_v.at[tile_rows(t)],
            sum_send.at[2, t],
            sum_recv.at[2, t],
            here.sibling,
        )

    def branch_copy(t):
        return remote(
            core_recv_v.at[tile_rows(t)],
            branch_out.at[pl.ds(rows + t * CHUNK, CHUNK)],
            sum_send.at[3, t],
            sum_recv.at[3, t],
            here.sibling,
        )

    for t in range(tiles):
        for cols in halves:
            core_send_v[tile_rows(t), cols] = dot_right_t(
                slope_v[pl.ds(rows + t * CHUNK, CHUNK), :], up_v[cols, :]
            ).astype(LOW)
        core_copy(t).start()
    for t in range(tiles):
        at = tile_rows(t)
        core_copy(t).wait_recv()
        for cols in halves:
            cross_send_v[at, cols] = (
                dot_right_t(slope_v[at, :], up_v[cols, :]) + core_recv_v[at, cols].astype(WIDE)
            ).astype(LOW)
        cross_copy(t).start()
    ring.to(5)

    for t in range(tiles):
        core_copy(t).wait_send()
        for cols in halves:
            core_send_v[tile_rows(t), cols] = dot_right_t(
                active_v[pl.ds(rows + t * CHUNK, CHUNK), :], down_v[cols, :]
            ).astype(LOW)
        second_copy(t).start()
    ring.to(6)
    for t in range(tiles):
        at = tile_rows(t)
        second_copy(t).wait_recv()
        for cols in halves:
            second_recv_v[at, cols] = (
                dot_right_t(active_v[at, :], down_v[cols, :])
                + second_recv_v[at, cols].astype(WIDE)
            ).astype(LOW)
    stores.append(pltpu.make_async_copy(second_recv_v, mlp_low_out, store_sem.at[1]))
    stores[1].start()
    ring.to(8)

    gain = vectors_ref[2:3, :]

    def hidden_load(t):
        return pltpu.make_async_copy(hidden_hbm.at[tile_rows(t)], hidden_v, load_sem.at[0])

    def hidden_store(t):
        return pltpu.make_async_copy(hidden_v, grad_hidden_out.at[tile_rows(t)], store_sem.at[2])

    hidden_load(0).start()
    for t in range(tiles):
        at = tile_rows(t)
        hidden_load(t).wait()
        cross_copy(t).wait_recv()
        for part in range(2):
            inner = pl.ds(part * (CHUNK // 2), CHUNK // 2)
            here_at = pl.ds(t * CHUNK + part * (CHUNK // 2), CHUNK // 2)
            grad = cross_send_v[here_at, :].astype(WIDE) + cross_recv_v[here_at, :].astype(WIDE)
            back, gain_terms, shift_terms = norm_back(hidden_v[inner, :], gain, grad)
            cot = cot_v[here_at, :].astype(WIDE)
            sums_ref[0:1, :] += gain_terms
            sums_ref[1:2, :] += shift_terms
            sums_ref[2:3, :] += jnp.sum(cot, axis=0, keepdims=True)
            back = back + cot
            hidden_v[inner, :] = back
            core_recv_v[here_at, :] = back.astype(LOW)
        branch_copy(t).start()
        hidden_store(t).start()
        if t == 0:
            ring.to(9)
        hidden_store(t).wait()
        if t + 1 < tiles:
            hidden_load(t + 1).start()
    stores.append(
        pltpu.make_async_copy(core_recv_v, branch_out.at[pl.ds(0, rows)], store_sem.at[3])
    )
    stores[2].start()
    ring.finish()
    for t in range(tiles):
        cross_copy(t).wait_send()
        second_copy(t).wait_send()
        branch_copy(t).wait()
    for copy in stores:
        copy.wait()


def run_down(dp_size, sol_size, shard, vectors, weights, cot, active, slope, hidden):
    rows, width = hidden.shape
    ff = active.shape[1]
    count = dp_size // 2 * sol_size
    tiles = rows // CHUNK
    dma = pltpu.SemaphoreType.DMA

    def shape(*dims, dtype=LOW):
        return jax.ShapeDtypeStruct(dims, dtype)

    outs = [
        shape(2 * rows, ff),
        shape(2 * rows, width),
        shape(rows, width, dtype=WIDE),
        shape(rows, width),
        shape(shard, 2 * ff, dtype=WIDE),
        shape(8, width, dtype=WIDE),
    ]
    return pl.pallas_call(
        functools.partial(down_kernel, dp_size, sol_size),
        out_shape=outs,
        in_specs=[vmem_spec()] + [any_spec()] * 5,
        out_specs=[any_spec()] * 5 + [vmem_spec()],
        scratch_shapes=[
            pltpu.VMEM((2 * rows, width), LOW),
            pltpu.VMEM((2 * rows, ff), LOW),
            pltpu.VMEM((2 * rows, ff), LOW),
            pltpu.VMEM((width, ff), LOW),
            pltpu.VMEM((width, ff), LOW),
            pltpu.VMEM((CHUNK, width), WIDE),
        ]
        + [pltpu.VMEM((rows, width), LOW)] * 5
        + ring_sum_scratch(count // 2, shard, ff, 1)
        + [
            dma((5,)),
            dma((4,)),
            dma((4, tiles)),
            dma((4, tiles)),
        ],
        compiler_params=pltpu.CompilerParams(
            collective_id=1, has_side_effects=True, vmem_limit_bytes=60 * 2**20
        ),
    )(vectors, weights, cot, active, slope, hidden)


def read_ordered(ref, at, blocks, part):
    return jnp.concatenate(
        [ref[at, pl.ds(pl.multiple_of(b * part, part), part)] for b in blocks], axis=1
    ).astype(WIDE)


def write_ordered(ref, at, blocks, part, values):
    for j, b in enumerate(blocks):
        ref[at, pl.ds(pl.multiple_of(b * part, part), part)] = values[
            :, j * part : (j + 1) * part
        ].astype(ref.dtype)


def attend_back_kernel(
    dp_size,
    sol_size,
    vectors_ref,
    weights,
    normed_two_hbm,
    grad_up_hbm,
    branch_hbm,
    query_hbm,
    key_hbm,
    value_hbm,
    probs_hbm,
    mlp_low_hbm,
    hidden_hbm,
    query_grad_out,
    kv_grad_out,
    own_low_out,
    prefix_half_out,
    up_grad_out,
    outputs_out,
    mlp_recv_out,
    normed_two_v,
    grad_up_v,
    branch_v,
    w_v,
    query_v,
    key_v,
    value_v,
    mixed_grad_v,
    probs_v,
    query_grad_v,
    kv_grad_v,
    core_recv_v,
    second_recv_v,
    half_recv_v,
    mlp_low_v,
    mlp_recv_v,
    hidden_v,
    ring_send_v,
    ring_recv_v,
    stage_v,
    ring_send,
    ring_recv,
    ring_end,
    load_sem,
    probs_sem,
    tile_sem,
    store_sem,
    sum_send,
    sum_recv,
    cross_send,
    cross_recv,
):
    here = Place(dp_size, sol_size)
    rows, width = core_recv_v.shape
    core_send_v = branch_v.at[pl.ds(0, rows)]
    half_send_v = branch_v.at[pl.ds(rows, CHUNK)]
    half_keep_v = branch_v.at[pl.ds(rows + CHUNK, CHUNK)]
    shard = stage_v.shape[1]
    ff = grad_up_v.shape[1]
    head_cols = query_v.shape[1]
    local_heads = head_cols // HEAD_DIM
    scale = 1.0 / math.sqrt(HEAD_DIM)
    tiles = rows // CHUNK
    blocks = here.blocks()
    halves = (pl.ds(0, width // 2), pl.ds(width // 2, width // 2))
    loads = [
        pltpu.make_async_copy(src, dst, load_sem.at[i])
        for i, (src, dst) in enumerate(
            (
                (normed_two_hbm, normed_two_v),
                (grad_up_hbm, grad_up_v),
                (branch_hbm, branch_v),
                (weights.at[0], w_v),
                (query_hbm, query_v),
                (key_hbm, key_v),
                (value_hbm, value_v),
            )
        )
    ]
    for copy in loads:
        copy.start()

    def probs_load(unit):
        return pltpu.make_async_copy(
            probs_hbm.at[unit], probs_v.at[unit % 2], probs_sem.at[unit % 2]
        )

    probs_load(0).start()
    here.greet()
    mlp_cross = remote(
        mlp_low_hbm, mlp_recv_out, cross_send.at[0], cross_recv.at[0], here.across
    )
    mlp_cross.start()

    def chunk(j, which):
        at = pl.ds(pl.multiple_of((2 * j + which) * shard, shard), shard)
        return dot_left_t(normed_two_v[:, at], grad_up_v[...])

    ring = RingSum(
        here,
        chunk,
        ring_send_v,
        ring_recv_v,
        stage_v,
        (ring_send, ring_recv, ring_end),
        ((up_grad_out, 0, ff),),
    )
    loads[0].wait()
    loads[1].wait()
    ring.to(2)
    loads[2].wait()
    loads[3].wait()

    @pl.loop(0, 2 * tiles)
    def _(t):
        at = pl.ds(pl.multiple_of(t * CHUNK, CHUNK), CHUNK)
        mixed_grad_v[at, :] = dot_plain(
            branch_v[at, :], w_v[:, 3 * head_cols : 4 * head_cols]
        ).astype(LOW)

    for i in range(4, 7):
        loads[i].wait()

    units = 2 * local_heads

    def back(unit):
        block, head = unit // local_heads, unit % local_heads
        cols = pl.ds(pl.multiple_of(head * HEAD_DIM, HEAD_DIM), HEAD_DIM)
        value_cols = pl.ds(
            pl.multiple_of(head_cols + head * HEAD_DIM, HEAD_DIM), HEAD_DIM
        )
        own_at = pl.ds(pl.multiple_of(block * rows, rows), rows)
        prefix_at = pl.ds(pl.multiple_of((2 + block) * rows, rows), rows)
        probs_load(unit).wait()

        @pl.when(unit + 1 < units)
        def _():
            probs_load(unit + 1).start()

        sums = None
        for t in range(tiles):
            at = pl.ds(pl.multiple_of(block * rows + t * CHUNK, CHUNK), CHUNK)
            grad = mixed_grad_v[at, cols]
            queries = query_v[at, cols]
            inner = pl.ds(t * CHUNK, CHUNK)
            first_low = probs_v[unit % 2, inner, pl.ds(0, rows)]
            second_low = probs_v[unit % 2, inner, pl.ds(rows, rows)]
            first, second = first_low.astype(WIDE), second_low.astype(WIDE)
            first_grad = dot_right_t(grad, value_v[prefix_at, cols])
            second_grad = dot_right_t(grad, value_v[own_at, cols])
            delta = jnp.sum(first * first_grad, axis=-1, keepdims=True) + jnp.sum(
                second * second_grad, axis=-1, keepdims=True
            )
            first_scores = (first * (first_grad - delta)).astype(LOW)
            second_scores = (second * (second_grad - delta)).astype(LOW)
            query_grad_v[at, cols] = (
                (
                    dot_plain(first_scores, key_v[prefix_at, cols])
                    + dot_plain(second_scores, key_v[own_at, cols])
                )
                * scale
            ).astype(LOW)
            terms = [
                dot_left_t(second_scores, queries),
                dot_left_t(second_low, grad),
                dot_left_t(first_scores, queries),
                dot_left_t(first_low, grad),
            ]
            sums = terms if sums is None else [a + b for a, b in zip(sums, terms)]
        kv_grad_v[own_at, cols] = (sums[0] * scale).astype(LOW)
        kv_grad_v[own_at, value_cols] = sums[1].astype(LOW)
        kv_grad_v[prefix_at, cols] = (sums[2] * scale).astype(LOW)
        kv_grad_v[prefix_at, value_cols] = sums[3].astype(LOW)

    for quarter in range(4):
        pl.loop(quarter * units // 4, (quarter + 1) * units // 4)(back)
        ring.to(3 + quarter)
    stores = []

    def store(src, dst):
        copy = pltpu.make_async_copy(src, dst, store_sem.at[len(stores)])
        copy.start()
        stores.append(copy)

    store(query_grad_v, query_grad_out)
    store(kv_grad_v, kv_grad_out)

    def core_copy(t):
        return remote(
            core_send_v.at[tile_rows(t)],
            core_recv_v.at[tile_rows(t)],
            sum_send.at[0, t],
            sum_recv.at[0, t],
            here.sibling,
        )

    def second_copy(t):
        return remote(
            core_send_v.at[tile_rows(t)],
            second_recv_v.at[tile_rows(t)],
            sum_send.at[1, t],
            sum_recv.at[1, t],
            here.sibling,
        )

    half_copy = remote(half_send_v, half_recv_v, cross_send.at[1], cross_recv.at[1], here.across)
    kv_cols = pl.ds(head_cols, 2 * head_cols)

    def prefix_terms(at, cols):
        return dot_right_t(kv_grad_v[at, :], w_v[cols, kv_cols])

    for t in range(tiles):
        for cols in halves:
            core_send_v[tile_rows(t), cols] = prefix_terms(
                pl.ds(3 * rows + t * CHUNK, CHUNK), cols
            ).astype(LOW)
        second_copy(t).start()
    for t in range(tiles):
        second_copy(t).wait_recv()
    for keep in range(2):
        which = here.y if keep else 1 - here.y
        at = pl.ds(pl.multiple_of(2 * rows + which * CHUNK, CHUNK), CHUNK)
        came = pl.ds(pl.multiple_of(which * CHUNK, CHUNK), CHUNK)
        for cols in halves:
            value = prefix_terms(at, cols) + second_recv_v[came, cols].astype(WIDE)
            if keep:
                half_keep_v[:, cols] = value.astype(LOW)
            else:
                half_send_v[:, cols] = value.astype(LOW)
        if not keep:
            half_copy.start()
    ring.to(7)

    def own_terms(at, cols):
        return dot_right_t(query_grad_v[at, :], w_v[cols, 0:head_cols]) + dot_right_t(
            kv_grad_v[at, :], w_v[cols, kv_cols]
        )

    for t in range(tiles):
        second_copy(t).wait_send()
        for cols in halves:
            core_send_v[tile_rows(t), cols] = own_terms(
                pl.ds(rows + t * CHUNK, CHUNK), cols
            ).astype(LOW)
        core_copy(t).start()
    for t in range(tiles):
        at = tile_rows(t)
        core_copy(t).wait_recv()
        for cols in halves:
            core_recv_v[at, cols] = (
                own_terms(at, cols) + core_recv_v[at, cols].astype(WIDE)
            ).astype(LOW)
    store(core_recv_v, own_low_out)
    ring.to(8)

    half_copy.wait()
    write_ordered(
        half_send_v,
        slice(None),
        blocks,
        shard,
        half_keep_v[...].astype(WIDE) + half_recv_v[...].astype(WIDE),
    )
    store(half_send_v, prefix_half_out)

    small = mlp_low_v.shape[0]
    pieces = rows // small

    def piece_rows(t):
        return pl.ds(t * small, small)

    def tile_loads(t):
        return (
            pltpu.make_async_copy(hidden_hbm.at[piece_rows(t)], hidden_v, tile_sem.at[0]),
            pltpu.make_async_copy(mlp_low_hbm.at[piece_rows(t)], mlp_low_v, tile_sem.at[1]),
            pltpu.make_async_copy(mlp_recv_out.at[piece_rows(t)], mlp_recv_v, tile_sem.at[2]),
        )

    def tile_store(t):
        return pltpu.make_async_copy(
            half_keep_v.at[pl.ds(t % 2 * small, small)],
            outputs_out.at[piece_rows(t)],
            tile_sem.at[3 + t % 2],
        )

    mlp_cross.wait()
    for copy in tile_loads(0):
        copy.start()
    for t in range(pieces):
        for copy in tile_loads(t):
            copy.wait()
        value = (
            hidden_v[...]
            + mlp_low_v[...].astype(WIDE)
            + mlp_recv_v[...].astype(WIDE)
            + vectors_ref[4:5, :]
        )
        if t > 1:
            tile_store(t - 2).wait()
        write_ordered(half_keep_v, pl.ds(t % 2 * small, small), blocks, shard, value)
        tile_store(t).start()
        if t + 1 < pieces:
            for copy in tile_loads(t + 1):
                copy.start()
    for t in (pieces - 2, pieces - 1):
        tile_store(t).wait()
    ring.finish()
    for t in range(tiles):
        core_copy(t).wait_send()
    for copy in stores:
        copy.wait()


def run_attend_back(
    dp_size,
    sol_size,
    shard,
    vectors,
    weights,
    normed_two,
    grad_up,
    branch,
    query_rows,
    key_rows,
    value_rows,
    probs,
    mlp_low,
    hidden,
):
    rows, width = hidden.shape
    ff = grad_up.shape[1]
    head_cols = query_rows.shape[1]
    count = dp_size // 2 * sol_size
    tiles = rows // CHUNK
    dma = pltpu.SemaphoreType.DMA

    def shape(*dims, dtype=LOW):
        return jax.ShapeDtypeStruct(dims, dtype)

    def low(*dims):
        return pltpu.VMEM(dims, LOW)

    outs = [
        shape(2 * rows, head_cols),
        shape(4 * rows, 2 * head_cols),
        shape(rows, width),
        shape(rows // 2, width),
        shape(shard, 2 * ff, dtype=WIDE),
        shape(rows, width),
        shape(rows, width),
    ]
    return pl.pallas_call(
        functools.partial(attend_back_kernel, dp_size, sol_size),
        out_shape=outs,
        in_specs=[vmem_spec()] + [any_spec()] * 10,
        out_specs=[any_spec()] * len(outs),
        scratch_shapes=[
            low(2 * rows, width),
            low(2 * rows, ff),
            low(2 * rows, width),
            low(width, width),
            low(2 * rows, head_cols),
            low(4 * rows, head_cols),
            low(4 * rows, head_cols),
            low(2 * rows, head_cols),
            low(2, rows, 2 * rows),
            low(2 * rows, head_cols),
            low(4 * rows, 2 * head_cols),
            low(rows, width),
            low(rows, width),
            low(CHUNK, width),
            low(CHUNK // 2, width),
            low(CHUNK // 2, width),
            pltpu.VMEM((CHUNK // 2, width), WIDE),
        ]
        + ring_sum_scratch(count // 2, shard, ff, 1)
        + [
            dma((7,)),
            dma((2,)),
            dma((5,)),
            dma((4,)),
            dma((2, tiles)),
            dma((2, tiles)),
            dma((2,)),
            dma((2,)),
        ],
        compiler_params=pltpu.CompilerParams(
            collective_id=2, has_side_effects=True, vmem_limit_bytes=60 * 2**20
        ),
    )(
        vectors,
        weights,
        normed_two,
        grad_up,
        branch,
        query_rows,
        key_rows,
        value_rows,
        probs,
        mlp_low,
        hidden,
    )


def last_kernel(
    dp_size,
    sol_size,
    x_ref,
    vectors_ref,
    normed_hbm,
    branch_hbm,
    query_grad_hbm,
    kv_grad_hbm,
    mixed_hbm,
    own_low_hbm,
    prefix_half_hbm,
    grad_hidden_hbm,
    query_out,
    key_out,
    value_out,
    out_out,
    input_grad_out,
    sums_ref,
    normed_v,
    branch_v,
    query_grad_v,
    kv_grad_v,
    mixed_v,
    own_low_v,
    own_recv_v,
    half_v,
    half_recv_v,
    prefix_v,
    grad_hidden_v,
    out_v,
    ring_send_v,
    ring_recv_v,
    stage_v,
    ring_send,
    ring_recv,
    ring_end,
    load_sem,
    tile_sem,
    cross_send,
    cross_recv,
    chain_send,
    chain_recv,
):
    here = Place(dp_size, sol_size)
    rows, width = x_ref.shape
    shard = stage_v.shape[1]
    head_cols = query_grad_v.shape[1]
    tiles = rows // CHUNK
    blocks = here.blocks()
    loads = [
        pltpu.make_async_copy(src, dst, load_sem.at[i])
        for i, (src, dst) in enumerate(
            (
                (query_grad_hbm, query_grad_v),
                (kv_grad_hbm, kv_grad_v),
                (mixed_hbm, mixed_v),
                (prefix_half_hbm, half_v),
                (normed_hbm, normed_v),
                (branch_hbm, branch_v),
                (own_low_hbm, own_low_v),
            )
        )
    ]
    for copy in loads:
        copy.start()
    here.greet()
    own_cross = remote(own_low_hbm, own_recv_v, cross_send.at[0], cross_recv.at[0], here.across)
    own_cross.start()

    def chunk(j, which):
        at = pl.ds(pl.multiple_of((2 * j + which) * shard, shard), shard)
        return jnp.concatenate(
            [
                dot_left_t(normed_v[: 2 * rows, at], query_grad_v[...]),
                dot_left_t(normed_v[:, at], kv_grad_v[...]),
                dot_left_t(branch_v[:, at], mixed_v[...]),
            ],
            axis=1,
        )

    ring = RingSum(
        here,
        chunk,
        ring_send_v,
        ring_recv_v,
        stage_v,
        (ring_send, ring_recv, ring_end),
        tuple(
            (ref, i * head_cols, head_cols)
            for i, ref in enumerate((query_out, key_out, value_out, out_out))
        ),
    )

    part = CHUNK // 2

    def chain_copy(i):
        at = pl.ds(i * part, part)
        return remote(
            half_v.at[at], half_recv_v.at[at], chain_send.at[i], chain_recv.at[i], here.along(-1)
        )

    def chain(stage, i):
        at = pl.ds(i * part, part)

        @pl.when(here.z == stage)
        def _():
            if stage < sol_size - 1:
                chain_copy(i).wait_recv()
                if stage > 0:
                    half_v[at, :] = (
                        half_v[at, :].astype(WIDE) + half_recv_v[at, :].astype(WIDE)
                    ).astype(LOW)
            if stage > 0:
                chain_copy(i).start()

    loads[3].wait()
    for i in range(2):
        chain(sol_size - 1, i)
    for i in (0, 1, 2, 4, 5):
        loads[i].wait()
    ring.to(2)
    for step in range(sol_size):
        if step < sol_size - 1:
            chain(sol_size - 2 - step, 0)
        if step > 0:
            chain(sol_size - 1 - step, 1)
        ring.to(3 + step)

    mine = pl.ds(pl.multiple_of(here.y * CHUNK, CHUNK), CHUNK)
    half_cross = remote(
        half_recv_v, prefix_v.at[mine], cross_send.at[1], cross_recv.at[1], here.across
    )

    @pl.when(here.z == 0)
    def _():
        half_cross.start()
        prefix_v[mine, :] = half_recv_v[...]

    @pl.when(here.z > 0)
    def _():
        prefix_v[...] = jnp.zeros_like(prefix_v)

    ring.to(7)
    loads[6].wait()
    own_cross.wait()

    @pl.when(here.z == 0)
    def _():
        half_cross.wait()

    gain = vectors_ref[0:1, :]
    sums_ref[...] = jnp.zeros_like(sums_ref)

    def tile_load(t):
        return pltpu.make_async_copy(
            grad_hidden_hbm.at[tile_rows(t)], grad_hidden_v, tile_sem.at[0]
        )

    def tile_store(t):
        return pltpu.make_async_copy(out_v, input_grad_out.at[tile_rows(t)], tile_sem.at[1])

    tile_load(0).start()
    for t in range(tiles):
        tile_load(t).wait()
        if t > 0:
            tile_store(t - 1).wait()
        for piece in range(2):
            at = pl.ds(t * CHUNK + piece * part, part)
            inner = pl.ds(piece * part, part)
            grad = (
                own_low_v[at, :].astype(WIDE)
                + own_recv_v[at, :].astype(WIDE)
                + read_ordered(prefix_v, at, blocks, shard)
            )
            back, gain_terms, shift_terms = norm_back(
                read_ordered(x_ref, at, blocks, shard), gain, grad
            )
            sums_ref[0:1, :] += gain_terms
            sums_ref[1:2, :] += shift_terms
            write_ordered(out_v, inner, blocks, shard, back + grad_hidden_v[inner, :])
        tile_store(t).start()
        if t + 1 < tiles:
            tile_load(t + 1).start()
        ring.to(8 + t)
    tile_store(tiles - 1).wait()
    ring.finish()
    for i in range(2):

        @pl.when(here.z > 0)
        def _():
            chain_copy(i).wait_send()


def run_last(
    dp_size,
    sol_size,
    shard,
    x,
    vectors,
    normed,
    branch,
    query_grad,
    kv_grad,
    mixed,
    own_low,
    prefix_half,
    grad_hidden,
):
    rows, width = x.shape
    head_cols = query_grad.shape[1]
    count = dp_size // 2 * sol_size
    dma = pltpu.SemaphoreType.DMA

    def shape(*dims, dtype=LOW):
        return jax.ShapeDtypeStruct(dims, dtype)

    def low(*dims):
        return pltpu.VMEM(dims, LOW)

    outs = [shape(shard, 2 * head_cols, dtype=WIDE)] * 4 + [
        shape(rows, width),
        shape(8, width, dtype=WIDE),
    ]
    return pl.pallas_call(
        functools.partial(last_kernel, dp_size, sol_size),
        out_shape=outs,
        in_specs=[vmem_spec()] * 2 + [any_spec()] * 8,
        out_specs=[any_spec()] * 5 + [vmem_spec()],
        scratch_shapes=[
            low(4 * rows, width),
            low(2 * rows, width),
            low(2 * rows, head_cols),
            low(4 * rows, 2 * head_cols),
            low(2 * rows, head_cols),
            low(rows, width),
            low(rows, width),
            low(CHUNK, width),
            low(CHUNK, width),
            low(rows, width),
            pltpu.VMEM((CHUNK, width), WIDE),
            low(CHUNK, width),
        ]
        + ring_sum_scratch(count // 2, shard, 4 * head_cols, 4)
        + [
            dma((7,)),
            dma((2,)),
            dma((2,)),
            dma((2,)),
            dma((2,)),
            dma((2,)),
        ],
        compiler_params=pltpu.CompilerParams(
            collective_id=3, has_side_effects=True, vmem_limit_bytes=60 * 2**20
        ),
    )(
        x,
        vectors,
        normed,
        branch,
        query_grad,
        kv_grad,
        mixed,
        own_low,
        prefix_half,
        grad_hidden,
    )


def ring_program(
    inputs,
    cotangent,
    attn_gain,
    attn_shift,
    query_weight,
    key_weight,
    value_weight,
    out_weight,
    mlp_gain,
    mlp_shift,
    up_weight,
    up_bias,
    down_weight,
    down_bias,
    live_rows,
):
    block_rows, width = inputs.shape
    shard_rows = query_weight.shape[0]
    head_cols = query_weight.shape[1] // 2
    ff_cols = up_weight.shape[1] // 2
    ff_part = ff_cols // 2
    local_heads = head_cols // HEAD_DIM
    score_scale = 1.0 / math.sqrt(HEAD_DIM)
    dp_size, sol_size = lax.axis_size("dp"), lax.axis_size("sol")
    count, ahead, back, cores = ring_pairs(dp_size, sol_size)
    dp_place, sol_place = lax.axis_index("dp"), lax.axis_index("sol")
    x_place, core = dp_place // 2, dp_place % 2
    first_core = core == 0
    along = jnp.where(x_place % 2 == 0, sol_place, sol_size - 1 - sol_place)
    ring_here = x_place * sol_size + along

    order_list = []
    for j in range(count):
        q = (ring_here + j) % count
        qx, qa = q // sol_size, q % sol_size
        qz = jnp.where(qx % 2 == 0, qa, sol_size - 1 - qa)
        order_list += [(qx * 2) * sol_size + qz, (qx * 2 + 1) * sol_size + qz]
    order = jnp.stack(order_list).astype(jnp.int32)
    back_order = jnp.argsort(order).astype(jnp.int32)

    def to_core(value):
        return lax.ppermute(value, ROWS_AXES, cores)

    def to_tensor(value):
        return lax.ppermute(value, "tensor", [(0, 1), (1, 0)])

    def reorder_vector(vector, by):
        return jnp.take(vector.reshape(by.shape[0], -1), by, axis=0).reshape(vector.shape)

    def gather_ring(piece, flip):
        hops_ahead = count // 2 - (1 if flip else 0)
        hops_back = count - 1 - hops_ahead
        got = {0: piece}
        moving_a, moving_b = piece, piece
        for k in range(1, count // 2 + 1):
            if k <= hops_ahead:
                moving_a = lax.ppermute(moving_a, ROWS_AXES, ahead)
                got[count - k] = moving_a
            if k <= hops_back:
                moving_b = lax.ppermute(moving_b, ROWS_AXES, back)
                got[k] = moving_b
        return jnp.concatenate([got[j] for j in range(count)], axis=0)

    def scatter_ring(chunk, flip):
        hops_ahead = count // 2 - (1 if flip else 0)
        hops_back = count - 1 - hops_ahead
        carried_a = carried_b = None
        for k in range(count // 2, 0, -1):
            if k <= hops_ahead:
                value = chunk(k)
                if carried_a is not None:
                    value = value + carried_a.astype(WIDE)
                carried_a = lax.ppermute(value.astype(LOW), ROWS_AXES, ahead)
            if k <= hops_back:
                value = chunk(count - k)
                if carried_b is not None:
                    value = value + carried_b.astype(WIDE)
                carried_b = lax.ppermute(value.astype(LOW), ROWS_AXES, back)
        return chunk(0) + carried_a.astype(WIDE) + carried_b.astype(WIDE)

    def own_part(shards):
        firsts, seconds = [], []
        for shard, start, size in shards:
            half = shard.shape[1] // 2
            firsts.append(shard[:, start : start + size])
            seconds.append(shard[:, half + start : half + start + size])
        low_half = jnp.concatenate(firsts, axis=1) if len(firsts) > 1 else firsts[0]
        high_half = jnp.concatenate(seconds, axis=1) if len(seconds) > 1 else seconds[0]
        mine = jnp.where(first_core, low_half, high_half)
        other = to_core(jnp.where(first_core, high_half, low_half))
        return jnp.concatenate(
            [jnp.where(first_core, mine, other), jnp.where(first_core, other, mine)], axis=0
        )

    def split_rows(full):
        upper, lower = full[:shard_rows], full[shard_rows:]
        mine = jnp.where(first_core, upper, lower)
        other = to_core(jnp.where(first_core, lower, upper))
        return jnp.where(first_core, mine, other), jnp.where(first_core, other, mine)

    def sum_partials(partial):
        mine = partial[:block_rows] + to_core(partial[block_rows:].astype(LOW)).astype(WIDE)
        low = mine.astype(LOW)
        return low.astype(WIDE) + to_tensor(low).astype(WIDE)

    def pair_rows(own):
        return jnp.concatenate([own, to_core(own)], axis=0)

    qk_piece = own_part([(query_weight, 0, head_cols), (key_weight, 0, head_cols)])
    vo_piece = own_part([(value_weight, 0, head_cols), (out_weight, 0, head_cols)])
    up_pieces = [own_part([(up_weight, s, ff_part)]) for s in (0, ff_part)]
    down_pieces = [own_part([(down_weight, s, ff_part)]) for s in (0, ff_part)]
    qk_full = gather_ring(qk_piece, False)
    vo_full = gather_ring(vo_piece, True)
    up_full = [gather_ring(up_pieces[0], False), gather_ring(up_pieces[1], True)]
    down_full = [gather_ring(down_pieces[0], False), gather_ring(down_pieces[1], True)]
    query_full, key_full = qk_full[:, :head_cols], qk_full[:, head_cols:]
    value_full, out_full = vo_full[:, :head_cols], vo_full[:, head_cols:]

    tensor_place = lax.axis_index("tensor")
    half_rows = block_rows // 2
    half = jnp.where(tensor_place == 0, inputs[:half_rows], inputs[half_rows:])
    prefix_half = half
    hop = half
    for k in range(1, sol_size):
        hop = lax.ppermute(hop, "sol", [(k - 1, k)])
        prefix_half = jnp.where(sol_place == k, hop, prefix_half)
    other_half = to_tensor(prefix_half)
    prefix_inputs = jnp.concatenate(
        [
            jnp.where(tensor_place == 0, prefix_half, other_half),
            jnp.where(tensor_place == 0, other_half, prefix_half),
        ],
        axis=0,
    )

    own_low = reorder(inputs, order)
    prefix_low = reorder(prefix_inputs, order)
    cot_low = reorder(cotangent, order)
    attn_gain_o, attn_shift_o, mlp_gain_o, mlp_shift_o, down_bias_o = [
        reorder_vector(v, order) for v in (attn_gain, attn_shift, mlp_gain, mlp_shift, down_bias)
    ]
    up_bias_c = jnp.where(first_core, up_bias[:ff_cols], up_bias[ff_cols:])
    up_bias_parts = [up_bias_c[:ff_part], up_bias_c[ff_part:]]

    features = own_low.astype(WIDE)
    normed = pair_rows(layer_norm(features, attn_gain_o, attn_shift_o).astype(LOW))
    normed_prefix = pair_rows(
        layer_norm(prefix_low.astype(WIDE), attn_gain_o, attn_shift_o).astype(LOW)
    )
    cot_pair = pair_rows(cot_low)

    query_rows = dot_plain(normed, query_full).astype(LOW)
    key_rows = dot_plain(normed, key_full).astype(LOW)
    value_rows = dot_plain(normed, value_full).astype(LOW)
    key_prefix = dot_plain(normed_prefix, key_full).astype(LOW)
    value_prefix = dot_plain(normed_prefix, value_full).astype(LOW)

    def heads_of(rows):
        return rows.reshape(2, -1, local_heads, HEAD_DIM)

    head_queries = heads_of(query_rows)
    all_keys = jnp.concatenate([heads_of(key_prefix), heads_of(key_rows)], axis=1)
    all_values = jnp.concatenate([heads_of(value_prefix), heads_of(value_rows)], axis=1)

    row_ids = jnp.arange(block_rows)[:, None]
    col_ids = jnp.arange(block_rows)[None, :]
    masks = []
    for place in (dp_place, dp_place + 1 - 2 * core):
        own_live = live_rows[place * sol_size + sol_place]
        prefix_live = live_rows[place * sol_size]
        prefix_ok = jnp.logical_and(col_ids < prefix_live, sol_place != 0)
        own_ok = jnp.logical_and(col_ids <= row_ids, col_ids < own_live)
        masks.append(
            jnp.concatenate(
                [jnp.broadcast_to(prefix_ok, (block_rows, block_rows)), own_ok], axis=1
            )
        )
    allowed = jnp.stack(masks)[:, None]

    def masked_scores():
        raw = jnp.einsum("bqhd,bkhd->bhqk", head_queries, all_keys, preferred_element_type=WIDE)
        return jnp.where(allowed, raw * score_scale, NEG_FILL)

    scores = masked_scores()
    row_peak = jnp.max(scores, axis=-1, keepdims=True)
    exp_scores = jnp.exp(scores - row_peak)
    totals = jnp.sum(exp_scores, axis=-1, keepdims=True)
    attn_probs = exp_scores / totals
    log_total = row_peak + jnp.log(totals)
    mixed = jnp.einsum(
        "bhqk,bkhd->bqhd", attn_probs.astype(LOW), all_values, preferred_element_type=WIDE
    )
    mixed_low = mixed.reshape(2 * block_rows, head_cols).astype(LOW)

    hidden = features + sum_partials(dot_right_t(mixed_low, out_full))
    normed_two = pair_rows(layer_norm(hidden, mlp_gain_o, mlp_shift_o).astype(LOW))
    upward = [dot_plain(normed_two, up_full[i]) + up_bias_parts[i] for i in range(2)]
    active = [gelu_tanh(u).astype(LOW) for u in upward]
    down_grads = [
        scatter_ring(
            lambda j, i=i: dot_left_t(
                cot_pair[:, j * 2 * shard_rows : (j + 1) * 2 * shard_rows], active[i]
            ),
            i == 1,
        )
        for i in range(2)
    ]
    grad_up = []
    for i in range(2):
        grad_active = dot_plain(cot_pair, down_full[i])
        unused_gelu, gelu_pull = jax.vjp(gelu_tanh, upward[i])
        grad_up.append(gelu_pull(grad_active)[0].astype(LOW))
    grad_normed_two = sum_partials(
        dot_right_t(grad_up[0], up_full[0]) + dot_right_t(grad_up[1], up_full[1])
    )
    up_grads = [
        scatter_ring(
            lambda j, i=i: dot_left_t(
                normed_two[:, j * 2 * shard_rows : (j + 1) * 2 * shard_rows], grad_up[i]
            ),
            i == 1,
        )
        for i in range(2)
    ]
    mlp_total = sum_partials(
        dot_right_t(active[0], down_full[0]) + dot_right_t(active[1], down_full[1])
    )
    outputs = reorder((hidden + mlp_total + down_bias_o).astype(LOW), back_order)

    grad_out = cot_low.astype(WIDE)
    down_bias_grad = jnp.sum(grad_out, axis=0)
    grad_hidden_norm, mlp_gain_grad, mlp_shift_grad = layer_norm_back(
        hidden, mlp_gain_o, grad_normed_two
    )
    grad_hidden = grad_out + grad_hidden_norm
    grad_branch = pair_rows(grad_hidden.astype(LOW))
    grad_mixed_low = dot_plain(grad_branch, out_full).astype(LOW)

    grad_head_mixed = heads_of(grad_mixed_low)
    attn_probs = jnp.exp(masked_scores() - log_total)
    grad_probs = jnp.einsum(
        "bqhd,bkhd->bhqk", grad_head_mixed, all_values, preferred_element_type=WIDE
    )
    row_delta = jnp.sum(attn_probs * grad_probs, axis=-1, keepdims=True)
    grad_scores = (attn_probs * (grad_probs - row_delta)).astype(LOW)
    grad_queries = (
        jnp.einsum("bhqk,bkhd->bqhd", grad_scores, all_keys, preferred_element_type=WIDE)
        * score_scale
    )
    grad_keys = (
        jnp.einsum("bhqk,bqhd->bkhd", grad_scores, head_queries, preferred_element_type=WIDE)
        * score_scale
    )
    grad_values = jnp.einsum(
        "bhqk,bqhd->bkhd", attn_probs.astype(LOW), grad_head_mixed, preferred_element_type=WIDE
    )

    def rows_of(heads):
        return heads.reshape(2 * block_rows, head_cols).astype(LOW)

    query_grad_low = rows_of(grad_queries)
    key_own = rows_of(grad_keys[:, block_rows:])
    value_own = rows_of(grad_values[:, block_rows:])
    key_pre = rows_of(grad_keys[:, :block_rows])
    value_pre = rows_of(grad_values[:, :block_rows])

    kv_pre = jnp.concatenate([key_pre, value_pre], axis=1)
    carried = kv_pre
    for k in range(sol_size - 1, 0, -1):
        came = lax.ppermute(carried, "sol", [(k, k - 1)])
        if k > 1:
            carried = (kv_pre.astype(WIDE) + came.astype(WIDE)).astype(LOW)
    key_all = (key_own.astype(WIDE) + came[:, :head_cols].astype(WIDE)).astype(LOW)
    value_all = (value_own.astype(WIDE) + came[:, head_cols:].astype(WIDE)).astype(LOW)

    normed_all = jnp.concatenate([normed, normed_prefix], axis=0)
    key_rows_grad = jnp.concatenate([key_own, key_pre], axis=0)
    value_rows_grad = jnp.concatenate([value_own, value_pre], axis=0)

    def qk_chunk(j):
        at = slice(j * 2 * shard_rows, (j + 1) * 2 * shard_rows)
        return jnp.concatenate(
            [
                dot_left_t(normed[:, at], query_grad_low),
                dot_left_t(normed_all[:, at], key_rows_grad),
            ],
            axis=1,
        )

    def vo_chunk(j):
        at = slice(j * 2 * shard_rows, (j + 1) * 2 * shard_rows)
        return jnp.concatenate(
            [
                dot_left_t(normed_all[:, at], value_rows_grad),
                dot_left_t(grad_branch[:, at], mixed_low),
            ],
            axis=1,
        )

    qk_grad = scatter_ring(qk_chunk, False)
    vo_grad = scatter_ring(vo_chunk, True)

    grad_normed = sum_partials(
        dot_right_t(query_grad_low, query_full)
        + dot_right_t(key_all, key_full)
        + dot_right_t(value_all, value_full)
    )
    grad_features, attn_gain_grad, attn_shift_grad = layer_norm_back(
        features, attn_gain_o, grad_normed
    )
    input_grad = reorder((grad_hidden + grad_features).astype(LOW), back_order)

    up_bias_grad = jnp.concatenate([jnp.sum(g.astype(WIDE), axis=0) for g in grad_up])
    up_bias_both = jnp.concatenate(
        [
            jnp.where(first_core, up_bias_grad, 0.0),
            jnp.where(first_core, 0.0, up_bias_grad),
        ]
    )

    def sum_rows_axes(vector):
        vector = vector + to_core(vector)
        step = 1
        while step < sol_size:
            vector = vector + lax.ppermute(vector, "sol", [(i, i ^ step) for i in range(sol_size)])
            step *= 2
        step = 2
        while step < dp_size:
            vector = vector + lax.ppermute(vector, "dp", [(i, i ^ step) for i in range(dp_size)])
            step *= 2
        return vector

    early = sum_rows_axes(
        jnp.concatenate(
            [reorder_vector(v, back_order) for v in (mlp_gain_grad, mlp_shift_grad, down_bias_grad)]
            + [up_bias_both]
        )
    )
    late = sum_rows_axes(
        jnp.concatenate([reorder_vector(v, back_order) for v in (attn_gain_grad, attn_shift_grad)])
    )

    qk_low, qk_high = split_rows(qk_grad)
    vo_low, vo_high = split_rows(vo_grad)
    up_low, up_high = zip(*[split_rows(g) for g in up_grads])
    down_low, down_high = zip(*[split_rows(g) for g in down_grads])

    def both(low_cols, high_cols):
        return jnp.concatenate([low_cols, high_cols], axis=1)

    return (
        outputs,
        input_grad,
        late[:width],
        late[width:],
        both(qk_low[:, :head_cols], qk_high[:, :head_cols]),
        both(qk_low[:, head_cols:], qk_high[:, head_cols:]),
        both(vo_low[:, :head_cols], vo_high[:, :head_cols]),
        both(vo_low[:, head_cols:], vo_high[:, head_cols:]),
        early[:width],
        early[width : 2 * width],
        jnp.concatenate(up_low + up_high, axis=1),
        early[3 * width :],
        jnp.concatenate(down_low + down_high, axis=1),
        early[2 * width : 3 * width],
    )


def per_device(*arrays):
    inputs, query_weight, up_weight = arrays[0], arrays[4], arrays[10]
    fits = (
        query_weight.shape[0] % 128 == 0
        and inputs.shape[0] % (2 * CHUNK) == 0
        and up_weight.shape[1] // 2 % inputs.shape[1] == 0
        and query_weight.shape[1] * 2 == inputs.shape[1]
    )
    return kernel_program(*arrays) if fits else ring_program(*arrays)


def kernel_program(
    inputs,
    cotangent,
    attn_gain,
    attn_shift,
    query_weight,
    key_weight,
    value_weight,
    out_weight,
    mlp_gain,
    mlp_shift,
    up_weight,
    up_bias,
    down_weight,
    down_bias,
    live_rows,
):
    width = inputs.shape[1]
    shard_rows = query_weight.shape[0]
    ff_cols = up_weight.shape[1] // 2
    dp_size, sol_size = lax.axis_size("dp"), lax.axis_size("sol")
    count, _, _, cores = ring_pairs(dp_size, sol_size)
    here = Place(dp_size, sol_size)
    core = here.core
    first_core = core == 0
    order = jnp.stack(here.blocks()).astype(jnp.int32)
    back_order = jnp.argsort(order).astype(jnp.int32)
    vectors = jnp.stack([attn_gain, attn_shift, mlp_gain, mlp_shift, down_bias])
    vectors = jnp.take(vectors.reshape(5, 2 * count, shard_rows), order, axis=1).reshape(5, width)
    up_bias_c = jnp.where(first_core, up_bias[:ff_cols], up_bias[ff_cols:])[None]
    (
        weights,
        normed_all,
        cot_pair,
        query_rows,
        key_rows,
        value_rows,
        probs,
        mixed_low,
        hidden,
        normed_two,
        slope,
        active,
    ) = run_forward(
        dp_size,
        sol_size,
        inputs,
        vectors,
        up_bias_c,
        live_rows,
        cotangent,
        (query_weight, key_weight, value_weight, out_weight, up_weight, down_weight),
    )
    grad_up, grad_branch, grad_hidden, mlp_low, down_grad, early_sums = run_down(
        dp_size, sol_size, shard_rows, vectors, weights, cot_pair, active, slope, hidden
    )
    query_grad, kv_grad, own_low, prefix_half, up_grad, outputs, _ = run_attend_back(
        dp_size,
        sol_size,
        shard_rows,
        vectors,
        weights,
        normed_two,
        grad_up,
        grad_branch,
        query_rows,
        key_rows,
        value_rows,
        probs,
        mlp_low,
        hidden,
    )
    query_grads, key_grads, value_grads, out_grads, input_grad, late_sums = run_last(
        dp_size,
        sol_size,
        shard_rows,
        inputs,
        vectors,
        normed_all,
        grad_branch,
        query_grad,
        kv_grad,
        mixed_low,
        own_low,
        prefix_half,
        grad_hidden,
    )

    def to_core(value):
        return lax.ppermute(value, ROWS_AXES, cores)

    def reorder_rows(table, by):
        return jnp.take(
            table.reshape(table.shape[0], 2 * count, shard_rows), by, axis=1
        ).reshape(table.shape)

    small = reorder_rows(jnp.concatenate([early_sums[:3], late_sums[:2]]), back_order)
    up_bias_grad = early_sums[3]
    up_bias_both = jnp.concatenate(
        [jnp.where(first_core, up_bias_grad, 0.0), jnp.where(first_core, 0.0, up_bias_grad)]
    )

    def sum_rows_axes(vector):
        vector = vector + to_core(vector)
        step = 1
        while step < sol_size:
            vector = vector + lax.ppermute(vector, "sol", [(i, i ^ step) for i in range(sol_size)])
            step *= 2
        step = 2
        while step < dp_size:
            vector = vector + lax.ppermute(vector, "dp", [(i, i ^ step) for i in range(dp_size)])
            step *= 2
        return vector

    total = sum_rows_axes(jnp.concatenate([small.reshape(-1), up_bias_both]))
    parts = total[: 5 * width].reshape(5, width)
    return (
        outputs,
        input_grad,
        parts[3],
        parts[4],
        query_grads,
        key_grads,
        value_grads,
        out_grads,
        parts[0],
        parts[1],
        up_grad,
        total[5 * width :],
        down_grad,
        parts[2],
    )


def solution(mesh):
    rows = P(("dp", "sol"), None)
    matrix = P(("dp", "sol"), "tensor")
    return jax.shard_map(
        per_device,
        mesh=mesh,
        in_specs=(
            rows,
            rows,
            P(),
            P(),
            matrix,
            matrix,
            matrix,
            matrix,
            P(),
            P(),
            matrix,
            P("tensor"),
            matrix,
            P(),
            P(),
        ),
        out_specs=(
            rows,
            rows,
            P(),
            P(),
            matrix,
            matrix,
            matrix,
            matrix,
            P(),
            P(),
            matrix,
            P("tensor"),
            matrix,
            P(),
        ),
        check_vma=False,
    )
```

```python
import functools
import math

import jax
import jax.numpy as jnp
from jax import lax
from jax.experimental import pallas as pl
from jax.experimental.pallas import tpu as pltpu
from jax.sharding import PartitionSpec as P

HEAD_DIM = 128
EPSILON = 1e-05
NEG_FILL = -1e30
ROWS_AXES = ("dp", "sol")
LOW = jnp.bfloat16
WIDE = jnp.float32


def ring_place(position, sol_size):
    x, along = position // sol_size, position % sol_size
    return x, (along if x % 2 == 0 else sol_size - 1 - along)


def ring_pairs(dp_size, sol_size):
    count = dp_size // 2 * sol_size

    def flat(position, core):
        x, z = ring_place(position % count, sol_size)
        return (x * 2 + core) * sol_size + z

    places = [(q, c) for q in range(count) for c in range(2)]
    ahead = [(flat(q, c), flat(q + 1, c)) for q, c in places]
    back = [(b, a) for a, b in ahead]
    cores = [(flat(q, c), flat(q, 1 - c)) for q, c in places]
    return count, ahead, back, cores


def dot_plain(left_side, right_side):
    return jnp.dot(left_side, right_side, preferred_element_type=WIDE)


def dot_right_t(left_side, right_side):
    return lax.dot_general(
        left_side, right_side, (((1,), (1,)), ((), ())), preferred_element_type=WIDE
    )


def dot_left_t(left_side, right_side):
    return lax.dot_general(
        left_side, right_side, (((0,), (0,)), ((), ())), preferred_element_type=WIDE
    )


def norm_stats(features):
    row_mean = jnp.mean(features, axis=-1, keepdims=True)
    centered = features - row_mean
    variance = jnp.mean(centered * centered, axis=-1, keepdims=True)
    return row_mean, lax.rsqrt(variance + EPSILON)


def layer_norm(features, norm_gain, norm_shift):
    row_mean, inverse = norm_stats(features)
    return (features - row_mean) * inverse * norm_gain + norm_shift


def layer_norm_back(features, norm_gain, grad):
    row_mean, inverse = norm_stats(features)
    unit = (features - row_mean) * inverse
    scaled = grad * norm_gain
    along = jnp.mean(scaled * unit, axis=-1, keepdims=True)
    level = jnp.mean(scaled, axis=-1, keepdims=True)
    grad_features = (scaled - level - unit * along) * inverse
    return grad_features, jnp.sum(grad * unit, axis=0), jnp.sum(grad, axis=0)


def gelu_tanh(upward):
    return jax.nn.gelu(upward, approximate=True)


def copy_block(order_ref, in_ref, out_ref):
    out_ref[...] = in_ref[...]


def reorder(rows, order):
    blocks = order.shape[0]
    height, width = rows.shape
    part = width // blocks
    if part % 128:
        return jnp.take(rows.reshape(height, blocks, part), order, axis=1).reshape(height, width)
    return pl.pallas_call(
        copy_block,
        grid_spec=pltpu.PrefetchScalarGridSpec(
            num_scalar_prefetch=1,
            grid=(blocks,),
            in_specs=[pl.BlockSpec((height, part), lambda j, order_ref: (0, order_ref[j]))],
            out_specs=pl.BlockSpec((height, part), lambda j, order_ref: (0, j)),
        ),
        out_shape=jax.ShapeDtypeStruct(rows.shape, rows.dtype),
        cost_estimate=pl.CostEstimate(
            flops=0, bytes_accessed=4 * height * width, transcendentals=0
        ),
    )(order, rows)


MESH = pl.DeviceIdType.MESH
CHUNK = 256


def any_spec():
    return pl.BlockSpec(memory_space=pl.ANY)


def vmem_spec():
    return pl.BlockSpec(memory_space=pltpu.VMEM)


class Place:
    def __init__(self, dp_size, sol_size):
        self.dp_size, self.sol_size = dp_size, sol_size
        self.count = dp_size // 2 * sol_size
        dp, self.z = lax.axis_index("dp"), lax.axis_index("sol")
        self.y = lax.axis_index("tensor")
        self.x, self.core = dp // 2, dp % 2
        self.dp = dp
        turned = jnp.where(self.x % 2 == 0, self.z, sol_size - 1 - self.z)
        self.at = self.x * sol_size + turned
        self.next = self._chip((self.at + 1) % self.count)
        self.prev = self._chip((self.at + self.count - 1) % self.count)
        self.sibling = (dp + 1 - 2 * self.core, self.z, self.y)
        self.across = (dp, self.z, 1 - self.y)

    def _coords(self, position):
        x, turned = position // self.sol_size, position % self.sol_size
        return x, jnp.where(x % 2 == 0, turned, self.sol_size - 1 - turned)

    def _chip(self, position):
        x, z = self._coords(position)
        return (x * 2 + self.core, z, self.y)

    def along(self, step):
        return (self.dp, self.z + step, self.y)

    def blocks(self):
        result = []
        for j in range(self.count):
            x, z = self._coords((self.at + j) % self.count)
            result += [(x * 2) * self.sol_size + z, (x * 2 + 1) * self.sol_size + z]
        return result

    def partners(self):
        result = [self.sibling]
        step = 1
        while step < self.sol_size:
            result.append((self.dp, self._flip(self.z, step), self.y))
            step *= 2
        step = 2
        while step < self.dp_size:
            result.append((self._flip(self.dp, step), self.z, self.y))
            step *= 2
        return result

    @staticmethod
    def _flip(place, step):
        return jnp.where(place // step % 2 == 0, place + step, place - step)

    def greet(self, others=()):
        barrier = pltpu.get_barrier_semaphore()
        peers = (self.next, self.prev, self.sibling, self.across) + tuple(others)
        for peer in peers:
            pl.semaphore_signal(barrier, inc=1, device_id=peer, device_id_type=MESH)
        pl.semaphore_wait(barrier, len(peers))


def remote(src, dst, send_sem, recv_sem, device):
    return pltpu.make_async_remote_copy(
        src_ref=src,
        dst_ref=dst,
        send_sem=send_sem,
        recv_sem=recv_sem,
        device_id=device,
        device_id_type=MESH,
    )


def norm_rows(values, gain, shift):
    row_mean = jnp.mean(values, axis=-1, keepdims=True)
    centered = values - row_mean
    variance = jnp.mean(centered * centered, axis=-1, keepdims=True)
    return centered * lax.rsqrt(variance + EPSILON) * gain + shift


def forward_kernel(
    dp_size,
    sol_size,
    x_ref,
    vectors_ref,
    up_bias_ref,
    live_ref,
    cot_hbm,
    query_ref,
    key_ref,
    value_ref,
    out_ref,
    up_ref,
    down_ref,
    weights,
    normed_out,
    cot_out,
    query_out,
    key_out,
    value_out,
    probs_out,
    mixed_out,
    hidden_out,
    normed_two_out,
    slope_out,
    active_out,
    w_v,
    normed_v,
    query_v,
    key_v,
    value_v,
    probs_v,
    mixed_v,
    hidden_v,
    normed_two_v,
    slope_v,
    active_v,
    core_send_v,
    core_recv_v,
    cross_send_v,
    cross_recv_v,
    ring_send,
    ring_recv,
    swap_local,
    swap_send,
    swap_recv,
    prefix_send,
    prefix_recv,
    pair_send,
    pair_recv,
    sum_send,
    sum_recv,
    cot_sem,
    load_sem,
    probs_sem,
    store_sem,
):
    here = Place(dp_size, sol_size)
    count, core = here.count, here.core
    rows, width = x_ref.shape
    prefix_v = slope_v
    shard = query_ref.shape[0]
    head_cols = query_ref.shape[1] // 2
    ff = up_ref.shape[1] // 2
    half = width // 2
    local_heads = head_cols // HEAD_DIM
    scale = 1.0 / math.sqrt(HEAD_DIM)
    blocks = here.blocks()
    far = count // 2
    own_class, other_class = core, 1 - core

    here.greet()

    def slot(j, which):
        return pl.ds(pl.multiple_of((2 * j + which) * shard, shard), shard)

    shards = (
        (0, 0, query_ref, head_cols),
        (0, head_cols, key_ref, head_cols),
        (0, 2 * head_cols, value_ref, head_cols),
        (0, 3 * head_cols, out_ref, head_cols),
        (1, 0, up_ref, ff),
        (2, 0, down_ref, ff),
    )

    def swap_copies(i):
        matrix, start, source, size = shards[i]
        target = weights.at[matrix, slot(0, own_class), pl.ds(start, size)]

        def columns(which):
            return source.at[:, pl.ds(pl.multiple_of(which * size, size), size)]

        return (
            pltpu.make_async_copy(columns(core), target, swap_local.at[i]),
            remote(columns(1 - core), target, swap_send.at[i], swap_recv.at[i], here.sibling),
        )

    def start_swap(matrix):
        for i in range(len(shards)):
            if shards[i][0] == matrix:
                for copy in swap_copies(i):
                    copy.start()

    def hops(matrix, k, sub):
        which = own_class if sub == 0 else other_class
        ahead_cols = pl.ds(0, half if k == far else width)
        back_cols = pl.ds(half if k == far else 0, half if k == far else width)
        return (
            remote(
                weights.at[matrix, slot((count - k + 1) % count, which), ahead_cols],
                weights.at[matrix, slot(count - k, which), ahead_cols],
                ring_send.at[matrix, 0, k - 1, sub],
                ring_recv.at[matrix, 0, k - 1, sub],
                here.next,
            ),
            remote(
                weights.at[matrix, slot(k - 1, which), back_cols],
                weights.at[matrix, slot(k, which), back_cols],
                ring_send.at[matrix, 1, k - 1, sub],
                ring_recv.at[matrix, 1, k - 1, sub],
                here.prev,
            ),
        )

    def start_ring(matrix, sub):
        for i in range(len(shards)):
            if shards[i][0] == matrix:
                if sub == 0:
                    swap_copies(i)[0].wait()
                else:
                    swap_copies(i)[1].wait_recv()
        for copy in hops(matrix, 1, sub):
            copy.start()

    def pump(matrix, k, sub):
        came = hops(matrix, k, sub)
        if k < far:
            further = hops(matrix, k + 1, sub)
        for i in range(2):
            came[i].wait_recv()
            if k < far:
                further[i].start()
        if k == far - 1 and matrix < 2:
            start_ring(matrix + 1, sub)

    steps = [
        (matrix, k, sub) for matrix in range(3) for k in range(1, far + 1) for sub in range(2)
    ]
    done = [0]

    def pump_to(number):
        while done[0] < min(number, len(steps)):
            pump(*steps[done[0]])
            done[0] += 1

    y_rows = rows // 2
    parts = 4
    part = y_rows // parts

    def prefix_rows(which_half, i):
        return pl.ds(pl.multiple_of(which_half * y_rows + i * part, part), part)

    def prefix_hop(i, from_input):
        at = prefix_rows(here.y, i)
        return remote(
            x_ref.at[at] if from_input else prefix_v.at[at],
            prefix_v.at[at],
            prefix_send.at[0, i],
            prefix_recv.at[0, i],
            here.along(1),
        )

    def prefix_cross(i, from_input):
        at = prefix_rows(here.y, i)
        return remote(
            x_ref.at[at] if from_input else prefix_v.at[at],
            prefix_v.at[at],
            prefix_send.at[1, i],
            prefix_recv.at[1, i],
            here.across,
        )

    def prefix_stage(stage, i):
        @pl.when(here.z == stage)
        def _():
            if stage == 0:
                prefix_hop(i, True).start()
                prefix_cross(i, True).start()
            else:
                prefix_hop(i, False).wait_recv()
                if stage < sol_size - 1:
                    prefix_hop(i, False).start()
                prefix_cross(i, False).start()

    def prefix_finish():
        for i in range(parts):
            prefix_cross(i, False).wait_recv()

        @pl.when(here.z == 0)
        def _():
            for i in range(parts):
                at = prefix_rows(here.y, i)
                prefix_v[at, :] = x_ref[at, :]

    cot_load = pltpu.make_async_copy(cot_hbm, active_v.at[pl.ds(0, rows)], cot_sem.at[1])
    start_swap(0)
    for i in range(parts):
        prefix_stage(0, i)
    start_swap(1)
    start_swap(2)
    cot_load.start()

    start_ring(0, 0)
    start_ring(0, 1)

    def ordered(ref, at):
        return jnp.concatenate(
            [ref[at, pl.ds(pl.multiple_of(b * shard, shard), shard)] for b in blocks], axis=1
        ).astype(WIDE)

    gain, shift = vectors_ref[0:1, :], vectors_ref[1:2, :]
    gain_two, shift_two = vectors_ref[2:3, :], vectors_ref[3:4, :]

    def norm_into(ref, start):
        @pl.loop(0, rows // 128)
        def _(t):
            at = pl.ds(pl.multiple_of(t * 128, 128), 128)
            to = pl.ds(pl.multiple_of(start + t * 128, 128), 128)
            normed_v[to, :] = norm_rows(ordered(ref, at), gain, shift).astype(LOW)

    normed_pair = remote(
        normed_v.at[pl.ds(0, rows)],
        normed_v.at[pl.ds(rows, rows)],
        pair_send.at[1],
        pair_recv.at[1],
        here.sibling,
    )
    prefix_pair = remote(
        normed_v.at[pl.ds(2 * rows, rows)],
        normed_v.at[pl.ds(3 * rows, rows)],
        pair_send.at[2],
        pair_recv.at[2],
        here.sibling,
    )
    norm_into(x_ref, 0)
    normed_pair.start()
    pump_to(1)
    for step in range(1, sol_size + parts - 1):
        for i in range(parts):
            if 1 <= step - i < sol_size:
                prefix_stage(step - i, i)
        pump_to(1 + step)
    pump_to(2 * far)

    cot_pair = remote(
        core_send_v,
        cot_out.at[pl.ds(rows, rows)],
        pair_send.at[0],
        pair_recv.at[0],
        here.sibling,
    )
    cot_own = pltpu.make_async_copy(core_send_v, cot_out.at[pl.ds(0, rows)], cot_sem.at[0])

    cot_load.wait()

    @pl.loop(0, rows // 128)
    def _(t):
        at = pl.ds(pl.multiple_of(t * 128, 128), 128)
        core_send_v[at, :] = ordered(active_v, at).astype(LOW)

    cot_pair.start()
    cot_own.start()

    load_first = pltpu.make_async_copy(weights.at[0], w_v, load_sem.at[0])
    load_first.start()
    normed_pair.wait_recv()
    load_first.wait()

    def row_tile(t):
        return pl.ds(pl.multiple_of(t * CHUNK, CHUNK), CHUNK)

    def project(first, last, with_queries):
        @pl.loop(first, last)
        def _(t):
            at = row_tile(t)
            tile = normed_v[at, :]
            kv = dot_plain(tile, w_v[:, head_cols : 3 * head_cols])
            key_v[at, :] = kv[:, :head_cols].astype(LOW)
            value_v[at, :] = kv[:, head_cols:].astype(LOW)
            if with_queries:
                query_v[at, :] = dot_plain(tile, w_v[:, :head_cols]).astype(LOW)

    tiles = rows // CHUNK
    project(0, 2 * tiles, True)
    pump_to(2 * far + 1)
    prefix_finish()
    norm_into(prefix_v, 2 * rows)
    prefix_pair.start()
    pump_to(2 * far + 2)
    prefix_pair.wait_recv()
    project(2 * tiles, 4 * tiles, False)

    stores = []

    def store(src, dst):
        copy = pltpu.make_async_copy(src, dst, store_sem.at[len(stores)])
        copy.start()
        stores.append(copy)

    store(normed_v, normed_out)
    store(query_v, query_out)
    store(key_v, key_out)
    store(value_v, value_out)

    def probs_copy(unit):
        return pltpu.make_async_copy(
            probs_v.at[unit % 2], probs_out.at[unit], probs_sem.at[unit % 2]
        )

    def attend(unit):
        block, head = unit // local_heads, unit % local_heads
        cols = pl.ds(pl.multiple_of(head * HEAD_DIM, HEAD_DIM), HEAD_DIM)
        place = jnp.where(block == 0, here.dp, here.dp + 1 - 2 * core)
        own_live = live_ref[place * sol_size + here.z]
        prefix_live = jnp.where(here.z == 0, 0, live_ref[place * sol_size])
        own_at = pl.ds(pl.multiple_of(block * rows, rows), rows)
        prefix_at = pl.ds(pl.multiple_of((2 + block) * rows, rows), rows)

        @pl.when(unit >= 2)
        def _():
            probs_copy(unit - 2).wait()

        for t in range(tiles):
            at = pl.ds(pl.multiple_of(block * rows + t * CHUNK, CHUNK), CHUNK)
            queries = query_v[at, cols]
            col = lax.broadcasted_iota(jnp.int32, (CHUNK, rows), 1)
            row = lax.broadcasted_iota(jnp.int32, (CHUNK, rows), 0) + t * CHUNK
            first = dot_right_t(queries, key_v[prefix_at, cols]) * scale
            second = dot_right_t(queries, key_v[own_at, cols]) * scale
            first = jnp.where(col < prefix_live, first, NEG_FILL)
            second = jnp.where(
                jnp.logical_and(col <= row, col < own_live), second, NEG_FILL
            )
            peak = jnp.maximum(
                jnp.max(first, axis=-1, keepdims=True), jnp.max(second, axis=-1, keepdims=True)
            )
            first = jnp.exp(first - peak)
            second = jnp.exp(second - peak)
            total = jnp.sum(first, axis=-1, keepdims=True) + jnp.sum(
                second, axis=-1, keepdims=True
            )
            inverse = 1.0 / total
            first = (first * inverse).astype(LOW)
            second = (second * inverse).astype(LOW)
            probs_v[unit % 2, pl.ds(t * CHUNK, CHUNK), pl.ds(0, rows)] = first
            probs_v[unit % 2, pl.ds(t * CHUNK, CHUNK), pl.ds(rows, rows)] = second
            mixed_v[at, cols] = (
                dot_plain(first, value_v[prefix_at, cols])
                + dot_plain(second, value_v[own_at, cols])
            ).astype(LOW)
        probs_copy(unit).start()

    units = 2 * local_heads
    for quarter in range(4):
        pl.loop(quarter * units // 4, (quarter + 1) * units // 4)(attend)
        pump_to(2 * far + (2, 3, 4, 4)[quarter])
    for unit in (units - 2, units - 1):
        probs_copy(unit).wait()
    store(mixed_v, mixed_out)

    out_cols = slice(3 * head_cols, 4 * head_cols)

    def core_copy(t):
        at = pl.ds(t * CHUNK, CHUNK)
        return remote(
            core_send_v.at[at], core_recv_v.at[at], sum_send.at[0, t], sum_recv.at[0, t], here.sibling
        )

    def cross_copy(t):
        at = pl.ds(t * CHUNK, CHUNK)
        return remote(
            cross_send_v.at[at], cross_recv_v.at[at], sum_send.at[1, t], sum_recv.at[1, t], here.across
        )

    def two_copy(t):
        return remote(
            normed_two_v.at[pl.ds(t * CHUNK, CHUNK)],
            normed_two_v.at[pl.ds(rows + t * CHUNK, CHUNK)],
            sum_send.at[2, t],
            sum_recv.at[2, t],
            here.sibling,
        )

    def hidden_store(t):
        return pltpu.make_async_copy(
            hidden_v, hidden_out.at[pl.ds(t * CHUNK, CHUNK)], load_sem.at[1]
        )

    cot_own.wait()
    cot_pair.wait_send()
    for t in range(tiles):
        core_send_v[pl.ds(t * CHUNK, CHUNK), :] = dot_right_t(
            mixed_v[pl.ds(rows + t * CHUNK, CHUNK), :], w_v[:, out_cols]
        ).astype(LOW)
        core_copy(t).start()
    for t in range(tiles):
        at = pl.ds(t * CHUNK, CHUNK)
        partial = dot_right_t(mixed_v[at, :], w_v[:, out_cols])
        core_copy(t).wait_recv()
        cross_send_v[at, :] = (partial + core_recv_v[at, :].astype(WIDE)).astype(LOW)
        cross_copy(t).start()
    pump_to(4 * far)
    load_second = pltpu.make_async_copy(weights.at[1], w_v, load_sem.at[0])
    load_second.start()
    for t in range(tiles):
        at = pl.ds(t * CHUNK, CHUNK)
        if t > 0:
            pump_to(4 * far + 2)
        cross_copy(t).wait_recv()
        hidden = (
            ordered(x_ref, at)
            + cross_send_v[at, :].astype(WIDE)
            + cross_recv_v[at, :].astype(WIDE)
        )
        if t > 0:
            hidden_store(t - 1).wait()
        hidden_v[...] = hidden
        hidden_store(t).start()
        normed_two_v[at, :] = norm_rows(hidden, gain_two, shift_two).astype(LOW)
        two_copy(t).start()
    hidden_store(tiles - 1).wait()
    load_second.wait()
    for t in range(tiles):
        two_copy(t).wait_recv()
    store(normed_two_v, normed_two_out)

    bend = math.sqrt(2.0 / math.pi)
    spans = ff // half

    def feed(i):
        at = row_tile(i // spans)
        cols = pl.ds(pl.multiple_of((i % spans) * half, half), half)
        upward = dot_plain(normed_two_v[at, :], w_v[:, cols]) + up_bias_ref[:, cols]
        square = upward * upward
        curve = jnp.tanh(bend * (upward + 0.044715 * (upward * square)))
        active_v[at, cols] = (0.5 * upward * (1.0 + curve)).astype(LOW)
        slope_v[at, cols] = (
            0.5 * (1.0 + curve)
            + 0.5 * upward * (1.0 - curve * curve) * (bend + (3.0 * 0.044715 * bend) * square)
        ).astype(LOW)

    for i in range(parts):

        @pl.when(here.z < sol_size - 1)
        def _():
            prefix_hop(i, False).wait_send()

        prefix_cross(i, False).wait_send()

    feeds = 2 * tiles * spans
    for quarter in range(4):
        pl.loop(quarter * feeds // 4, (quarter + 1) * feeds // 4)(feed)
        pump_to(4 * far + 3 + quarter)
    store(active_v, active_out)
    store(slope_v, slope_out)

    pump_to(len(steps))
    cot_pair.wait_recv()
    normed_pair.wait_send()
    prefix_pair.wait_send()
    for i in range(len(shards)):
        swap_copies(i)[1].wait_send()
    for step in steps:
        for copy in hops(*step):
            copy.wait_send()
    for t in range(tiles):
        core_copy(t).wait_send()
        cross_copy(t).wait_send()
        two_copy(t).wait_send()
    for copy in stores:
        copy.wait()


def run_forward(dp_size, sol_size, x, vectors, up_bias, live_rows, cot, matrices):
    rows, width = x.shape
    head_cols = matrices[0].shape[1] // 2
    ff = matrices[4].shape[1] // 2
    heads = head_cols // HEAD_DIM
    count = dp_size // 2 * sol_size
    far = count // 2

    def shape(*dims, dtype=LOW):
        return jax.ShapeDtypeStruct(dims, dtype)

    outs = [
        shape(3, width, width),
        shape(4 * rows, width),
        shape(2 * rows, width),
        shape(2 * rows, head_cols),
        shape(4 * rows, head_cols),
        shape(4 * rows, head_cols),
        shape(2 * heads, rows, 2 * rows),
        shape(2 * rows, head_cols),
        shape(rows, width, dtype=WIDE),
        shape(2 * rows, width),
        shape(2 * rows, ff),
        shape(2 * rows, ff),
    ]
    dma = pltpu.SemaphoreType.DMA
    return pl.pallas_call(
        functools.partial(forward_kernel, dp_size, sol_size),
        out_shape=outs,
        in_specs=[
            vmem_spec(),
            vmem_spec(),
            vmem_spec(),
            pl.BlockSpec(memory_space=pltpu.SMEM),
        ]
        + [any_spec()]
        + [vmem_spec()] * 6,
        out_specs=[any_spec()] * len(outs),
        scratch_shapes=[
            pltpu.VMEM((width, width), LOW),
            pltpu.VMEM((4 * rows, width), LOW),
            pltpu.VMEM((2 * rows, head_cols), LOW),
            pltpu.VMEM((4 * rows, head_cols), LOW),
            pltpu.VMEM((4 * rows, head_cols), LOW),
            pltpu.VMEM((2, rows, 2 * rows), LOW),
            pltpu.VMEM((2 * rows, head_cols), LOW),
            pltpu.VMEM((CHUNK, width), WIDE),
            pltpu.VMEM((2 * rows, width), LOW),
            pltpu.VMEM((2 * rows, ff), LOW),
            pltpu.VMEM((2 * rows, ff), LOW),
        ]
        + [pltpu.VMEM((rows, width), LOW)] * 4
        + [
            dma((3, 2, far, 2)),
            dma((3, 2, far, 2)),
            dma((6,)),
            dma((6,)),
            dma((6,)),
            dma((2, 4)),
            dma((2, 4)),
            dma((3,)),
            dma((3,)),
            dma((3, rows // CHUNK)),
            dma((3, rows // CHUNK)),
            dma((2,)),
            dma((2,)),
            dma((2,)),
            dma((16,)),
        ],
        compiler_params=pltpu.CompilerParams(
            collective_id=0, has_side_effects=True, vmem_limit_bytes=60 * 2**20
        ),
    )(x, vectors, up_bias, live_rows, cot, *matrices)


class RingSum:
    def __init__(self, here, chunk, send_v, recv_v, stage_v, sems, target):
        self.here, self.chunk = here, chunk
        self.send_v, self.recv_v, self.stage_v = send_v, recv_v, stage_v
        self.send_sem, self.recv_sem, self.end_sem = sems
        self.target = target
        self.far = here.count // 2
        self.cols = stage_v.shape[2]
        self.steps = [(t, sub) for t in range(1, self.far + 1) for sub in range(2)]
        self.done = 0

    def _class(self, sub):
        return self.here.core if sub == 0 else 1 - self.here.core

    def _columns(self, t, way):
        if t > 1:
            return pl.ds(0, self.cols)
        return pl.ds(way * (self.cols // 2), self.cols // 2)

    def _copy(self, t, way, sub):
        at = self._columns(t, way)
        return remote(
            self.send_v.at[way, sub, :, at],
            self.recv_v.at[(t - 1) % 3, way, sub, :, at],
            self.send_sem.at[t - 1, way, sub],
            self.recv_sem.at[t - 1, way, sub],
            self.here.prev if way else self.here.next,
        )

    def _event(self, t, sub):
        far, count = self.far, self.here.count
        half = self.cols // 2
        if t == 1:
            value = self.chunk(far, self._class(sub))
            self.send_v[0, sub, :, :half] = value[:, :half].astype(LOW)
            self.send_v[1, sub, :, half:] = value[:, half:].astype(LOW)
            for way in range(2):
                self._copy(1, way, sub).start()
            return
        for way in range(2):
            j = far + 1 - t if way == 0 else count - (far + 1 - t)
            value = self.chunk(j, self._class(sub))
            self._copy(t - 1, way, sub).wait()
            if t == 2:
                near = slice(0, half) if way == 0 else slice(half, 2 * half)
                rest = slice(half, 2 * half) if way == 0 else slice(0, half)
                self.send_v[way, sub, :, near] = (
                    value[:, near] + self.recv_v[0, way, sub, :, near].astype(WIDE)
                ).astype(LOW)
                self.send_v[way, sub, :, rest] = value[:, rest].astype(LOW)
            else:
                self.send_v[way, sub] = (
                    value + self.recv_v[(t - 2) % 3, way, sub].astype(WIDE)
                ).astype(LOW)
            self._copy(t, way, sub).start()

    def _last(self, sub):
        value = self.chunk(0, self._class(sub))
        for way in range(2):
            self._copy(self.far, way, sub).wait()
        value = value + self.recv_v[(self.far - 1) % 3, 0, sub].astype(WIDE)
        self.stage_v[sub] = value + self.recv_v[(self.far - 1) % 3, 1, sub].astype(WIDE)
        for copy in self._results(sub):
            copy.start()

    def _results(self, sub):
        copies = []
        core = self.here.core
        for i, (ref, start, size) in enumerate(self.target):
            to = ref.at[:, pl.ds(pl.multiple_of(core * size, size), size)]
            source = self.stage_v.at[sub, :, pl.ds(start, size)]
            if sub == 0:
                copies.append(pltpu.make_async_copy(source, to, self.end_sem.at[0, i]))
            else:
                copies.append(
                    remote(
                        source, to, self.end_sem.at[1, i], self.end_sem.at[2, i], self.here.sibling
                    )
                )
        return copies

    def to(self, number):
        while self.done < min(number, len(self.steps) + 2):
            if self.done < len(self.steps):
                self._event(*self.steps[self.done])
            else:
                self._last(self.done - len(self.steps))
            self.done += 1

    def finish(self):
        self.to(len(self.steps) + 2)
        for sub in range(2):
            for copy in self._results(sub):
                copy.wait()


def ring_sum_scratch(far, shard, cols, results):
    dma = pltpu.SemaphoreType.DMA
    return [
        pltpu.VMEM((2, 2, shard, cols), LOW),
        pltpu.VMEM((3, 2, 2, shard, cols), LOW),
        pltpu.VMEM((2, shard, cols), WIDE),
        dma((far, 2, 2)),
        dma((far, 2, 2)),
        dma((3, results)),
    ]


def norm_back(values, gain, grad):
    row_mean = jnp.mean(values, axis=-1, keepdims=True)
    centered = values - row_mean
    variance = jnp.mean(centered * centered, axis=-1, keepdims=True)
    inverse = lax.rsqrt(variance + EPSILON)
    unit = centered * inverse
    scaled = grad * gain
    terms = grad * unit
    along = jnp.mean(scaled * unit, axis=-1, keepdims=True)
    level = jnp.mean(scaled, axis=-1, keepdims=True)
    return (
        (scaled - level - unit * along) * inverse,
        jnp.sum(terms, axis=0, keepdims=True),
        jnp.sum(grad, axis=0, keepdims=True),
    )


def tile_rows(t):
    return pl.ds(t * CHUNK, CHUNK)


def down_kernel(
    dp_size,
    sol_size,
    vectors_ref,
    weights,
    cot_hbm,
    active_hbm,
    slope_hbm,
    hidden_hbm,
    grad_up_out,
    branch_out,
    grad_hidden_out,
    mlp_low_out,
    down_grad_out,
    sums_ref,
    cot_v,
    active_v,
    slope_v,
    down_v,
    up_v,
    hidden_v,
    core_send_v,
    core_recv_v,
    second_recv_v,
    cross_send_v,
    cross_recv_v,
    ring_send_v,
    ring_recv_v,
    stage_v,
    ring_send,
    ring_recv,
    ring_end,
    load_sem,
    store_sem,
    sum_send,
    sum_recv,
):
    here = Place(dp_size, sol_size)
    rows, width = core_send_v.shape
    shard = stage_v.shape[1]
    ff = active_v.shape[1]
    tiles = rows // CHUNK
    halves = (pl.ds(0, width // 2), pl.ds(width // 2, width // 2))
    loads = [
        pltpu.make_async_copy(src, dst, load_sem.at[i])
        for i, (src, dst) in enumerate(
            (
                (cot_hbm, cot_v),
                (active_hbm, active_v),
                (weights.at[2], down_v),
                (slope_hbm, slope_v),
                (weights.at[1], up_v),
            )
        )
    ]
    for copy in loads:
        copy.start()
    here.greet()

    def chunk(j, which):
        at = pl.ds(pl.multiple_of((2 * j + which) * shard, shard), shard)
        return dot_left_t(cot_v[:, at], active_v[...])

    ring = RingSum(
        here,
        chunk,
        ring_send_v,
        ring_recv_v,
        stage_v,
        (ring_send, ring_recv, ring_end),
        ((down_grad_out, 0, ff),),
    )
    loads[0].wait()
    loads[1].wait()
    ring.to(2)
    loads[2].wait()
    loads[3].wait()

    sums_ref[...] = jnp.zeros_like(sums_ref)
    spans = 2

    def back_feed(i):
        at = pl.ds(pl.multiple_of(i // spans * CHUNK, CHUNK), CHUNK)
        cols = pl.ds(pl.multiple_of(i % spans * (ff // spans), ff // spans), ff // spans)
        grad = dot_plain(cot_v[at, :], down_v[:, cols]) * slope_v[at, cols].astype(WIDE)
        low = grad.astype(LOW)
        slope_v[at, cols] = low
        sums_ref[3:4, cols] += jnp.sum(low.astype(WIDE), axis=0, keepdims=True)

    pl.loop(0, tiles * spans)(back_feed)
    ring.to(3)
    pl.loop(tiles * spans, 2 * tiles * spans)(back_feed)
    ring.to(4)
    loads[4].wait()
    stores = [pltpu.make_async_copy(slope_v, grad_up_out, store_sem.at[0])]
    stores[0].start()

    def core_copy(t):
        return remote(
            core_send_v.at[tile_rows(t)],
            core_recv_v.at[tile_rows(t)],
            sum_send.at[0, t],
            sum_recv.at[0, t],
            here.sibling,
        )

    def cross_copy(t):
        return remote(
            cross_send_v.at[tile_rows(t)],
            cross_recv_v.at[tile_rows(t)],
            sum_send.at[1, t],
            sum_recv.at[1, t],
            here.across,
        )

    def second_copy(t):
        return remote(
            core_send_v.at[tile_rows(t)],
            second_recv_v.at[tile_rows(t)],
            sum_send.at[2, t],
            sum_recv.at[2, t],
            here.sibling,
        )

    def branch_copy(t):
        return remote(
            core_recv_v.at[tile_rows(t)],
            branch_out.at[pl.ds(rows + t * CHUNK, CHUNK)],
            sum_send.at[3, t],
            sum_recv.at[3, t],
            here.sibling,
        )

    for t in range(tiles):
        for cols in halves:
            core_send_v[tile_rows(t), cols] = dot_right_t(
                slope_v[pl.ds(rows + t * CHUNK, CHUNK), :], up_v[cols, :]
            ).astype(LOW)
        core_copy(t).start()
    for t in range(tiles):
        at = tile_rows(t)
        core_copy(t).wait_recv()
        for cols in halves:
            cross_send_v[at, cols] = (
                dot_right_t(slope_v[at, :], up_v[cols, :]) + core_recv_v[at, cols].astype(WIDE)
            ).astype(LOW)
        cross_copy(t).start()
    ring.to(5)

    for t in range(tiles):
        core_copy(t).wait_send()
        for cols in halves:
            core_send_v[tile_rows(t), cols] = dot_right_t(
                active_v[pl.ds(rows + t * CHUNK, CHUNK), :], down_v[cols, :]
            ).astype(LOW)
        second_copy(t).start()
    ring.to(6)
    for t in range(tiles):
        at = tile_rows(t)
        second_copy(t).wait_recv()
        for cols in halves:
            second_recv_v[at, cols] = (
                dot_right_t(active_v[at, :], down_v[cols, :])
                + second_recv_v[at, cols].astype(WIDE)
            ).astype(LOW)
    stores.append(pltpu.make_async_copy(second_recv_v, mlp_low_out, store_sem.at[1]))
    stores[1].start()
    ring.to(8)

    gain = vectors_ref[2:3, :]

    def hidden_load(t):
        return pltpu.make_async_copy(hidden_hbm.at[tile_rows(t)], hidden_v, load_sem.at[0])

    def hidden_store(t):
        return pltpu.make_async_copy(hidden_v, grad_hidden_out.at[tile_rows(t)], store_sem.at[2])

    hidden_load(0).start()
    for t in range(tiles):
        at = tile_rows(t)
        hidden_load(t).wait()
        cross_copy(t).wait_recv()
        for part in range(2):
            inner = pl.ds(part * (CHUNK // 2), CHUNK // 2)
            here_at = pl.ds(t * CHUNK + part * (CHUNK // 2), CHUNK // 2)
            grad = cross_send_v[here_at, :].astype(WIDE) + cross_recv_v[here_at, :].astype(WIDE)
            back, gain_terms, shift_terms = norm_back(hidden_v[inner, :], gain, grad)
            cot = cot_v[here_at, :].astype(WIDE)
            sums_ref[0:1, :] += gain_terms
            sums_ref[1:2, :] += shift_terms
            sums_ref[2:3, :] += jnp.sum(cot, axis=0, keepdims=True)
            back = back + cot
            hidden_v[inner, :] = back
            core_recv_v[here_at, :] = back.astype(LOW)
        branch_copy(t).start()
        hidden_store(t).start()
        if t == 0:
            ring.to(9)
        hidden_store(t).wait()
        if t + 1 < tiles:
            hidden_load(t + 1).start()
    stores.append(
        pltpu.make_async_copy(core_recv_v, branch_out.at[pl.ds(0, rows)], store_sem.at[3])
    )
    stores[2].start()
    ring.finish()
    for t in range(tiles):
        cross_copy(t).wait_send()
        second_copy(t).wait_send()
        branch_copy(t).wait()
    for copy in stores:
        copy.wait()


def run_down(dp_size, sol_size, shard, vectors, weights, cot, active, slope, hidden):
    rows, width = hidden.shape
    ff = active.shape[1]
    count = dp_size // 2 * sol_size
    tiles = rows // CHUNK
    dma = pltpu.SemaphoreType.DMA

    def shape(*dims, dtype=LOW):
        return jax.ShapeDtypeStruct(dims, dtype)

    outs = [
        shape(2 * rows, ff),
        shape(2 * rows, width),
        shape(rows, width, dtype=WIDE),
        shape(rows, width),
        shape(shard, 2 * ff, dtype=WIDE),
        shape(8, width, dtype=WIDE),
    ]
    return pl.pallas_call(
        functools.partial(down_kernel, dp_size, sol_size),
        out_shape=outs,
        in_specs=[vmem_spec()] + [any_spec()] * 5,
        out_specs=[any_spec()] * 5 + [vmem_spec()],
        scratch_shapes=[
            pltpu.VMEM((2 * rows, width), LOW),
            pltpu.VMEM((2 * rows, ff), LOW),
            pltpu.VMEM((2 * rows, ff), LOW),
            pltpu.VMEM((width, ff), LOW),
            pltpu.VMEM((width, ff), LOW),
            pltpu.VMEM((CHUNK, width), WIDE),
        ]
        + [pltpu.VMEM((rows, width), LOW)] * 5
        + ring_sum_scratch(count // 2, shard, ff, 1)
        + [
            dma((5,)),
            dma((4,)),
            dma((4, tiles)),
            dma((4, tiles)),
        ],
        compiler_params=pltpu.CompilerParams(
            collective_id=1, has_side_effects=True, vmem_limit_bytes=60 * 2**20
        ),
    )(vectors, weights, cot, active, slope, hidden)


def read_ordered(ref, at, blocks, part):
    return jnp.concatenate(
        [ref[at, pl.ds(pl.multiple_of(b * part, part), part)] for b in blocks], axis=1
    ).astype(WIDE)


def write_ordered(ref, at, blocks, part, values):
    for j, b in enumerate(blocks):
        ref[at, pl.ds(pl.multiple_of(b * part, part), part)] = values[
            :, j * part : (j + 1) * part
        ].astype(ref.dtype)


def attend_back_kernel(
    dp_size,
    sol_size,
    vectors_ref,
    weights,
    normed_two_hbm,
    grad_up_hbm,
    branch_hbm,
    query_hbm,
    key_hbm,
    value_hbm,
    probs_hbm,
    mlp_low_hbm,
    hidden_hbm,
    query_grad_out,
    kv_grad_out,
    own_low_out,
    prefix_half_out,
    up_grad_out,
    outputs_out,
    mlp_recv_out,
    normed_two_v,
    grad_up_v,
    branch_v,
    w_v,
    query_v,
    key_v,
    value_v,
    mixed_grad_v,
    probs_v,
    query_grad_v,
    kv_grad_v,
    core_recv_v,
    second_recv_v,
    half_recv_v,
    mlp_low_v,
    mlp_recv_v,
    hidden_v,
    ring_send_v,
    ring_recv_v,
    stage_v,
    ring_send,
    ring_recv,
    ring_end,
    load_sem,
    probs_sem,
    tile_sem,
    store_sem,
    sum_send,
    sum_recv,
    cross_send,
    cross_recv,
):
    here = Place(dp_size, sol_size)
    rows, width = core_recv_v.shape
    core_send_v = branch_v.at[pl.ds(0, rows)]
    half_send_v = branch_v.at[pl.ds(rows, CHUNK)]
    half_keep_v = branch_v.at[pl.ds(rows + CHUNK, CHUNK)]
    shard = stage_v.shape[1]
    ff = grad_up_v.shape[1]
    head_cols = query_v.shape[1]
    local_heads = head_cols // HEAD_DIM
    scale = 1.0 / math.sqrt(HEAD_DIM)
    tiles = rows // CHUNK
    blocks = here.blocks()
    halves = (pl.ds(0, width // 2), pl.ds(width // 2, width // 2))
    loads = [
        pltpu.make_async_copy(src, dst, load_sem.at[i])
        for i, (src, dst) in enumerate(
            (
                (normed_two_hbm, normed_two_v),
                (grad_up_hbm, grad_up_v),
                (branch_hbm, branch_v),
                (weights.at[0], w_v),
                (query_hbm, query_v),
                (key_hbm, key_v),
                (value_hbm, value_v),
            )
        )
    ]
    for copy in loads:
        copy.start()

    def probs_load(unit):
        return pltpu.make_async_copy(
            probs_hbm.at[unit], probs_v.at[unit % 2], probs_sem.at[unit % 2]
        )

    probs_load(0).start()
    here.greet()
    mlp_cross = remote(
        mlp_low_hbm, mlp_recv_out, cross_send.at[0], cross_recv.at[0], here.across
    )
    mlp_cross.start()

    def chunk(j, which):
        at = pl.ds(pl.multiple_of((2 * j + which) * shard, shard), shard)
        return dot_left_t(normed_two_v[:, at], grad_up_v[...])

    ring = RingSum(
        here,
        chunk,
        ring_send_v,
        ring_recv_v,
        stage_v,
        (ring_send, ring_recv, ring_end),
        ((up_grad_out, 0, ff),),
    )
    loads[0].wait()
    loads[1].wait()
    ring.to(2)
    loads[2].wait()
    loads[3].wait()

    @pl.loop(0, 2 * tiles)
    def _(t):
        at = pl.ds(pl.multiple_of(t * CHUNK, CHUNK), CHUNK)
        mixed_grad_v[at, :] = dot_plain(
            branch_v[at, :], w_v[:, 3 * head_cols : 4 * head_cols]
        ).astype(LOW)

    for i in range(4, 7):
        loads[i].wait()

    units = 2 * local_heads

    def back(unit):
        block, head = unit // local_heads, unit % local_heads
        cols = pl.ds(pl.multiple_of(head * HEAD_DIM, HEAD_DIM), HEAD_DIM)
        value_cols = pl.ds(
            pl.multiple_of(head_cols + head * HEAD_DIM, HEAD_DIM), HEAD_DIM
        )
        own_at = pl.ds(pl.multiple_of(block * rows, rows), rows)
        prefix_at = pl.ds(pl.multiple_of((2 + block) * rows, rows), rows)
        probs_load(unit).wait()

        @pl.when(unit + 1 < units)
        def _():
            probs_load(unit + 1).start()

        sums = None
        for t in range(tiles):
            at = pl.ds(pl.multiple_of(block * rows + t * CHUNK, CHUNK), CHUNK)
            grad = mixed_grad_v[at, cols]
            queries = query_v[at, cols]
            inner = pl.ds(t * CHUNK, CHUNK)
            first_low = probs_v[unit % 2, inner, pl.ds(0, rows)]
            second_low = probs_v[unit % 2, inner, pl.ds(rows, rows)]
            first, second = first_low.astype(WIDE), second_low.astype(WIDE)
            first_grad = dot_right_t(grad, value_v[prefix_at, cols])
            second_grad = dot_right_t(grad, value_v[own_at, cols])
            delta = jnp.sum(first * first_grad, axis=-1, keepdims=True) + jnp.sum(
                second * second_grad, axis=-1, keepdims=True
            )
            first_scores = (first * (first_grad - delta)).astype(LOW)
            second_scores = (second * (second_grad - delta)).astype(LOW)
            query_grad_v[at, cols] = (
                (
                    dot_plain(first_scores, key_v[prefix_at, cols])
                    + dot_plain(second_scores, key_v[own_at, cols])
                )
                * scale
            ).astype(LOW)
            terms = [
                dot_left_t(second_scores, queries),
                dot_left_t(second_low, grad),
                dot_left_t(first_scores, queries),
                dot_left_t(first_low, grad),
            ]
            sums = terms if sums is None else [a + b for a, b in zip(sums, terms)]
        kv_grad_v[own_at, cols] = (sums[0] * scale).astype(LOW)
        kv_grad_v[own_at, value_cols] = sums[1].astype(LOW)
        kv_grad_v[prefix_at, cols] = (sums[2] * scale).astype(LOW)
        kv_grad_v[prefix_at, value_cols] = sums[3].astype(LOW)

    for quarter in range(4):
        pl.loop(quarter * units // 4, (quarter + 1) * units // 4)(back)
        ring.to(3 + quarter)
    stores = []

    def store(src, dst):
        copy = pltpu.make_async_copy(src, dst, store_sem.at[len(stores)])
        copy.start()
        stores.append(copy)

    store(query_grad_v, query_grad_out)
    store(kv_grad_v, kv_grad_out)

    def core_copy(t):
        return remote(
            core_send_v.at[tile_rows(t)],
            core_recv_v.at[tile_rows(t)],
            sum_send.at[0, t],
            sum_recv.at[0, t],
            here.sibling,
        )

    def second_copy(t):
        return remote(
            core_send_v.at[tile_rows(t)],
            second_recv_v.at[tile_rows(t)],
            sum_send.at[1, t],
            sum_recv.at[1, t],
            here.sibling,
        )

    half_copy = remote(half_send_v, half_recv_v, cross_send.at[1], cross_recv.at[1], here.across)
    kv_cols = pl.ds(head_cols, 2 * head_cols)

    def prefix_terms(at, cols):
        return dot_right_t(kv_grad_v[at, :], w_v[cols, kv_cols])

    for t in range(tiles):
        for cols in halves:
            core_send_v[tile_rows(t), cols] = prefix_terms(
                pl.ds(3 * rows + t * CHUNK, CHUNK), cols
            ).astype(LOW)
        second_copy(t).start()
    for t in range(tiles):
        second_copy(t).wait_recv()
    for keep in range(2):
        which = here.y if keep else 1 - here.y
        at = pl.ds(pl.multiple_of(2 * rows + which * CHUNK, CHUNK), CHUNK)
        came = pl.ds(pl.multiple_of(which * CHUNK, CHUNK), CHUNK)
        for cols in halves:
            value = prefix_terms(at, cols) + second_recv_v[came, cols].astype(WIDE)
            if keep:
                half_keep_v[:, cols] = value.astype(LOW)
            else:
                half_send_v[:, cols] = value.astype(LOW)
        if not keep:
            half_copy.start()
    ring.to(7)

    def own_terms(at, cols):
        return dot_right_t(query_grad_v[at, :], w_v[cols, 0:head_cols]) + dot_right_t(
            kv_grad_v[at, :], w_v[cols, kv_cols]
        )

    for t in range(tiles):
        second_copy(t).wait_send()
        for cols in halves:
            core_send_v[tile_rows(t), cols] = own_terms(
                pl.ds(rows + t * CHUNK, CHUNK), cols
            ).astype(LOW)
        core_copy(t).start()
    for t in range(tiles):
        at = tile_rows(t)
        core_copy(t).wait_recv()
        for cols in halves:
            core_recv_v[at, cols] = (
                own_terms(at, cols) + core_recv_v[at, cols].astype(WIDE)
            ).astype(LOW)
    store(core_recv_v, own_low_out)
    ring.to(8)

    half_copy.wait()
    write_ordered(
        half_send_v,
        slice(None),
        blocks,
        shard,
        half_keep_v[...].astype(WIDE) + half_recv_v[...].astype(WIDE),
    )
    store(half_send_v, prefix_half_out)

    small = mlp_low_v.shape[0]
    pieces = rows // small

    def piece_rows(t):
        return pl.ds(t * small, small)

    def tile_loads(t):
        return (
            pltpu.make_async_copy(hidden_hbm.at[piece_rows(t)], hidden_v, tile_sem.at[0]),
            pltpu.make_async_copy(mlp_low_hbm.at[piece_rows(t)], mlp_low_v, tile_sem.at[1]),
            pltpu.make_async_copy(mlp_recv_out.at[piece_rows(t)], mlp_recv_v, tile_sem.at[2]),
        )

    def tile_store(t):
        return pltpu.make_async_copy(
            half_keep_v.at[pl.ds(t % 2 * small, small)],
            outputs_out.at[piece_rows(t)],
            tile_sem.at[3 + t % 2],
        )

    mlp_cross.wait()
    for copy in tile_loads(0):
        copy.start()
    for t in range(pieces):
        for copy in tile_loads(t):
            copy.wait()
        value = (
            hidden_v[...]
            + mlp_low_v[...].astype(WIDE)
            + mlp_recv_v[...].astype(WIDE)
            + vectors_ref[4:5, :]
        )
        if t > 1:
            tile_store(t - 2).wait()
        write_ordered(half_keep_v, pl.ds(t % 2 * small, small), blocks, shard, value)
        tile_store(t).start()
        if t + 1 < pieces:
            for copy in tile_loads(t + 1):
                copy.start()
    for t in (pieces - 2, pieces - 1):
        tile_store(t).wait()
    ring.finish()
    for t in range(tiles):
        core_copy(t).wait_send()
    for copy in stores:
        copy.wait()


def run_attend_back(
    dp_size,
    sol_size,
    shard,
    vectors,
    weights,
    normed_two,
    grad_up,
    branch,
    query_rows,
    key_rows,
    value_rows,
    probs,
    mlp_low,
    hidden,
):
    rows, width = hidden.shape
    ff = grad_up.shape[1]
    head_cols = query_rows.shape[1]
    count = dp_size // 2 * sol_size
    tiles = rows // CHUNK
    dma = pltpu.SemaphoreType.DMA

    def shape(*dims, dtype=LOW):
        return jax.ShapeDtypeStruct(dims, dtype)

    def low(*dims):
        return pltpu.VMEM(dims, LOW)

    outs = [
        shape(2 * rows, head_cols),
        shape(4 * rows, 2 * head_cols),
        shape(rows, width),
        shape(rows // 2, width),
        shape(shard, 2 * ff, dtype=WIDE),
        shape(rows, width),
        shape(rows, width),
    ]
    return pl.pallas_call(
        functools.partial(attend_back_kernel, dp_size, sol_size),
        out_shape=outs,
        in_specs=[vmem_spec()] + [any_spec()] * 10,
        out_specs=[any_spec()] * len(outs),
        scratch_shapes=[
            low(2 * rows, width),
            low(2 * rows, ff),
            low(2 * rows, width),
            low(width, width),
            low(2 * rows, head_cols),
            low(4 * rows, head_cols),
            low(4 * rows, head_cols),
            low(2 * rows, head_cols),
            low(2, rows, 2 * rows),
            low(2 * rows, head_cols),
            low(4 * rows, 2 * head_cols),
            low(rows, width),
            low(rows, width),
            low(CHUNK, width),
            low(CHUNK // 2, width),
            low(CHUNK // 2, width),
            pltpu.VMEM((CHUNK // 2, width), WIDE),
        ]
        + ring_sum_scratch(count // 2, shard, ff, 1)
        + [
            dma((7,)),
            dma((2,)),
            dma((5,)),
            dma((4,)),
            dma((2, tiles)),
            dma((2, tiles)),
            dma((2,)),
            dma((2,)),
        ],
        compiler_params=pltpu.CompilerParams(
            collective_id=2, has_side_effects=True, vmem_limit_bytes=60 * 2**20
        ),
    )(
        vectors,
        weights,
        normed_two,
        grad_up,
        branch,
        query_rows,
        key_rows,
        value_rows,
        probs,
        mlp_low,
        hidden,
    )


def last_kernel(
    dp_size,
    sol_size,
    x_ref,
    vectors_ref,
    early_ref,
    normed_hbm,
    branch_hbm,
    query_grad_hbm,
    kv_grad_hbm,
    mixed_hbm,
    own_low_hbm,
    prefix_half_hbm,
    grad_hidden_hbm,
    query_out,
    key_out,
    value_out,
    out_out,
    input_grad_out,
    sums_ref,
    normed_v,
    branch_v,
    query_grad_v,
    kv_grad_v,
    mixed_v,
    own_low_v,
    own_recv_v,
    half_v,
    half_recv_v,
    prefix_v,
    grad_hidden_v,
    out_v,
    table_v,
    table_recv_v,
    ring_send_v,
    ring_recv_v,
    stage_v,
    ring_send,
    ring_recv,
    ring_end,
    load_sem,
    tile_sem,
    cross_send,
    cross_recv,
    chain_send,
    chain_recv,
    table_send,
    table_recv,
):
    here = Place(dp_size, sol_size)
    rows, width = x_ref.shape
    shard = stage_v.shape[1]
    head_cols = query_grad_v.shape[1]
    tiles = rows // CHUNK
    blocks = here.blocks()
    loads = [
        pltpu.make_async_copy(src, dst, load_sem.at[i])
        for i, (src, dst) in enumerate(
            (
                (query_grad_hbm, query_grad_v),
                (kv_grad_hbm, kv_grad_v),
                (mixed_hbm, mixed_v),
                (prefix_half_hbm, half_v),
                (normed_hbm, normed_v),
                (branch_hbm, branch_v),
                (own_low_hbm, own_low_v),
            )
        )
    ]
    for copy in loads:
        copy.start()
    partners = here.partners()
    here.greet(partners[1:])
    own_cross = remote(own_low_hbm, own_recv_v, cross_send.at[0], cross_recv.at[0], here.across)
    own_cross.start()

    def chunk(j, which):
        at = pl.ds(pl.multiple_of((2 * j + which) * shard, shard), shard)
        return jnp.concatenate(
            [
                dot_left_t(normed_v[: 2 * rows, at], query_grad_v[...]),
                dot_left_t(normed_v[:, at], kv_grad_v[...]),
                dot_left_t(branch_v[:, at], mixed_v[...]),
            ],
            axis=1,
        )

    ring = RingSum(
        here,
        chunk,
        ring_send_v,
        ring_recv_v,
        stage_v,
        (ring_send, ring_recv, ring_end),
        tuple(
            (ref, i * head_cols, head_cols)
            for i, ref in enumerate((query_out, key_out, value_out, out_out))
        ),
    )

    parts = chain_send.shape[0]
    part = CHUNK // parts

    def chain_copy(i):
        at = pl.ds(i * part, part)
        return remote(
            half_v.at[at], half_recv_v.at[at], chain_send.at[i], chain_recv.at[i], here.along(-1)
        )

    def mine(i):
        return pl.ds(pl.multiple_of(here.y * CHUNK + i * part, part), part)

    def half_cross(i):
        return remote(
            half_recv_v.at[pl.ds(i * part, part)],
            prefix_v.at[mine(i)],
            cross_send.at[1 + i],
            cross_recv.at[1 + i],
            here.across,
        )

    def chain(stage, i):
        at = pl.ds(i * part, part)

        @pl.when(here.z == stage)
        def _():
            if stage < sol_size - 1:
                chain_copy(i).wait_recv()
            if 0 < stage < sol_size - 1:
                half_v[at, :] = (
                    half_v[at, :].astype(WIDE) + half_recv_v[at, :].astype(WIDE)
                ).astype(LOW)
            if stage > 0:
                chain_copy(i).start()
            else:
                half_cross(i).start()
                prefix_v[mine(i), :] = half_recv_v[at, :]

    loads[3].wait()
    for i in range(parts):
        chain(sol_size - 1, i)

    @pl.when(here.z > 0)
    def _():
        prefix_v[...] = jnp.zeros_like(prefix_v)

    for i in (0, 1, 2, 4, 5):
        loads[i].wait()
    ring.to(2)
    for step in range(1, sol_size + parts - 1):
        for i in range(parts):
            if 1 <= step - i < sol_size:
                chain(sol_size - 1 - (step - i), i)
        ring.to(2 + step)

    loads[6].wait()
    own_cross.wait()

    @pl.when(here.z == 0)
    def _():
        for i in range(parts):
            half_cross(i).wait()

    gain = vectors_ref[0:1, :]

    def tile_load(t):
        return pltpu.make_async_copy(
            grad_hidden_hbm.at[tile_rows(t)], grad_hidden_v, tile_sem.at[0]
        )

    def tile_store(t):
        return pltpu.make_async_copy(out_v, input_grad_out.at[tile_rows(t)], tile_sem.at[1])

    tile_load(0).start()
    totals = [jnp.zeros((1, width), WIDE)] * 2
    small = CHUNK // 2
    for t in range(tiles):
        tile_load(t).wait()
        if t > 0:
            tile_store(t - 1).wait()
        for piece in range(2):
            at = pl.ds(t * CHUNK + piece * small, small)
            inner = pl.ds(piece * small, small)
            grad = (
                own_low_v[at, :].astype(WIDE)
                + own_recv_v[at, :].astype(WIDE)
                + read_ordered(prefix_v, at, blocks, shard)
            )
            back, gain_terms, shift_terms = norm_back(
                read_ordered(x_ref, at, blocks, shard), gain, grad
            )
            totals = [totals[0] + gain_terms, totals[1] + shift_terms]
            write_ordered(out_v, inner, blocks, shard, back + grad_hidden_v[inner, :])
        tile_store(t).start()
        if t + 1 < tiles:
            tile_load(t + 1).start()

    for row in range(2):
        write_ordered(table_v.at[0], pl.ds(row, 1), blocks, shard, totals[row])
    for row in range(3):
        write_ordered(
            table_v.at[0], pl.ds(2 + row, 1), blocks, shard, early_ref[row : row + 1, :]
        )
    bias = early_ref[3:4, :]
    table_v[0, 5:6, :] = jnp.where(here.core == 0, bias, 0.0)
    table_v[0, 6:7, :] = jnp.where(here.core == 0, 0.0, bias)
    table_v[0, 7:8, :] = jnp.zeros((1, width), WIDE)

    def table_copy(k):
        return remote(
            table_v.at[k], table_recv_v.at[k], table_send.at[k], table_recv.at[k], partners[k]
        )

    for k in range(len(partners)):
        table_copy(k).start()
        ring.to(9 + k)
        table_copy(k).wait_recv()
        if k + 1 < len(partners):
            table_v[k + 1] = table_v[k] + table_recv_v[k]
        else:
            sums_ref[...] = table_v[k] + table_recv_v[k]
    tile_store(tiles - 1).wait()
    ring.finish()
    for k in range(len(partners)):
        table_copy(k).wait_send()
    for i in range(parts):

        @pl.when(here.z > 0)
        def _():
            chain_copy(i).wait_send()


def run_last(
    dp_size,
    sol_size,
    shard,
    x,
    vectors,
    early,
    normed,
    branch,
    query_grad,
    kv_grad,
    mixed,
    own_low,
    prefix_half,
    grad_hidden,
):
    rows, width = x.shape
    head_cols = query_grad.shape[1]
    count = dp_size // 2 * sol_size
    bits = (dp_size * sol_size).bit_length() - 1
    dma = pltpu.SemaphoreType.DMA

    def shape(*dims, dtype=LOW):
        return jax.ShapeDtypeStruct(dims, dtype)

    def low(*dims):
        return pltpu.VMEM(dims, LOW)

    outs = [shape(shard, 2 * head_cols, dtype=WIDE)] * 4 + [
        shape(rows, width),
        shape(8, width, dtype=WIDE),
    ]
    return pl.pallas_call(
        functools.partial(last_kernel, dp_size, sol_size),
        out_shape=outs,
        in_specs=[vmem_spec()] * 3 + [any_spec()] * 8,
        out_specs=[any_spec()] * 5 + [vmem_spec()],
        scratch_shapes=[
            low(4 * rows, width),
            low(2 * rows, width),
            low(2 * rows, head_cols),
            low(4 * rows, 2 * head_cols),
            low(2 * rows, head_cols),
            low(rows, width),
            low(rows, width),
            low(CHUNK, width),
            low(CHUNK, width),
            low(rows, width),
            pltpu.VMEM((CHUNK, width), WIDE),
            low(CHUNK, width),
            pltpu.VMEM((bits, 8, width), WIDE),
            pltpu.VMEM((bits, 8, width), WIDE),
        ]
        + ring_sum_scratch(count // 2, shard, 4 * head_cols, 4)
        + [
            dma((7,)),
            dma((2,)),
            dma((5,)),
            dma((5,)),
            dma((4,)),
            dma((4,)),
            dma((bits,)),
            dma((bits,)),
        ],
        compiler_params=pltpu.CompilerParams(
            collective_id=3, has_side_effects=True, vmem_limit_bytes=60 * 2**20
        ),
    )(
        x,
        vectors,
        early,
        normed,
        branch,
        query_grad,
        kv_grad,
        mixed,
        own_low,
        prefix_half,
        grad_hidden,
    )


def ring_program(
    inputs,
    cotangent,
    attn_gain,
    attn_shift,
    query_weight,
    key_weight,
    value_weight,
    out_weight,
    mlp_gain,
    mlp_shift,
    up_weight,
    up_bias,
    down_weight,
    down_bias,
    live_rows,
):
    block_rows, width = inputs.shape
    shard_rows = query_weight.shape[0]
    head_cols = query_weight.shape[1] // 2
    ff_cols = up_weight.shape[1] // 2
    ff_part = ff_cols // 2
    local_heads = head_cols // HEAD_DIM
    score_scale = 1.0 / math.sqrt(HEAD_DIM)
    dp_size, sol_size = lax.axis_size("dp"), lax.axis_size("sol")
    count, ahead, back, cores = ring_pairs(dp_size, sol_size)
    dp_place, sol_place = lax.axis_index("dp"), lax.axis_index("sol")
    x_place, core = dp_place // 2, dp_place % 2
    first_core = core == 0
    along = jnp.where(x_place % 2 == 0, sol_place, sol_size - 1 - sol_place)
    ring_here = x_place * sol_size + along

    order_list = []
    for j in range(count):
        q = (ring_here + j) % count
        qx, qa = q // sol_size, q % sol_size
        qz = jnp.where(qx % 2 == 0, qa, sol_size - 1 - qa)
        order_list += [(qx * 2) * sol_size + qz, (qx * 2 + 1) * sol_size + qz]
    order = jnp.stack(order_list).astype(jnp.int32)
    back_order = jnp.argsort(order).astype(jnp.int32)

    def to_core(value):
        return lax.ppermute(value, ROWS_AXES, cores)

    def to_tensor(value):
        return lax.ppermute(value, "tensor", [(0, 1), (1, 0)])

    def reorder_vector(vector, by):
        return jnp.take(vector.reshape(by.shape[0], -1), by, axis=0).reshape(vector.shape)

    def gather_ring(piece, flip):
        hops_ahead = count // 2 - (1 if flip else 0)
        hops_back = count - 1 - hops_ahead
        got = {0: piece}
        moving_a, moving_b = piece, piece
        for k in range(1, count // 2 + 1):
            if k <= hops_ahead:
                moving_a = lax.ppermute(moving_a, ROWS_AXES, ahead)
                got[count - k] = moving_a
            if k <= hops_back:
                moving_b = lax.ppermute(moving_b, ROWS_AXES, back)
                got[k] = moving_b
        return jnp.concatenate([got[j] for j in range(count)], axis=0)

    def scatter_ring(chunk, flip):
        hops_ahead = count // 2 - (1 if flip else 0)
        hops_back = count - 1 - hops_ahead
        carried_a = carried_b = None
        for k in range(count // 2, 0, -1):
            if k <= hops_ahead:
                value = chunk(k)
                if carried_a is not None:
                    value = value + carried_a.astype(WIDE)
                carried_a = lax.ppermute(value.astype(LOW), ROWS_AXES, ahead)
            if k <= hops_back:
                value = chunk(count - k)
                if carried_b is not None:
                    value = value + carried_b.astype(WIDE)
                carried_b = lax.ppermute(value.astype(LOW), ROWS_AXES, back)
        return chunk(0) + carried_a.astype(WIDE) + carried_b.astype(WIDE)

    def own_part(shards):
        firsts, seconds = [], []
        for shard, start, size in shards:
            half = shard.shape[1] // 2
            firsts.append(shard[:, start : start + size])
            seconds.append(shard[:, half + start : half + start + size])
        low_half = jnp.concatenate(firsts, axis=1) if len(firsts) > 1 else firsts[0]
        high_half = jnp.concatenate(seconds, axis=1) if len(seconds) > 1 else seconds[0]
        mine = jnp.where(first_core, low_half, high_half)
        other = to_core(jnp.where(first_core, high_half, low_half))
        return jnp.concatenate(
            [jnp.where(first_core, mine, other), jnp.where(first_core, other, mine)], axis=0
        )

    def split_rows(full):
        upper, lower = full[:shard_rows], full[shard_rows:]
        mine = jnp.where(first_core, upper, lower)
        other = to_core(jnp.where(first_core, lower, upper))
        return jnp.where(first_core, mine, other), jnp.where(first_core, other, mine)

    def sum_partials(partial):
        mine = partial[:block_rows] + to_core(partial[block_rows:].astype(LOW)).astype(WIDE)
        low = mine.astype(LOW)
        return low.astype(WIDE) + to_tensor(low).astype(WIDE)

    def pair_rows(own):
        return jnp.concatenate([own, to_core(own)], axis=0)

    qk_piece = own_part([(query_weight, 0, head_cols), (key_weight, 0, head_cols)])
    vo_piece = own_part([(value_weight, 0, head_cols), (out_weight, 0, head_cols)])
    up_pieces = [own_part([(up_weight, s, ff_part)]) for s in (0, ff_part)]
    down_pieces = [own_part([(down_weight, s, ff_part)]) for s in (0, ff_part)]
    qk_full = gather_ring(qk_piece, False)
    vo_full = gather_ring(vo_piece, True)
    up_full = [gather_ring(up_pieces[0], False), gather_ring(up_pieces[1], True)]
    down_full = [gather_ring(down_pieces[0], False), gather_ring(down_pieces[1], True)]
    query_full, key_full = qk_full[:, :head_cols], qk_full[:, head_cols:]
    value_full, out_full = vo_full[:, :head_cols], vo_full[:, head_cols:]

    tensor_place = lax.axis_index("tensor")
    half_rows = block_rows // 2
    half = jnp.where(tensor_place == 0, inputs[:half_rows], inputs[half_rows:])
    prefix_half = half
    hop = half
    for k in range(1, sol_size):
        hop = lax.ppermute(hop, "sol", [(k - 1, k)])
        prefix_half = jnp.where(sol_place == k, hop, prefix_half)
    other_half = to_tensor(prefix_half)
    prefix_inputs = jnp.concatenate(
        [
            jnp.where(tensor_place == 0, prefix_half, other_half),
            jnp.where(tensor_place == 0, other_half, prefix_half),
        ],
        axis=0,
    )

    own_low = reorder(inputs, order)
    prefix_low = reorder(prefix_inputs, order)
    cot_low = reorder(cotangent, order)
    attn_gain_o, attn_shift_o, mlp_gain_o, mlp_shift_o, down_bias_o = [
        reorder_vector(v, order) for v in (attn_gain, attn_shift, mlp_gain, mlp_shift, down_bias)
    ]
    up_bias_c = jnp.where(first_core, up_bias[:ff_cols], up_bias[ff_cols:])
    up_bias_parts = [up_bias_c[:ff_part], up_bias_c[ff_part:]]

    features = own_low.astype(WIDE)
    normed = pair_rows(layer_norm(features, attn_gain_o, attn_shift_o).astype(LOW))
    normed_prefix = pair_rows(
        layer_norm(prefix_low.astype(WIDE), attn_gain_o, attn_shift_o).astype(LOW)
    )
    cot_pair = pair_rows(cot_low)

    query_rows = dot_plain(normed, query_full).astype(LOW)
    key_rows = dot_plain(normed, key_full).astype(LOW)
    value_rows = dot_plain(normed, value_full).astype(LOW)
    key_prefix = dot_plain(normed_prefix, key_full).astype(LOW)
    value_prefix = dot_plain(normed_prefix, value_full).astype(LOW)

    def heads_of(rows):
        return rows.reshape(2, -1, local_heads, HEAD_DIM)

    head_queries = heads_of(query_rows)
    all_keys = jnp.concatenate([heads_of(key_prefix), heads_of(key_rows)], axis=1)
    all_values = jnp.concatenate([heads_of(value_prefix), heads_of(value_rows)], axis=1)

    row_ids = jnp.arange(block_rows)[:, None]
    col_ids = jnp.arange(block_rows)[None, :]
    masks = []
    for place in (dp_place, dp_place + 1 - 2 * core):
        own_live = live_rows[place * sol_size + sol_place]
        prefix_live = live_rows[place * sol_size]
        prefix_ok = jnp.logical_and(col_ids < prefix_live, sol_place != 0)
        own_ok = jnp.logical_and(col_ids <= row_ids, col_ids < own_live)
        masks.append(
            jnp.concatenate(
                [jnp.broadcast_to(prefix_ok, (block_rows, block_rows)), own_ok], axis=1
            )
        )
    allowed = jnp.stack(masks)[:, None]

    def masked_scores():
        raw = jnp.einsum("bqhd,bkhd->bhqk", head_queries, all_keys, preferred_element_type=WIDE)
        return jnp.where(allowed, raw * score_scale, NEG_FILL)

    scores = masked_scores()
    row_peak = jnp.max(scores, axis=-1, keepdims=True)
    exp_scores = jnp.exp(scores - row_peak)
    totals = jnp.sum(exp_scores, axis=-1, keepdims=True)
    attn_probs = exp_scores / totals
    log_total = row_peak + jnp.log(totals)
    mixed = jnp.einsum(
        "bhqk,bkhd->bqhd", attn_probs.astype(LOW), all_values, preferred_element_type=WIDE
    )
    mixed_low = mixed.reshape(2 * block_rows, head_cols).astype(LOW)

    hidden = features + sum_partials(dot_right_t(mixed_low, out_full))
    normed_two = pair_rows(layer_norm(hidden, mlp_gain_o, mlp_shift_o).astype(LOW))
    upward = [dot_plain(normed_two, up_full[i]) + up_bias_parts[i] for i in range(2)]
    active = [gelu_tanh(u).astype(LOW) for u in upward]
    down_grads = [
        scatter_ring(
            lambda j, i=i: dot_left_t(
                cot_pair[:, j * 2 * shard_rows : (j + 1) * 2 * shard_rows], active[i]
            ),
            i == 1,
        )
        for i in range(2)
    ]
    grad_up = []
    for i in range(2):
        grad_active = dot_plain(cot_pair, down_full[i])
        unused_gelu, gelu_pull = jax.vjp(gelu_tanh, upward[i])
        grad_up.append(gelu_pull(grad_active)[0].astype(LOW))
    grad_normed_two = sum_partials(
        dot_right_t(grad_up[0], up_full[0]) + dot_right_t(grad_up[1], up_full[1])
    )
    up_grads = [
        scatter_ring(
            lambda j, i=i: dot_left_t(
                normed_two[:, j * 2 * shard_rows : (j + 1) * 2 * shard_rows], grad_up[i]
            ),
            i == 1,
        )
        for i in range(2)
    ]
    mlp_total = sum_partials(
        dot_right_t(active[0], down_full[0]) + dot_right_t(active[1], down_full[1])
    )
    outputs = reorder((hidden + mlp_total + down_bias_o).astype(LOW), back_order)

    grad_out = cot_low.astype(WIDE)
    down_bias_grad = jnp.sum(grad_out, axis=0)
    grad_hidden_norm, mlp_gain_grad, mlp_shift_grad = layer_norm_back(
        hidden, mlp_gain_o, grad_normed_two
    )
    grad_hidden = grad_out + grad_hidden_norm
    grad_branch = pair_rows(grad_hidden.astype(LOW))
    grad_mixed_low = dot_plain(grad_branch, out_full).astype(LOW)

    grad_head_mixed = heads_of(grad_mixed_low)
    attn_probs = jnp.exp(masked_scores() - log_total)
    grad_probs = jnp.einsum(
        "bqhd,bkhd->bhqk", grad_head_mixed, all_values, preferred_element_type=WIDE
    )
    row_delta = jnp.sum(attn_probs * grad_probs, axis=-1, keepdims=True)
    grad_scores = (attn_probs * (grad_probs - row_delta)).astype(LOW)
    grad_queries = (
        jnp.einsum("bhqk,bkhd->bqhd", grad_scores, all_keys, preferred_element_type=WIDE)
        * score_scale
    )
    grad_keys = (
        jnp.einsum("bhqk,bqhd->bkhd", grad_scores, head_queries, preferred_element_type=WIDE)
        * score_scale
    )
    grad_values = jnp.einsum(
        "bhqk,bqhd->bkhd", attn_probs.astype(LOW), grad_head_mixed, preferred_element_type=WIDE
    )

    def rows_of(heads):
        return heads.reshape(2 * block_rows, head_cols).astype(LOW)

    query_grad_low = rows_of(grad_queries)
    key_own = rows_of(grad_keys[:, block_rows:])
    value_own = rows_of(grad_values[:, block_rows:])
    key_pre = rows_of(grad_keys[:, :block_rows])
    value_pre = rows_of(grad_values[:, :block_rows])

    kv_pre = jnp.concatenate([key_pre, value_pre], axis=1)
    carried = kv_pre
    for k in range(sol_size - 1, 0, -1):
        came = lax.ppermute(carried, "sol", [(k, k - 1)])
        if k > 1:
            carried = (kv_pre.astype(WIDE) + came.astype(WIDE)).astype(LOW)
    key_all = (key_own.astype(WIDE) + came[:, :head_cols].astype(WIDE)).astype(LOW)
    value_all = (value_own.astype(WIDE) + came[:, head_cols:].astype(WIDE)).astype(LOW)

    normed_all = jnp.concatenate([normed, normed_prefix], axis=0)
    key_rows_grad = jnp.concatenate([key_own, key_pre], axis=0)
    value_rows_grad = jnp.concatenate([value_own, value_pre], axis=0)

    def qk_chunk(j):
        at = slice(j * 2 * shard_rows, (j + 1) * 2 * shard_rows)
        return jnp.concatenate(
            [
                dot_left_t(normed[:, at], query_grad_low),
                dot_left_t(normed_all[:, at], key_rows_grad),
            ],
            axis=1,
        )

    def vo_chunk(j):
        at = slice(j * 2 * shard_rows, (j + 1) * 2 * shard_rows)
        return jnp.concatenate(
            [
                dot_left_t(normed_all[:, at], value_rows_grad),
                dot_left_t(grad_branch[:, at], mixed_low),
            ],
            axis=1,
        )

    qk_grad = scatter_ring(qk_chunk, False)
    vo_grad = scatter_ring(vo_chunk, True)

    grad_normed = sum_partials(
        dot_right_t(query_grad_low, query_full)
        + dot_right_t(key_all, key_full)
        + dot_right_t(value_all, value_full)
    )
    grad_features, attn_gain_grad, attn_shift_grad = layer_norm_back(
        features, attn_gain_o, grad_normed
    )
    input_grad = reorder((grad_hidden + grad_features).astype(LOW), back_order)

    up_bias_grad = jnp.concatenate([jnp.sum(g.astype(WIDE), axis=0) for g in grad_up])
    up_bias_both = jnp.concatenate(
        [
            jnp.where(first_core, up_bias_grad, 0.0),
            jnp.where(first_core, 0.0, up_bias_grad),
        ]
    )

    def sum_rows_axes(vector):
        vector = vector + to_core(vector)
        step = 1
        while step < sol_size:
            vector = vector + lax.ppermute(vector, "sol", [(i, i ^ step) for i in range(sol_size)])
            step *= 2
        step = 2
        while step < dp_size:
            vector = vector + lax.ppermute(vector, "dp", [(i, i ^ step) for i in range(dp_size)])
            step *= 2
        return vector

    early = sum_rows_axes(
        jnp.concatenate(
            [reorder_vector(v, back_order) for v in (mlp_gain_grad, mlp_shift_grad, down_bias_grad)]
            + [up_bias_both]
        )
    )
    late = sum_rows_axes(
        jnp.concatenate([reorder_vector(v, back_order) for v in (attn_gain_grad, attn_shift_grad)])
    )

    qk_low, qk_high = split_rows(qk_grad)
    vo_low, vo_high = split_rows(vo_grad)
    up_low, up_high = zip(*[split_rows(g) for g in up_grads])
    down_low, down_high = zip(*[split_rows(g) for g in down_grads])

    def both(low_cols, high_cols):
        return jnp.concatenate([low_cols, high_cols], axis=1)

    return (
        outputs,
        input_grad,
        late[:width],
        late[width:],
        both(qk_low[:, :head_cols], qk_high[:, :head_cols]),
        both(qk_low[:, head_cols:], qk_high[:, head_cols:]),
        both(vo_low[:, :head_cols], vo_high[:, :head_cols]),
        both(vo_low[:, head_cols:], vo_high[:, head_cols:]),
        early[:width],
        early[width : 2 * width],
        jnp.concatenate(up_low + up_high, axis=1),
        early[3 * width :],
        jnp.concatenate(down_low + down_high, axis=1),
        early[2 * width : 3 * width],
    )


def per_device(*arrays):
    inputs, query_weight, up_weight = arrays[0], arrays[4], arrays[10]
    width = inputs.shape[1]
    fits = (
        query_weight.shape[0] % 128 == 0
        and inputs.shape[0] == 2 * CHUNK
        and up_weight.shape[1] == 2 * width
        and query_weight.shape[1] * 2 == width
        and lax.axis_size("dp") % 2 == 0
        and lax.axis_size("dp") * lax.axis_size("sol") == 16
        and lax.axis_size("tensor") == 2
    )
    return kernel_program(*arrays) if fits else ring_program(*arrays)


def kernel_program(
    inputs,
    cotangent,
    attn_gain,
    attn_shift,
    query_weight,
    key_weight,
    value_weight,
    out_weight,
    mlp_gain,
    mlp_shift,
    up_weight,
    up_bias,
    down_weight,
    down_bias,
    live_rows,
):
    width = inputs.shape[1]
    shard_rows = query_weight.shape[0]
    ff_cols = up_weight.shape[1] // 2
    dp_size, sol_size = lax.axis_size("dp"), lax.axis_size("sol")
    here = Place(dp_size, sol_size)
    core = here.core
    first_core = core == 0
    order = jnp.stack(here.blocks()).astype(jnp.int32)
    vectors = jnp.stack([attn_gain, attn_shift, mlp_gain, mlp_shift, down_bias])
    vectors = jnp.take(vectors.reshape(5, here.count * 2, shard_rows), order, axis=1).reshape(5, width)
    up_bias_c = jnp.where(first_core, up_bias[:ff_cols], up_bias[ff_cols:])[None]
    (
        weights,
        normed_all,
        cot_pair,
        query_rows,
        key_rows,
        value_rows,
        probs,
        mixed_low,
        hidden,
        normed_two,
        slope,
        active,
    ) = run_forward(
        dp_size,
        sol_size,
        inputs,
        vectors,
        up_bias_c,
        live_rows,
        cotangent,
        (query_weight, key_weight, value_weight, out_weight, up_weight, down_weight),
    )
    grad_up, grad_branch, grad_hidden, mlp_low, down_grad, early_sums = run_down(
        dp_size, sol_size, shard_rows, vectors, weights, cot_pair, active, slope, hidden
    )
    query_grad, kv_grad, own_low, prefix_half, up_grad, outputs, _ = run_attend_back(
        dp_size,
        sol_size,
        shard_rows,
        vectors,
        weights,
        normed_two,
        grad_up,
        grad_branch,
        query_rows,
        key_rows,
        value_rows,
        probs,
        mlp_low,
        hidden,
    )
    query_grads, key_grads, value_grads, out_grads, input_grad, sums = run_last(
        dp_size,
        sol_size,
        shard_rows,
        inputs,
        vectors,
        early_sums,
        normed_all,
        grad_branch,
        query_grad,
        kv_grad,
        mixed_low,
        own_low,
        prefix_half,
        grad_hidden,
    )

    return (
        outputs,
        input_grad,
        sums[0],
        sums[1],
        query_grads,
        key_grads,
        value_grads,
        out_grads,
        sums[2],
        sums[3],
        up_grad,
        sums[5:7].reshape(-1),
        down_grad,
        sums[4],
    )


def solution(mesh):
    rows = P(("dp", "sol"), None)
    matrix = P(("dp", "sol"), "tensor")
    return jax.shard_map(
        per_device,
        mesh=mesh,
        in_specs=(
            rows,
            rows,
            P(),
            P(),
            matrix,
            matrix,
            matrix,
            matrix,
            P(),
            P(),
            matrix,
            P("tensor"),
            matrix,
            P(),
            P(),
        ),
        out_specs=(
            rows,
            rows,
            P(),
            P(),
            matrix,
            matrix,
            matrix,
            matrix,
            P(),
            P(),
            matrix,
            P("tensor"),
            matrix,
            P(),
        ),
        check_vma=False,
    )
```

```python
import functools
import math

import jax
import jax.numpy as jnp
from jax import lax
from jax.experimental import pallas as pl
from jax.experimental.pallas import tpu as pltpu
from jax.sharding import PartitionSpec as P

HEAD_DIM = 128
EPSILON = 1e-05
NEG_FILL = -1e30
ROWS_AXES = ("dp", "sol")
LOW = jnp.bfloat16
WIDE = jnp.float32


def ring_place(position, sol_size):
    x, along = position // sol_size, position % sol_size
    return x, (along if x % 2 == 0 else sol_size - 1 - along)


def ring_pairs(dp_size, sol_size):
    count = dp_size // 2 * sol_size

    def flat(position, core):
        x, z = ring_place(position % count, sol_size)
        return (x * 2 + core) * sol_size + z

    places = [(q, c) for q in range(count) for c in range(2)]
    ahead = [(flat(q, c), flat(q + 1, c)) for q, c in places]
    back = [(b, a) for a, b in ahead]
    cores = [(flat(q, c), flat(q, 1 - c)) for q, c in places]
    return count, ahead, back, cores


def dot_plain(left_side, right_side):
    return jnp.dot(left_side, right_side, preferred_element_type=WIDE)


def dot_right_t(left_side, right_side):
    return lax.dot_general(
        left_side, right_side, (((1,), (1,)), ((), ())), preferred_element_type=WIDE
    )


def dot_left_t(left_side, right_side):
    return lax.dot_general(
        left_side, right_side, (((0,), (0,)), ((), ())), preferred_element_type=WIDE
    )


def norm_stats(features):
    row_mean = jnp.mean(features, axis=-1, keepdims=True)
    centered = features - row_mean
    variance = jnp.mean(centered * centered, axis=-1, keepdims=True)
    return row_mean, lax.rsqrt(variance + EPSILON)


def layer_norm(features, norm_gain, norm_shift):
    row_mean, inverse = norm_stats(features)
    return (features - row_mean) * inverse * norm_gain + norm_shift


def layer_norm_back(features, norm_gain, grad):
    row_mean, inverse = norm_stats(features)
    unit = (features - row_mean) * inverse
    scaled = grad * norm_gain
    along = jnp.mean(scaled * unit, axis=-1, keepdims=True)
    level = jnp.mean(scaled, axis=-1, keepdims=True)
    grad_features = (scaled - level - unit * along) * inverse
    return grad_features, jnp.sum(grad * unit, axis=0), jnp.sum(grad, axis=0)


def gelu_tanh(upward):
    return jax.nn.gelu(upward, approximate=True)


def copy_block(order_ref, in_ref, out_ref):
    out_ref[...] = in_ref[...]


def reorder(rows, order):
    blocks = order.shape[0]
    height, width = rows.shape
    part = width // blocks
    if part % 128:
        return jnp.take(rows.reshape(height, blocks, part), order, axis=1).reshape(height, width)
    return pl.pallas_call(
        copy_block,
        grid_spec=pltpu.PrefetchScalarGridSpec(
            num_scalar_prefetch=1,
            grid=(blocks,),
            in_specs=[pl.BlockSpec((height, part), lambda j, order_ref: (0, order_ref[j]))],
            out_specs=pl.BlockSpec((height, part), lambda j, order_ref: (0, j)),
        ),
        out_shape=jax.ShapeDtypeStruct(rows.shape, rows.dtype),
        cost_estimate=pl.CostEstimate(
            flops=0, bytes_accessed=4 * height * width, transcendentals=0
        ),
    )(order, rows)


MESH = pl.DeviceIdType.MESH
CHUNK = 256


def any_spec():
    return pl.BlockSpec(memory_space=pl.ANY)


def vmem_spec():
    return pl.BlockSpec(memory_space=pltpu.VMEM)


class Place:
    def __init__(self, dp_size, sol_size):
        self.dp_size, self.sol_size = dp_size, sol_size
        self.count = dp_size // 2 * sol_size
        dp, self.z = lax.axis_index("dp"), lax.axis_index("sol")
        self.y = lax.axis_index("tensor")
        self.x, self.core = dp // 2, dp % 2
        self.dp = dp
        turned = jnp.where(self.x % 2 == 0, self.z, sol_size - 1 - self.z)
        self.at = self.x * sol_size + turned
        self.next = self._chip((self.at + 1) % self.count)
        self.prev = self._chip((self.at + self.count - 1) % self.count)
        self.sibling = (dp + 1 - 2 * self.core, self.z, self.y)
        self.across = (dp, self.z, 1 - self.y)

    def _coords(self, position):
        x, turned = position // self.sol_size, position % self.sol_size
        return x, jnp.where(x % 2 == 0, turned, self.sol_size - 1 - turned)

    def _chip(self, position):
        x, z = self._coords(position)
        return (x * 2 + self.core, z, self.y)

    def up_ahead(self, step=0):
        x, z = self._coords((self.at + step + self.count) % self.count)
        return (x % 2 == 0) == (z > 0)

    def along(self, step):
        return (self.dp, self.z + step, self.y)

    def blocks(self):
        result = []
        for j in range(self.count):
            x, z = self._coords((self.at + j) % self.count)
            result += [(x * 2) * self.sol_size + z, (x * 2 + 1) * self.sol_size + z]
        return result

    def partners(self):
        result = [self.sibling]
        step = 1
        while step < self.sol_size:
            result.append((self.dp, self._flip(self.z, step), self.y))
            step *= 2
        step = 2
        while step < self.dp_size:
            result.append((self._flip(self.dp, step), self.z, self.y))
            step *= 2
        return result

    @staticmethod
    def _flip(place, step):
        return jnp.where(place // step % 2 == 0, place + step, place - step)

    def greet(self, others=()):
        barrier = pltpu.get_barrier_semaphore()
        peers = (self.next, self.prev, self.sibling, self.across) + tuple(others)
        for peer in peers:
            pl.semaphore_signal(barrier, inc=1, device_id=peer, device_id_type=MESH)
        pl.semaphore_wait(barrier, len(peers))


def remote(src, dst, send_sem, recv_sem, device):
    return pltpu.make_async_remote_copy(
        src_ref=src,
        dst_ref=dst,
        send_sem=send_sem,
        recv_sem=recv_sem,
        device_id=device,
        device_id_type=MESH,
    )


def norm_rows(values, gain, shift):
    row_mean = jnp.mean(values, axis=-1, keepdims=True)
    centered = values - row_mean
    variance = jnp.mean(centered * centered, axis=-1, keepdims=True)
    return centered * lax.rsqrt(variance + EPSILON) * gain + shift


def forward_kernel(
    dp_size,
    sol_size,
    x_ref,
    vectors_ref,
    up_bias_ref,
    live_ref,
    cot_hbm,
    query_ref,
    key_ref,
    value_ref,
    out_ref,
    up_ref,
    down_ref,
    weights,
    normed_out,
    cot_out,
    query_out,
    key_out,
    value_out,
    probs_out,
    mixed_out,
    hidden_out,
    normed_two_out,
    slope_out,
    active_out,
    w_v,
    normed_v,
    query_v,
    key_v,
    value_v,
    probs_v,
    mixed_v,
    hidden_v,
    normed_two_v,
    slope_v,
    active_v,
    core_send_v,
    core_recv_v,
    cross_send_v,
    cross_recv_v,
    ring_send,
    ring_recv,
    swap_local,
    swap_send,
    swap_recv,
    prefix_send,
    prefix_recv,
    pair_send,
    pair_recv,
    sum_send,
    sum_recv,
    cot_sem,
    load_sem,
    probs_sem,
    store_sem,
):
    here = Place(dp_size, sol_size)
    count, core = here.count, here.core
    rows, width = x_ref.shape
    prefix_v = slope_v
    shard = query_ref.shape[0]
    head_cols = query_ref.shape[1] // 2
    ff = up_ref.shape[1] // 2
    half = width // 2
    local_heads = head_cols // HEAD_DIM
    scale = 1.0 / math.sqrt(HEAD_DIM)
    blocks = here.blocks()
    far = count // 2
    own_class, other_class = core, 1 - core

    here.greet()

    def slot(j, which):
        return pl.ds(pl.multiple_of((2 * j + which) * shard, shard), shard)

    shards = (
        (0, 0, query_ref, head_cols),
        (0, head_cols, key_ref, head_cols),
        (0, 2 * head_cols, value_ref, head_cols),
        (0, 3 * head_cols, out_ref, head_cols),
        (1, 0, up_ref, ff),
        (2, 0, down_ref, ff),
    )

    def swap_copies(i):
        matrix, start, source, size = shards[i]
        target = weights.at[matrix, slot(0, own_class), pl.ds(start, size)]

        def columns(which):
            return source.at[:, pl.ds(pl.multiple_of(which * size, size), size)]

        return (
            pltpu.make_async_copy(columns(core), target, swap_local.at[i]),
            remote(columns(1 - core), target, swap_send.at[i], swap_recv.at[i], here.sibling),
        )

    def start_swap(matrix):
        for i in range(len(shards)):
            if shards[i][0] == matrix:
                for copy in swap_copies(i):
                    copy.start()

    def hops(matrix, k, sub):
        which = own_class if sub == 0 else other_class
        ahead_cols = pl.ds(0, half if k == far else width)
        back_cols = pl.ds(half if k == far else 0, half if k == far else width)
        return (
            remote(
                weights.at[matrix, slot((count - k + 1) % count, which), ahead_cols],
                weights.at[matrix, slot(count - k, which), ahead_cols],
                ring_send.at[matrix, 0, k - 1, sub],
                ring_recv.at[matrix, 0, k - 1, sub],
                here.next,
            ),
            remote(
                weights.at[matrix, slot(k - 1, which), back_cols],
                weights.at[matrix, slot(k, which), back_cols],
                ring_send.at[matrix, 1, k - 1, sub],
                ring_recv.at[matrix, 1, k - 1, sub],
                here.prev,
            ),
        )

    def start_ring(matrix, sub):
        for i in range(len(shards)):
            if shards[i][0] == matrix:
                if sub == 0:
                    swap_copies(i)[0].wait()
                else:
                    swap_copies(i)[1].wait_recv()
        for copy in hops(matrix, 1, sub):
            copy.start()

    def pump(matrix, k, sub):
        came = hops(matrix, k, sub)
        if k < far:
            further = hops(matrix, k + 1, sub)
        for i in range(2):
            came[i].wait_recv()
            if k < far:
                further[i].start()
        if k == far - 1 and matrix < 2:
            start_ring(matrix + 1, sub)

    steps = [
        (matrix, k, sub) for matrix in range(3) for k in range(1, far + 1) for sub in range(2)
    ]
    done = [0]

    def pump_to(number):
        while done[0] < min(number, len(steps)):
            pump(*steps[done[0]])
            done[0] += 1

    y_rows = rows // 2
    parts = 4
    part = y_rows // parts

    def prefix_rows(which_half, i):
        return pl.ds(pl.multiple_of(which_half * y_rows + i * part, part), part)

    def prefix_hop(i, from_input):
        at = prefix_rows(here.y, i)
        return remote(
            x_ref.at[at] if from_input else prefix_v.at[at],
            prefix_v.at[at],
            prefix_send.at[0, i],
            prefix_recv.at[0, i],
            here.along(1),
        )

    def prefix_cross(i, from_input):
        at = prefix_rows(here.y, i)
        return remote(
            x_ref.at[at] if from_input else prefix_v.at[at],
            prefix_v.at[at],
            prefix_send.at[1, i],
            prefix_recv.at[1, i],
            here.across,
        )

    def prefix_stage(stage, i):
        @pl.when(here.z == stage)
        def _():
            if stage == 0:
                prefix_hop(i, True).start()
                prefix_cross(i, True).start()
            else:
                prefix_hop(i, False).wait_recv()
                if stage < sol_size - 1:
                    prefix_hop(i, False).start()
                prefix_cross(i, False).start()

    def prefix_finish():
        for i in range(parts):
            prefix_cross(i, False).wait_recv()

        @pl.when(here.z == 0)
        def _():
            for i in range(parts):
                at = prefix_rows(here.y, i)
                prefix_v[at, :] = x_ref[at, :]

    cot_load = pltpu.make_async_copy(cot_hbm, active_v.at[pl.ds(0, rows)], cot_sem.at[1])
    start_swap(0)
    for i in range(parts):
        prefix_stage(0, i)
    start_swap(1)
    start_swap(2)
    cot_load.start()

    start_ring(0, 0)
    start_ring(0, 1)

    def ordered(ref, at):
        return jnp.concatenate(
            [ref[at, pl.ds(pl.multiple_of(b * shard, shard), shard)] for b in blocks], axis=1
        ).astype(WIDE)

    gain, shift = vectors_ref[0:1, :], vectors_ref[1:2, :]
    gain_two, shift_two = vectors_ref[2:3, :], vectors_ref[3:4, :]

    def norm_into(ref, start):
        @pl.loop(0, rows // 128)
        def _(t):
            at = pl.ds(pl.multiple_of(t * 128, 128), 128)
            to = pl.ds(pl.multiple_of(start + t * 128, 128), 128)
            normed_v[to, :] = norm_rows(ordered(ref, at), gain, shift).astype(LOW)

    normed_pair = remote(
        normed_v.at[pl.ds(0, rows)],
        normed_v.at[pl.ds(rows, rows)],
        pair_send.at[1],
        pair_recv.at[1],
        here.sibling,
    )
    prefix_pair = remote(
        normed_v.at[pl.ds(2 * rows, rows)],
        normed_v.at[pl.ds(3 * rows, rows)],
        pair_send.at[2],
        pair_recv.at[2],
        here.sibling,
    )
    norm_into(x_ref, 0)
    normed_pair.start()
    pump_to(1)
    for step in range(1, sol_size + parts - 1):
        for i in range(parts):
            if 1 <= step - i < sol_size:
                prefix_stage(step - i, i)
        pump_to(1 + step)
    pump_to(2 * far)

    cot_pair = remote(
        core_send_v,
        cot_out.at[pl.ds(rows, rows)],
        pair_send.at[0],
        pair_recv.at[0],
        here.sibling,
    )
    cot_own = pltpu.make_async_copy(core_send_v, cot_out.at[pl.ds(0, rows)], cot_sem.at[0])

    cot_load.wait()

    @pl.loop(0, rows // 128)
    def _(t):
        at = pl.ds(pl.multiple_of(t * 128, 128), 128)
        core_send_v[at, :] = ordered(active_v, at).astype(LOW)

    cot_pair.start()
    cot_own.start()

    load_first = pltpu.make_async_copy(weights.at[0], w_v, load_sem.at[0])
    load_first.start()
    normed_pair.wait_recv()
    load_first.wait()

    def row_tile(t):
        return pl.ds(pl.multiple_of(t * CHUNK, CHUNK), CHUNK)

    def project(first, last, with_queries):
        @pl.loop(first, last)
        def _(t):
            at = row_tile(t)
            tile = normed_v[at, :]
            kv = dot_plain(tile, w_v[:, head_cols : 3 * head_cols])
            key_v[at, :] = kv[:, :head_cols].astype(LOW)
            value_v[at, :] = kv[:, head_cols:].astype(LOW)
            if with_queries:
                query_v[at, :] = dot_plain(tile, w_v[:, :head_cols]).astype(LOW)

    tiles = rows // CHUNK
    project(0, 2 * tiles, True)
    pump_to(2 * far + 1)
    prefix_finish()
    norm_into(prefix_v, 2 * rows)
    prefix_pair.start()
    pump_to(2 * far + 2)
    prefix_pair.wait_recv()
    project(2 * tiles, 4 * tiles, False)

    stores = []

    def store(src, dst):
        copy = pltpu.make_async_copy(src, dst, store_sem.at[len(stores)])
        copy.start()
        stores.append(copy)

    store(normed_v, normed_out)
    store(query_v, query_out)
    store(key_v, key_out)
    store(value_v, value_out)

    def probs_copy(unit):
        return pltpu.make_async_copy(
            probs_v.at[unit % 2], probs_out.at[unit], probs_sem.at[unit % 2]
        )

    def attend(unit):
        block, head = unit // local_heads, unit % local_heads
        cols = pl.ds(pl.multiple_of(head * HEAD_DIM, HEAD_DIM), HEAD_DIM)
        place = jnp.where(block == 0, here.dp, here.dp + 1 - 2 * core)
        own_live = live_ref[place * sol_size + here.z]
        prefix_live = jnp.where(here.z == 0, 0, live_ref[place * sol_size])
        own_at = pl.ds(pl.multiple_of(block * rows, rows), rows)
        prefix_at = pl.ds(pl.multiple_of((2 + block) * rows, rows), rows)

        @pl.when(unit >= 2)
        def _():
            probs_copy(unit - 2).wait()

        for t in range(tiles):
            at = pl.ds(pl.multiple_of(block * rows + t * CHUNK, CHUNK), CHUNK)
            queries = query_v[at, cols]
            col = lax.broadcasted_iota(jnp.int32, (CHUNK, rows), 1)
            row = lax.broadcasted_iota(jnp.int32, (CHUNK, rows), 0) + t * CHUNK
            first = dot_right_t(queries, key_v[prefix_at, cols]) * scale
            second = dot_right_t(queries, key_v[own_at, cols]) * scale
            first = jnp.where(col < prefix_live, first, NEG_FILL)
            second = jnp.where(
                jnp.logical_and(col <= row, col < own_live), second, NEG_FILL
            )
            peak = jnp.maximum(
                jnp.max(first, axis=-1, keepdims=True), jnp.max(second, axis=-1, keepdims=True)
            )
            first = jnp.exp(first - peak)
            second = jnp.exp(second - peak)
            total = jnp.sum(first, axis=-1, keepdims=True) + jnp.sum(
                second, axis=-1, keepdims=True
            )
            inverse = 1.0 / total
            first = (first * inverse).astype(LOW)
            second = (second * inverse).astype(LOW)
            probs_v[unit % 2, pl.ds(t * CHUNK, CHUNK), pl.ds(0, rows)] = first
            probs_v[unit % 2, pl.ds(t * CHUNK, CHUNK), pl.ds(rows, rows)] = second
            mixed_v[at, cols] = (
                dot_plain(first, value_v[prefix_at, cols])
                + dot_plain(second, value_v[own_at, cols])
            ).astype(LOW)
        probs_copy(unit).start()

    units = 2 * local_heads
    for quarter in range(4):
        pl.loop(quarter * units // 4, (quarter + 1) * units // 4)(attend)
        pump_to(2 * far + (2, 3, 4, 4)[quarter])
    for unit in (units - 2, units - 1):
        probs_copy(unit).wait()
    store(mixed_v, mixed_out)

    out_cols = slice(3 * head_cols, 4 * head_cols)

    def core_copy(t):
        at = pl.ds(t * CHUNK, CHUNK)
        return remote(
            core_send_v.at[at], core_recv_v.at[at], sum_send.at[0, t], sum_recv.at[0, t], here.sibling
        )

    def cross_copy(t):
        at = pl.ds(t * CHUNK, CHUNK)
        return remote(
            cross_send_v.at[at], cross_recv_v.at[at], sum_send.at[1, t], sum_recv.at[1, t], here.across
        )

    def two_copy(t):
        return remote(
            normed_two_v.at[pl.ds(t * CHUNK, CHUNK)],
            normed_two_v.at[pl.ds(rows + t * CHUNK, CHUNK)],
            sum_send.at[2, t],
            sum_recv.at[2, t],
            here.sibling,
        )

    def hidden_store(t):
        return pltpu.make_async_copy(
            hidden_v, hidden_out.at[pl.ds(t * CHUNK, CHUNK)], load_sem.at[1]
        )

    cot_own.wait()
    cot_pair.wait_send()
    for t in range(tiles):
        core_send_v[pl.ds(t * CHUNK, CHUNK), :] = dot_right_t(
            mixed_v[pl.ds(rows + t * CHUNK, CHUNK), :], w_v[:, out_cols]
        ).astype(LOW)
        core_copy(t).start()
    for t in range(tiles):
        at = pl.ds(t * CHUNK, CHUNK)
        partial = dot_right_t(mixed_v[at, :], w_v[:, out_cols])
        core_copy(t).wait_recv()
        cross_send_v[at, :] = (partial + core_recv_v[at, :].astype(WIDE)).astype(LOW)
        cross_copy(t).start()
    pump_to(4 * far)
    load_second = pltpu.make_async_copy(weights.at[1], w_v, load_sem.at[0])
    load_second.start()
    for t in range(tiles):
        at = pl.ds(t * CHUNK, CHUNK)
        if t > 0:
            pump_to(4 * far + 2)
        cross_copy(t).wait_recv()
        hidden = (
            ordered(x_ref, at)
            + cross_send_v[at, :].astype(WIDE)
            + cross_recv_v[at, :].astype(WIDE)
        )
        if t > 0:
            hidden_store(t - 1).wait()
        hidden_v[...] = hidden
        hidden_store(t).start()
        normed_two_v[at, :] = norm_rows(hidden, gain_two, shift_two).astype(LOW)
        two_copy(t).start()
    hidden_store(tiles - 1).wait()
    load_second.wait()
    for t in range(tiles):
        two_copy(t).wait_recv()
    store(normed_two_v, normed_two_out)

    bend = math.sqrt(2.0 / math.pi)
    spans = ff // half

    def feed(i):
        at = row_tile(i // spans)
        cols = pl.ds(pl.multiple_of((i % spans) * half, half), half)
        upward = dot_plain(normed_two_v[at, :], w_v[:, cols]) + up_bias_ref[:, cols]
        square = upward * upward
        curve = jnp.tanh(bend * (upward + 0.044715 * (upward * square)))
        active_v[at, cols] = (0.5 * upward * (1.0 + curve)).astype(LOW)
        slope_v[at, cols] = (
            0.5 * (1.0 + curve)
            + 0.5 * upward * (1.0 - curve * curve) * (bend + (3.0 * 0.044715 * bend) * square)
        ).astype(LOW)

    for i in range(parts):

        @pl.when(here.z < sol_size - 1)
        def _():
            prefix_hop(i, False).wait_send()

        prefix_cross(i, False).wait_send()

    feeds = 2 * tiles * spans
    for quarter in range(4):
        pl.loop(quarter * feeds // 4, (quarter + 1) * feeds // 4)(feed)
        pump_to(4 * far + 3 + quarter)
    store(active_v, active_out)
    store(slope_v, slope_out)

    pump_to(len(steps))
    cot_pair.wait_recv()
    normed_pair.wait_send()
    prefix_pair.wait_send()
    for i in range(len(shards)):
        swap_copies(i)[1].wait_send()
    for step in steps:
        for copy in hops(*step):
            copy.wait_send()
    for t in range(tiles):
        core_copy(t).wait_send()
        cross_copy(t).wait_send()
        two_copy(t).wait_send()
    for copy in stores:
        copy.wait()


def run_forward(dp_size, sol_size, x, vectors, up_bias, live_rows, cot, matrices):
    rows, width = x.shape
    head_cols = matrices[0].shape[1] // 2
    ff = matrices[4].shape[1] // 2
    heads = head_cols // HEAD_DIM
    count = dp_size // 2 * sol_size
    far = count // 2

    def shape(*dims, dtype=LOW):
        return jax.ShapeDtypeStruct(dims, dtype)

    outs = [
        shape(3, width, width),
        shape(4 * rows, width),
        shape(2 * rows, width),
        shape(2 * rows, head_cols),
        shape(4 * rows, head_cols),
        shape(4 * rows, head_cols),
        shape(2 * heads, rows, 2 * rows),
        shape(2 * rows, head_cols),
        shape(rows, width, dtype=WIDE),
        shape(2 * rows, width),
        shape(2 * rows, ff),
        shape(2 * rows, ff),
    ]
    dma = pltpu.SemaphoreType.DMA
    return pl.pallas_call(
        functools.partial(forward_kernel, dp_size, sol_size),
        out_shape=outs,
        in_specs=[
            vmem_spec(),
            vmem_spec(),
            vmem_spec(),
            pl.BlockSpec(memory_space=pltpu.SMEM),
        ]
        + [any_spec()]
        + [vmem_spec()] * 6,
        out_specs=[any_spec()] * len(outs),
        scratch_shapes=[
            pltpu.VMEM((width, width), LOW),
            pltpu.VMEM((4 * rows, width), LOW),
            pltpu.VMEM((2 * rows, head_cols), LOW),
            pltpu.VMEM((4 * rows, head_cols), LOW),
            pltpu.VMEM((4 * rows, head_cols), LOW),
            pltpu.VMEM((2, rows, 2 * rows), LOW),
            pltpu.VMEM((2 * rows, head_cols), LOW),
            pltpu.VMEM((CHUNK, width), WIDE),
            pltpu.VMEM((2 * rows, width), LOW),
            pltpu.VMEM((2 * rows, ff), LOW),
            pltpu.VMEM((2 * rows, ff), LOW),
        ]
        + [pltpu.VMEM((rows, width), LOW)] * 4
        + [
            dma((3, 2, far, 2)),
            dma((3, 2, far, 2)),
            dma((6,)),
            dma((6,)),
            dma((6,)),
            dma((2, 4)),
            dma((2, 4)),
            dma((3,)),
            dma((3,)),
            dma((3, rows // CHUNK)),
            dma((3, rows // CHUNK)),
            dma((2,)),
            dma((2,)),
            dma((2,)),
            dma((16,)),
        ],
        compiler_params=pltpu.CompilerParams(
            collective_id=0, has_side_effects=True, vmem_limit_bytes=60 * 2**20
        ),
    )(x, vectors, up_bias, live_rows, cot, *matrices)


class RingSum:
    def __init__(self, here, chunk, send_v, recv_v, stage_v, sems, target, upward=False):
        self.here, self.chunk = here, chunk
        self.prepared = False
        self.upward = upward
        if upward:
            mine = here.up_ahead()
            self.sends = (mine, jnp.logical_not(mine))
            self.gets = (here.up_ahead(-1), jnp.logical_not(here.up_ahead(1)))
        self.send_v, self.recv_v, self.stage_v = send_v, recv_v, stage_v
        self.send_sem, self.recv_sem, self.end_sem = sems
        self.target = target
        self.far = here.count // 2
        self.cols = stage_v.shape[2]
        self.steps = [(t, sub) for t in range(1, self.far + 1) for sub in range(2)]
        self.done = 0

    def _class(self, sub):
        return self.here.core if sub == 0 else 1 - self.here.core

    def _columns(self, t, way):
        if t > 1 or self.upward:
            return pl.ds(0, self.cols)
        return pl.ds(way * (self.cols // 2), self.cols // 2)

    def _copy(self, t, way, sub):
        at = self._columns(t, way)
        return remote(
            self.send_v.at[way, sub, :, at],
            self.recv_v.at[(t - 1) % 3, way, sub, :, at],
            self.send_sem.at[t - 1, way, sub],
            self.recv_sem.at[t - 1, way, sub],
            self.here.prev if way else self.here.next,
        )

    def _event(self, t, sub):
        far, count = self.far, self.here.count
        half = self.cols // 2
        if t == 1 and self.upward:
            value = self.chunk(far, self._class(sub)).astype(LOW)
            for way in range(2):
                self.send_v[way, sub] = value
                pl.when(self.sends[way])(self._copy(1, way, sub).start)
            return
        if t == 1:
            value = self.chunk(far, self._class(sub))
            self.send_v[0, sub, :, :half] = value[:, :half].astype(LOW)
            self.send_v[1, sub, :, half:] = value[:, half:].astype(LOW)
            for way in range(2):
                self._copy(1, way, sub).start()
            return
        for way in range(2):
            j = far + 1 - t if way == 0 else count - (far + 1 - t)
            value = self.chunk(j, self._class(sub))
            if t == 2 and self.upward:
                pl.when(self.sends[way])(self._copy(1, way, sub).wait_send)
                pl.when(self.gets[way])(self._copy(1, way, sub).wait_recv)
                came = self.recv_v[0, way, sub].astype(WIDE)
                self.send_v[way, sub] = (
                    value + jnp.where(self.gets[way], came, 0.0)
                ).astype(LOW)
                self._copy(t, way, sub).start()
                continue
            self._copy(t - 1, way, sub).wait()
            if t == 2:
                near = slice(0, half) if way == 0 else slice(half, 2 * half)
                rest = slice(half, 2 * half) if way == 0 else slice(0, half)
                self.send_v[way, sub, :, near] = (
                    value[:, near] + self.recv_v[0, way, sub, :, near].astype(WIDE)
                ).astype(LOW)
                self.send_v[way, sub, :, rest] = value[:, rest].astype(LOW)
            else:
                self.send_v[way, sub] = (
                    value + self.recv_v[(t - 2) % 3, way, sub].astype(WIDE)
                ).astype(LOW)
            self._copy(t, way, sub).start()

    def prepare(self):
        for sub in range(2):
            self.stage_v[sub] = self.chunk(0, self._class(sub))
        self.prepared = True

    def _last(self, sub):
        for way in range(2):
            self._copy(self.far, way, sub).wait()
        value = self.stage_v[sub] + self.recv_v[(self.far - 1) % 3, 0, sub].astype(WIDE)
        self.stage_v[sub] = value + self.recv_v[(self.far - 1) % 3, 1, sub].astype(WIDE)
        for copy in self._results(sub):
            copy.start()

    def _results(self, sub):
        copies = []
        core = self.here.core
        for i, (ref, start, size) in enumerate(self.target):
            to = ref.at[:, pl.ds(pl.multiple_of(core * size, size), size)]
            source = self.stage_v.at[sub, :, pl.ds(start, size)]
            if sub == 0:
                copies.append(pltpu.make_async_copy(source, to, self.end_sem.at[0, i]))
            else:
                copies.append(
                    remote(
                        source, to, self.end_sem.at[1, i], self.end_sem.at[2, i], self.here.sibling
                    )
                )
        return copies

    def to(self, number):
        while self.done < min(number, len(self.steps) + 2):
            if self.done < len(self.steps):
                self._event(*self.steps[self.done])
            else:
                self._last(self.done - len(self.steps))
            self.done += 1

    def finish(self):
        self.to(len(self.steps) + 2)
        for sub in range(2):
            for copy in self._results(sub):
                copy.wait()


def ring_sum_scratch(far, shard, cols, results):
    dma = pltpu.SemaphoreType.DMA
    return [
        pltpu.VMEM((2, 2, shard, cols), LOW),
        pltpu.VMEM((3, 2, 2, shard, cols), LOW),
        pltpu.VMEM((2, shard, cols), WIDE),
        dma((far, 2, 2)),
        dma((far, 2, 2)),
        dma((3, results)),
    ]


def norm_back(values, gain, grad):
    row_mean = jnp.mean(values, axis=-1, keepdims=True)
    centered = values - row_mean
    variance = jnp.mean(centered * centered, axis=-1, keepdims=True)
    inverse = lax.rsqrt(variance + EPSILON)
    unit = centered * inverse
    scaled = grad * gain
    terms = grad * unit
    along = jnp.mean(scaled * unit, axis=-1, keepdims=True)
    level = jnp.mean(scaled, axis=-1, keepdims=True)
    return (
        (scaled - level - unit * along) * inverse,
        jnp.sum(terms, axis=0, keepdims=True),
        jnp.sum(grad, axis=0, keepdims=True),
    )


def tile_rows(t):
    return pl.ds(t * CHUNK, CHUNK)


def down_kernel(
    dp_size,
    sol_size,
    vectors_ref,
    weights,
    cot_hbm,
    active_hbm,
    slope_hbm,
    hidden_hbm,
    grad_up_out,
    branch_out,
    grad_hidden_out,
    mlp_low_out,
    down_grad_out,
    sums_ref,
    cot_v,
    active_v,
    slope_v,
    down_v,
    up_v,
    hidden_v,
    core_send_v,
    core_recv_v,
    second_recv_v,
    cross_send_v,
    cross_recv_v,
    ring_send_v,
    ring_recv_v,
    stage_v,
    ring_send,
    ring_recv,
    ring_end,
    load_sem,
    store_sem,
    sum_send,
    sum_recv,
):
    here = Place(dp_size, sol_size)
    rows, width = core_send_v.shape
    shard = stage_v.shape[1]
    ff = active_v.shape[1]
    tiles = rows // CHUNK
    halves = (pl.ds(0, width // 2), pl.ds(width // 2, width // 2))
    def chunk(j, which):
        at = pl.ds(pl.multiple_of((2 * j + which) * shard, shard), shard)
        return dot_left_t(cot_v[:, at], active_v[...])

    ring = RingSum(
        here,
        chunk,
        ring_send_v,
        ring_recv_v,
        stage_v,
        (ring_send, ring_recv, ring_end),
        ((down_grad_out, 0, ff),),
    )
    loads = [
        pltpu.make_async_copy(src, dst, load_sem.at[i])
        for i, (src, dst) in enumerate(
            (
                (cot_hbm, cot_v),
                (active_hbm, active_v),
                (weights.at[2], down_v),
                (slope_hbm, slope_v),
                (weights.at[1], up_v),
            )
        )
    ]
    for copy in loads:
        copy.start()
    here.greet()

    loads[0].wait()
    loads[1].wait()
    ring.to(1)

    sums_ref[...] = jnp.zeros_like(sums_ref)
    spans = 2

    def back_feed(tile):
        at = pl.ds(tile * CHUNK, CHUNK)

        @pl.loop(0, spans)
        def _(i):
            cols = pl.ds(pl.multiple_of(i * (ff // spans), ff // spans), ff // spans)
            grad = dot_plain(cot_v[at, :], down_v[:, cols]) * slope_v[at, cols].astype(WIDE)
            low = grad.astype(LOW)
            slope_v[at, cols] = low
            sums_ref[3:4, cols] += jnp.sum(low.astype(WIDE), axis=0, keepdims=True)

    def core_copy(t):
        return remote(
            core_send_v.at[tile_rows(t)],
            core_recv_v.at[tile_rows(t)],
            sum_send.at[0, t],
            sum_recv.at[0, t],
            here.sibling,
        )

    def cross_copy(t):
        return remote(
            cross_send_v.at[tile_rows(t)],
            cross_recv_v.at[tile_rows(t)],
            sum_send.at[1, t],
            sum_recv.at[1, t],
            here.across,
        )

    def second_copy(t):
        return remote(
            core_send_v.at[tile_rows(t)],
            second_recv_v.at[tile_rows(t)],
            sum_send.at[2, t],
            sum_recv.at[2, t],
            here.sibling,
        )

    def branch_copy(t):
        return remote(
            core_recv_v.at[tile_rows(t)],
            branch_out.at[pl.ds(rows + t * CHUNK, CHUNK)],
            sum_send.at[3, t],
            sum_recv.at[3, t],
            here.sibling,
        )

    def sibling_terms(t):
        for cols in halves:
            core_send_v[tile_rows(t), cols] = dot_right_t(
                slope_v[pl.ds(rows + t * CHUNK, CHUNK), :], up_v[cols, :]
            ).astype(LOW)
        core_copy(t).start()

    def own_terms(t):
        at = tile_rows(t)
        core_copy(t).wait_recv()
        for cols in halves:
            cross_send_v[at, cols] = (
                dot_right_t(slope_v[at, :], up_v[cols, :]) + core_recv_v[at, cols].astype(WIDE)
            ).astype(LOW)
        cross_copy(t).start()

    def sibling_output(t):
        core_copy(t).wait_send()
        for cols in halves:
            core_send_v[tile_rows(t), cols] = dot_right_t(
                active_v[pl.ds(rows + t * CHUNK, CHUNK), :], down_v[cols, :]
            ).astype(LOW)
        second_copy(t).start()

    def own_output(t):
        at = tile_rows(t)
        second_copy(t).wait_recv()
        for cols in halves:
            second_recv_v[at, cols] = (
                dot_right_t(active_v[at, :], down_v[cols, :])
                + second_recv_v[at, cols].astype(WIDE)
            ).astype(LOW)

    gain = vectors_ref[2:3, :]

    def hidden_load(t):
        return pltpu.make_async_copy(hidden_hbm.at[tile_rows(t)], hidden_v, load_sem.at[0])

    def hidden_store(t):
        return pltpu.make_async_copy(hidden_v, grad_hidden_out.at[tile_rows(t)], store_sem.at[2])

    def norm_tile(t):
        hidden_load(t).wait()
        cross_copy(t).wait_recv()
        for part in range(2):
            inner = pl.ds(part * (CHUNK // 2), CHUNK // 2)
            here_at = pl.ds(t * CHUNK + part * (CHUNK // 2), CHUNK // 2)
            grad = cross_send_v[here_at, :].astype(WIDE) + cross_recv_v[here_at, :].astype(WIDE)
            back, gain_terms, shift_terms = norm_back(hidden_v[inner, :], gain, grad)
            cot = cot_v[here_at, :].astype(WIDE)
            sums_ref[0:1, :] += gain_terms
            sums_ref[1:2, :] += shift_terms
            sums_ref[2:3, :] += jnp.sum(cot, axis=0, keepdims=True)
            back = back + cot
            hidden_v[inner, :] = back
            core_recv_v[here_at, :] = back.astype(LOW)
        branch_copy(t).start()
        hidden_store(t).start()

    stores = []

    def store(src, dst, i):
        copy = pltpu.make_async_copy(src, dst, store_sem.at[i])
        copy.start()
        stores.append(copy)

    loads[2].wait()
    loads[3].wait()
    ring.to(2)
    hidden_load(0).start()
    back_feed(0)
    ring.to(3)
    back_feed(tiles)
    loads[4].wait()
    sibling_terms(0)
    ring.to(4)
    own_terms(0)
    back_feed(1)
    ring.to(5)
    back_feed(tiles + 1)
    store(slope_v, grad_up_out, 0)
    sibling_terms(1)
    ring.to(6)
    own_terms(1)
    sibling_output(0)
    ring.to(7)
    own_output(0)
    sibling_output(1)
    ring.to(8)
    norm_tile(0)
    own_output(1)
    store(second_recv_v, mlp_low_out, 1)
    hidden_store(0).wait()
    hidden_load(1).start()
    ring.prepare()
    ring.to(9)
    norm_tile(1)
    store(core_recv_v, branch_out.at[pl.ds(0, rows)], 3)
    hidden_store(1).wait()
    ring.finish()
    for t in range(tiles):
        cross_copy(t).wait_send()
        second_copy(t).wait_send()
        branch_copy(t).wait()
    for copy in stores:
        copy.wait()


def run_down(
    dp_size, sol_size, shard, vectors, weights, cot, active, slope, hidden
):
    rows, width = hidden.shape
    ff = active.shape[1]
    count = dp_size // 2 * sol_size
    tiles = rows // CHUNK
    dma = pltpu.SemaphoreType.DMA

    def shape(*dims, dtype=LOW):
        return jax.ShapeDtypeStruct(dims, dtype)

    outs = [
        shape(2 * rows, ff),
        shape(2 * rows, width),
        shape(rows, width, dtype=WIDE),
        shape(rows, width),
        shape(shard, 2 * ff, dtype=WIDE),
        shape(8, width, dtype=WIDE),
    ]
    return pl.pallas_call(
        functools.partial(down_kernel, dp_size, sol_size),
        out_shape=outs,
        in_specs=[vmem_spec()] + [any_spec()] * 5,
        out_specs=[any_spec()] * 5 + [vmem_spec()],
        scratch_shapes=[
            pltpu.VMEM((2 * rows, width), LOW),
            pltpu.VMEM((2 * rows, ff), LOW),
            pltpu.VMEM((2 * rows, ff), LOW),
            pltpu.VMEM((width, ff), LOW),
            pltpu.VMEM((width, ff), LOW),
            pltpu.VMEM((CHUNK, width), WIDE),
        ]
        + [pltpu.VMEM((rows, width), LOW)] * 5
        + ring_sum_scratch(count // 2, shard, ff, 1)
        + [
            dma((5,)),
            dma((6,)),
            dma((4, tiles)),
            dma((4, tiles)),
        ],
        compiler_params=pltpu.CompilerParams(
            collective_id=1, has_side_effects=True, vmem_limit_bytes=60 * 2**20
        ),
    )(vectors, weights, cot, active, slope, hidden)


def read_ordered(ref, at, blocks, part):
    return jnp.concatenate(
        [ref[at, pl.ds(pl.multiple_of(b * part, part), part)] for b in blocks], axis=1
    ).astype(WIDE)


def write_ordered(ref, at, blocks, part, values):
    for j, b in enumerate(blocks):
        ref[at, pl.ds(pl.multiple_of(b * part, part), part)] = values[
            :, j * part : (j + 1) * part
        ].astype(ref.dtype)


def attend_back_kernel(
    dp_size,
    sol_size,
    vectors_ref,
    weights,
    normed_two_hbm,
    grad_up_hbm,
    branch_hbm,
    query_hbm,
    key_hbm,
    value_hbm,
    probs_hbm,
    mlp_low_hbm,
    hidden_hbm,
    query_grad_out,
    kv_grad_out,
    own_low_out,
    prefix_half_out,
    up_grad_out,
    outputs_out,
    mlp_recv_out,
    normed_two_v,
    grad_up_v,
    branch_v,
    w_v,
    query_v,
    key_v,
    value_v,
    mixed_grad_v,
    probs_v,
    query_grad_v,
    kv_grad_v,
    core_recv_v,
    second_recv_v,
    half_recv_v,
    mlp_low_v,
    mlp_recv_v,
    hidden_v,
    ring_send_v,
    ring_recv_v,
    stage_v,
    ring_send,
    ring_recv,
    ring_end,
    load_sem,
    probs_sem,
    tile_sem,
    store_sem,
    sum_send,
    sum_recv,
    cross_send,
    cross_recv,
):
    here = Place(dp_size, sol_size)
    rows, width = core_recv_v.shape
    core_send_v = branch_v.at[pl.ds(0, rows)]
    half_send_v = branch_v.at[pl.ds(rows, CHUNK)]
    half_keep_v = branch_v.at[pl.ds(rows + CHUNK, CHUNK)]
    shard = stage_v.shape[1]
    ff = grad_up_v.shape[1]
    head_cols = query_v.shape[1]
    local_heads = head_cols // HEAD_DIM
    scale = 1.0 / math.sqrt(HEAD_DIM)
    tiles = rows // CHUNK
    blocks = here.blocks()
    halves = (pl.ds(0, width // 2), pl.ds(width // 2, width // 2))
    loads = [
        pltpu.make_async_copy(src, dst, load_sem.at[i])
        for i, (src, dst) in enumerate(
            (
                (normed_two_hbm, normed_two_v),
                (grad_up_hbm, grad_up_v),
                (branch_hbm, branch_v),
                (weights.at[0], w_v),
                (query_hbm, query_v),
                (key_hbm, key_v),
                (value_hbm, value_v),
            )
        )
    ]
    for copy in loads:
        copy.start()

    def probs_load(unit):
        return pltpu.make_async_copy(
            probs_hbm.at[unit], probs_v.at[unit % 2], probs_sem.at[unit % 2]
        )

    probs_load(0).start()
    here.greet()
    mlp_cross = remote(
        mlp_low_hbm, mlp_recv_out, cross_send.at[0], cross_recv.at[0], here.across
    )
    mlp_cross.start()

    def chunk(j, which):
        at = pl.ds(pl.multiple_of((2 * j + which) * shard, shard), shard)
        return dot_left_t(normed_two_v[:, at], grad_up_v[...])

    ring = RingSum(
        here,
        chunk,
        ring_send_v,
        ring_recv_v,
        stage_v,
        (ring_send, ring_recv, ring_end),
        ((up_grad_out, 0, ff),),
    )
    loads[0].wait()
    loads[1].wait()
    ring.to(2)
    loads[2].wait()
    loads[3].wait()

    @pl.loop(0, 2 * tiles)
    def _(t):
        at = pl.ds(pl.multiple_of(t * CHUNK, CHUNK), CHUNK)
        mixed_grad_v[at, :] = dot_plain(
            branch_v[at, :], w_v[:, 3 * head_cols : 4 * head_cols]
        ).astype(LOW)

    for i in range(4, 7):
        loads[i].wait()

    units = 2 * local_heads

    def back(unit):
        block, head = unit // local_heads, unit % local_heads
        cols = pl.ds(pl.multiple_of(head * HEAD_DIM, HEAD_DIM), HEAD_DIM)
        value_cols = pl.ds(
            pl.multiple_of(head_cols + head * HEAD_DIM, HEAD_DIM), HEAD_DIM
        )
        own_at = pl.ds(pl.multiple_of(block * rows, rows), rows)
        prefix_at = pl.ds(pl.multiple_of((2 + block) * rows, rows), rows)
        probs_load(unit).wait()

        @pl.when(unit + 1 < units)
        def _():
            probs_load(unit + 1).start()

        sums = None
        for t in range(tiles):
            at = pl.ds(pl.multiple_of(block * rows + t * CHUNK, CHUNK), CHUNK)
            grad = mixed_grad_v[at, cols]
            queries = query_v[at, cols]
            inner = pl.ds(t * CHUNK, CHUNK)
            first_low = probs_v[unit % 2, inner, pl.ds(0, rows)]
            second_low = probs_v[unit % 2, inner, pl.ds(rows, rows)]
            first, second = first_low.astype(WIDE), second_low.astype(WIDE)
            first_grad = dot_right_t(grad, value_v[prefix_at, cols])
            second_grad = dot_right_t(grad, value_v[own_at, cols])
            delta = jnp.sum(first * first_grad, axis=-1, keepdims=True) + jnp.sum(
                second * second_grad, axis=-1, keepdims=True
            )
            first_scores = (first * (first_grad - delta)).astype(LOW)
            second_scores = (second * (second_grad - delta)).astype(LOW)
            query_grad_v[at, cols] = (
                (
                    dot_plain(first_scores, key_v[prefix_at, cols])
                    + dot_plain(second_scores, key_v[own_at, cols])
                )
                * scale
            ).astype(LOW)
            terms = [
                dot_left_t(second_scores, queries),
                dot_left_t(second_low, grad),
                dot_left_t(first_scores, queries),
                dot_left_t(first_low, grad),
            ]
            sums = terms if sums is None else [a + b for a, b in zip(sums, terms)]
        kv_grad_v[own_at, cols] = (sums[0] * scale).astype(LOW)
        kv_grad_v[own_at, value_cols] = sums[1].astype(LOW)
        kv_grad_v[prefix_at, cols] = (sums[2] * scale).astype(LOW)
        kv_grad_v[prefix_at, value_cols] = sums[3].astype(LOW)

    for quarter in range(4):
        pl.loop(quarter * units // 4, (quarter + 1) * units // 4)(back)
        ring.to(3 + quarter)
    stores = []

    def store(src, dst):
        copy = pltpu.make_async_copy(src, dst, store_sem.at[len(stores)])
        copy.start()
        stores.append(copy)

    store(query_grad_v, query_grad_out)
    store(kv_grad_v, kv_grad_out)

    def core_copy(t):
        return remote(
            core_send_v.at[tile_rows(t)],
            core_recv_v.at[tile_rows(t)],
            sum_send.at[0, t],
            sum_recv.at[0, t],
            here.sibling,
        )

    def second_copy(t):
        return remote(
            core_send_v.at[tile_rows(t)],
            second_recv_v.at[tile_rows(t)],
            sum_send.at[1, t],
            sum_recv.at[1, t],
            here.sibling,
        )

    half_copy = remote(half_send_v, half_recv_v, cross_send.at[1], cross_recv.at[1], here.across)
    kv_cols = pl.ds(head_cols, 2 * head_cols)

    def prefix_terms(at, cols):
        return dot_right_t(kv_grad_v[at, :], w_v[cols, kv_cols])

    for t in range(tiles):
        for cols in halves:
            core_send_v[tile_rows(t), cols] = prefix_terms(
                pl.ds(3 * rows + t * CHUNK, CHUNK), cols
            ).astype(LOW)
        second_copy(t).start()
    for t in range(tiles):
        second_copy(t).wait_recv()
    for keep in range(2):
        which = here.y if keep else 1 - here.y
        at = pl.ds(pl.multiple_of(2 * rows + which * CHUNK, CHUNK), CHUNK)
        came = pl.ds(pl.multiple_of(which * CHUNK, CHUNK), CHUNK)
        for cols in halves:
            value = prefix_terms(at, cols) + second_recv_v[came, cols].astype(WIDE)
            if keep:
                half_keep_v[:, cols] = value.astype(LOW)
            else:
                half_send_v[:, cols] = value.astype(LOW)
        if not keep:
            half_copy.start()
    ring.to(7)

    def own_terms(at, cols):
        return dot_right_t(query_grad_v[at, :], w_v[cols, 0:head_cols]) + dot_right_t(
            kv_grad_v[at, :], w_v[cols, kv_cols]
        )

    for t in range(tiles):
        second_copy(t).wait_send()
        for cols in halves:
            core_send_v[tile_rows(t), cols] = own_terms(
                pl.ds(rows + t * CHUNK, CHUNK), cols
            ).astype(LOW)
        core_copy(t).start()
    for t in range(tiles):
        at = tile_rows(t)
        core_copy(t).wait_recv()
        for cols in halves:
            core_recv_v[at, cols] = (
                own_terms(at, cols) + core_recv_v[at, cols].astype(WIDE)
            ).astype(LOW)
    store(core_recv_v, own_low_out)
    ring.to(8)
    ring.prepare()

    half_copy.wait()
    write_ordered(
        half_send_v,
        slice(None),
        blocks,
        shard,
        half_keep_v[...].astype(WIDE) + half_recv_v[...].astype(WIDE),
    )
    store(half_send_v, prefix_half_out)

    small = mlp_low_v.shape[0]
    pieces = rows // small

    def piece_rows(t):
        return pl.ds(t * small, small)

    def tile_loads(t):
        return (
            pltpu.make_async_copy(hidden_hbm.at[piece_rows(t)], hidden_v, tile_sem.at[0]),
            pltpu.make_async_copy(mlp_low_hbm.at[piece_rows(t)], mlp_low_v, tile_sem.at[1]),
            pltpu.make_async_copy(mlp_recv_out.at[piece_rows(t)], mlp_recv_v, tile_sem.at[2]),
        )

    def tile_store(t):
        return pltpu.make_async_copy(
            half_keep_v.at[pl.ds(t % 2 * small, small)],
            outputs_out.at[piece_rows(t)],
            tile_sem.at[3 + t % 2],
        )

    mlp_cross.wait()
    for copy in tile_loads(0):
        copy.start()
    for t in range(pieces):
        for copy in tile_loads(t):
            copy.wait()
        value = (
            hidden_v[...]
            + mlp_low_v[...].astype(WIDE)
            + mlp_recv_v[...].astype(WIDE)
            + vectors_ref[4:5, :]
        )
        if t > 1:
            tile_store(t - 2).wait()
        write_ordered(half_keep_v, pl.ds(t % 2 * small, small), blocks, shard, value)
        tile_store(t).start()
        if t + 1 < pieces:
            for copy in tile_loads(t + 1):
                copy.start()
    for t in (pieces - 2, pieces - 1):
        tile_store(t).wait()
    ring.finish()
    for t in range(tiles):
        core_copy(t).wait_send()
    for copy in stores:
        copy.wait()


def run_attend_back(
    dp_size,
    sol_size,
    shard,
    vectors,
    weights,
    normed_two,
    grad_up,
    branch,
    query_rows,
    key_rows,
    value_rows,
    probs,
    mlp_low,
    hidden,
):
    rows, width = hidden.shape
    ff = grad_up.shape[1]
    head_cols = query_rows.shape[1]
    count = dp_size // 2 * sol_size
    tiles = rows // CHUNK
    dma = pltpu.SemaphoreType.DMA

    def shape(*dims, dtype=LOW):
        return jax.ShapeDtypeStruct(dims, dtype)

    def low(*dims):
        return pltpu.VMEM(dims, LOW)

    outs = [
        shape(2 * rows, head_cols),
        shape(4 * rows, 2 * head_cols),
        shape(rows, width),
        shape(rows // 2, width),
        shape(shard, 2 * ff, dtype=WIDE),
        shape(rows, width),
        shape(rows, width),
    ]
    return pl.pallas_call(
        functools.partial(attend_back_kernel, dp_size, sol_size),
        out_shape=outs,
        in_specs=[vmem_spec()] + [any_spec()] * 10,
        out_specs=[any_spec()] * len(outs),
        scratch_shapes=[
            low(2 * rows, width),
            low(2 * rows, ff),
            low(2 * rows, width),
            low(width, width),
            low(2 * rows, head_cols),
            low(4 * rows, head_cols),
            low(4 * rows, head_cols),
            low(2 * rows, head_cols),
            low(2, rows, 2 * rows),
            low(2 * rows, head_cols),
            low(4 * rows, 2 * head_cols),
            low(rows, width),
            low(rows, width),
            low(CHUNK, width),
            low(CHUNK // 2, width),
            low(CHUNK // 2, width),
            pltpu.VMEM((CHUNK // 2, width), WIDE),
        ]
        + ring_sum_scratch(count // 2, shard, ff, 1)
        + [
            dma((7,)),
            dma((2,)),
            dma((5,)),
            dma((4,)),
            dma((2, tiles)),
            dma((2, tiles)),
            dma((2,)),
            dma((2,)),
        ],
        compiler_params=pltpu.CompilerParams(
            collective_id=2, has_side_effects=True, vmem_limit_bytes=60 * 2**20
        ),
    )(
        vectors,
        weights,
        normed_two,
        grad_up,
        branch,
        query_rows,
        key_rows,
        value_rows,
        probs,
        mlp_low,
        hidden,
    )


def last_kernel(
    dp_size,
    sol_size,
    x_ref,
    vectors_ref,
    early_ref,
    normed_hbm,
    branch_hbm,
    query_grad_hbm,
    kv_grad_hbm,
    mixed_hbm,
    own_low_hbm,
    prefix_half_hbm,
    grad_hidden_hbm,
    query_out,
    key_out,
    value_out,
    out_out,
    input_grad_out,
    sums_ref,
    normed_v,
    branch_v,
    query_grad_v,
    kv_grad_v,
    mixed_v,
    own_low_v,
    own_recv_v,
    half_v,
    half_recv_v,
    prefix_v,
    grad_hidden_v,
    out_v,
    table_v,
    table_recv_v,
    ring_send_v,
    ring_recv_v,
    stage_v,
    ring_send,
    ring_recv,
    ring_end,
    load_sem,
    tile_sem,
    cross_send,
    cross_recv,
    chain_send,
    chain_recv,
    table_send,
    table_recv,
):
    here = Place(dp_size, sol_size)
    rows, width = x_ref.shape
    shard = stage_v.shape[1]
    head_cols = query_grad_v.shape[1]
    tiles = rows // CHUNK
    blocks = here.blocks()
    loads = [
        pltpu.make_async_copy(src, dst, load_sem.at[i])
        for i, (src, dst) in enumerate(
            (
                (query_grad_hbm, query_grad_v),
                (kv_grad_hbm, kv_grad_v),
                (mixed_hbm, mixed_v),
                (prefix_half_hbm, half_v),
                (normed_hbm, normed_v),
                (branch_hbm, branch_v),
                (own_low_hbm, own_low_v),
            )
        )
    ]
    for copy in loads:
        copy.start()
    partners = here.partners()
    here.greet(partners[1:])
    own_cross = remote(own_low_hbm, own_recv_v, cross_send.at[0], cross_recv.at[0], here.across)
    own_cross.start()

    def chunk(j, which):
        at = pl.ds(pl.multiple_of((2 * j + which) * shard, shard), shard)
        return jnp.concatenate(
            [
                dot_left_t(normed_v[: 2 * rows, at], query_grad_v[...]),
                dot_left_t(normed_v[:, at], kv_grad_v[...]),
                dot_left_t(branch_v[:, at], mixed_v[...]),
            ],
            axis=1,
        )

    ring = RingSum(
        here,
        chunk,
        ring_send_v,
        ring_recv_v,
        stage_v,
        (ring_send, ring_recv, ring_end),
        tuple(
            (ref, i * head_cols, head_cols)
            for i, ref in enumerate((query_out, key_out, value_out, out_out))
        ),
        upward=True,
    )

    parts = chain_send.shape[0]
    part = CHUNK // parts

    def chain_copy(i):
        at = pl.ds(i * part, part)
        return remote(
            half_v.at[at], half_recv_v.at[at], chain_send.at[i], chain_recv.at[i], here.along(-1)
        )

    def mine(i):
        return pl.ds(pl.multiple_of(here.y * CHUNK + i * part, part), part)

    def half_cross(i):
        return remote(
            half_recv_v.at[pl.ds(i * part, part)],
            prefix_v.at[mine(i)],
            cross_send.at[1 + i],
            cross_recv.at[1 + i],
            here.across,
        )

    def chain(stage, i):
        at = pl.ds(i * part, part)

        @pl.when(here.z == stage)
        def _():
            if stage < sol_size - 1:
                chain_copy(i).wait_recv()
            if 0 < stage < sol_size - 1:
                half_v[at, :] = (
                    half_v[at, :].astype(WIDE) + half_recv_v[at, :].astype(WIDE)
                ).astype(LOW)
            if stage > 0:
                chain_copy(i).start()
            else:
                half_cross(i).start()
                prefix_v[mine(i), :] = half_recv_v[at, :]

    loads[3].wait()
    for i in range(parts):
        chain(sol_size - 1, i)

    @pl.when(here.z > 0)
    def _():
        prefix_v[...] = jnp.zeros_like(prefix_v)

    for i in (0, 1, 2, 4, 5):
        loads[i].wait()
    ring.to(2)
    for step in range(1, sol_size + parts - 1):
        for i in range(parts):
            if 1 <= step - i < sol_size:
                chain(sol_size - 1 - (step - i), i)
        ring.to(2 + step)
        if step == 4:
            ring.prepare()

    loads[6].wait()
    own_cross.wait()

    @pl.when(here.z == 0)
    def _():
        for i in range(parts):
            half_cross(i).wait()

    gain = vectors_ref[0:1, :]

    def tile_load(t):
        return pltpu.make_async_copy(
            grad_hidden_hbm.at[tile_rows(t)], grad_hidden_v, tile_sem.at[0]
        )

    def tile_store(t):
        return pltpu.make_async_copy(out_v, input_grad_out.at[tile_rows(t)], tile_sem.at[1])

    tile_load(0).start()
    totals = [jnp.zeros((1, width), WIDE)] * 2
    small = CHUNK // 2
    for t in range(tiles):
        tile_load(t).wait()
        if t > 0:
            tile_store(t - 1).wait()
        for piece in range(2):
            at = pl.ds(t * CHUNK + piece * small, small)
            inner = pl.ds(piece * small, small)
            grad = (
                own_low_v[at, :].astype(WIDE)
                + own_recv_v[at, :].astype(WIDE)
                + read_ordered(prefix_v, at, blocks, shard)
            )
            back, gain_terms, shift_terms = norm_back(
                read_ordered(x_ref, at, blocks, shard), gain, grad
            )
            totals = [totals[0] + gain_terms, totals[1] + shift_terms]
            write_ordered(out_v, inner, blocks, shard, back + grad_hidden_v[inner, :])
        tile_store(t).start()
        if t + 1 < tiles:
            tile_load(t + 1).start()

    for row in range(2):
        write_ordered(table_v.at[0], pl.ds(row, 1), blocks, shard, totals[row])
    for row in range(3):
        write_ordered(
            table_v.at[0], pl.ds(2 + row, 1), blocks, shard, early_ref[row : row + 1, :]
        )
    bias = early_ref[3:4, :]
    table_v[0, 5:6, :] = jnp.where(here.core == 0, bias, 0.0)
    table_v[0, 6:7, :] = jnp.where(here.core == 0, 0.0, bias)
    table_v[0, 7:8, :] = jnp.zeros((1, width), WIDE)

    def table_copy(k):
        return remote(
            table_v.at[k], table_recv_v.at[k], table_send.at[k], table_recv.at[k], partners[k]
        )

    for k in range(len(partners)):
        table_copy(k).start()
        table_copy(k).wait_recv()
        if k + 1 < len(partners):
            table_v[k + 1] = table_v[k] + table_recv_v[k]
        else:
            sums_ref[...] = table_v[k] + table_recv_v[k]
    tile_store(tiles - 1).wait()
    ring.finish()
    for k in range(len(partners)):
        table_copy(k).wait_send()
    for i in range(parts):

        @pl.when(here.z > 0)
        def _():
            chain_copy(i).wait_send()


def run_last(
    dp_size,
    sol_size,
    shard,
    x,
    vectors,
    early,
    normed,
    branch,
    query_grad,
    kv_grad,
    mixed,
    own_low,
    prefix_half,
    grad_hidden,
):
    rows, width = x.shape
    head_cols = query_grad.shape[1]
    count = dp_size // 2 * sol_size
    bits = (dp_size * sol_size).bit_length() - 1
    dma = pltpu.SemaphoreType.DMA

    def shape(*dims, dtype=LOW):
        return jax.ShapeDtypeStruct(dims, dtype)

    def low(*dims):
        return pltpu.VMEM(dims, LOW)

    outs = [shape(shard, 2 * head_cols, dtype=WIDE)] * 4 + [
        shape(rows, width),
        shape(8, width, dtype=WIDE),
    ]
    return pl.pallas_call(
        functools.partial(last_kernel, dp_size, sol_size),
        out_shape=outs,
        in_specs=[vmem_spec()] * 3 + [any_spec()] * 8,
        out_specs=[any_spec()] * 5 + [vmem_spec()],
        scratch_shapes=[
            low(4 * rows, width),
            low(2 * rows, width),
            low(2 * rows, head_cols),
            low(4 * rows, 2 * head_cols),
            low(2 * rows, head_cols),
            low(rows, width),
            low(rows, width),
            low(CHUNK, width),
            low(CHUNK, width),
            low(rows, width),
            pltpu.VMEM((CHUNK, width), WIDE),
            low(CHUNK, width),
            pltpu.VMEM((bits, 8, width), WIDE),
            pltpu.VMEM((bits, 8, width), WIDE),
        ]
        + ring_sum_scratch(count // 2, shard, 4 * head_cols, 4)
        + [
            dma((7,)),
            dma((2,)),
            dma((5,)),
            dma((5,)),
            dma((4,)),
            dma((4,)),
            dma((bits,)),
            dma((bits,)),
        ],
        compiler_params=pltpu.CompilerParams(
            collective_id=3, has_side_effects=True, vmem_limit_bytes=60 * 2**20
        ),
    )(
        x,
        vectors,
        early,
        normed,
        branch,
        query_grad,
        kv_grad,
        mixed,
        own_low,
        prefix_half,
        grad_hidden,
    )


def finish_kernel(*refs):
    count = (len(refs) - 2) // 3
    ins, outs, rooms = refs[:count], refs[count : 2 * count], refs[2 * count : 3 * count]
    in_sem, out_sem = refs[3 * count :]
    loads = [
        pltpu.make_async_copy(src, room, in_sem.at[i])
        for i, (src, room) in enumerate(zip(ins, rooms))
    ]
    stores = [
        pltpu.make_async_copy(room, dst, out_sem.at[i])
        for i, (room, dst) in enumerate(zip(rooms, outs))
    ]
    for copy in loads:
        copy.start()
    for load, store in zip(loads, stores):
        load.wait()
        store.start()
    for copy in stores:
        copy.wait()


def run_finish(arrays):
    dma = pltpu.SemaphoreType.DMA
    return pl.pallas_call(
        finish_kernel,
        out_shape=[jax.ShapeDtypeStruct(a.shape, a.dtype) for a in arrays],
        in_specs=[any_spec()] * len(arrays),
        out_specs=[any_spec()] * len(arrays),
        scratch_shapes=[pltpu.VMEM(a.shape, a.dtype) for a in arrays]
        + [dma((len(arrays),)), dma((len(arrays),))],
        compiler_params=pltpu.CompilerParams(vmem_limit_bytes=60 * 2**20),
    )(*arrays)


def ring_program(
    inputs,
    cotangent,
    attn_gain,
    attn_shift,
    query_weight,
    key_weight,
    value_weight,
    out_weight,
    mlp_gain,
    mlp_shift,
    up_weight,
    up_bias,
    down_weight,
    down_bias,
    live_rows,
):
    block_rows, width = inputs.shape
    shard_rows = query_weight.shape[0]
    head_cols = query_weight.shape[1] // 2
    ff_cols = up_weight.shape[1] // 2
    ff_part = ff_cols // 2
    local_heads = head_cols // HEAD_DIM
    score_scale = 1.0 / math.sqrt(HEAD_DIM)
    dp_size, sol_size = lax.axis_size("dp"), lax.axis_size("sol")
    count, ahead, back, cores = ring_pairs(dp_size, sol_size)
    dp_place, sol_place = lax.axis_index("dp"), lax.axis_index("sol")
    x_place, core = dp_place // 2, dp_place % 2
    first_core = core == 0
    along = jnp.where(x_place % 2 == 0, sol_place, sol_size - 1 - sol_place)
    ring_here = x_place * sol_size + along

    order_list = []
    for j in range(count):
        q = (ring_here + j) % count
        qx, qa = q // sol_size, q % sol_size
        qz = jnp.where(qx % 2 == 0, qa, sol_size - 1 - qa)
        order_list += [(qx * 2) * sol_size + qz, (qx * 2 + 1) * sol_size + qz]
    order = jnp.stack(order_list).astype(jnp.int32)
    back_order = jnp.argsort(order).astype(jnp.int32)

    def to_core(value):
        return lax.ppermute(value, ROWS_AXES, cores)

    def to_tensor(value):
        return lax.ppermute(value, "tensor", [(0, 1), (1, 0)])

    def reorder_vector(vector, by):
        return jnp.take(vector.reshape(by.shape[0], -1), by, axis=0).reshape(vector.shape)

    def gather_ring(piece, flip):
        hops_ahead = count // 2 - (1 if flip else 0)
        hops_back = count - 1 - hops_ahead
        got = {0: piece}
        moving_a, moving_b = piece, piece
        for k in range(1, count // 2 + 1):
            if k <= hops_ahead:
                moving_a = lax.ppermute(moving_a, ROWS_AXES, ahead)
                got[count - k] = moving_a
            if k <= hops_back:
                moving_b = lax.ppermute(moving_b, ROWS_AXES, back)
                got[k] = moving_b
        return jnp.concatenate([got[j] for j in range(count)], axis=0)

    def scatter_ring(chunk, flip):
        hops_ahead = count // 2 - (1 if flip else 0)
        hops_back = count - 1 - hops_ahead
        carried_a = carried_b = None
        for k in range(count // 2, 0, -1):
            if k <= hops_ahead:
                value = chunk(k)
                if carried_a is not None:
                    value = value + carried_a.astype(WIDE)
                carried_a = lax.ppermute(value.astype(LOW), ROWS_AXES, ahead)
            if k <= hops_back:
                value = chunk(count - k)
                if carried_b is not None:
                    value = value + carried_b.astype(WIDE)
                carried_b = lax.ppermute(value.astype(LOW), ROWS_AXES, back)
        return chunk(0) + carried_a.astype(WIDE) + carried_b.astype(WIDE)

    def own_part(shards):
        firsts, seconds = [], []
        for shard, start, size in shards:
            half = shard.shape[1] // 2
            firsts.append(shard[:, start : start + size])
            seconds.append(shard[:, half + start : half + start + size])
        low_half = jnp.concatenate(firsts, axis=1) if len(firsts) > 1 else firsts[0]
        high_half = jnp.concatenate(seconds, axis=1) if len(seconds) > 1 else seconds[0]
        mine = jnp.where(first_core, low_half, high_half)
        other = to_core(jnp.where(first_core, high_half, low_half))
        return jnp.concatenate(
            [jnp.where(first_core, mine, other), jnp.where(first_core, other, mine)], axis=0
        )

    def split_rows(full):
        upper, lower = full[:shard_rows], full[shard_rows:]
        mine = jnp.where(first_core, upper, lower)
        other = to_core(jnp.where(first_core, lower, upper))
        return jnp.where(first_core, mine, other), jnp.where(first_core, other, mine)

    def sum_partials(partial):
        mine = partial[:block_rows] + to_core(partial[block_rows:].astype(LOW)).astype(WIDE)
        low = mine.astype(LOW)
        return low.astype(WIDE) + to_tensor(low).astype(WIDE)

    def pair_rows(own):
        return jnp.concatenate([own, to_core(own)], axis=0)

    qk_piece = own_part([(query_weight, 0, head_cols), (key_weight, 0, head_cols)])
    vo_piece = own_part([(value_weight, 0, head_cols), (out_weight, 0, head_cols)])
    up_pieces = [own_part([(up_weight, s, ff_part)]) for s in (0, ff_part)]
    down_pieces = [own_part([(down_weight, s, ff_part)]) for s in (0, ff_part)]
    qk_full = gather_ring(qk_piece, False)
    vo_full = gather_ring(vo_piece, True)
    up_full = [gather_ring(up_pieces[0], False), gather_ring(up_pieces[1], True)]
    down_full = [gather_ring(down_pieces[0], False), gather_ring(down_pieces[1], True)]
    query_full, key_full = qk_full[:, :head_cols], qk_full[:, head_cols:]
    value_full, out_full = vo_full[:, :head_cols], vo_full[:, head_cols:]

    tensor_place = lax.axis_index("tensor")
    half_rows = block_rows // 2
    half = jnp.where(tensor_place == 0, inputs[:half_rows], inputs[half_rows:])
    prefix_half = half
    hop = half
    for k in range(1, sol_size):
        hop = lax.ppermute(hop, "sol", [(k - 1, k)])
        prefix_half = jnp.where(sol_place == k, hop, prefix_half)
    other_half = to_tensor(prefix_half)
    prefix_inputs = jnp.concatenate(
        [
            jnp.where(tensor_place == 0, prefix_half, other_half),
            jnp.where(tensor_place == 0, other_half, prefix_half),
        ],
        axis=0,
    )

    own_low = reorder(inputs, order)
    prefix_low = reorder(prefix_inputs, order)
    cot_low = reorder(cotangent, order)
    attn_gain_o, attn_shift_o, mlp_gain_o, mlp_shift_o, down_bias_o = [
        reorder_vector(v, order) for v in (attn_gain, attn_shift, mlp_gain, mlp_shift, down_bias)
    ]
    up_bias_c = jnp.where(first_core, up_bias[:ff_cols], up_bias[ff_cols:])
    up_bias_parts = [up_bias_c[:ff_part], up_bias_c[ff_part:]]

    features = own_low.astype(WIDE)
    normed = pair_rows(layer_norm(features, attn_gain_o, attn_shift_o).astype(LOW))
    normed_prefix = pair_rows(
        layer_norm(prefix_low.astype(WIDE), attn_gain_o, attn_shift_o).astype(LOW)
    )
    cot_pair = pair_rows(cot_low)

    query_rows = dot_plain(normed, query_full).astype(LOW)
    key_rows = dot_plain(normed, key_full).astype(LOW)
    value_rows = dot_plain(normed, value_full).astype(LOW)
    key_prefix = dot_plain(normed_prefix, key_full).astype(LOW)
    value_prefix = dot_plain(normed_prefix, value_full).astype(LOW)

    def heads_of(rows):
        return rows.reshape(2, -1, local_heads, HEAD_DIM)

    head_queries = heads_of(query_rows)
    all_keys = jnp.concatenate([heads_of(key_prefix), heads_of(key_rows)], axis=1)
    all_values = jnp.concatenate([heads_of(value_prefix), heads_of(value_rows)], axis=1)

    row_ids = jnp.arange(block_rows)[:, None]
    col_ids = jnp.arange(block_rows)[None, :]
    masks = []
    for place in (dp_place, dp_place + 1 - 2 * core):
        own_live = live_rows[place * sol_size + sol_place]
        prefix_live = live_rows[place * sol_size]
        prefix_ok = jnp.logical_and(col_ids < prefix_live, sol_place != 0)
        own_ok = jnp.logical_and(col_ids <= row_ids, col_ids < own_live)
        masks.append(
            jnp.concatenate(
                [jnp.broadcast_to(prefix_ok, (block_rows, block_rows)), own_ok], axis=1
            )
        )
    allowed = jnp.stack(masks)[:, None]

    def masked_scores():
        raw = jnp.einsum("bqhd,bkhd->bhqk", head_queries, all_keys, preferred_element_type=WIDE)
        return jnp.where(allowed, raw * score_scale, NEG_FILL)

    scores = masked_scores()
    row_peak = jnp.max(scores, axis=-1, keepdims=True)
    exp_scores = jnp.exp(scores - row_peak)
    totals = jnp.sum(exp_scores, axis=-1, keepdims=True)
    attn_probs = exp_scores / totals
    log_total = row_peak + jnp.log(totals)
    mixed = jnp.einsum(
        "bhqk,bkhd->bqhd", attn_probs.astype(LOW), all_values, preferred_element_type=WIDE
    )
    mixed_low = mixed.reshape(2 * block_rows, head_cols).astype(LOW)

    hidden = features + sum_partials(dot_right_t(mixed_low, out_full))
    normed_two = pair_rows(layer_norm(hidden, mlp_gain_o, mlp_shift_o).astype(LOW))
    upward = [dot_plain(normed_two, up_full[i]) + up_bias_parts[i] for i in range(2)]
    active = [gelu_tanh(u).astype(LOW) for u in upward]
    down_grads = [
        scatter_ring(
            lambda j, i=i: dot_left_t(
                cot_pair[:, j * 2 * shard_rows : (j + 1) * 2 * shard_rows], active[i]
            ),
            i == 1,
        )
        for i in range(2)
    ]
    grad_up = []
    for i in range(2):
        grad_active = dot_plain(cot_pair, down_full[i])
        unused_gelu, gelu_pull = jax.vjp(gelu_tanh, upward[i])
        grad_up.append(gelu_pull(grad_active)[0].astype(LOW))
    grad_normed_two = sum_partials(
        dot_right_t(grad_up[0], up_full[0]) + dot_right_t(grad_up[1], up_full[1])
    )
    up_grads = [
        scatter_ring(
            lambda j, i=i: dot_left_t(
                normed_two[:, j * 2 * shard_rows : (j + 1) * 2 * shard_rows], grad_up[i]
            ),
            i == 1,
        )
        for i in range(2)
    ]
    mlp_total = sum_partials(
        dot_right_t(active[0], down_full[0]) + dot_right_t(active[1], down_full[1])
    )
    outputs = reorder((hidden + mlp_total + down_bias_o).astype(LOW), back_order)

    grad_out = cot_low.astype(WIDE)
    down_bias_grad = jnp.sum(grad_out, axis=0)
    grad_hidden_norm, mlp_gain_grad, mlp_shift_grad = layer_norm_back(
        hidden, mlp_gain_o, grad_normed_two
    )
    grad_hidden = grad_out + grad_hidden_norm
    grad_branch = pair_rows(grad_hidden.astype(LOW))
    grad_mixed_low = dot_plain(grad_branch, out_full).astype(LOW)

    grad_head_mixed = heads_of(grad_mixed_low)
    attn_probs = jnp.exp(masked_scores() - log_total)
    grad_probs = jnp.einsum(
        "bqhd,bkhd->bhqk", grad_head_mixed, all_values, preferred_element_type=WIDE
    )
    row_delta = jnp.sum(attn_probs * grad_probs, axis=-1, keepdims=True)
    grad_scores = (attn_probs * (grad_probs - row_delta)).astype(LOW)
    grad_queries = (
        jnp.einsum("bhqk,bkhd->bqhd", grad_scores, all_keys, preferred_element_type=WIDE)
        * score_scale
    )
    grad_keys = (
        jnp.einsum("bhqk,bqhd->bkhd", grad_scores, head_queries, preferred_element_type=WIDE)
        * score_scale
    )
    grad_values = jnp.einsum(
        "bhqk,bqhd->bkhd", attn_probs.astype(LOW), grad_head_mixed, preferred_element_type=WIDE
    )

    def rows_of(heads):
        return heads.reshape(2 * block_rows, head_cols).astype(LOW)

    query_grad_low = rows_of(grad_queries)
    key_own = rows_of(grad_keys[:, block_rows:])
    value_own = rows_of(grad_values[:, block_rows:])
    key_pre = rows_of(grad_keys[:, :block_rows])
    value_pre = rows_of(grad_values[:, :block_rows])

    kv_pre = jnp.concatenate([key_pre, value_pre], axis=1)
    carried = kv_pre
    for k in range(sol_size - 1, 0, -1):
        came = lax.ppermute(carried, "sol", [(k, k - 1)])
        if k > 1:
            carried = (kv_pre.astype(WIDE) + came.astype(WIDE)).astype(LOW)
    key_all = (key_own.astype(WIDE) + came[:, :head_cols].astype(WIDE)).astype(LOW)
    value_all = (value_own.astype(WIDE) + came[:, head_cols:].astype(WIDE)).astype(LOW)

    normed_all = jnp.concatenate([normed, normed_prefix], axis=0)
    key_rows_grad = jnp.concatenate([key_own, key_pre], axis=0)
    value_rows_grad = jnp.concatenate([value_own, value_pre], axis=0)

    def qk_chunk(j):
        at = slice(j * 2 * shard_rows, (j + 1) * 2 * shard_rows)
        return jnp.concatenate(
            [
                dot_left_t(normed[:, at], query_grad_low),
                dot_left_t(normed_all[:, at], key_rows_grad),
            ],
            axis=1,
        )

    def vo_chunk(j):
        at = slice(j * 2 * shard_rows, (j + 1) * 2 * shard_rows)
        return jnp.concatenate(
            [
                dot_left_t(normed_all[:, at], value_rows_grad),
                dot_left_t(grad_branch[:, at], mixed_low),
            ],
            axis=1,
        )

    qk_grad = scatter_ring(qk_chunk, False)
    vo_grad = scatter_ring(vo_chunk, True)

    grad_normed = sum_partials(
        dot_right_t(query_grad_low, query_full)
        + dot_right_t(key_all, key_full)
        + dot_right_t(value_all, value_full)
    )
    grad_features, attn_gain_grad, attn_shift_grad = layer_norm_back(
        features, attn_gain_o, grad_normed
    )
    input_grad = reorder((grad_hidden + grad_features).astype(LOW), back_order)

    up_bias_grad = jnp.concatenate([jnp.sum(g.astype(WIDE), axis=0) for g in grad_up])
    up_bias_both = jnp.concatenate(
        [
            jnp.where(first_core, up_bias_grad, 0.0),
            jnp.where(first_core, 0.0, up_bias_grad),
        ]
    )

    def sum_rows_axes(vector):
        vector = vector + to_core(vector)
        step = 1
        while step < sol_size:
            vector = vector + lax.ppermute(vector, "sol", [(i, i ^ step) for i in range(sol_size)])
            step *= 2
        step = 2
        while step < dp_size:
            vector = vector + lax.ppermute(vector, "dp", [(i, i ^ step) for i in range(dp_size)])
            step *= 2
        return vector

    early = sum_rows_axes(
        jnp.concatenate(
            [reorder_vector(v, back_order) for v in (mlp_gain_grad, mlp_shift_grad, down_bias_grad)]
            + [up_bias_both]
        )
    )
    late = sum_rows_axes(
        jnp.concatenate([reorder_vector(v, back_order) for v in (attn_gain_grad, attn_shift_grad)])
    )

    qk_low, qk_high = split_rows(qk_grad)
    vo_low, vo_high = split_rows(vo_grad)
    up_low, up_high = zip(*[split_rows(g) for g in up_grads])
    down_low, down_high = zip(*[split_rows(g) for g in down_grads])

    def both(low_cols, high_cols):
        return jnp.concatenate([low_cols, high_cols], axis=1)

    return (
        outputs,
        input_grad,
        late[:width],
        late[width:],
        both(qk_low[:, :head_cols], qk_high[:, :head_cols]),
        both(qk_low[:, head_cols:], qk_high[:, head_cols:]),
        both(vo_low[:, :head_cols], vo_high[:, :head_cols]),
        both(vo_low[:, head_cols:], vo_high[:, head_cols:]),
        early[:width],
        early[width : 2 * width],
        jnp.concatenate(up_low + up_high, axis=1),
        early[3 * width :],
        jnp.concatenate(down_low + down_high, axis=1),
        early[2 * width : 3 * width],
    )


def per_device(*arrays):
    inputs, query_weight, up_weight = arrays[0], arrays[4], arrays[10]
    width = inputs.shape[1]
    fits = (
        query_weight.shape[0] % 128 == 0
        and inputs.shape[0] == 2 * CHUNK
        and up_weight.shape[1] == 2 * width
        and query_weight.shape[1] * 2 == width
        and lax.axis_size("dp") % 2 == 0
        and lax.axis_size("dp") * lax.axis_size("sol") == 16
        and lax.axis_size("tensor") == 2
    )
    return kernel_program(*arrays) if fits else ring_program(*arrays)


def kernel_program(
    inputs,
    cotangent,
    attn_gain,
    attn_shift,
    query_weight,
    key_weight,
    value_weight,
    out_weight,
    mlp_gain,
    mlp_shift,
    up_weight,
    up_bias,
    down_weight,
    down_bias,
    live_rows,
):
    width = inputs.shape[1]
    shard_rows = query_weight.shape[0]
    ff_cols = up_weight.shape[1] // 2
    dp_size, sol_size = lax.axis_size("dp"), lax.axis_size("sol")
    here = Place(dp_size, sol_size)
    core = here.core
    first_core = core == 0
    order = jnp.stack(here.blocks()).astype(jnp.int32)
    vectors = jnp.stack([attn_gain, attn_shift, mlp_gain, mlp_shift, down_bias])
    vectors = jnp.take(vectors.reshape(5, here.count * 2, shard_rows), order, axis=1).reshape(5, width)
    up_bias_c = jnp.where(first_core, up_bias[:ff_cols], up_bias[ff_cols:])[None]
    (
        weights,
        normed_all,
        cot_pair,
        query_rows,
        key_rows,
        value_rows,
        probs,
        mixed_low,
        hidden,
        normed_two,
        slope,
        active,
    ) = run_forward(
        dp_size,
        sol_size,
        inputs,
        vectors,
        up_bias_c,
        live_rows,
        cotangent,
        (query_weight, key_weight, value_weight, out_weight, up_weight, down_weight),
    )
    grad_up, grad_branch, grad_hidden, mlp_low, down_grad, early_sums = run_down(
        dp_size, sol_size, shard_rows, vectors, weights, cot_pair, active, slope, hidden
    )
    query_grad, kv_grad, own_low, prefix_half, up_grad, outputs, _ = run_attend_back(
        dp_size,
        sol_size,
        shard_rows,
        vectors,
        weights,
        normed_two,
        grad_up,
        grad_branch,
        query_rows,
        key_rows,
        value_rows,
        probs,
        mlp_low,
        hidden,
    )
    query_grads, key_grads, value_grads, out_grads, input_grad, sums = run_last(
        dp_size,
        sol_size,
        shard_rows,
        inputs,
        vectors,
        early_sums,
        normed_all,
        grad_branch,
        query_grad,
        kv_grad,
        mixed_low,
        own_low,
        prefix_half,
        grad_hidden,
    )

    (
        outputs,
        input_grad,
        query_grads,
        key_grads,
        value_grads,
        out_grads,
        up_grad,
        down_grad,
    ) = run_finish(
        [
            outputs,
            input_grad,
            query_grads,
            key_grads,
            value_grads,
            out_grads,
            up_grad,
            down_grad,
        ]
    )
    return (
        outputs,
        input_grad,
        sums[0],
        sums[1],
        query_grads,
        key_grads,
        value_grads,
        out_grads,
        sums[2],
        sums[3],
        up_grad,
        sums[5:7].reshape(-1),
        down_grad,
        sums[4],
    )


def solution(mesh):
    rows = P(("dp", "sol"), None)
    matrix = P(("dp", "sol"), "tensor")
    return jax.shard_map(
        per_device,
        mesh=mesh,
        in_specs=(
            rows,
            rows,
            P(),
            P(),
            matrix,
            matrix,
            matrix,
            matrix,
            P(),
            P(),
            matrix,
            P("tensor"),
            matrix,
            P(),
            P(),
        ),
        out_specs=(
            rows,
            rows,
            P(),
            P(),
            matrix,
            matrix,
            matrix,
            matrix,
            P(),
            P(),
            matrix,
            P("tensor"),
            matrix,
            P(),
        ),
        check_vma=False,
    )
```

```python
import functools
import math

import jax
import jax.numpy as jnp
from jax import lax
from jax.experimental import pallas as pl
from jax.experimental.pallas import tpu as pltpu
from jax.sharding import PartitionSpec as P

HEAD_DIM = 128
EPSILON = 1e-05
NEG_FILL = -1e30
ROWS_AXES = ("dp", "sol")
LOW = jnp.bfloat16
WIDE = jnp.float32


def ring_place(position, sol_size):
    x, along = position // sol_size, position % sol_size
    return x, (along if x % 2 == 0 else sol_size - 1 - along)


def ring_pairs(dp_size, sol_size):
    count = dp_size // 2 * sol_size

    def flat(position, core):
        x, z = ring_place(position % count, sol_size)
        return (x * 2 + core) * sol_size + z

    places = [(q, c) for q in range(count) for c in range(2)]
    ahead = [(flat(q, c), flat(q + 1, c)) for q, c in places]
    back = [(b, a) for a, b in ahead]
    cores = [(flat(q, c), flat(q, 1 - c)) for q, c in places]
    return count, ahead, back, cores


def dot_plain(left_side, right_side):
    return jnp.dot(left_side, right_side, preferred_element_type=WIDE)


def dot_right_t(left_side, right_side):
    return lax.dot_general(
        left_side, right_side, (((1,), (1,)), ((), ())), preferred_element_type=WIDE
    )


def dot_left_t(left_side, right_side):
    return lax.dot_general(
        left_side, right_side, (((0,), (0,)), ((), ())), preferred_element_type=WIDE
    )


def norm_stats(features):
    row_mean = jnp.mean(features, axis=-1, keepdims=True)
    centered = features - row_mean
    variance = jnp.mean(centered * centered, axis=-1, keepdims=True)
    return row_mean, lax.rsqrt(variance + EPSILON)


def layer_norm(features, norm_gain, norm_shift):
    row_mean, inverse = norm_stats(features)
    return (features - row_mean) * inverse * norm_gain + norm_shift


def layer_norm_back(features, norm_gain, grad):
    row_mean, inverse = norm_stats(features)
    unit = (features - row_mean) * inverse
    scaled = grad * norm_gain
    along = jnp.mean(scaled * unit, axis=-1, keepdims=True)
    level = jnp.mean(scaled, axis=-1, keepdims=True)
    grad_features = (scaled - level - unit * along) * inverse
    return grad_features, jnp.sum(grad * unit, axis=0), jnp.sum(grad, axis=0)


def gelu_tanh(upward):
    return jax.nn.gelu(upward, approximate=True)


def copy_block(order_ref, in_ref, out_ref):
    out_ref[...] = in_ref[...]


def reorder(rows, order):
    blocks = order.shape[0]
    height, width = rows.shape
    part = width // blocks
    if part % 128:
        return jnp.take(rows.reshape(height, blocks, part), order, axis=1).reshape(height, width)
    return pl.pallas_call(
        copy_block,
        grid_spec=pltpu.PrefetchScalarGridSpec(
            num_scalar_prefetch=1,
            grid=(blocks,),
            in_specs=[pl.BlockSpec((height, part), lambda j, order_ref: (0, order_ref[j]))],
            out_specs=pl.BlockSpec((height, part), lambda j, order_ref: (0, j)),
        ),
        out_shape=jax.ShapeDtypeStruct(rows.shape, rows.dtype),
        cost_estimate=pl.CostEstimate(
            flops=0, bytes_accessed=4 * height * width, transcendentals=0
        ),
    )(order, rows)


MESH = pl.DeviceIdType.MESH
CHUNK = 256


def any_spec():
    return pl.BlockSpec(memory_space=pl.ANY)


def vmem_spec():
    return pl.BlockSpec(memory_space=pltpu.VMEM)


class Place:
    def __init__(self, dp_size, sol_size):
        self.dp_size, self.sol_size = dp_size, sol_size
        self.count = dp_size // 2 * sol_size
        dp, self.z = lax.axis_index("dp"), lax.axis_index("sol")
        self.y = lax.axis_index("tensor")
        self.x, self.core = dp // 2, dp % 2
        self.dp = dp
        turned = jnp.where(self.x % 2 == 0, self.z, sol_size - 1 - self.z)
        self.at = self.x * sol_size + turned
        self.next = self._chip((self.at + 1) % self.count)
        self.prev = self._chip((self.at + self.count - 1) % self.count)
        self.sibling = (dp + 1 - 2 * self.core, self.z, self.y)
        self.across = (dp, self.z, 1 - self.y)

    def _coords(self, position):
        x, turned = position // self.sol_size, position % self.sol_size
        return x, jnp.where(x % 2 == 0, turned, self.sol_size - 1 - turned)

    def _chip(self, position):
        x, z = self._coords(position)
        return (x * 2 + self.core, z, self.y)

    def up_ahead(self, step=0):
        x, z = self._coords((self.at + step + self.count) % self.count)
        return (x % 2 == 0) == (z > 0)

    def along(self, step):
        return (self.dp, self.z + step, self.y)

    def blocks(self):
        result = []
        for j in range(self.count):
            x, z = self._coords((self.at + j) % self.count)
            result += [(x * 2) * self.sol_size + z, (x * 2 + 1) * self.sol_size + z]
        return result

    def partners(self):
        result = [self.sibling]
        step = 1
        while step < self.sol_size:
            result.append((self.dp, self._flip(self.z, step), self.y))
            step *= 2
        step = 2
        while step < self.dp_size:
            result.append((self._flip(self.dp, step), self.z, self.y))
            step *= 2
        return result

    @staticmethod
    def _flip(place, step):
        return jnp.where(place // step % 2 == 0, place + step, place - step)

    def greet(self, others=()):
        barrier = pltpu.get_barrier_semaphore()
        peers = (self.next, self.prev, self.sibling, self.across) + tuple(others)
        for peer in peers:
            pl.semaphore_signal(barrier, inc=1, device_id=peer, device_id_type=MESH)
        pl.semaphore_wait(barrier, len(peers))


def remote(src, dst, send_sem, recv_sem, device):
    return pltpu.make_async_remote_copy(
        src_ref=src,
        dst_ref=dst,
        send_sem=send_sem,
        recv_sem=recv_sem,
        device_id=device,
        device_id_type=MESH,
    )


def norm_rows(values, gain, shift):
    row_mean = jnp.mean(values, axis=-1, keepdims=True)
    centered = values - row_mean
    variance = jnp.mean(centered * centered, axis=-1, keepdims=True)
    return centered * lax.rsqrt(variance + EPSILON) * gain + shift


def forward_kernel(
    dp_size,
    sol_size,
    x_ref,
    attn_gain_ref,
    attn_shift_ref,
    mlp_gain_ref,
    mlp_shift_ref,
    up_bias_ref,
    live_ref,
    cot_hbm,
    query_ref,
    key_ref,
    value_ref,
    out_ref,
    up_ref,
    down_ref,
    weights,
    normed_out,
    cot_out,
    query_out,
    key_out,
    value_out,
    probs_out,
    mixed_out,
    hidden_out,
    normed_two_out,
    slope_out,
    active_out,
    w_v,
    normed_v,
    query_v,
    key_v,
    value_v,
    probs_v,
    mixed_v,
    hidden_v,
    normed_two_v,
    slope_v,
    active_v,
    core_send_v,
    core_recv_v,
    cross_send_v,
    cross_recv_v,
    ring_send,
    ring_recv,
    swap_local,
    swap_send,
    swap_recv,
    prefix_send,
    prefix_recv,
    pair_send,
    pair_recv,
    sum_send,
    sum_recv,
    cot_sem,
    load_sem,
    probs_sem,
    store_sem,
):
    here = Place(dp_size, sol_size)
    count, core = here.count, here.core
    rows, width = x_ref.shape
    prefix_v = slope_v
    shard = query_ref.shape[0]
    head_cols = query_ref.shape[1] // 2
    ff = up_ref.shape[1] // 2
    half = width // 2
    local_heads = head_cols // HEAD_DIM
    scale = 1.0 / math.sqrt(HEAD_DIM)
    blocks = here.blocks()
    far = count // 2
    own_class, other_class = core, 1 - core

    here.greet()

    def slot(j, which):
        return pl.ds(pl.multiple_of((2 * j + which) * shard, shard), shard)

    shards = (
        (0, 0, query_ref, head_cols),
        (0, head_cols, key_ref, head_cols),
        (0, 2 * head_cols, value_ref, head_cols),
        (0, 3 * head_cols, out_ref, head_cols),
        (1, 0, up_ref, ff),
        (2, 0, down_ref, ff),
    )

    def swap_copies(i):
        matrix, start, source, size = shards[i]
        target = weights.at[matrix, slot(0, own_class), pl.ds(start, size)]

        def columns(which):
            return source.at[:, pl.ds(pl.multiple_of(which * size, size), size)]

        return (
            pltpu.make_async_copy(columns(core), target, swap_local.at[i]),
            remote(columns(1 - core), target, swap_send.at[i], swap_recv.at[i], here.sibling),
        )

    def start_swap(matrix):
        for i in range(len(shards)):
            if shards[i][0] == matrix:
                for copy in swap_copies(i):
                    copy.start()

    def hops(matrix, k, sub):
        which = own_class if sub == 0 else other_class
        halved = k == far and matrix > 0
        ahead_cols = pl.ds(0, half if halved else width)
        back_cols = pl.ds(half if halved else 0, half if halved else width)
        return (
            remote(
                weights.at[matrix, slot((count - k + 1) % count, which), ahead_cols],
                weights.at[matrix, slot(count - k, which), ahead_cols],
                ring_send.at[matrix, 0, k - 1, sub],
                ring_recv.at[matrix, 0, k - 1, sub],
                here.next,
            ),
            remote(
                weights.at[matrix, slot(k - 1, which), back_cols],
                weights.at[matrix, slot(k, which), back_cols],
                ring_send.at[matrix, 1, k - 1, sub],
                ring_recv.at[matrix, 1, k - 1, sub],
                here.prev,
            ),
        )

    def start_ring(matrix, sub):
        for i in range(len(shards)):
            if shards[i][0] == matrix:
                if sub == 0:
                    swap_copies(i)[0].wait()
                else:
                    swap_copies(i)[1].wait_recv()
        for copy in hops(matrix, 1, sub):
            copy.start()

    def only_when(matrix, k, condition, action):
        if matrix == 0 and k == far:
            pl.when(condition)(action)
        else:
            action()

    came_ahead = jnp.logical_not(here.up_ahead())
    goes = (jnp.logical_not(here.up_ahead(1)), here.up_ahead(-1))

    def pump(matrix, k, sub):
        came = hops(matrix, k, sub)
        if k < far:
            further = hops(matrix, k + 1, sub)
        for i in range(2):
            only_when(
                matrix, k, came_ahead if i == 0 else jnp.logical_not(came_ahead), came[i].wait_recv
            )
            if k < far:
                only_when(matrix, k + 1, goes[i], further[i].start)
        if k == far - 1 and matrix < 2:
            start_ring(matrix + 1, sub)

    steps = [
        (matrix, k, sub) for matrix in range(3) for k in range(1, far + 1) for sub in range(2)
    ]
    done = [0]

    def pump_to(number):
        while done[0] < min(number, len(steps)):
            pump(*steps[done[0]])
            done[0] += 1

    y_rows = rows // 2
    parts = 4
    part = y_rows // parts

    def prefix_rows(which_half, i):
        return pl.ds(pl.multiple_of(which_half * y_rows + i * part, part), part)

    def prefix_hop(i, from_input):
        at = prefix_rows(here.y, i)
        return remote(
            x_ref.at[at] if from_input else prefix_v.at[at],
            prefix_v.at[at],
            prefix_send.at[0, i],
            prefix_recv.at[0, i],
            here.along(1),
        )

    def prefix_cross(i, from_input):
        at = prefix_rows(here.y, i)
        return remote(
            x_ref.at[at] if from_input else prefix_v.at[at],
            prefix_v.at[at],
            prefix_send.at[1, i],
            prefix_recv.at[1, i],
            here.across,
        )

    def prefix_stage(stage, i):
        @pl.when(here.z == stage)
        def _():
            if stage == 0:
                prefix_hop(i, True).start()
                prefix_cross(i, True).start()
            else:
                prefix_hop(i, False).wait_recv()
                if stage < sol_size - 1:
                    prefix_hop(i, False).start()
                prefix_cross(i, False).start()

    def prefix_finish():
        for i in range(parts):
            prefix_cross(i, False).wait_recv()

        @pl.when(here.z == 0)
        def _():
            for i in range(parts):
                at = prefix_rows(here.y, i)
                prefix_v[at, :] = x_ref[at, :]

    cot_load = pltpu.make_async_copy(cot_hbm, active_v.at[pl.ds(0, rows)], cot_sem.at[1])
    start_swap(0)
    start_swap(1)
    start_swap(2)
    cot_load.start()

    start_ring(0, 0)
    start_ring(0, 1)

    def ordered(ref, at):
        return jnp.concatenate(
            [ref[at, pl.ds(pl.multiple_of(b * shard, shard), shard)] for b in blocks], axis=1
        ).astype(WIDE)

    gain, shift, gain_two, shift_two = [
        ordered(ref, pl.ds(0, 1))
        for ref in (attn_gain_ref, attn_shift_ref, mlp_gain_ref, mlp_shift_ref)
    ]

    def norm_into(ref, start):
        @pl.loop(0, rows // 128)
        def _(t):
            at = pl.ds(pl.multiple_of(t * 128, 128), 128)
            to = pl.ds(pl.multiple_of(start + t * 128, 128), 128)
            normed_v[to, :] = norm_rows(ordered(ref, at), gain, shift).astype(LOW)

    normed_pair = remote(
        normed_v.at[pl.ds(0, rows)],
        normed_v.at[pl.ds(rows, rows)],
        pair_send.at[1],
        pair_recv.at[1],
        here.sibling,
    )
    prefix_pair = remote(
        normed_v.at[pl.ds(2 * rows, rows)],
        normed_v.at[pl.ds(3 * rows, rows)],
        pair_send.at[2],
        pair_recv.at[2],
        here.sibling,
    )
    norm_into(x_ref, 0)
    normed_pair.start()
    pump_to(2)
    for i in range(parts):
        prefix_stage(0, i)
    for step in range(1, sol_size + parts - 1):
        for i in range(parts):
            if 1 <= step - i < sol_size:
                prefix_stage(step - i, i)
        pump_to(2 + step)
    pump_to(2 * far)

    cot_pair = remote(
        core_send_v,
        cot_out.at[pl.ds(rows, rows)],
        pair_send.at[0],
        pair_recv.at[0],
        here.sibling,
    )
    cot_own = pltpu.make_async_copy(core_send_v, cot_out.at[pl.ds(0, rows)], cot_sem.at[0])

    cot_load.wait()

    @pl.loop(0, rows // 128)
    def _(t):
        at = pl.ds(pl.multiple_of(t * 128, 128), 128)
        core_send_v[at, :] = ordered(active_v, at).astype(LOW)

    cot_pair.start()
    cot_own.start()

    load_first = pltpu.make_async_copy(weights.at[0], w_v, load_sem.at[0])
    load_first.start()
    normed_pair.wait_recv()
    load_first.wait()

    def row_tile(t):
        return pl.ds(pl.multiple_of(t * CHUNK, CHUNK), CHUNK)

    def project(first, last, with_queries):
        @pl.loop(first, last)
        def _(t):
            at = row_tile(t)
            tile = normed_v[at, :]
            kv = dot_plain(tile, w_v[:, head_cols : 3 * head_cols])
            key_v[at, :] = kv[:, :head_cols].astype(LOW)
            value_v[at, :] = kv[:, head_cols:].astype(LOW)
            if with_queries:
                query_v[at, :] = dot_plain(tile, w_v[:, :head_cols]).astype(LOW)

    tiles = rows // CHUNK
    project(0, 2 * tiles, True)
    pump_to(2 * far + 1)
    prefix_finish()
    norm_into(prefix_v, 2 * rows)
    prefix_pair.start()
    pump_to(2 * far + 2)
    prefix_pair.wait_recv()
    project(2 * tiles, 4 * tiles, False)

    stores = []

    def store(src, dst):
        copy = pltpu.make_async_copy(src, dst, store_sem.at[len(stores)])
        copy.start()
        stores.append(copy)

    store(normed_v, normed_out)
    store(query_v, query_out)
    store(key_v, key_out)
    store(value_v, value_out)

    def probs_copy(unit):
        return pltpu.make_async_copy(
            probs_v.at[unit % 2], probs_out.at[unit], probs_sem.at[unit % 2]
        )

    def attend(unit):
        block, head = unit // local_heads, unit % local_heads
        cols = pl.ds(pl.multiple_of(head * HEAD_DIM, HEAD_DIM), HEAD_DIM)
        place = jnp.where(block == 0, here.dp, here.dp + 1 - 2 * core)
        own_live = live_ref[place * sol_size + here.z]
        prefix_live = jnp.where(here.z == 0, 0, live_ref[place * sol_size])
        own_at = pl.ds(pl.multiple_of(block * rows, rows), rows)
        prefix_at = pl.ds(pl.multiple_of((2 + block) * rows, rows), rows)

        @pl.when(unit >= 2)
        def _():
            probs_copy(unit - 2).wait()

        for t in range(tiles):
            at = pl.ds(pl.multiple_of(block * rows + t * CHUNK, CHUNK), CHUNK)
            queries = query_v[at, cols]
            col = lax.broadcasted_iota(jnp.int32, (CHUNK, rows), 1)
            row = lax.broadcasted_iota(jnp.int32, (CHUNK, rows), 0) + t * CHUNK
            first = dot_right_t(queries, key_v[prefix_at, cols]) * scale
            second = dot_right_t(queries, key_v[own_at, cols]) * scale
            first = jnp.where(col < prefix_live, first, NEG_FILL)
            second = jnp.where(
                jnp.logical_and(col <= row, col < own_live), second, NEG_FILL
            )
            peak = jnp.maximum(
                jnp.max(first, axis=-1, keepdims=True), jnp.max(second, axis=-1, keepdims=True)
            )
            first = jnp.exp(first - peak)
            second = jnp.exp(second - peak)
            total = jnp.sum(first, axis=-1, keepdims=True) + jnp.sum(
                second, axis=-1, keepdims=True
            )
            inverse = 1.0 / total
            first = (first * inverse).astype(LOW)
            second = (second * inverse).astype(LOW)
            probs_v[unit % 2, pl.ds(t * CHUNK, CHUNK), pl.ds(0, rows)] = first
            probs_v[unit % 2, pl.ds(t * CHUNK, CHUNK), pl.ds(rows, rows)] = second
            mixed_v[at, cols] = (
                dot_plain(first, value_v[prefix_at, cols])
                + dot_plain(second, value_v[own_at, cols])
            ).astype(LOW)
        probs_copy(unit).start()

    units = 2 * local_heads
    for quarter in range(4):
        pl.loop(quarter * units // 4, (quarter + 1) * units // 4)(attend)
        pump_to(2 * far + (2, 3, 4, 4)[quarter])
    for unit in (units - 2, units - 1):
        probs_copy(unit).wait()
    store(mixed_v, mixed_out)

    out_cols = slice(3 * head_cols, 4 * head_cols)

    def core_copy(t):
        at = pl.ds(t * CHUNK, CHUNK)
        return remote(
            core_send_v.at[at], core_recv_v.at[at], sum_send.at[0, t], sum_recv.at[0, t], here.sibling
        )

    def cross_copy(t):
        at = pl.ds(t * CHUNK, CHUNK)
        return remote(
            cross_send_v.at[at], cross_recv_v.at[at], sum_send.at[1, t], sum_recv.at[1, t], here.across
        )

    def two_copy(t):
        return remote(
            normed_two_v.at[pl.ds(t * CHUNK, CHUNK)],
            normed_two_v.at[pl.ds(rows + t * CHUNK, CHUNK)],
            sum_send.at[2, t],
            sum_recv.at[2, t],
            here.sibling,
        )

    def hidden_store(t):
        return pltpu.make_async_copy(
            hidden_v, hidden_out.at[pl.ds(t * CHUNK, CHUNK)], load_sem.at[1]
        )

    cot_own.wait()
    cot_pair.wait_send()
    for t in range(tiles):
        core_send_v[pl.ds(t * CHUNK, CHUNK), :] = dot_right_t(
            mixed_v[pl.ds(rows + t * CHUNK, CHUNK), :], w_v[:, out_cols]
        ).astype(LOW)
        core_copy(t).start()
    for t in range(tiles):
        at = pl.ds(t * CHUNK, CHUNK)
        partial = dot_right_t(mixed_v[at, :], w_v[:, out_cols])
        core_copy(t).wait_recv()
        cross_send_v[at, :] = (partial + core_recv_v[at, :].astype(WIDE)).astype(LOW)
        cross_copy(t).start()
    pump_to(4 * far)
    load_second = pltpu.make_async_copy(weights.at[1], w_v, load_sem.at[0])
    load_second.start()
    for t in range(tiles):
        at = pl.ds(t * CHUNK, CHUNK)
        if t > 0:
            pump_to(4 * far + 2)
        cross_copy(t).wait_recv()
        hidden = (
            ordered(x_ref, at)
            + cross_send_v[at, :].astype(WIDE)
            + cross_recv_v[at, :].astype(WIDE)
        )
        if t > 0:
            hidden_store(t - 1).wait()
        hidden_v[...] = hidden
        hidden_store(t).start()
        normed_two_v[at, :] = norm_rows(hidden, gain_two, shift_two).astype(LOW)
        two_copy(t).start()
    hidden_store(tiles - 1).wait()
    load_second.wait()
    for t in range(tiles):
        two_copy(t).wait_recv()
    store(normed_two_v, normed_two_out)

    bend = math.sqrt(2.0 / math.pi)
    spans = ff // half

    def feed(i):
        at = row_tile(i // spans)
        cols = pl.ds(pl.multiple_of((i % spans) * half, half), half)
        bias_cols = pl.ds(pl.multiple_of(core * ff + (i % spans) * half, half), half)
        upward = dot_plain(normed_two_v[at, :], w_v[:, cols]) + up_bias_ref[:, bias_cols]
        square = upward * upward
        curve = jnp.tanh(bend * (upward + 0.044715 * (upward * square)))
        active_v[at, cols] = (0.5 * upward * (1.0 + curve)).astype(LOW)
        slope_v[at, cols] = (
            0.5 * (1.0 + curve)
            + 0.5 * upward * (1.0 - curve * curve) * (bend + (3.0 * 0.044715 * bend) * square)
        ).astype(LOW)

    for i in range(parts):

        @pl.when(here.z < sol_size - 1)
        def _():
            prefix_hop(i, False).wait_send()

        prefix_cross(i, False).wait_send()

    feeds = 2 * tiles * spans
    for quarter in range(4):
        pl.loop(quarter * feeds // 4, (quarter + 1) * feeds // 4)(feed)
        pump_to(4 * far + 3 + quarter)
    store(active_v, active_out)
    store(slope_v, slope_out)

    pump_to(len(steps))
    cot_pair.wait_recv()
    normed_pair.wait_send()
    prefix_pair.wait_send()
    for i in range(len(shards)):
        swap_copies(i)[1].wait_send()
    for step in steps:
        for i, copy in enumerate(hops(*step)):
            only_when(step[0], step[1], goes[i], copy.wait_send)
    for t in range(tiles):
        core_copy(t).wait_send()
        cross_copy(t).wait_send()
        two_copy(t).wait_send()
    for copy in stores:
        copy.wait()


def run_forward(dp_size, sol_size, x, vectors, live_rows, cot, matrices):
    rows, width = x.shape
    head_cols = matrices[0].shape[1] // 2
    ff = matrices[4].shape[1] // 2
    heads = head_cols // HEAD_DIM
    count = dp_size // 2 * sol_size
    far = count // 2

    def shape(*dims, dtype=LOW):
        return jax.ShapeDtypeStruct(dims, dtype)

    outs = [
        shape(3, width, width),
        shape(4 * rows, width),
        shape(2 * rows, width),
        shape(2 * rows, head_cols),
        shape(4 * rows, head_cols),
        shape(4 * rows, head_cols),
        shape(2 * heads, rows, 2 * rows),
        shape(2 * rows, head_cols),
        shape(rows, width, dtype=WIDE),
        shape(2 * rows, width),
        shape(2 * rows, ff),
        shape(2 * rows, ff),
    ]
    dma = pltpu.SemaphoreType.DMA
    return pl.pallas_call(
        functools.partial(forward_kernel, dp_size, sol_size),
        out_shape=outs,
        in_specs=[
            vmem_spec(),
            vmem_spec(),
            vmem_spec(),
            vmem_spec(),
            vmem_spec(),
            vmem_spec(),
            pl.BlockSpec(memory_space=pltpu.SMEM),
        ]
        + [any_spec()]
        + [vmem_spec()] * 6,
        out_specs=[any_spec()] * len(outs),
        scratch_shapes=[
            pltpu.VMEM((width, width), LOW),
            pltpu.VMEM((4 * rows, width), LOW),
            pltpu.VMEM((2 * rows, head_cols), LOW),
            pltpu.VMEM((4 * rows, head_cols), LOW),
            pltpu.VMEM((4 * rows, head_cols), LOW),
            pltpu.VMEM((2, rows, 2 * rows), LOW),
            pltpu.VMEM((2 * rows, head_cols), LOW),
            pltpu.VMEM((CHUNK, width), WIDE),
            pltpu.VMEM((2 * rows, width), LOW),
            pltpu.VMEM((2 * rows, ff), LOW),
            pltpu.VMEM((2 * rows, ff), LOW),
        ]
        + [pltpu.VMEM((rows, width), LOW)] * 4
        + [
            dma((3, 2, far, 2)),
            dma((3, 2, far, 2)),
            dma((6,)),
            dma((6,)),
            dma((6,)),
            dma((2, 4)),
            dma((2, 4)),
            dma((3,)),
            dma((3,)),
            dma((3, rows // CHUNK)),
            dma((3, rows // CHUNK)),
            dma((2,)),
            dma((2,)),
            dma((2,)),
            dma((16,)),
        ],
        compiler_params=pltpu.CompilerParams(
            collective_id=0, has_side_effects=True, vmem_limit_bytes=60 * 2**20
        ),
    )(x, *vectors, live_rows, cot, *matrices)


class RingSum:
    def __init__(self, here, chunk, send_v, recv_v, stage_v, sems, target, upward=False):
        self.here, self.chunk = here, chunk
        self.prepared = False
        self.upward = upward
        if upward:
            mine = here.up_ahead()
            self.sends = (mine, jnp.logical_not(mine))
            self.gets = (here.up_ahead(-1), jnp.logical_not(here.up_ahead(1)))
        self.send_v, self.recv_v, self.stage_v = send_v, recv_v, stage_v
        self.send_sem, self.recv_sem, self.end_sem = sems
        self.target = target
        self.far = here.count // 2
        self.cols = stage_v.shape[2]
        self.steps = [(t, sub) for t in range(1, self.far + 1) for sub in range(2)]
        self.done = 0

    def _class(self, sub):
        return self.here.core if sub == 0 else 1 - self.here.core

    def _columns(self, t, way):
        if t > 1 or self.upward:
            return pl.ds(0, self.cols)
        return pl.ds(way * (self.cols // 2), self.cols // 2)

    def _copy(self, t, way, sub):
        at = self._columns(t, way)
        return remote(
            self.send_v.at[way, sub, :, at],
            self.recv_v.at[(t - 1) % 3, way, sub, :, at],
            self.send_sem.at[t - 1, way, sub],
            self.recv_sem.at[t - 1, way, sub],
            self.here.prev if way else self.here.next,
        )

    def _event(self, t, sub):
        far, count = self.far, self.here.count
        half = self.cols // 2
        if t == 1 and self.upward:
            value = self.chunk(far, self._class(sub)).astype(LOW)
            for way in range(2):
                self.send_v[way, sub] = value
                pl.when(self.sends[way])(self._copy(1, way, sub).start)
            return
        if t == 1:
            value = self.chunk(far, self._class(sub))
            self.send_v[0, sub, :, :half] = value[:, :half].astype(LOW)
            self.send_v[1, sub, :, half:] = value[:, half:].astype(LOW)
            for way in range(2):
                self._copy(1, way, sub).start()
            return
        for way in range(2):
            j = far + 1 - t if way == 0 else count - (far + 1 - t)
            value = self.chunk(j, self._class(sub))
            if t == 2 and self.upward:
                pl.when(self.sends[way])(self._copy(1, way, sub).wait_send)
                pl.when(self.gets[way])(self._copy(1, way, sub).wait_recv)
                came = self.recv_v[0, way, sub].astype(WIDE)
                self.send_v[way, sub] = (
                    value + jnp.where(self.gets[way], came, 0.0)
                ).astype(LOW)
                self._copy(t, way, sub).start()
                continue
            self._copy(t - 1, way, sub).wait()
            if t == 2:
                near = slice(0, half) if way == 0 else slice(half, 2 * half)
                rest = slice(half, 2 * half) if way == 0 else slice(0, half)
                self.send_v[way, sub, :, near] = (
                    value[:, near] + self.recv_v[0, way, sub, :, near].astype(WIDE)
                ).astype(LOW)
                self.send_v[way, sub, :, rest] = value[:, rest].astype(LOW)
            else:
                self.send_v[way, sub] = (
                    value + self.recv_v[(t - 2) % 3, way, sub].astype(WIDE)
                ).astype(LOW)
            self._copy(t, way, sub).start()

    def prepare(self):
        for sub in range(2):
            self.stage_v[sub] = self.chunk(0, self._class(sub))
        self.prepared = True

    def _last(self, sub):
        for way in range(2):
            self._copy(self.far, way, sub).wait()
        value = self.stage_v[sub] + self.recv_v[(self.far - 1) % 3, 0, sub].astype(WIDE)
        self.stage_v[sub] = value + self.recv_v[(self.far - 1) % 3, 1, sub].astype(WIDE)
        for copy in self._results(sub):
            copy.start()

    def _results(self, sub):
        copies = []
        core = self.here.core
        for i, (ref, start, size) in enumerate(self.target):
            to = ref.at[:, pl.ds(pl.multiple_of(core * size, size), size)]
            source = self.stage_v.at[sub, :, pl.ds(start, size)]
            if sub == 0:
                copies.append(pltpu.make_async_copy(source, to, self.end_sem.at[0, i]))
            else:
                copies.append(
                    remote(
                        source, to, self.end_sem.at[1, i], self.end_sem.at[2, i], self.here.sibling
                    )
                )
        return copies

    def to(self, number):
        while self.done < min(number, len(self.steps) + 2):
            if self.done < len(self.steps):
                self._event(*self.steps[self.done])
            else:
                self._last(self.done - len(self.steps))
            self.done += 1

    def finish(self):
        self.to(len(self.steps) + 2)
        for sub in range(2):
            for copy in self._results(sub):
                copy.wait()


def ring_sum_scratch(far, shard, cols, results):
    dma = pltpu.SemaphoreType.DMA
    return [
        pltpu.VMEM((2, 2, shard, cols), LOW),
        pltpu.VMEM((3, 2, 2, shard, cols), LOW),
        pltpu.VMEM((2, shard, cols), WIDE),
        dma((far, 2, 2)),
        dma((far, 2, 2)),
        dma((3, results)),
    ]


def norm_back(values, gain, grad):
    row_mean = jnp.mean(values, axis=-1, keepdims=True)
    centered = values - row_mean
    variance = jnp.mean(centered * centered, axis=-1, keepdims=True)
    inverse = lax.rsqrt(variance + EPSILON)
    unit = centered * inverse
    scaled = grad * gain
    terms = grad * unit
    along = jnp.mean(scaled * unit, axis=-1, keepdims=True)
    level = jnp.mean(scaled, axis=-1, keepdims=True)
    return (
        (scaled - level - unit * along) * inverse,
        jnp.sum(terms, axis=0, keepdims=True),
        jnp.sum(grad, axis=0, keepdims=True),
    )


def tile_rows(t):
    return pl.ds(t * CHUNK, CHUNK)


def down_kernel(
    dp_size,
    sol_size,
    gain_ref,
    weights,
    cot_hbm,
    active_hbm,
    slope_hbm,
    hidden_hbm,
    grad_up_out,
    branch_out,
    grad_hidden_out,
    mlp_low_out,
    down_grad_out,
    sums_ref,
    cot_v,
    active_v,
    slope_v,
    down_v,
    up_v,
    hidden_v,
    core_send_v,
    core_recv_v,
    second_recv_v,
    cross_send_v,
    cross_recv_v,
    ring_send_v,
    ring_recv_v,
    stage_v,
    ring_send,
    ring_recv,
    ring_end,
    load_sem,
    store_sem,
    sum_send,
    sum_recv,
):
    here = Place(dp_size, sol_size)
    rows, width = core_send_v.shape
    shard = stage_v.shape[1]
    ff = active_v.shape[1]
    tiles = rows // CHUNK
    halves = (pl.ds(0, width // 2), pl.ds(width // 2, width // 2))
    def chunk(j, which):
        at = pl.ds(pl.multiple_of((2 * j + which) * shard, shard), shard)
        return dot_left_t(cot_v[:, at], active_v[...])

    ring = RingSum(
        here,
        chunk,
        ring_send_v,
        ring_recv_v,
        stage_v,
        (ring_send, ring_recv, ring_end),
        ((down_grad_out, 0, ff),),
    )
    loads = [
        pltpu.make_async_copy(src, dst, load_sem.at[i])
        for i, (src, dst) in enumerate(
            (
                (cot_hbm, cot_v),
                (active_hbm, active_v),
                (weights.at[2], down_v),
                (slope_hbm, slope_v),
                (weights.at[1], up_v),
            )
        )
    ]
    for copy in loads:
        copy.start()
    here.greet()

    loads[0].wait()
    loads[1].wait()
    ring.to(1)

    sums_ref[...] = jnp.zeros_like(sums_ref)
    spans = 2

    def back_feed(tile):
        at = pl.ds(tile * CHUNK, CHUNK)

        @pl.loop(0, spans)
        def _(i):
            cols = pl.ds(pl.multiple_of(i * (ff // spans), ff // spans), ff // spans)
            grad = dot_plain(cot_v[at, :], down_v[:, cols]) * slope_v[at, cols].astype(WIDE)
            low = grad.astype(LOW)
            slope_v[at, cols] = low
            sums_ref[3:4, cols] += jnp.sum(low.astype(WIDE), axis=0, keepdims=True)

    def core_copy(t):
        return remote(
            core_send_v.at[tile_rows(t)],
            core_recv_v.at[tile_rows(t)],
            sum_send.at[0, t],
            sum_recv.at[0, t],
            here.sibling,
        )

    def cross_copy(t):
        return remote(
            cross_send_v.at[tile_rows(t)],
            cross_recv_v.at[tile_rows(t)],
            sum_send.at[1, t],
            sum_recv.at[1, t],
            here.across,
        )

    def second_copy(t):
        return remote(
            core_send_v.at[tile_rows(t)],
            second_recv_v.at[tile_rows(t)],
            sum_send.at[2, t],
            sum_recv.at[2, t],
            here.sibling,
        )

    def branch_copy(t):
        return remote(
            core_recv_v.at[tile_rows(t)],
            branch_out.at[pl.ds(rows + t * CHUNK, CHUNK)],
            sum_send.at[3, t],
            sum_recv.at[3, t],
            here.sibling,
        )

    def sibling_terms(t):
        for cols in halves:
            core_send_v[tile_rows(t), cols] = dot_right_t(
                slope_v[pl.ds(rows + t * CHUNK, CHUNK), :], up_v[cols, :]
            ).astype(LOW)
        core_copy(t).start()

    def own_terms(t):
        at = tile_rows(t)
        core_copy(t).wait_recv()
        for cols in halves:
            cross_send_v[at, cols] = (
                dot_right_t(slope_v[at, :], up_v[cols, :]) + core_recv_v[at, cols].astype(WIDE)
            ).astype(LOW)
        cross_copy(t).start()

    def sibling_output(t):
        core_copy(t).wait_send()
        for cols in halves:
            core_send_v[tile_rows(t), cols] = dot_right_t(
                active_v[pl.ds(rows + t * CHUNK, CHUNK), :], down_v[cols, :]
            ).astype(LOW)
        second_copy(t).start()

    def own_output(t):
        at = tile_rows(t)
        second_copy(t).wait_recv()
        for cols in halves:
            second_recv_v[at, cols] = (
                dot_right_t(active_v[at, :], down_v[cols, :])
                + second_recv_v[at, cols].astype(WIDE)
            ).astype(LOW)

    gain = read_ordered(gain_ref, pl.ds(0, 1), here.blocks(), shard)

    def hidden_load(t):
        return pltpu.make_async_copy(hidden_hbm.at[tile_rows(t)], hidden_v, load_sem.at[0])

    def hidden_store(t):
        return pltpu.make_async_copy(hidden_v, grad_hidden_out.at[tile_rows(t)], store_sem.at[2])

    def norm_tile(t):
        hidden_load(t).wait()
        cross_copy(t).wait_recv()
        for part in range(2):
            inner = pl.ds(part * (CHUNK // 2), CHUNK // 2)
            here_at = pl.ds(t * CHUNK + part * (CHUNK // 2), CHUNK // 2)
            grad = cross_send_v[here_at, :].astype(WIDE) + cross_recv_v[here_at, :].astype(WIDE)
            back, gain_terms, shift_terms = norm_back(hidden_v[inner, :], gain, grad)
            cot = cot_v[here_at, :].astype(WIDE)
            sums_ref[0:1, :] += gain_terms
            sums_ref[1:2, :] += shift_terms
            sums_ref[2:3, :] += jnp.sum(cot, axis=0, keepdims=True)
            back = back + cot
            hidden_v[inner, :] = back
            core_recv_v[here_at, :] = back.astype(LOW)
        branch_copy(t).start()
        hidden_store(t).start()

    stores = []

    def store(src, dst, i):
        copy = pltpu.make_async_copy(src, dst, store_sem.at[i])
        copy.start()
        stores.append(copy)

    loads[2].wait()
    loads[3].wait()
    ring.to(2)
    hidden_load(0).start()
    back_feed(0)
    ring.to(3)
    back_feed(tiles)
    loads[4].wait()
    sibling_terms(0)
    ring.to(4)
    own_terms(0)
    back_feed(1)
    ring.to(5)
    back_feed(tiles + 1)
    store(slope_v, grad_up_out, 0)
    sibling_terms(1)
    ring.to(6)
    own_terms(1)
    sibling_output(0)
    ring.to(7)
    own_output(0)
    sibling_output(1)
    ring.to(8)
    norm_tile(0)
    own_output(1)
    store(second_recv_v, mlp_low_out, 1)
    hidden_store(0).wait()
    hidden_load(1).start()
    ring.prepare()
    ring.to(9)
    norm_tile(1)
    store(core_recv_v, branch_out.at[pl.ds(0, rows)], 3)
    hidden_store(1).wait()
    ring.finish()
    for t in range(tiles):
        cross_copy(t).wait_send()
        second_copy(t).wait_send()
        branch_copy(t).wait()
    for copy in stores:
        copy.wait()


def run_down(
    dp_size, sol_size, shard, gain, weights, cot, active, slope, hidden
):
    rows, width = hidden.shape
    ff = active.shape[1]
    count = dp_size // 2 * sol_size
    tiles = rows // CHUNK
    dma = pltpu.SemaphoreType.DMA

    def shape(*dims, dtype=LOW):
        return jax.ShapeDtypeStruct(dims, dtype)

    outs = [
        shape(2 * rows, ff),
        shape(2 * rows, width),
        shape(rows, width, dtype=WIDE),
        shape(rows, width),
        shape(shard, 2 * ff, dtype=WIDE),
        shape(8, width, dtype=WIDE),
    ]
    return pl.pallas_call(
        functools.partial(down_kernel, dp_size, sol_size),
        out_shape=outs,
        in_specs=[vmem_spec()] + [any_spec()] * 5,
        out_specs=[any_spec()] * 5 + [vmem_spec()],
        scratch_shapes=[
            pltpu.VMEM((2 * rows, width), LOW),
            pltpu.VMEM((2 * rows, ff), LOW),
            pltpu.VMEM((2 * rows, ff), LOW),
            pltpu.VMEM((width, ff), LOW),
            pltpu.VMEM((width, ff), LOW),
            pltpu.VMEM((CHUNK, width), WIDE),
        ]
        + [pltpu.VMEM((rows, width), LOW)] * 5
        + ring_sum_scratch(count // 2, shard, ff, 1)
        + [
            dma((5,)),
            dma((6,)),
            dma((4, tiles)),
            dma((4, tiles)),
        ],
        compiler_params=pltpu.CompilerParams(
            collective_id=1, has_side_effects=True, vmem_limit_bytes=60 * 2**20
        ),
    )(gain, weights, cot, active, slope, hidden)


def read_ordered(ref, at, blocks, part):
    return jnp.concatenate(
        [ref[at, pl.ds(pl.multiple_of(b * part, part), part)] for b in blocks], axis=1
    ).astype(WIDE)


def write_ordered(ref, at, blocks, part, values):
    for j, b in enumerate(blocks):
        ref[at, pl.ds(pl.multiple_of(b * part, part), part)] = values[
            :, j * part : (j + 1) * part
        ].astype(ref.dtype)


def attend_back_kernel(
    dp_size,
    sol_size,
    bias_ref,
    weights,
    normed_two_hbm,
    grad_up_hbm,
    branch_hbm,
    query_hbm,
    key_hbm,
    value_hbm,
    probs_hbm,
    mlp_low_hbm,
    hidden_hbm,
    query_grad_out,
    kv_grad_out,
    own_low_out,
    prefix_half_out,
    up_grad_out,
    outputs_out,
    mlp_recv_out,
    normed_two_v,
    grad_up_v,
    branch_v,
    w_v,
    query_v,
    key_v,
    value_v,
    mixed_grad_v,
    probs_v,
    query_grad_v,
    kv_grad_v,
    core_recv_v,
    second_recv_v,
    half_recv_v,
    mlp_low_v,
    mlp_recv_v,
    hidden_v,
    ring_send_v,
    ring_recv_v,
    stage_v,
    ring_send,
    ring_recv,
    ring_end,
    load_sem,
    probs_sem,
    tile_sem,
    store_sem,
    sum_send,
    sum_recv,
    cross_send,
    cross_recv,
):
    here = Place(dp_size, sol_size)
    rows, width = core_recv_v.shape
    core_send_v = branch_v.at[pl.ds(0, rows)]
    half_send_v = branch_v.at[pl.ds(rows, CHUNK)]
    half_keep_v = branch_v.at[pl.ds(rows + CHUNK, CHUNK)]
    shard = stage_v.shape[1]
    ff = grad_up_v.shape[1]
    head_cols = query_v.shape[1]
    local_heads = head_cols // HEAD_DIM
    scale = 1.0 / math.sqrt(HEAD_DIM)
    tiles = rows // CHUNK
    blocks = here.blocks()
    halves = (pl.ds(0, width // 2), pl.ds(width // 2, width // 2))
    loads = [
        pltpu.make_async_copy(src, dst, load_sem.at[i])
        for i, (src, dst) in enumerate(
            (
                (normed_two_hbm, normed_two_v),
                (grad_up_hbm, grad_up_v),
                (branch_hbm, branch_v),
                (weights.at[0], w_v),
                (query_hbm, query_v),
                (key_hbm, key_v),
                (value_hbm, value_v),
            )
        )
    ]
    for copy in loads:
        copy.start()

    def probs_load(unit):
        return pltpu.make_async_copy(
            probs_hbm.at[unit], probs_v.at[unit % 2], probs_sem.at[unit % 2]
        )

    probs_load(0).start()
    here.greet()
    mlp_cross = remote(
        mlp_low_hbm, mlp_recv_out, cross_send.at[0], cross_recv.at[0], here.across
    )
    mlp_cross.start()

    def chunk(j, which):
        at = pl.ds(pl.multiple_of((2 * j + which) * shard, shard), shard)
        return dot_left_t(normed_two_v[:, at], grad_up_v[...])

    ring = RingSum(
        here,
        chunk,
        ring_send_v,
        ring_recv_v,
        stage_v,
        (ring_send, ring_recv, ring_end),
        ((up_grad_out, 0, ff),),
    )
    loads[0].wait()
    loads[1].wait()
    ring.to(2)
    loads[2].wait()
    loads[3].wait()

    @pl.loop(0, 2 * tiles)
    def _(t):
        at = pl.ds(pl.multiple_of(t * CHUNK, CHUNK), CHUNK)
        mixed_grad_v[at, :] = dot_plain(
            branch_v[at, :], w_v[:, 3 * head_cols : 4 * head_cols]
        ).astype(LOW)

    for i in range(4, 7):
        loads[i].wait()

    units = 2 * local_heads

    def back(unit):
        block, head = unit // local_heads, unit % local_heads
        cols = pl.ds(pl.multiple_of(head * HEAD_DIM, HEAD_DIM), HEAD_DIM)
        value_cols = pl.ds(
            pl.multiple_of(head_cols + head * HEAD_DIM, HEAD_DIM), HEAD_DIM
        )
        own_at = pl.ds(pl.multiple_of(block * rows, rows), rows)
        prefix_at = pl.ds(pl.multiple_of((2 + block) * rows, rows), rows)
        probs_load(unit).wait()

        @pl.when(unit + 1 < units)
        def _():
            probs_load(unit + 1).start()

        sums = None
        for t in range(tiles):
            at = pl.ds(pl.multiple_of(block * rows + t * CHUNK, CHUNK), CHUNK)
            grad = mixed_grad_v[at, cols]
            queries = query_v[at, cols]
            inner = pl.ds(t * CHUNK, CHUNK)
            first_low = probs_v[unit % 2, inner, pl.ds(0, rows)]
            second_low = probs_v[unit % 2, inner, pl.ds(rows, rows)]
            first, second = first_low.astype(WIDE), second_low.astype(WIDE)
            first_grad = dot_right_t(grad, value_v[prefix_at, cols])
            second_grad = dot_right_t(grad, value_v[own_at, cols])
            delta = jnp.sum(first * first_grad, axis=-1, keepdims=True) + jnp.sum(
                second * second_grad, axis=-1, keepdims=True
            )
            first_scores = (first * (first_grad - delta)).astype(LOW)
            second_scores = (second * (second_grad - delta)).astype(LOW)
            query_grad_v[at, cols] = (
                (
                    dot_plain(first_scores, key_v[prefix_at, cols])
                    + dot_plain(second_scores, key_v[own_at, cols])
                )
                * scale
            ).astype(LOW)
            terms = [
                dot_left_t(second_scores, queries),
                dot_left_t(second_low, grad),
                dot_left_t(first_scores, queries),
                dot_left_t(first_low, grad),
            ]
            sums = terms if sums is None else [a + b for a, b in zip(sums, terms)]
        kv_grad_v[own_at, cols] = (sums[0] * scale).astype(LOW)
        kv_grad_v[own_at, value_cols] = sums[1].astype(LOW)
        kv_grad_v[prefix_at, cols] = (sums[2] * scale).astype(LOW)
        kv_grad_v[prefix_at, value_cols] = sums[3].astype(LOW)

    for quarter in range(4):
        pl.loop(quarter * units // 4, (quarter + 1) * units // 4)(back)
        ring.to(3 + quarter)
    stores = []

    def store(src, dst):
        copy = pltpu.make_async_copy(src, dst, store_sem.at[len(stores)])
        copy.start()
        stores.append(copy)

    store(query_grad_v, query_grad_out)
    store(kv_grad_v, kv_grad_out)

    def core_copy(t):
        return remote(
            core_send_v.at[tile_rows(t)],
            core_recv_v.at[tile_rows(t)],
            sum_send.at[0, t],
            sum_recv.at[0, t],
            here.sibling,
        )

    def second_copy(t):
        return remote(
            core_send_v.at[tile_rows(t)],
            second_recv_v.at[tile_rows(t)],
            sum_send.at[1, t],
            sum_recv.at[1, t],
            here.sibling,
        )

    half_copy = remote(half_send_v, half_recv_v, cross_send.at[1], cross_recv.at[1], here.across)
    kv_cols = pl.ds(head_cols, 2 * head_cols)

    def prefix_terms(at, cols):
        return dot_right_t(kv_grad_v[at, :], w_v[cols, kv_cols])

    for t in range(tiles):
        for cols in halves:
            core_send_v[tile_rows(t), cols] = prefix_terms(
                pl.ds(3 * rows + t * CHUNK, CHUNK), cols
            ).astype(LOW)
        second_copy(t).start()
    for t in range(tiles):
        second_copy(t).wait_recv()
    for keep in range(2):
        which = here.y if keep else 1 - here.y
        at = pl.ds(pl.multiple_of(2 * rows + which * CHUNK, CHUNK), CHUNK)
        came = pl.ds(pl.multiple_of(which * CHUNK, CHUNK), CHUNK)
        for cols in halves:
            value = prefix_terms(at, cols) + second_recv_v[came, cols].astype(WIDE)
            if keep:
                half_keep_v[:, cols] = value.astype(LOW)
            else:
                half_send_v[:, cols] = value.astype(LOW)
        if not keep:
            half_copy.start()
    ring.to(7)

    def own_terms(at, cols):
        return dot_right_t(query_grad_v[at, :], w_v[cols, 0:head_cols]) + dot_right_t(
            kv_grad_v[at, :], w_v[cols, kv_cols]
        )

    for t in range(tiles):
        second_copy(t).wait_send()
        for cols in halves:
            core_send_v[tile_rows(t), cols] = own_terms(
                pl.ds(rows + t * CHUNK, CHUNK), cols
            ).astype(LOW)
        core_copy(t).start()
    for t in range(tiles):
        at = tile_rows(t)
        core_copy(t).wait_recv()
        for cols in halves:
            core_recv_v[at, cols] = (
                own_terms(at, cols) + core_recv_v[at, cols].astype(WIDE)
            ).astype(LOW)
    store(core_recv_v, own_low_out)
    ring.to(8)
    ring.prepare()

    half_copy.wait()
    write_ordered(
        half_send_v,
        slice(None),
        blocks,
        shard,
        half_keep_v[...].astype(WIDE) + half_recv_v[...].astype(WIDE),
    )
    store(half_send_v, prefix_half_out)

    bias = read_ordered(bias_ref, pl.ds(0, 1), blocks, shard)
    small = mlp_low_v.shape[0]
    pieces = rows // small

    def piece_rows(t):
        return pl.ds(t * small, small)

    def tile_loads(t):
        return (
            pltpu.make_async_copy(hidden_hbm.at[piece_rows(t)], hidden_v, tile_sem.at[0]),
            pltpu.make_async_copy(mlp_low_hbm.at[piece_rows(t)], mlp_low_v, tile_sem.at[1]),
            pltpu.make_async_copy(mlp_recv_out.at[piece_rows(t)], mlp_recv_v, tile_sem.at[2]),
        )

    def tile_store(t):
        return pltpu.make_async_copy(
            half_keep_v.at[pl.ds(t % 2 * small, small)],
            outputs_out.at[piece_rows(t)],
            tile_sem.at[3 + t % 2],
        )

    mlp_cross.wait()
    for copy in tile_loads(0):
        copy.start()
    for t in range(pieces):
        for copy in tile_loads(t):
            copy.wait()
        value = (
            hidden_v[...]
            + mlp_low_v[...].astype(WIDE)
            + mlp_recv_v[...].astype(WIDE)
            + bias
        )
        if t > 1:
            tile_store(t - 2).wait()
        write_ordered(half_keep_v, pl.ds(t % 2 * small, small), blocks, shard, value)
        tile_store(t).start()
        if t + 1 < pieces:
            for copy in tile_loads(t + 1):
                copy.start()
    for t in (pieces - 2, pieces - 1):
        tile_store(t).wait()
    ring.finish()
    for t in range(tiles):
        core_copy(t).wait_send()
    for copy in stores:
        copy.wait()


def run_attend_back(
    dp_size,
    sol_size,
    shard,
    bias,
    weights,
    normed_two,
    grad_up,
    branch,
    query_rows,
    key_rows,
    value_rows,
    probs,
    mlp_low,
    hidden,
):
    rows, width = hidden.shape
    ff = grad_up.shape[1]
    head_cols = query_rows.shape[1]
    count = dp_size // 2 * sol_size
    tiles = rows // CHUNK
    dma = pltpu.SemaphoreType.DMA

    def shape(*dims, dtype=LOW):
        return jax.ShapeDtypeStruct(dims, dtype)

    def low(*dims):
        return pltpu.VMEM(dims, LOW)

    outs = [
        shape(2 * rows, head_cols),
        shape(4 * rows, 2 * head_cols),
        shape(rows, width),
        shape(rows // 2, width),
        shape(shard, 2 * ff, dtype=WIDE),
        shape(rows, width),
        shape(rows, width),
    ]
    return pl.pallas_call(
        functools.partial(attend_back_kernel, dp_size, sol_size),
        out_shape=outs,
        in_specs=[vmem_spec()] + [any_spec()] * 10,
        out_specs=[any_spec()] * len(outs),
        scratch_shapes=[
            low(2 * rows, width),
            low(2 * rows, ff),
            low(2 * rows, width),
            low(width, width),
            low(2 * rows, head_cols),
            low(4 * rows, head_cols),
            low(4 * rows, head_cols),
            low(2 * rows, head_cols),
            low(2, rows, 2 * rows),
            low(2 * rows, head_cols),
            low(4 * rows, 2 * head_cols),
            low(rows, width),
            low(rows, width),
            low(CHUNK, width),
            low(CHUNK // 2, width),
            low(CHUNK // 2, width),
            pltpu.VMEM((CHUNK // 2, width), WIDE),
        ]
        + ring_sum_scratch(count // 2, shard, ff, 1)
        + [
            dma((7,)),
            dma((2,)),
            dma((5,)),
            dma((4,)),
            dma((2, tiles)),
            dma((2, tiles)),
            dma((2,)),
            dma((2,)),
        ],
        compiler_params=pltpu.CompilerParams(
            collective_id=2, has_side_effects=True, vmem_limit_bytes=60 * 2**20
        ),
    )(
        bias,
        weights,
        normed_two,
        grad_up,
        branch,
        query_rows,
        key_rows,
        value_rows,
        probs,
        mlp_low,
        hidden,
    )


def last_kernel(
    dp_size,
    sol_size,
    x_ref,
    gain_ref,
    early_ref,
    normed_hbm,
    branch_hbm,
    query_grad_hbm,
    kv_grad_hbm,
    mixed_hbm,
    own_low_hbm,
    prefix_half_hbm,
    grad_hidden_hbm,
    query_out,
    key_out,
    value_out,
    out_out,
    input_grad_out,
    sums_ref,
    normed_v,
    branch_v,
    query_grad_v,
    kv_grad_v,
    mixed_v,
    own_low_v,
    own_recv_v,
    half_v,
    half_recv_v,
    prefix_v,
    grad_hidden_v,
    out_v,
    table_v,
    table_recv_v,
    ring_send_v,
    ring_recv_v,
    stage_v,
    ring_send,
    ring_recv,
    ring_end,
    load_sem,
    tile_sem,
    cross_send,
    cross_recv,
    chain_send,
    chain_recv,
    table_send,
    table_recv,
):
    here = Place(dp_size, sol_size)
    rows, width = x_ref.shape
    shard = stage_v.shape[1]
    head_cols = query_grad_v.shape[1]
    tiles = rows // CHUNK
    blocks = here.blocks()
    loads = [
        pltpu.make_async_copy(src, dst, load_sem.at[i])
        for i, (src, dst) in enumerate(
            (
                (query_grad_hbm, query_grad_v),
                (kv_grad_hbm, kv_grad_v),
                (mixed_hbm, mixed_v),
                (prefix_half_hbm, half_v),
                (normed_hbm, normed_v),
                (branch_hbm, branch_v),
                (own_low_hbm, own_low_v),
            )
        )
    ]
    for copy in loads:
        copy.start()
    partners = here.partners()
    here.greet(partners[1:])
    own_cross = remote(own_low_hbm, own_recv_v, cross_send.at[0], cross_recv.at[0], here.across)
    own_cross.start()

    def chunk(j, which):
        at = pl.ds(pl.multiple_of((2 * j + which) * shard, shard), shard)
        return jnp.concatenate(
            [
                dot_left_t(normed_v[: 2 * rows, at], query_grad_v[...]),
                dot_left_t(normed_v[:, at], kv_grad_v[...]),
                dot_left_t(branch_v[:, at], mixed_v[...]),
            ],
            axis=1,
        )

    ring = RingSum(
        here,
        chunk,
        ring_send_v,
        ring_recv_v,
        stage_v,
        (ring_send, ring_recv, ring_end),
        tuple(
            (ref, i * head_cols, head_cols)
            for i, ref in enumerate((query_out, key_out, value_out, out_out))
        ),
        upward=True,
    )

    parts = chain_send.shape[0]
    part = CHUNK // parts

    def chain_copy(i):
        at = pl.ds(i * part, part)
        return remote(
            half_v.at[at], half_recv_v.at[at], chain_send.at[i], chain_recv.at[i], here.along(-1)
        )

    def mine(i):
        return pl.ds(pl.multiple_of(here.y * CHUNK + i * part, part), part)

    def half_cross(i):
        return remote(
            half_recv_v.at[pl.ds(i * part, part)],
            prefix_v.at[mine(i)],
            cross_send.at[1 + i],
            cross_recv.at[1 + i],
            here.across,
        )

    def chain(stage, i):
        at = pl.ds(i * part, part)

        @pl.when(here.z == stage)
        def _():
            if stage < sol_size - 1:
                chain_copy(i).wait_recv()
            if 0 < stage < sol_size - 1:
                half_v[at, :] = (
                    half_v[at, :].astype(WIDE) + half_recv_v[at, :].astype(WIDE)
                ).astype(LOW)
            if stage > 0:
                chain_copy(i).start()
            else:
                half_cross(i).start()
                prefix_v[mine(i), :] = half_recv_v[at, :]

    loads[3].wait()
    for i in range(parts):
        chain(sol_size - 1, i)

    @pl.when(here.z > 0)
    def _():
        prefix_v[...] = jnp.zeros_like(prefix_v)

    for i in (0, 1, 2, 4, 5):
        loads[i].wait()
    ring.to(2)
    for step in range(1, sol_size + parts - 1):
        for i in range(parts):
            if 1 <= step - i < sol_size:
                chain(sol_size - 1 - (step - i), i)
        ring.to(1 + step)
        if step == 4:
            ring.prepare()

    loads[6].wait()
    own_cross.wait()

    @pl.when(here.z == 0)
    def _():
        for i in range(parts):
            half_cross(i).wait()

    gain = read_ordered(gain_ref, pl.ds(0, 1), blocks, shard)

    def tile_load(t):
        return pltpu.make_async_copy(
            grad_hidden_hbm.at[tile_rows(t)], grad_hidden_v, tile_sem.at[0]
        )

    def tile_store(t):
        return pltpu.make_async_copy(out_v, input_grad_out.at[tile_rows(t)], tile_sem.at[1])

    tile_load(0).start()
    totals = [jnp.zeros((1, width), WIDE)] * 2
    small = CHUNK // 2
    for t in range(tiles):
        tile_load(t).wait()
        if t > 0:
            tile_store(t - 1).wait()
        for piece in range(2):
            at = pl.ds(t * CHUNK + piece * small, small)
            inner = pl.ds(piece * small, small)
            grad = (
                own_low_v[at, :].astype(WIDE)
                + own_recv_v[at, :].astype(WIDE)
                + read_ordered(prefix_v, at, blocks, shard)
            )
            back, gain_terms, shift_terms = norm_back(
                read_ordered(x_ref, at, blocks, shard), gain, grad
            )
            totals = [totals[0] + gain_terms, totals[1] + shift_terms]
            write_ordered(out_v, inner, blocks, shard, back + grad_hidden_v[inner, :])
        tile_store(t).start()
        if t + 1 < tiles:
            tile_load(t + 1).start()

    for row in range(2):
        write_ordered(table_v.at[0], pl.ds(row, 1), blocks, shard, totals[row])
    for row in range(3):
        write_ordered(
            table_v.at[0], pl.ds(2 + row, 1), blocks, shard, early_ref[row : row + 1, :]
        )
    bias = early_ref[3:4, :]
    table_v[0, 5:6, :] = jnp.where(here.core == 0, bias, 0.0)
    table_v[0, 6:7, :] = jnp.where(here.core == 0, 0.0, bias)
    table_v[0, 7:8, :] = jnp.zeros((1, width), WIDE)

    def table_copy(k):
        return remote(
            table_v.at[k], table_recv_v.at[k], table_send.at[k], table_recv.at[k], partners[k]
        )

    for k in range(len(partners)):
        table_copy(k).start()
        ring.to(9 + k)
        table_copy(k).wait_recv()
        if k + 1 < len(partners):
            table_v[k + 1] = table_v[k] + table_recv_v[k]
        else:
            sums_ref[...] = table_v[k] + table_recv_v[k]
    tile_store(tiles - 1).wait()
    ring.finish()
    for k in range(len(partners)):
        table_copy(k).wait_send()
    for i in range(parts):

        @pl.when(here.z > 0)
        def _():
            chain_copy(i).wait_send()


def run_last(
    dp_size,
    sol_size,
    shard,
    x,
    gain,
    early,
    normed,
    branch,
    query_grad,
    kv_grad,
    mixed,
    own_low,
    prefix_half,
    grad_hidden,
):
    rows, width = x.shape
    head_cols = query_grad.shape[1]
    count = dp_size // 2 * sol_size
    bits = (dp_size * sol_size).bit_length() - 1
    dma = pltpu.SemaphoreType.DMA

    def shape(*dims, dtype=LOW):
        return jax.ShapeDtypeStruct(dims, dtype)

    def low(*dims):
        return pltpu.VMEM(dims, LOW)

    outs = [shape(shard, 2 * head_cols, dtype=WIDE)] * 4 + [
        shape(rows, width),
        shape(8, width, dtype=WIDE),
    ]
    return pl.pallas_call(
        functools.partial(last_kernel, dp_size, sol_size),
        out_shape=outs,
        in_specs=[vmem_spec()] * 3 + [any_spec()] * 8,
        out_specs=[any_spec()] * 5 + [vmem_spec()],
        scratch_shapes=[
            low(4 * rows, width),
            low(2 * rows, width),
            low(2 * rows, head_cols),
            low(4 * rows, 2 * head_cols),
            low(2 * rows, head_cols),
            low(rows, width),
            low(rows, width),
            low(CHUNK, width),
            low(CHUNK, width),
            low(rows, width),
            pltpu.VMEM((CHUNK, width), WIDE),
            low(CHUNK, width),
            pltpu.VMEM((bits, 8, width), WIDE),
            pltpu.VMEM((bits, 8, width), WIDE),
        ]
        + ring_sum_scratch(count // 2, shard, 4 * head_cols, 4)
        + [
            dma((7,)),
            dma((2,)),
            dma((5,)),
            dma((5,)),
            dma((4,)),
            dma((4,)),
            dma((bits,)),
            dma((bits,)),
        ],
        compiler_params=pltpu.CompilerParams(
            collective_id=3, has_side_effects=True, vmem_limit_bytes=60 * 2**20
        ),
    )(
        x,
        gain,
        early,
        normed,
        branch,
        query_grad,
        kv_grad,
        mixed,
        own_low,
        prefix_half,
        grad_hidden,
    )


def finish_kernel(*refs):
    count = (len(refs) - 2) // 3
    ins, outs, rooms = refs[:count], refs[count : 2 * count], refs[2 * count : 3 * count]
    in_sem, out_sem = refs[3 * count :]
    loads = [
        pltpu.make_async_copy(src, room, in_sem.at[i])
        for i, (src, room) in enumerate(zip(ins, rooms))
    ]
    stores = [
        pltpu.make_async_copy(room, dst, out_sem.at[i])
        for i, (room, dst) in enumerate(zip(rooms, outs))
    ]
    for copy in loads:
        copy.start()
    for load, store in zip(loads, stores):
        load.wait()
        store.start()
    for copy in stores:
        copy.wait()


def run_finish(arrays):
    dma = pltpu.SemaphoreType.DMA
    return pl.pallas_call(
        finish_kernel,
        out_shape=[jax.ShapeDtypeStruct(a.shape, a.dtype) for a in arrays],
        in_specs=[any_spec()] * len(arrays),
        out_specs=[any_spec()] * len(arrays),
        scratch_shapes=[pltpu.VMEM(a.shape, a.dtype) for a in arrays]
        + [dma((len(arrays),)), dma((len(arrays),))],
        compiler_params=pltpu.CompilerParams(vmem_limit_bytes=60 * 2**20),
    )(*arrays)


def ring_program(
    inputs,
    cotangent,
    attn_gain,
    attn_shift,
    query_weight,
    key_weight,
    value_weight,
    out_weight,
    mlp_gain,
    mlp_shift,
    up_weight,
    up_bias,
    down_weight,
    down_bias,
    live_rows,
):
    block_rows, width = inputs.shape
    shard_rows = query_weight.shape[0]
    head_cols = query_weight.shape[1] // 2
    ff_cols = up_weight.shape[1] // 2
    ff_part = ff_cols // 2
    local_heads = head_cols // HEAD_DIM
    score_scale = 1.0 / math.sqrt(HEAD_DIM)
    dp_size, sol_size = lax.axis_size("dp"), lax.axis_size("sol")
    count, ahead, back, cores = ring_pairs(dp_size, sol_size)
    dp_place, sol_place = lax.axis_index("dp"), lax.axis_index("sol")
    x_place, core = dp_place // 2, dp_place % 2
    first_core = core == 0
    along = jnp.where(x_place % 2 == 0, sol_place, sol_size - 1 - sol_place)
    ring_here = x_place * sol_size + along

    order_list = []
    for j in range(count):
        q = (ring_here + j) % count
        qx, qa = q // sol_size, q % sol_size
        qz = jnp.where(qx % 2 == 0, qa, sol_size - 1 - qa)
        order_list += [(qx * 2) * sol_size + qz, (qx * 2 + 1) * sol_size + qz]
    order = jnp.stack(order_list).astype(jnp.int32)
    back_order = jnp.argsort(order).astype(jnp.int32)

    def to_core(value):
        return lax.ppermute(value, ROWS_AXES, cores)

    def to_tensor(value):
        return lax.ppermute(value, "tensor", [(0, 1), (1, 0)])

    def reorder_vector(vector, by):
        return jnp.take(vector.reshape(by.shape[0], -1), by, axis=0).reshape(vector.shape)

    def gather_ring(piece, flip):
        hops_ahead = count // 2 - (1 if flip else 0)
        hops_back = count - 1 - hops_ahead
        got = {0: piece}
        moving_a, moving_b = piece, piece
        for k in range(1, count // 2 + 1):
            if k <= hops_ahead:
                moving_a = lax.ppermute(moving_a, ROWS_AXES, ahead)
                got[count - k] = moving_a
            if k <= hops_back:
                moving_b = lax.ppermute(moving_b, ROWS_AXES, back)
                got[k] = moving_b
        return jnp.concatenate([got[j] for j in range(count)], axis=0)

    def scatter_ring(chunk, flip):
        hops_ahead = count // 2 - (1 if flip else 0)
        hops_back = count - 1 - hops_ahead
        carried_a = carried_b = None
        for k in range(count // 2, 0, -1):
            if k <= hops_ahead:
                value = chunk(k)
                if carried_a is not None:
                    value = value + carried_a.astype(WIDE)
                carried_a = lax.ppermute(value.astype(LOW), ROWS_AXES, ahead)
            if k <= hops_back:
                value = chunk(count - k)
                if carried_b is not None:
                    value = value + carried_b.astype(WIDE)
                carried_b = lax.ppermute(value.astype(LOW), ROWS_AXES, back)
        return chunk(0) + carried_a.astype(WIDE) + carried_b.astype(WIDE)

    def own_part(shards):
        firsts, seconds = [], []
        for shard, start, size in shards:
            half = shard.shape[1] // 2
            firsts.append(shard[:, start : start + size])
            seconds.append(shard[:, half + start : half + start + size])
        low_half = jnp.concatenate(firsts, axis=1) if len(firsts) > 1 else firsts[0]
        high_half = jnp.concatenate(seconds, axis=1) if len(seconds) > 1 else seconds[0]
        mine = jnp.where(first_core, low_half, high_half)
        other = to_core(jnp.where(first_core, high_half, low_half))
        return jnp.concatenate(
            [jnp.where(first_core, mine, other), jnp.where(first_core, other, mine)], axis=0
        )

    def split_rows(full):
        upper, lower = full[:shard_rows], full[shard_rows:]
        mine = jnp.where(first_core, upper, lower)
        other = to_core(jnp.where(first_core, lower, upper))
        return jnp.where(first_core, mine, other), jnp.where(first_core, other, mine)

    def sum_partials(partial):
        mine = partial[:block_rows] + to_core(partial[block_rows:].astype(LOW)).astype(WIDE)
        low = mine.astype(LOW)
        return low.astype(WIDE) + to_tensor(low).astype(WIDE)

    def pair_rows(own):
        return jnp.concatenate([own, to_core(own)], axis=0)

    qk_piece = own_part([(query_weight, 0, head_cols), (key_weight, 0, head_cols)])
    vo_piece = own_part([(value_weight, 0, head_cols), (out_weight, 0, head_cols)])
    up_pieces = [own_part([(up_weight, s, ff_part)]) for s in (0, ff_part)]
    down_pieces = [own_part([(down_weight, s, ff_part)]) for s in (0, ff_part)]
    qk_full = gather_ring(qk_piece, False)
    vo_full = gather_ring(vo_piece, True)
    up_full = [gather_ring(up_pieces[0], False), gather_ring(up_pieces[1], True)]
    down_full = [gather_ring(down_pieces[0], False), gather_ring(down_pieces[1], True)]
    query_full, key_full = qk_full[:, :head_cols], qk_full[:, head_cols:]
    value_full, out_full = vo_full[:, :head_cols], vo_full[:, head_cols:]

    tensor_place = lax.axis_index("tensor")
    half_rows = block_rows // 2
    half = jnp.where(tensor_place == 0, inputs[:half_rows], inputs[half_rows:])
    prefix_half = half
    hop = half
    for k in range(1, sol_size):
        hop = lax.ppermute(hop, "sol", [(k - 1, k)])
        prefix_half = jnp.where(sol_place == k, hop, prefix_half)
    other_half = to_tensor(prefix_half)
    prefix_inputs = jnp.concatenate(
        [
            jnp.where(tensor_place == 0, prefix_half, other_half),
            jnp.where(tensor_place == 0, other_half, prefix_half),
        ],
        axis=0,
    )

    own_low = reorder(inputs, order)
    prefix_low = reorder(prefix_inputs, order)
    cot_low = reorder(cotangent, order)
    attn_gain_o, attn_shift_o, mlp_gain_o, mlp_shift_o, down_bias_o = [
        reorder_vector(v, order) for v in (attn_gain, attn_shift, mlp_gain, mlp_shift, down_bias)
    ]
    up_bias_c = jnp.where(first_core, up_bias[:ff_cols], up_bias[ff_cols:])
    up_bias_parts = [up_bias_c[:ff_part], up_bias_c[ff_part:]]

    features = own_low.astype(WIDE)
    normed = pair_rows(layer_norm(features, attn_gain_o, attn_shift_o).astype(LOW))
    normed_prefix = pair_rows(
        layer_norm(prefix_low.astype(WIDE), attn_gain_o, attn_shift_o).astype(LOW)
    )
    cot_pair = pair_rows(cot_low)

    query_rows = dot_plain(normed, query_full).astype(LOW)
    key_rows = dot_plain(normed, key_full).astype(LOW)
    value_rows = dot_plain(normed, value_full).astype(LOW)
    key_prefix = dot_plain(normed_prefix, key_full).astype(LOW)
    value_prefix = dot_plain(normed_prefix, value_full).astype(LOW)

    def heads_of(rows):
        return rows.reshape(2, -1, local_heads, HEAD_DIM)

    head_queries = heads_of(query_rows)
    all_keys = jnp.concatenate([heads_of(key_prefix), heads_of(key_rows)], axis=1)
    all_values = jnp.concatenate([heads_of(value_prefix), heads_of(value_rows)], axis=1)

    row_ids = jnp.arange(block_rows)[:, None]
    col_ids = jnp.arange(block_rows)[None, :]
    masks = []
    for place in (dp_place, dp_place + 1 - 2 * core):
        own_live = live_rows[place * sol_size + sol_place]
        prefix_live = live_rows[place * sol_size]
        prefix_ok = jnp.logical_and(col_ids < prefix_live, sol_place != 0)
        own_ok = jnp.logical_and(col_ids <= row_ids, col_ids < own_live)
        masks.append(
            jnp.concatenate(
                [jnp.broadcast_to(prefix_ok, (block_rows, block_rows)), own_ok], axis=1
            )
        )
    allowed = jnp.stack(masks)[:, None]

    def masked_scores():
        raw = jnp.einsum("bqhd,bkhd->bhqk", head_queries, all_keys, preferred_element_type=WIDE)
        return jnp.where(allowed, raw * score_scale, NEG_FILL)

    scores = masked_scores()
    row_peak = jnp.max(scores, axis=-1, keepdims=True)
    exp_scores = jnp.exp(scores - row_peak)
    totals = jnp.sum(exp_scores, axis=-1, keepdims=True)
    attn_probs = exp_scores / totals
    log_total = row_peak + jnp.log(totals)
    mixed = jnp.einsum(
        "bhqk,bkhd->bqhd", attn_probs.astype(LOW), all_values, preferred_element_type=WIDE
    )
    mixed_low = mixed.reshape(2 * block_rows, head_cols).astype(LOW)

    hidden = features + sum_partials(dot_right_t(mixed_low, out_full))
    normed_two = pair_rows(layer_norm(hidden, mlp_gain_o, mlp_shift_o).astype(LOW))
    upward = [dot_plain(normed_two, up_full[i]) + up_bias_parts[i] for i in range(2)]
    active = [gelu_tanh(u).astype(LOW) for u in upward]
    down_grads = [
        scatter_ring(
            lambda j, i=i: dot_left_t(
                cot_pair[:, j * 2 * shard_rows : (j + 1) * 2 * shard_rows], active[i]
            ),
            i == 1,
        )
        for i in range(2)
    ]
    grad_up = []
    for i in range(2):
        grad_active = dot_plain(cot_pair, down_full[i])
        unused_gelu, gelu_pull = jax.vjp(gelu_tanh, upward[i])
        grad_up.append(gelu_pull(grad_active)[0].astype(LOW))
    grad_normed_two = sum_partials(
        dot_right_t(grad_up[0], up_full[0]) + dot_right_t(grad_up[1], up_full[1])
    )
    up_grads = [
        scatter_ring(
            lambda j, i=i: dot_left_t(
                normed_two[:, j * 2 * shard_rows : (j + 1) * 2 * shard_rows], grad_up[i]
            ),
            i == 1,
        )
        for i in range(2)
    ]
    mlp_total = sum_partials(
        dot_right_t(active[0], down_full[0]) + dot_right_t(active[1], down_full[1])
    )
    outputs = reorder((hidden + mlp_total + down_bias_o).astype(LOW), back_order)

    grad_out = cot_low.astype(WIDE)
    down_bias_grad = jnp.sum(grad_out, axis=0)
    grad_hidden_norm, mlp_gain_grad, mlp_shift_grad = layer_norm_back(
        hidden, mlp_gain_o, grad_normed_two
    )
    grad_hidden = grad_out + grad_hidden_norm
    grad_branch = pair_rows(grad_hidden.astype(LOW))
    grad_mixed_low = dot_plain(grad_branch, out_full).astype(LOW)

    grad_head_mixed = heads_of(grad_mixed_low)
    attn_probs = jnp.exp(masked_scores() - log_total)
    grad_probs = jnp.einsum(
        "bqhd,bkhd->bhqk", grad_head_mixed, all_values, preferred_element_type=WIDE
    )
    row_delta = jnp.sum(attn_probs * grad_probs, axis=-1, keepdims=True)
    grad_scores = (attn_probs * (grad_probs - row_delta)).astype(LOW)
    grad_queries = (
        jnp.einsum("bhqk,bkhd->bqhd", grad_scores, all_keys, preferred_element_type=WIDE)
        * score_scale
    )
    grad_keys = (
        jnp.einsum("bhqk,bqhd->bkhd", grad_scores, head_queries, preferred_element_type=WIDE)
        * score_scale
    )
    grad_values = jnp.einsum(
        "bhqk,bqhd->bkhd", attn_probs.astype(LOW), grad_head_mixed, preferred_element_type=WIDE
    )

    def rows_of(heads):
        return heads.reshape(2 * block_rows, head_cols).astype(LOW)

    query_grad_low = rows_of(grad_queries)
    key_own = rows_of(grad_keys[:, block_rows:])
    value_own = rows_of(grad_values[:, block_rows:])
    key_pre = rows_of(grad_keys[:, :block_rows])
    value_pre = rows_of(grad_values[:, :block_rows])

    kv_pre = jnp.concatenate([key_pre, value_pre], axis=1)
    carried = kv_pre
    for k in range(sol_size - 1, 0, -1):
        came = lax.ppermute(carried, "sol", [(k, k - 1)])
        if k > 1:
            carried = (kv_pre.astype(WIDE) + came.astype(WIDE)).astype(LOW)
    key_all = (key_own.astype(WIDE) + came[:, :head_cols].astype(WIDE)).astype(LOW)
    value_all = (value_own.astype(WIDE) + came[:, head_cols:].astype(WIDE)).astype(LOW)

    normed_all = jnp.concatenate([normed, normed_prefix], axis=0)
    key_rows_grad = jnp.concatenate([key_own, key_pre], axis=0)
    value_rows_grad = jnp.concatenate([value_own, value_pre], axis=0)

    def qk_chunk(j):
        at = slice(j * 2 * shard_rows, (j + 1) * 2 * shard_rows)
        return jnp.concatenate(
            [
                dot_left_t(normed[:, at], query_grad_low),
                dot_left_t(normed_all[:, at], key_rows_grad),
            ],
            axis=1,
        )

    def vo_chunk(j):
        at = slice(j * 2 * shard_rows, (j + 1) * 2 * shard_rows)
        return jnp.concatenate(
            [
                dot_left_t(normed_all[:, at], value_rows_grad),
                dot_left_t(grad_branch[:, at], mixed_low),
            ],
            axis=1,
        )

    qk_grad = scatter_ring(qk_chunk, False)
    vo_grad = scatter_ring(vo_chunk, True)

    grad_normed = sum_partials(
        dot_right_t(query_grad_low, query_full)
        + dot_right_t(key_all, key_full)
        + dot_right_t(value_all, value_full)
    )
    grad_features, attn_gain_grad, attn_shift_grad = layer_norm_back(
        features, attn_gain_o, grad_normed
    )
    input_grad = reorder((grad_hidden + grad_features).astype(LOW), back_order)

    up_bias_grad = jnp.concatenate([jnp.sum(g.astype(WIDE), axis=0) for g in grad_up])
    up_bias_both = jnp.concatenate(
        [
            jnp.where(first_core, up_bias_grad, 0.0),
            jnp.where(first_core, 0.0, up_bias_grad),
        ]
    )

    def sum_rows_axes(vector):
        vector = vector + to_core(vector)
        step = 1
        while step < sol_size:
            vector = vector + lax.ppermute(vector, "sol", [(i, i ^ step) for i in range(sol_size)])
            step *= 2
        step = 2
        while step < dp_size:
            vector = vector + lax.ppermute(vector, "dp", [(i, i ^ step) for i in range(dp_size)])
            step *= 2
        return vector

    early = sum_rows_axes(
        jnp.concatenate(
            [reorder_vector(v, back_order) for v in (mlp_gain_grad, mlp_shift_grad, down_bias_grad)]
            + [up_bias_both]
        )
    )
    late = sum_rows_axes(
        jnp.concatenate([reorder_vector(v, back_order) for v in (attn_gain_grad, attn_shift_grad)])
    )

    qk_low, qk_high = split_rows(qk_grad)
    vo_low, vo_high = split_rows(vo_grad)
    up_low, up_high = zip(*[split_rows(g) for g in up_grads])
    down_low, down_high = zip(*[split_rows(g) for g in down_grads])

    def both(low_cols, high_cols):
        return jnp.concatenate([low_cols, high_cols], axis=1)

    return (
        outputs,
        input_grad,
        late[:width],
        late[width:],
        both(qk_low[:, :head_cols], qk_high[:, :head_cols]),
        both(qk_low[:, head_cols:], qk_high[:, head_cols:]),
        both(vo_low[:, :head_cols], vo_high[:, :head_cols]),
        both(vo_low[:, head_cols:], vo_high[:, head_cols:]),
        early[:width],
        early[width : 2 * width],
        jnp.concatenate(up_low + up_high, axis=1),
        early[3 * width :],
        jnp.concatenate(down_low + down_high, axis=1),
        early[2 * width : 3 * width],
    )


def per_device(*arrays):
    inputs, query_weight, up_weight = arrays[0], arrays[4], arrays[10]
    width = inputs.shape[1]
    fits = (
        query_weight.shape[0] % 128 == 0
        and inputs.shape[0] == 2 * CHUNK
        and up_weight.shape[1] == 2 * width
        and query_weight.shape[1] * 2 == width
        and lax.axis_size("dp") % 2 == 0
        and lax.axis_size("dp") * lax.axis_size("sol") == 16
        and lax.axis_size("tensor") == 2
    )
    return kernel_program(*arrays) if fits else ring_program(*arrays)


def kernel_program(
    inputs,
    cotangent,
    attn_gain,
    attn_shift,
    query_weight,
    key_weight,
    value_weight,
    out_weight,
    mlp_gain,
    mlp_shift,
    up_weight,
    up_bias,
    down_weight,
    down_bias,
    live_rows,
):
    width = inputs.shape[1]
    shard_rows = query_weight.shape[0]
    dp_size, sol_size = lax.axis_size("dp"), lax.axis_size("sol")
    attn_gain, attn_shift, mlp_gain, mlp_shift, up_bias, down_bias = [
        v.reshape(1, -1) for v in (attn_gain, attn_shift, mlp_gain, mlp_shift, up_bias, down_bias)
    ]
    (
        weights,
        normed_all,
        cot_pair,
        query_rows,
        key_rows,
        value_rows,
        probs,
        mixed_low,
        hidden,
        normed_two,
        slope,
        active,
    ) = run_forward(
        dp_size,
        sol_size,
        inputs,
        (attn_gain, attn_shift, mlp_gain, mlp_shift, up_bias),
        live_rows,
        cotangent,
        (query_weight, key_weight, value_weight, out_weight, up_weight, down_weight),
    )
    grad_up, grad_branch, grad_hidden, mlp_low, down_grad, early_sums = run_down(
        dp_size, sol_size, shard_rows, mlp_gain, weights, cot_pair, active, slope, hidden
    )
    query_grad, kv_grad, own_low, prefix_half, up_grad, outputs, _ = run_attend_back(
        dp_size,
        sol_size,
        shard_rows,
        down_bias,
        weights,
        normed_two,
        grad_up,
        grad_branch,
        query_rows,
        key_rows,
        value_rows,
        probs,
        mlp_low,
        hidden,
    )
    query_grads, key_grads, value_grads, out_grads, input_grad, sums = run_last(
        dp_size,
        sol_size,
        shard_rows,
        inputs,
        attn_gain,
        early_sums,
        normed_all,
        grad_branch,
        query_grad,
        kv_grad,
        mixed_low,
        own_low,
        prefix_half,
        grad_hidden,
    )

    (
        outputs,
        input_grad,
        query_grads,
        key_grads,
        value_grads,
        out_grads,
        up_grad,
        down_grad,
    ) = run_finish(
        [
            outputs,
            input_grad,
            query_grads,
            key_grads,
            value_grads,
            out_grads,
            up_grad,
            down_grad,
        ]
    )
    return (
        outputs,
        input_grad,
        sums[0],
        sums[1],
        query_grads,
        key_grads,
        value_grads,
        out_grads,
        sums[2],
        sums[3],
        up_grad,
        sums[5:7].reshape(-1),
        down_grad,
        sums[4],
    )


def solution(mesh):
    rows = P(("dp", "sol"), None)
    matrix = P(("dp", "sol"), "tensor")
    return jax.shard_map(
        per_device,
        mesh=mesh,
        in_specs=(
            rows,
            rows,
            P(),
            P(),
            matrix,
            matrix,
            matrix,
            matrix,
            P(),
            P(),
            matrix,
            P("tensor"),
            matrix,
            P(),
            P(),
        ),
        out_specs=(
            rows,
            rows,
            P(),
            P(),
            matrix,
            matrix,
            matrix,
            matrix,
            P(),
            P(),
            matrix,
            P("tensor"),
            matrix,
            P(),
        ),
        check_vma=False,
    )
```

```python
import functools
import math

import jax
import jax.numpy as jnp
from jax import lax
from jax.experimental import pallas as pl
from jax.experimental.pallas import tpu as pltpu
from jax.sharding import PartitionSpec as P

HEAD_DIM = 128
EPSILON = 1e-05
NEG_FILL = -1e30
ROWS_AXES = ("dp", "sol")
LOW = jnp.bfloat16
WIDE = jnp.float32


def ring_place(position, sol_size):
    x, along = position // sol_size, position % sol_size
    return x, (along if x % 2 == 0 else sol_size - 1 - along)


def ring_pairs(dp_size, sol_size):
    count = dp_size // 2 * sol_size

    def flat(position, core):
        x, z = ring_place(position % count, sol_size)
        return (x * 2 + core) * sol_size + z

    places = [(q, c) for q in range(count) for c in range(2)]
    ahead = [(flat(q, c), flat(q + 1, c)) for q, c in places]
    back = [(b, a) for a, b in ahead]
    cores = [(flat(q, c), flat(q, 1 - c)) for q, c in places]
    return count, ahead, back, cores


def dot_plain(left_side, right_side):
    return jnp.dot(left_side, right_side, preferred_element_type=WIDE)


def dot_right_t(left_side, right_side):
    return lax.dot_general(
        left_side, right_side, (((1,), (1,)), ((), ())), preferred_element_type=WIDE
    )


def dot_left_t(left_side, right_side):
    return lax.dot_general(
        left_side, right_side, (((0,), (0,)), ((), ())), preferred_element_type=WIDE
    )


def norm_stats(features):
    row_mean = jnp.mean(features, axis=-1, keepdims=True)
    centered = features - row_mean
    variance = jnp.mean(centered * centered, axis=-1, keepdims=True)
    return row_mean, lax.rsqrt(variance + EPSILON)


def layer_norm(features, norm_gain, norm_shift):
    row_mean, inverse = norm_stats(features)
    return (features - row_mean) * inverse * norm_gain + norm_shift


def layer_norm_back(features, norm_gain, grad):
    row_mean, inverse = norm_stats(features)
    unit = (features - row_mean) * inverse
    scaled = grad * norm_gain
    along = jnp.mean(scaled * unit, axis=-1, keepdims=True)
    level = jnp.mean(scaled, axis=-1, keepdims=True)
    grad_features = (scaled - level - unit * along) * inverse
    return grad_features, jnp.sum(grad * unit, axis=0), jnp.sum(grad, axis=0)


def gelu_tanh(upward):
    return jax.nn.gelu(upward, approximate=True)


def copy_block(order_ref, in_ref, out_ref):
    out_ref[...] = in_ref[...]


def reorder(rows, order):
    blocks = order.shape[0]
    height, width = rows.shape
    part = width // blocks
    if part % 128:
        return jnp.take(rows.reshape(height, blocks, part), order, axis=1).reshape(height, width)
    return pl.pallas_call(
        copy_block,
        grid_spec=pltpu.PrefetchScalarGridSpec(
            num_scalar_prefetch=1,
            grid=(blocks,),
            in_specs=[pl.BlockSpec((height, part), lambda j, order_ref: (0, order_ref[j]))],
            out_specs=pl.BlockSpec((height, part), lambda j, order_ref: (0, j)),
        ),
        out_shape=jax.ShapeDtypeStruct(rows.shape, rows.dtype),
        cost_estimate=pl.CostEstimate(
            flops=0, bytes_accessed=4 * height * width, transcendentals=0
        ),
    )(order, rows)


MESH = pl.DeviceIdType.MESH
CHUNK = 256


def any_spec():
    return pl.BlockSpec(memory_space=pl.ANY)


def vmem_spec():
    return pl.BlockSpec(memory_space=pltpu.VMEM)


class Place:
    def __init__(self, dp_size, sol_size):
        self.dp_size, self.sol_size = dp_size, sol_size
        self.count = dp_size // 2 * sol_size
        dp, self.z = lax.axis_index("dp"), lax.axis_index("sol")
        self.y = lax.axis_index("tensor")
        self.x, self.core = dp // 2, dp % 2
        self.dp = dp
        turned = jnp.where(self.x % 2 == 0, self.z, sol_size - 1 - self.z)
        self.at = self.x * sol_size + turned
        self.next = self._chip((self.at + 1) % self.count)
        self.prev = self._chip((self.at + self.count - 1) % self.count)
        self.sibling = (dp + 1 - 2 * self.core, self.z, self.y)
        self.across = (dp, self.z, 1 - self.y)

    def _coords(self, position):
        x, turned = position // self.sol_size, position % self.sol_size
        return x, jnp.where(x % 2 == 0, turned, self.sol_size - 1 - turned)

    def _chip(self, position):
        x, z = self._coords(position)
        return (x * 2 + self.core, z, self.y)

    def up_ahead(self, step=0):
        x, z = self._coords((self.at + step + self.count) % self.count)
        return (x % 2 == 0) == (z > 0)

    def along(self, step):
        return (self.dp, self.z + step, self.y)

    def blocks(self):
        result = []
        for j in range(self.count):
            x, z = self._coords((self.at + j) % self.count)
            result += [(x * 2) * self.sol_size + z, (x * 2 + 1) * self.sol_size + z]
        return result

    def partners(self):
        result = [self.sibling]
        step = 1
        while step < self.sol_size:
            result.append((self.dp, self._flip(self.z, step), self.y))
            step *= 2
        step = 2
        while step < self.dp_size:
            result.append((self._flip(self.dp, step), self.z, self.y))
            step *= 2
        return result

    @staticmethod
    def _flip(place, step):
        return jnp.where(place // step % 2 == 0, place + step, place - step)

    def greet(self, others=()):
        barrier = pltpu.get_barrier_semaphore()
        peers = (self.next, self.prev, self.sibling, self.across) + tuple(others)
        for peer in peers:
            pl.semaphore_signal(barrier, inc=1, device_id=peer, device_id_type=MESH)
        pl.semaphore_wait(barrier, len(peers))


def remote(src, dst, send_sem, recv_sem, device):
    return pltpu.make_async_remote_copy(
        src_ref=src,
        dst_ref=dst,
        send_sem=send_sem,
        recv_sem=recv_sem,
        device_id=device,
        device_id_type=MESH,
    )


def norm_rows(values, gain, shift):
    row_mean = jnp.mean(values, axis=-1, keepdims=True)
    centered = values - row_mean
    variance = jnp.mean(centered * centered, axis=-1, keepdims=True)
    return centered * lax.rsqrt(variance + EPSILON) * gain + shift


def forward_kernel(
    dp_size,
    sol_size,
    x_ref,
    attn_gain_ref,
    attn_shift_ref,
    mlp_gain_ref,
    mlp_shift_ref,
    up_bias_ref,
    live_ref,
    cot_hbm,
    query_ref,
    key_ref,
    value_ref,
    out_ref,
    up_ref,
    down_ref,
    weights,
    normed_out,
    cot_out,
    query_out,
    key_out,
    value_out,
    probs_out,
    mixed_out,
    hidden_out,
    normed_two_out,
    slope_out,
    active_out,
    w_v,
    normed_v,
    query_v,
    key_v,
    value_v,
    probs_v,
    mixed_v,
    hidden_v,
    normed_two_v,
    slope_v,
    active_v,
    core_send_v,
    core_recv_v,
    cross_send_v,
    cross_recv_v,
    ring_send,
    ring_recv,
    swap_local,
    swap_send,
    swap_recv,
    prefix_send,
    prefix_recv,
    pair_send,
    pair_recv,
    sum_send,
    sum_recv,
    cot_sem,
    load_sem,
    probs_sem,
    store_sem,
):
    here = Place(dp_size, sol_size)
    count, core = here.count, here.core
    rows, width = x_ref.shape
    prefix_v = slope_v
    shard = query_ref.shape[0]
    head_cols = query_ref.shape[1] // 2
    ff = up_ref.shape[1] // 2
    half = width // 2
    local_heads = head_cols // HEAD_DIM
    scale = 1.0 / math.sqrt(HEAD_DIM)
    blocks = here.blocks()
    far = count // 2
    own_class, other_class = core, 1 - core

    here.greet()

    def slot(j, which):
        return pl.ds(pl.multiple_of((2 * j + which) * shard, shard), shard)

    shards = (
        (0, 0, query_ref, head_cols),
        (0, head_cols, key_ref, head_cols),
        (0, 2 * head_cols, value_ref, head_cols),
        (0, 3 * head_cols, out_ref, head_cols),
        (1, 0, up_ref, ff),
        (2, 0, down_ref, ff),
    )

    def swap_copies(i):
        matrix, start, source, size = shards[i]
        target = weights.at[matrix, slot(0, own_class), pl.ds(start, size)]

        def columns(which):
            return source.at[:, pl.ds(pl.multiple_of(which * size, size), size)]

        return (
            pltpu.make_async_copy(columns(core), target, swap_local.at[i]),
            remote(columns(1 - core), target, swap_send.at[i], swap_recv.at[i], here.sibling),
        )

    def start_swap(matrix):
        for i in range(len(shards)):
            if shards[i][0] == matrix:
                for copy in swap_copies(i):
                    copy.start()

    def hops(matrix, k, sub):
        which = own_class if sub == 0 else other_class
        halved = k == far and matrix > 0
        ahead_cols = pl.ds(0, half if halved else width)
        back_cols = pl.ds(half if halved else 0, half if halved else width)
        return (
            remote(
                weights.at[matrix, slot((count - k + 1) % count, which), ahead_cols],
                weights.at[matrix, slot(count - k, which), ahead_cols],
                ring_send.at[matrix, 0, k - 1, sub],
                ring_recv.at[matrix, 0, k - 1, sub],
                here.next,
            ),
            remote(
                weights.at[matrix, slot(k - 1, which), back_cols],
                weights.at[matrix, slot(k, which), back_cols],
                ring_send.at[matrix, 1, k - 1, sub],
                ring_recv.at[matrix, 1, k - 1, sub],
                here.prev,
            ),
        )

    def start_ring(matrix, sub):
        for i in range(len(shards)):
            if shards[i][0] == matrix:
                if sub == 0:
                    swap_copies(i)[0].wait()
                else:
                    swap_copies(i)[1].wait_recv()
        for copy in hops(matrix, 1, sub):
            copy.start()

    def only_when(matrix, k, condition, action):
        if matrix == 0 and k == far:
            pl.when(condition)(action)
        else:
            action()

    came_ahead = jnp.logical_not(here.up_ahead())
    goes = (jnp.logical_not(here.up_ahead(1)), here.up_ahead(-1))

    def pump(matrix, k, sub):
        came = hops(matrix, k, sub)
        if k < far:
            further = hops(matrix, k + 1, sub)
        for i in range(2):
            only_when(
                matrix, k, came_ahead if i == 0 else jnp.logical_not(came_ahead), came[i].wait_recv
            )
            if k < far:
                only_when(matrix, k + 1, goes[i], further[i].start)
        if k == far - 1 and matrix < 2:
            start_ring(matrix + 1, sub)

    steps = [
        (matrix, k, sub) for matrix in range(3) for k in range(1, far + 1) for sub in range(2)
    ]
    done = [0]

    def pump_to(number):
        while done[0] < min(number, len(steps)):
            pump(*steps[done[0]])
            done[0] += 1

    y_rows = rows // 2
    parts = 4
    part = y_rows // parts

    def prefix_rows(which_half, i):
        return pl.ds(pl.multiple_of(which_half * y_rows + i * part, part), part)

    def prefix_hop(i, from_input):
        at = prefix_rows(here.y, i)
        return remote(
            x_ref.at[at] if from_input else prefix_v.at[at],
            prefix_v.at[at],
            prefix_send.at[0, i],
            prefix_recv.at[0, i],
            here.along(1),
        )

    def prefix_cross(i, from_input):
        at = prefix_rows(here.y, i)
        return remote(
            x_ref.at[at] if from_input else prefix_v.at[at],
            prefix_v.at[at],
            prefix_send.at[1, i],
            prefix_recv.at[1, i],
            here.across,
        )

    def prefix_stage(stage, i):
        @pl.when(here.z == stage)
        def _():
            if stage == 0:
                prefix_hop(i, True).start()
                prefix_cross(i, True).start()
            else:
                prefix_hop(i, False).wait_recv()
                if stage < sol_size - 1:
                    prefix_hop(i, False).start()
                prefix_cross(i, False).start()

    def prefix_finish():
        for i in range(parts):
            prefix_cross(i, False).wait_recv()

        @pl.when(here.z == 0)
        def _():
            for i in range(parts):
                at = prefix_rows(here.y, i)
                prefix_v[at, :] = x_ref[at, :]

    cot_load = pltpu.make_async_copy(cot_hbm, active_v.at[pl.ds(0, rows)], cot_sem.at[1])
    start_swap(0)

    start_ring(0, 0)
    start_ring(0, 1)
    start_swap(1)
    start_swap(2)
    cot_load.start()

    def ordered(ref, at):
        return jnp.concatenate(
            [ref[at, pl.ds(pl.multiple_of(b * shard, shard), shard)] for b in blocks], axis=1
        ).astype(WIDE)

    gain, shift, gain_two, shift_two = [
        ordered(ref, pl.ds(0, 1))
        for ref in (attn_gain_ref, attn_shift_ref, mlp_gain_ref, mlp_shift_ref)
    ]

    def norm_into(ref, start):
        @pl.loop(0, rows // 128)
        def _(t):
            at = pl.ds(pl.multiple_of(t * 128, 128), 128)
            to = pl.ds(pl.multiple_of(start + t * 128, 128), 128)
            normed_v[to, :] = norm_rows(ordered(ref, at), gain, shift).astype(LOW)

    normed_pair = remote(
        normed_v.at[pl.ds(0, rows)],
        normed_v.at[pl.ds(rows, rows)],
        pair_send.at[1],
        pair_recv.at[1],
        here.sibling,
    )
    prefix_pair = remote(
        normed_v.at[pl.ds(2 * rows, rows)],
        normed_v.at[pl.ds(3 * rows, rows)],
        pair_send.at[2],
        pair_recv.at[2],
        here.sibling,
    )
    norm_into(x_ref, 0)
    normed_pair.start()
    pump_to(2)
    for i in range(parts):
        prefix_stage(0, i)
    for step in range(1, sol_size + parts - 1):
        for i in range(parts):
            if 1 <= step - i < sol_size:
                prefix_stage(step - i, i)
        pump_to(2 + step)
    pump_to(2 * far)

    cot_pair = remote(
        core_send_v,
        cot_out.at[pl.ds(rows, rows)],
        pair_send.at[0],
        pair_recv.at[0],
        here.sibling,
    )
    cot_own = pltpu.make_async_copy(core_send_v, cot_out.at[pl.ds(0, rows)], cot_sem.at[0])

    cot_load.wait()

    @pl.loop(0, rows // 128)
    def _(t):
        at = pl.ds(pl.multiple_of(t * 128, 128), 128)
        core_send_v[at, :] = ordered(active_v, at).astype(LOW)

    cot_pair.start()
    cot_own.start()

    load_first = pltpu.make_async_copy(weights.at[0], w_v, load_sem.at[0])
    load_first.start()
    normed_pair.wait_recv()
    load_first.wait()

    def row_tile(t):
        return pl.ds(pl.multiple_of(t * CHUNK, CHUNK), CHUNK)

    def project(first, last, with_queries):
        @pl.loop(first, last)
        def _(t):
            at = row_tile(t)
            tile = normed_v[at, :]
            kv = dot_plain(tile, w_v[:, head_cols : 3 * head_cols])
            key_v[at, :] = kv[:, :head_cols].astype(LOW)
            value_v[at, :] = kv[:, head_cols:].astype(LOW)
            if with_queries:
                query_v[at, :] = dot_plain(tile, w_v[:, :head_cols]).astype(LOW)

    tiles = rows // CHUNK
    project(0, 2 * tiles, True)
    pump_to(2 * far + 1)
    prefix_finish()
    norm_into(prefix_v, 2 * rows)
    prefix_pair.start()
    pump_to(2 * far + 2)
    prefix_pair.wait_recv()
    project(2 * tiles, 4 * tiles, False)

    stores = []

    def store(src, dst):
        copy = pltpu.make_async_copy(src, dst, store_sem.at[len(stores)])
        copy.start()
        stores.append(copy)

    store(normed_v, normed_out)
    store(query_v, query_out)
    store(key_v, key_out)
    store(value_v, value_out)

    def probs_copy(unit):
        return pltpu.make_async_copy(
            probs_v.at[unit % 2], probs_out.at[unit], probs_sem.at[unit % 2]
        )

    def attend(unit):
        block, head = unit // local_heads, unit % local_heads
        cols = pl.ds(pl.multiple_of(head * HEAD_DIM, HEAD_DIM), HEAD_DIM)
        place = jnp.where(block == 0, here.dp, here.dp + 1 - 2 * core)
        own_live = live_ref[place * sol_size + here.z]
        prefix_live = jnp.where(here.z == 0, 0, live_ref[place * sol_size])
        own_at = pl.ds(pl.multiple_of(block * rows, rows), rows)
        prefix_at = pl.ds(pl.multiple_of((2 + block) * rows, rows), rows)

        @pl.when(unit >= 2)
        def _():
            probs_copy(unit - 2).wait()

        for t in range(tiles):
            at = pl.ds(pl.multiple_of(block * rows + t * CHUNK, CHUNK), CHUNK)
            queries = query_v[at, cols]
            col = lax.broadcasted_iota(jnp.int32, (CHUNK, rows), 1)
            row = lax.broadcasted_iota(jnp.int32, (CHUNK, rows), 0) + t * CHUNK
            first = dot_right_t(queries, key_v[prefix_at, cols]) * scale
            second = dot_right_t(queries, key_v[own_at, cols]) * scale
            first = jnp.where(col < prefix_live, first, NEG_FILL)
            second = jnp.where(
                jnp.logical_and(col <= row, col < own_live), second, NEG_FILL
            )
            peak = jnp.maximum(
                jnp.max(first, axis=-1, keepdims=True), jnp.max(second, axis=-1, keepdims=True)
            )
            first = jnp.exp(first - peak)
            second = jnp.exp(second - peak)
            total = jnp.sum(first, axis=-1, keepdims=True) + jnp.sum(
                second, axis=-1, keepdims=True
            )
            inverse = 1.0 / total
            first = (first * inverse).astype(LOW)
            second = (second * inverse).astype(LOW)
            probs_v[unit % 2, pl.ds(t * CHUNK, CHUNK), pl.ds(0, rows)] = first
            probs_v[unit % 2, pl.ds(t * CHUNK, CHUNK), pl.ds(rows, rows)] = second
            mixed_v[at, cols] = (
                dot_plain(first, value_v[prefix_at, cols])
                + dot_plain(second, value_v[own_at, cols])
            ).astype(LOW)
        probs_copy(unit).start()

    units = 2 * local_heads
    for quarter in range(4):
        pl.loop(quarter * units // 4, (quarter + 1) * units // 4)(attend)
        pump_to(2 * far + (2, 3, 4, 4)[quarter])
    for unit in (units - 2, units - 1):
        probs_copy(unit).wait()
    store(mixed_v, mixed_out)

    out_cols = slice(3 * head_cols, 4 * head_cols)

    def core_copy(t):
        at = pl.ds(t * CHUNK, CHUNK)
        return remote(
            core_send_v.at[at], core_recv_v.at[at], sum_send.at[0, t], sum_recv.at[0, t], here.sibling
        )

    def cross_copy(t):
        at = pl.ds(t * CHUNK, CHUNK)
        return remote(
            cross_send_v.at[at], cross_recv_v.at[at], sum_send.at[1, t], sum_recv.at[1, t], here.across
        )

    def two_copy(t):
        return remote(
            normed_two_v.at[pl.ds(t * CHUNK, CHUNK)],
            normed_two_v.at[pl.ds(rows + t * CHUNK, CHUNK)],
            sum_send.at[2, t],
            sum_recv.at[2, t],
            here.sibling,
        )

    def hidden_store(t):
        return pltpu.make_async_copy(
            hidden_v, hidden_out.at[pl.ds(t * CHUNK, CHUNK)], load_sem.at[1]
        )

    cot_own.wait()
    cot_pair.wait_send()
    for t in range(tiles):
        core_send_v[pl.ds(t * CHUNK, CHUNK), :] = dot_right_t(
            mixed_v[pl.ds(rows + t * CHUNK, CHUNK), :], w_v[:, out_cols]
        ).astype(LOW)
        core_copy(t).start()
    for t in range(tiles):
        at = pl.ds(t * CHUNK, CHUNK)
        partial = dot_right_t(mixed_v[at, :], w_v[:, out_cols])
        core_copy(t).wait_recv()
        cross_send_v[at, :] = (partial + core_recv_v[at, :].astype(WIDE)).astype(LOW)
        cross_copy(t).start()
    pump_to(4 * far)
    load_second = pltpu.make_async_copy(weights.at[1], w_v, load_sem.at[0])
    load_second.start()
    for t in range(tiles):
        at = pl.ds(t * CHUNK, CHUNK)
        if t > 0:
            pump_to(4 * far + 2)
        cross_copy(t).wait_recv()
        hidden = (
            ordered(x_ref, at)
            + cross_send_v[at, :].astype(WIDE)
            + cross_recv_v[at, :].astype(WIDE)
        )
        if t > 0:
            hidden_store(t - 1).wait()
        hidden_v[...] = hidden
        hidden_store(t).start()
        normed_two_v[at, :] = norm_rows(hidden, gain_two, shift_two).astype(LOW)
        two_copy(t).start()
    hidden_store(tiles - 1).wait()
    load_second.wait()
    for t in range(tiles):
        two_copy(t).wait_recv()
    store(normed_two_v, normed_two_out)

    bend = math.sqrt(2.0 / math.pi)
    spans = ff // half

    def feed(i):
        at = row_tile(i // spans)
        cols = pl.ds(pl.multiple_of((i % spans) * half, half), half)
        bias_cols = pl.ds(pl.multiple_of(core * ff + (i % spans) * half, half), half)
        upward = dot_plain(normed_two_v[at, :], w_v[:, cols]) + up_bias_ref[:, bias_cols]
        square = upward * upward
        curve = jnp.tanh(bend * (upward + 0.044715 * (upward * square)))
        active_v[at, cols] = (0.5 * upward * (1.0 + curve)).astype(LOW)
        slope_v[at, cols] = (
            0.5 * (1.0 + curve)
            + 0.5 * upward * (1.0 - curve * curve) * (bend + (3.0 * 0.044715 * bend) * square)
        ).astype(LOW)

    for i in range(parts):

        @pl.when(here.z < sol_size - 1)
        def _():
            prefix_hop(i, False).wait_send()

        prefix_cross(i, False).wait_send()

    feeds = 2 * tiles * spans
    for quarter in range(4):
        pl.loop(quarter * feeds // 4, (quarter + 1) * feeds // 4)(feed)
        pump_to(4 * far + 3 + quarter)
    store(active_v, active_out)
    store(slope_v, slope_out)

    pump_to(len(steps))
    cot_pair.wait_recv()
    normed_pair.wait_send()
    prefix_pair.wait_send()
    for i in range(len(shards)):
        swap_copies(i)[1].wait_send()
    for step in steps:
        for i, copy in enumerate(hops(*step)):
            only_when(step[0], step[1], goes[i], copy.wait_send)
    for t in range(tiles):
        core_copy(t).wait_send()
        cross_copy(t).wait_send()
        two_copy(t).wait_send()
    for copy in stores:
        copy.wait()


def run_forward(dp_size, sol_size, x, vectors, live_rows, cot, matrices):
    rows, width = x.shape
    head_cols = matrices[0].shape[1] // 2
    ff = matrices[4].shape[1] // 2
    heads = head_cols // HEAD_DIM
    count = dp_size // 2 * sol_size
    far = count // 2

    def shape(*dims, dtype=LOW):
        return jax.ShapeDtypeStruct(dims, dtype)

    outs = [
        shape(3, width, width),
        shape(4 * rows, width),
        shape(2 * rows, width),
        shape(2 * rows, head_cols),
        shape(4 * rows, head_cols),
        shape(4 * rows, head_cols),
        shape(2 * heads, rows, 2 * rows),
        shape(2 * rows, head_cols),
        shape(rows, width, dtype=WIDE),
        shape(2 * rows, width),
        shape(2 * rows, ff),
        shape(2 * rows, ff),
    ]
    dma = pltpu.SemaphoreType.DMA
    return pl.pallas_call(
        functools.partial(forward_kernel, dp_size, sol_size),
        out_shape=outs,
        in_specs=[
            vmem_spec(),
            vmem_spec(),
            vmem_spec(),
            vmem_spec(),
            vmem_spec(),
            vmem_spec(),
            pl.BlockSpec(memory_space=pltpu.SMEM),
        ]
        + [any_spec()]
        + [vmem_spec()] * 6,
        out_specs=[any_spec()] * len(outs),
        scratch_shapes=[
            pltpu.VMEM((width, width), LOW),
            pltpu.VMEM((4 * rows, width), LOW),
            pltpu.VMEM((2 * rows, head_cols), LOW),
            pltpu.VMEM((4 * rows, head_cols), LOW),
            pltpu.VMEM((4 * rows, head_cols), LOW),
            pltpu.VMEM((2, rows, 2 * rows), LOW),
            pltpu.VMEM((2 * rows, head_cols), LOW),
            pltpu.VMEM((CHUNK, width), WIDE),
            pltpu.VMEM((2 * rows, width), LOW),
            pltpu.VMEM((2 * rows, ff), LOW),
            pltpu.VMEM((2 * rows, ff), LOW),
        ]
        + [pltpu.VMEM((rows, width), LOW)] * 4
        + [
            dma((3, 2, far, 2)),
            dma((3, 2, far, 2)),
            dma((6,)),
            dma((6,)),
            dma((6,)),
            dma((2, 4)),
            dma((2, 4)),
            dma((3,)),
            dma((3,)),
            dma((3, rows // CHUNK)),
            dma((3, rows // CHUNK)),
            dma((2,)),
            dma((2,)),
            dma((2,)),
            dma((16,)),
        ],
        compiler_params=pltpu.CompilerParams(
            collective_id=0, has_side_effects=True, vmem_limit_bytes=60 * 2**20
        ),
    )(x, *vectors, live_rows, cot, *matrices)


class RingSum:
    def __init__(self, here, chunk, send_v, recv_v, stage_v, sems, target, upward=False):
        self.here, self.chunk = here, chunk
        self.prepared = False
        self.upward = upward
        if upward:
            mine = here.up_ahead()
            self.sends = (mine, jnp.logical_not(mine))
            self.gets = (here.up_ahead(-1), jnp.logical_not(here.up_ahead(1)))
        self.send_v, self.recv_v, self.stage_v = send_v, recv_v, stage_v
        self.send_sem, self.recv_sem, self.end_sem = sems
        self.target = target
        self.far = here.count // 2
        self.cols = stage_v.shape[2]
        self.steps = [(t, sub) for t in range(1, self.far + 1) for sub in range(2)]
        self.done = 0

    def _class(self, sub):
        return self.here.core if sub == 0 else 1 - self.here.core

    def _columns(self, t, way):
        if t > 1 or self.upward:
            return pl.ds(0, self.cols)
        return pl.ds(way * (self.cols // 2), self.cols // 2)

    def _copy(self, t, way, sub):
        at = self._columns(t, way)
        return remote(
            self.send_v.at[way, sub, :, at],
            self.recv_v.at[(t - 1) % 3, way, sub, :, at],
            self.send_sem.at[t - 1, way, sub],
            self.recv_sem.at[t - 1, way, sub],
            self.here.prev if way else self.here.next,
        )

    def _event(self, t, sub):
        far, count = self.far, self.here.count
        half = self.cols // 2
        if t == 1 and self.upward:
            value = self.chunk(far, self._class(sub)).astype(LOW)
            for way in range(2):
                self.send_v[way, sub] = value
                pl.when(self.sends[way])(self._copy(1, way, sub).start)
            return
        if t == 1:
            value = self.chunk(far, self._class(sub))
            self.send_v[0, sub, :, :half] = value[:, :half].astype(LOW)
            self.send_v[1, sub, :, half:] = value[:, half:].astype(LOW)
            for way in range(2):
                self._copy(1, way, sub).start()
            return
        for way in range(2):
            j = far + 1 - t if way == 0 else count - (far + 1 - t)
            value = self.chunk(j, self._class(sub))
            if t == 2 and self.upward:
                pl.when(self.sends[way])(self._copy(1, way, sub).wait_send)
                pl.when(self.gets[way])(self._copy(1, way, sub).wait_recv)
                came = self.recv_v[0, way, sub].astype(WIDE)
                self.send_v[way, sub] = (
                    value + jnp.where(self.gets[way], came, 0.0)
                ).astype(LOW)
                self._copy(t, way, sub).start()
                continue
            self._copy(t - 1, way, sub).wait()
            if t == 2:
                near = slice(0, half) if way == 0 else slice(half, 2 * half)
                rest = slice(half, 2 * half) if way == 0 else slice(0, half)
                self.send_v[way, sub, :, near] = (
                    value[:, near] + self.recv_v[0, way, sub, :, near].astype(WIDE)
                ).astype(LOW)
                self.send_v[way, sub, :, rest] = value[:, rest].astype(LOW)
            else:
                self.send_v[way, sub] = (
                    value + self.recv_v[(t - 2) % 3, way, sub].astype(WIDE)
                ).astype(LOW)
            self._copy(t, way, sub).start()

    def prepare(self):
        for sub in range(2):
            self.stage_v[sub] = self.chunk(0, self._class(sub))
        self.prepared = True

    def _last(self, sub):
        for way in range(2):
            self._copy(self.far, way, sub).wait()
        value = self.stage_v[sub] + self.recv_v[(self.far - 1) % 3, 0, sub].astype(WIDE)
        self.stage_v[sub] = value + self.recv_v[(self.far - 1) % 3, 1, sub].astype(WIDE)
        for copy in self._results(sub):
            copy.start()

    def _results(self, sub):
        copies = []
        core = self.here.core
        for i, (ref, start, size) in enumerate(self.target):
            to = ref.at[:, pl.ds(pl.multiple_of(core * size, size), size)]
            source = self.stage_v.at[sub, :, pl.ds(start, size)]
            if sub == 0:
                copies.append(pltpu.make_async_copy(source, to, self.end_sem.at[0, i]))
            else:
                copies.append(
                    remote(
                        source, to, self.end_sem.at[1, i], self.end_sem.at[2, i], self.here.sibling
                    )
                )
        return copies

    def to(self, number):
        while self.done < min(number, len(self.steps) + 2):
            if self.done < len(self.steps):
                self._event(*self.steps[self.done])
            else:
                self._last(self.done - len(self.steps))
            self.done += 1

    def finish(self):
        self.to(len(self.steps) + 2)
        for sub in range(2):
            for copy in self._results(sub):
                copy.wait()


def ring_sum_scratch(far, shard, cols, results):
    dma = pltpu.SemaphoreType.DMA
    return [
        pltpu.VMEM((2, 2, shard, cols), LOW),
        pltpu.VMEM((3, 2, 2, shard, cols), LOW),
        pltpu.VMEM((2, shard, cols), WIDE),
        dma((far, 2, 2)),
        dma((far, 2, 2)),
        dma((3, results)),
    ]


def norm_back(values, gain, grad):
    row_mean = jnp.mean(values, axis=-1, keepdims=True)
    centered = values - row_mean
    variance = jnp.mean(centered * centered, axis=-1, keepdims=True)
    inverse = lax.rsqrt(variance + EPSILON)
    unit = centered * inverse
    scaled = grad * gain
    terms = grad * unit
    along = jnp.mean(scaled * unit, axis=-1, keepdims=True)
    level = jnp.mean(scaled, axis=-1, keepdims=True)
    return (
        (scaled - level - unit * along) * inverse,
        jnp.sum(terms, axis=0, keepdims=True),
        jnp.sum(grad, axis=0, keepdims=True),
    )


def tile_rows(t):
    return pl.ds(t * CHUNK, CHUNK)


def down_kernel(
    dp_size,
    sol_size,
    gain_ref,
    weights,
    cot_hbm,
    active_hbm,
    slope_hbm,
    hidden_hbm,
    grad_up_out,
    branch_out,
    grad_hidden_out,
    mlp_low_out,
    down_grad_out,
    sums_ref,
    cot_v,
    active_v,
    slope_v,
    down_v,
    up_v,
    hidden_v,
    core_send_v,
    core_recv_v,
    second_recv_v,
    cross_send_v,
    cross_recv_v,
    ring_send_v,
    ring_recv_v,
    stage_v,
    ring_send,
    ring_recv,
    ring_end,
    load_sem,
    store_sem,
    sum_send,
    sum_recv,
):
    here = Place(dp_size, sol_size)
    rows, width = core_send_v.shape
    shard = stage_v.shape[1]
    ff = active_v.shape[1]
    tiles = rows // CHUNK
    halves = (pl.ds(0, width // 2), pl.ds(width // 2, width // 2))
    def chunk(j, which):
        at = pl.ds(pl.multiple_of((2 * j + which) * shard, shard), shard)
        return dot_left_t(cot_v[:, at], active_v[...])

    ring = RingSum(
        here,
        chunk,
        ring_send_v,
        ring_recv_v,
        stage_v,
        (ring_send, ring_recv, ring_end),
        ((down_grad_out, 0, ff),),
    )
    loads = [
        pltpu.make_async_copy(src, dst, load_sem.at[i])
        for i, (src, dst) in enumerate(
            (
                (cot_hbm, cot_v),
                (active_hbm, active_v),
                (weights.at[2], down_v),
                (slope_hbm, slope_v),
                (weights.at[1], up_v),
            )
        )
    ]
    for copy in loads:
        copy.start()
    here.greet()

    loads[0].wait()
    loads[1].wait()
    ring.to(1)

    sums_ref[...] = jnp.zeros_like(sums_ref)
    spans = 2

    def back_feed(tile):
        at = pl.ds(tile * CHUNK, CHUNK)

        @pl.loop(0, spans)
        def _(i):
            cols = pl.ds(pl.multiple_of(i * (ff // spans), ff // spans), ff // spans)
            grad = dot_plain(cot_v[at, :], down_v[:, cols]) * slope_v[at, cols].astype(WIDE)
            low = grad.astype(LOW)
            slope_v[at, cols] = low
            sums_ref[3:4, cols] += jnp.sum(low.astype(WIDE), axis=0, keepdims=True)

    def core_copy(t):
        return remote(
            core_send_v.at[tile_rows(t)],
            core_recv_v.at[tile_rows(t)],
            sum_send.at[0, t],
            sum_recv.at[0, t],
            here.sibling,
        )

    def cross_copy(t):
        return remote(
            cross_send_v.at[tile_rows(t)],
            cross_recv_v.at[tile_rows(t)],
            sum_send.at[1, t],
            sum_recv.at[1, t],
            here.across,
        )

    def second_copy(t):
        return remote(
            core_send_v.at[tile_rows(t)],
            second_recv_v.at[tile_rows(t)],
            sum_send.at[2, t],
            sum_recv.at[2, t],
            here.sibling,
        )

    def branch_copy(t):
        return remote(
            core_recv_v.at[tile_rows(t)],
            branch_out.at[pl.ds(rows + t * CHUNK, CHUNK)],
            sum_send.at[3, t],
            sum_recv.at[3, t],
            here.sibling,
        )

    def sibling_terms(t):
        for cols in halves:
            core_send_v[tile_rows(t), cols] = dot_right_t(
                slope_v[pl.ds(rows + t * CHUNK, CHUNK), :], up_v[cols, :]
            ).astype(LOW)
        core_copy(t).start()

    def own_terms(t):
        at = tile_rows(t)
        core_copy(t).wait_recv()
        for cols in halves:
            cross_send_v[at, cols] = (
                dot_right_t(slope_v[at, :], up_v[cols, :]) + core_recv_v[at, cols].astype(WIDE)
            ).astype(LOW)
        cross_copy(t).start()

    def sibling_output(t):
        core_copy(t).wait_send()
        for cols in halves:
            core_send_v[tile_rows(t), cols] = dot_right_t(
                active_v[pl.ds(rows + t * CHUNK, CHUNK), :], down_v[cols, :]
            ).astype(LOW)
        second_copy(t).start()

    def own_output(t):
        at = tile_rows(t)
        second_copy(t).wait_recv()
        for cols in halves:
            second_recv_v[at, cols] = (
                dot_right_t(active_v[at, :], down_v[cols, :])
                + second_recv_v[at, cols].astype(WIDE)
            ).astype(LOW)

    gain = read_ordered(gain_ref, pl.ds(0, 1), here.blocks(), shard)

    def hidden_load(t):
        return pltpu.make_async_copy(hidden_hbm.at[tile_rows(t)], hidden_v, load_sem.at[0])

    def hidden_store(t):
        return pltpu.make_async_copy(hidden_v, grad_hidden_out.at[tile_rows(t)], store_sem.at[2])

    def norm_tile(t):
        hidden_load(t).wait()
        cross_copy(t).wait_recv()
        for part in range(2):
            inner = pl.ds(part * (CHUNK // 2), CHUNK // 2)
            here_at = pl.ds(t * CHUNK + part * (CHUNK // 2), CHUNK // 2)
            grad = cross_send_v[here_at, :].astype(WIDE) + cross_recv_v[here_at, :].astype(WIDE)
            back, gain_terms, shift_terms = norm_back(hidden_v[inner, :], gain, grad)
            cot = cot_v[here_at, :].astype(WIDE)
            sums_ref[0:1, :] += gain_terms
            sums_ref[1:2, :] += shift_terms
            sums_ref[2:3, :] += jnp.sum(cot, axis=0, keepdims=True)
            back = back + cot
            hidden_v[inner, :] = back
            core_recv_v[here_at, :] = back.astype(LOW)
        branch_copy(t).start()
        hidden_store(t).start()

    stores = []

    def store(src, dst, i):
        copy = pltpu.make_async_copy(src, dst, store_sem.at[i])
        copy.start()
        stores.append(copy)

    loads[2].wait()
    loads[3].wait()
    ring.to(2)
    hidden_load(0).start()
    back_feed(0)
    ring.to(3)
    back_feed(tiles)
    loads[4].wait()
    sibling_terms(0)
    ring.to(4)
    own_terms(0)
    back_feed(1)
    ring.to(5)
    back_feed(tiles + 1)
    store(slope_v, grad_up_out, 0)
    sibling_terms(1)
    ring.to(6)
    own_terms(1)
    sibling_output(0)
    ring.to(7)
    own_output(0)
    sibling_output(1)
    ring.to(8)
    norm_tile(0)
    own_output(1)
    store(second_recv_v, mlp_low_out, 1)
    hidden_store(0).wait()
    hidden_load(1).start()
    ring.prepare()
    ring.to(9)
    norm_tile(1)
    store(core_recv_v, branch_out.at[pl.ds(0, rows)], 3)
    hidden_store(1).wait()
    ring.finish()
    for t in range(tiles):
        cross_copy(t).wait_send()
        second_copy(t).wait_send()
        branch_copy(t).wait()
    for copy in stores:
        copy.wait()


def run_down(
    dp_size, sol_size, shard, gain, weights, cot, active, slope, hidden
):
    rows, width = hidden.shape
    ff = active.shape[1]
    count = dp_size // 2 * sol_size
    tiles = rows // CHUNK
    dma = pltpu.SemaphoreType.DMA

    def shape(*dims, dtype=LOW):
        return jax.ShapeDtypeStruct(dims, dtype)

    outs = [
        shape(2 * rows, ff),
        shape(2 * rows, width),
        shape(rows, width, dtype=WIDE),
        shape(rows, width),
        shape(shard, 2 * ff, dtype=WIDE),
        shape(8, width, dtype=WIDE),
    ]
    return pl.pallas_call(
        functools.partial(down_kernel, dp_size, sol_size),
        out_shape=outs,
        in_specs=[vmem_spec()] + [any_spec()] * 5,
        out_specs=[any_spec()] * 5 + [vmem_spec()],
        scratch_shapes=[
            pltpu.VMEM((2 * rows, width), LOW),
            pltpu.VMEM((2 * rows, ff), LOW),
            pltpu.VMEM((2 * rows, ff), LOW),
            pltpu.VMEM((width, ff), LOW),
            pltpu.VMEM((width, ff), LOW),
            pltpu.VMEM((CHUNK, width), WIDE),
        ]
        + [pltpu.VMEM((rows, width), LOW)] * 5
        + ring_sum_scratch(count // 2, shard, ff, 1)
        + [
            dma((5,)),
            dma((6,)),
            dma((4, tiles)),
            dma((4, tiles)),
        ],
        compiler_params=pltpu.CompilerParams(
            collective_id=1, has_side_effects=True, vmem_limit_bytes=60 * 2**20
        ),
    )(gain, weights, cot, active, slope, hidden)


def read_ordered(ref, at, blocks, part):
    return jnp.concatenate(
        [ref[at, pl.ds(pl.multiple_of(b * part, part), part)] for b in blocks], axis=1
    ).astype(WIDE)


def write_ordered(ref, at, blocks, part, values):
    for j, b in enumerate(blocks):
        ref[at, pl.ds(pl.multiple_of(b * part, part), part)] = values[
            :, j * part : (j + 1) * part
        ].astype(ref.dtype)


def attend_back_kernel(
    dp_size,
    sol_size,
    bias_ref,
    weights,
    normed_two_hbm,
    grad_up_hbm,
    branch_hbm,
    query_hbm,
    key_hbm,
    value_hbm,
    probs_hbm,
    mlp_low_hbm,
    hidden_hbm,
    query_grad_out,
    kv_grad_out,
    own_low_out,
    prefix_half_out,
    up_grad_out,
    outputs_out,
    mlp_recv_out,
    normed_two_v,
    grad_up_v,
    branch_v,
    w_v,
    query_v,
    key_v,
    value_v,
    mixed_grad_v,
    probs_v,
    query_grad_v,
    kv_grad_v,
    core_recv_v,
    second_recv_v,
    half_recv_v,
    mlp_low_v,
    mlp_recv_v,
    hidden_v,
    ring_send_v,
    ring_recv_v,
    stage_v,
    ring_send,
    ring_recv,
    ring_end,
    load_sem,
    probs_sem,
    tile_sem,
    store_sem,
    sum_send,
    sum_recv,
    cross_send,
    cross_recv,
):
    here = Place(dp_size, sol_size)
    rows, width = core_recv_v.shape
    core_send_v = branch_v.at[pl.ds(0, rows)]
    half_send_v = branch_v.at[pl.ds(rows, CHUNK)]
    half_keep_v = branch_v.at[pl.ds(rows + CHUNK, CHUNK)]
    shard = stage_v.shape[1]
    ff = grad_up_v.shape[1]
    head_cols = query_v.shape[1]
    local_heads = head_cols // HEAD_DIM
    scale = 1.0 / math.sqrt(HEAD_DIM)
    tiles = rows // CHUNK
    blocks = here.blocks()
    halves = (pl.ds(0, width // 2), pl.ds(width // 2, width // 2))
    loads = [
        pltpu.make_async_copy(src, dst, load_sem.at[i])
        for i, (src, dst) in enumerate(
            (
                (normed_two_hbm, normed_two_v),
                (grad_up_hbm, grad_up_v),
                (branch_hbm, branch_v),
                (weights.at[0], w_v),
                (query_hbm, query_v),
                (key_hbm, key_v),
                (value_hbm, value_v),
            )
        )
    ]
    for copy in loads:
        copy.start()

    def probs_load(unit):
        return pltpu.make_async_copy(
            probs_hbm.at[unit], probs_v.at[unit % 2], probs_sem.at[unit % 2]
        )

    probs_load(0).start()
    here.greet()
    mlp_cross = remote(
        mlp_low_hbm, mlp_recv_out, cross_send.at[0], cross_recv.at[0], here.across
    )
    mlp_cross.start()

    def chunk(j, which):
        at = pl.ds(pl.multiple_of((2 * j + which) * shard, shard), shard)
        return dot_left_t(normed_two_v[:, at], grad_up_v[...])

    ring = RingSum(
        here,
        chunk,
        ring_send_v,
        ring_recv_v,
        stage_v,
        (ring_send, ring_recv, ring_end),
        ((up_grad_out, 0, ff),),
    )
    loads[0].wait()
    loads[1].wait()
    ring.to(2)
    loads[2].wait()
    loads[3].wait()

    @pl.loop(0, 2 * tiles)
    def _(t):
        at = pl.ds(pl.multiple_of(t * CHUNK, CHUNK), CHUNK)
        mixed_grad_v[at, :] = dot_plain(
            branch_v[at, :], w_v[:, 3 * head_cols : 4 * head_cols]
        ).astype(LOW)

    for i in range(4, 7):
        loads[i].wait()

    units = 2 * local_heads

    def back(unit):
        block, head = unit // local_heads, unit % local_heads
        cols = pl.ds(pl.multiple_of(head * HEAD_DIM, HEAD_DIM), HEAD_DIM)
        value_cols = pl.ds(
            pl.multiple_of(head_cols + head * HEAD_DIM, HEAD_DIM), HEAD_DIM
        )
        own_at = pl.ds(pl.multiple_of(block * rows, rows), rows)
        prefix_at = pl.ds(pl.multiple_of((2 + block) * rows, rows), rows)
        probs_load(unit).wait()

        @pl.when(unit + 1 < units)
        def _():
            probs_load(unit + 1).start()

        sums = None
        for t in range(tiles):
            at = pl.ds(pl.multiple_of(block * rows + t * CHUNK, CHUNK), CHUNK)
            grad = mixed_grad_v[at, cols]
            queries = query_v[at, cols]
            inner = pl.ds(t * CHUNK, CHUNK)
            first_low = probs_v[unit % 2, inner, pl.ds(0, rows)]
            second_low = probs_v[unit % 2, inner, pl.ds(rows, rows)]
            first, second = first_low.astype(WIDE), second_low.astype(WIDE)
            first_grad = dot_right_t(grad, value_v[prefix_at, cols])
            second_grad = dot_right_t(grad, value_v[own_at, cols])
            delta = jnp.sum(first * first_grad, axis=-1, keepdims=True) + jnp.sum(
                second * second_grad, axis=-1, keepdims=True
            )
            first_scores = (first * (first_grad - delta)).astype(LOW)
            second_scores = (second * (second_grad - delta)).astype(LOW)
            query_grad_v[at, cols] = (
                (
                    dot_plain(first_scores, key_v[prefix_at, cols])
                    + dot_plain(second_scores, key_v[own_at, cols])
                )
                * scale
            ).astype(LOW)
            terms = [
                dot_left_t(second_scores, queries),
                dot_left_t(second_low, grad),
                dot_left_t(first_scores, queries),
                dot_left_t(first_low, grad),
            ]
            sums = terms if sums is None else [a + b for a, b in zip(sums, terms)]
        kv_grad_v[own_at, cols] = (sums[0] * scale).astype(LOW)
        kv_grad_v[own_at, value_cols] = sums[1].astype(LOW)
        kv_grad_v[prefix_at, cols] = (sums[2] * scale).astype(LOW)
        kv_grad_v[prefix_at, value_cols] = sums[3].astype(LOW)

    for quarter in range(4):
        pl.loop(quarter * units // 4, (quarter + 1) * units // 4)(back)
        ring.to(3 + quarter)
    stores = []

    def store(src, dst):
        copy = pltpu.make_async_copy(src, dst, store_sem.at[len(stores)])
        copy.start()
        stores.append(copy)

    store(query_grad_v, query_grad_out)
    store(kv_grad_v, kv_grad_out)

    def core_copy(t):
        return remote(
            core_send_v.at[tile_rows(t)],
            core_recv_v.at[tile_rows(t)],
            sum_send.at[0, t],
            sum_recv.at[0, t],
            here.sibling,
        )

    def second_copy(t):
        return remote(
            core_send_v.at[tile_rows(t)],
            second_recv_v.at[tile_rows(t)],
            sum_send.at[1, t],
            sum_recv.at[1, t],
            here.sibling,
        )

    half_copy = remote(half_send_v, half_recv_v, cross_send.at[1], cross_recv.at[1], here.across)
    kv_cols = pl.ds(head_cols, 2 * head_cols)

    def prefix_terms(at, cols):
        return dot_right_t(kv_grad_v[at, :], w_v[cols, kv_cols])

    for t in range(tiles):
        for cols in halves:
            core_send_v[tile_rows(t), cols] = prefix_terms(
                pl.ds(3 * rows + t * CHUNK, CHUNK), cols
            ).astype(LOW)
        second_copy(t).start()
    for t in range(tiles):
        second_copy(t).wait_recv()
    for keep in range(2):
        which = here.y if keep else 1 - here.y
        at = pl.ds(pl.multiple_of(2 * rows + which * CHUNK, CHUNK), CHUNK)
        came = pl.ds(pl.multiple_of(which * CHUNK, CHUNK), CHUNK)
        for cols in halves:
            value = prefix_terms(at, cols) + second_recv_v[came, cols].astype(WIDE)
            if keep:
                half_keep_v[:, cols] = value.astype(LOW)
            else:
                half_send_v[:, cols] = value.astype(LOW)
        if not keep:
            half_copy.start()
    ring.to(7)

    def own_terms(at, cols):
        return dot_right_t(query_grad_v[at, :], w_v[cols, 0:head_cols]) + dot_right_t(
            kv_grad_v[at, :], w_v[cols, kv_cols]
        )

    for t in range(tiles):
        second_copy(t).wait_send()
        for cols in halves:
            core_send_v[tile_rows(t), cols] = own_terms(
                pl.ds(rows + t * CHUNK, CHUNK), cols
            ).astype(LOW)
        core_copy(t).start()
    for t in range(tiles):
        at = tile_rows(t)
        core_copy(t).wait_recv()
        for cols in halves:
            core_recv_v[at, cols] = (
                own_terms(at, cols) + core_recv_v[at, cols].astype(WIDE)
            ).astype(LOW)
    store(core_recv_v, own_low_out)
    ring.to(8)
    ring.prepare()

    half_copy.wait()
    write_ordered(
        half_send_v,
        slice(None),
        blocks,
        shard,
        half_keep_v[...].astype(WIDE) + half_recv_v[...].astype(WIDE),
    )
    store(half_send_v, prefix_half_out)

    bias = read_ordered(bias_ref, pl.ds(0, 1), blocks, shard)
    small = mlp_low_v.shape[0]
    pieces = rows // small

    def piece_rows(t):
        return pl.ds(t * small, small)

    def tile_loads(t):
        return (
            pltpu.make_async_copy(hidden_hbm.at[piece_rows(t)], hidden_v, tile_sem.at[0]),
            pltpu.make_async_copy(mlp_low_hbm.at[piece_rows(t)], mlp_low_v, tile_sem.at[1]),
            pltpu.make_async_copy(mlp_recv_out.at[piece_rows(t)], mlp_recv_v, tile_sem.at[2]),
        )

    def tile_store(t):
        return pltpu.make_async_copy(
            half_keep_v.at[pl.ds(t % 2 * small, small)],
            outputs_out.at[piece_rows(t)],
            tile_sem.at[3 + t % 2],
        )

    mlp_cross.wait()
    for copy in tile_loads(0):
        copy.start()
    for t in range(pieces):
        for copy in tile_loads(t):
            copy.wait()
        value = (
            hidden_v[...]
            + mlp_low_v[...].astype(WIDE)
            + mlp_recv_v[...].astype(WIDE)
            + bias
        )
        if t > 1:
            tile_store(t - 2).wait()
        write_ordered(half_keep_v, pl.ds(t % 2 * small, small), blocks, shard, value)
        tile_store(t).start()
        if t + 1 < pieces:
            for copy in tile_loads(t + 1):
                copy.start()
    for t in (pieces - 2, pieces - 1):
        tile_store(t).wait()
    ring.finish()
    for t in range(tiles):
        core_copy(t).wait_send()
    for copy in stores:
        copy.wait()


def run_attend_back(
    dp_size,
    sol_size,
    shard,
    bias,
    weights,
    normed_two,
    grad_up,
    branch,
    query_rows,
    key_rows,
    value_rows,
    probs,
    mlp_low,
    hidden,
):
    rows, width = hidden.shape
    ff = grad_up.shape[1]
    head_cols = query_rows.shape[1]
    count = dp_size // 2 * sol_size
    tiles = rows // CHUNK
    dma = pltpu.SemaphoreType.DMA

    def shape(*dims, dtype=LOW):
        return jax.ShapeDtypeStruct(dims, dtype)

    def low(*dims):
        return pltpu.VMEM(dims, LOW)

    outs = [
        shape(2 * rows, head_cols),
        shape(4 * rows, 2 * head_cols),
        shape(rows, width),
        shape(rows // 2, width),
        shape(shard, 2 * ff, dtype=WIDE),
        shape(rows, width),
        shape(rows, width),
    ]
    return pl.pallas_call(
        functools.partial(attend_back_kernel, dp_size, sol_size),
        out_shape=outs,
        in_specs=[vmem_spec()] + [any_spec()] * 10,
        out_specs=[any_spec()] * len(outs),
        scratch_shapes=[
            low(2 * rows, width),
            low(2 * rows, ff),
            low(2 * rows, width),
            low(width, width),
            low(2 * rows, head_cols),
            low(4 * rows, head_cols),
            low(4 * rows, head_cols),
            low(2 * rows, head_cols),
            low(2, rows, 2 * rows),
            low(2 * rows, head_cols),
            low(4 * rows, 2 * head_cols),
            low(rows, width),
            low(rows, width),
            low(CHUNK, width),
            low(CHUNK // 2, width),
            low(CHUNK // 2, width),
            pltpu.VMEM((CHUNK // 2, width), WIDE),
        ]
        + ring_sum_scratch(count // 2, shard, ff, 1)
        + [
            dma((7,)),
            dma((2,)),
            dma((5,)),
            dma((4,)),
            dma((2, tiles)),
            dma((2, tiles)),
            dma((2,)),
            dma((2,)),
        ],
        compiler_params=pltpu.CompilerParams(
            collective_id=2, has_side_effects=True, vmem_limit_bytes=60 * 2**20
        ),
    )(
        bias,
        weights,
        normed_two,
        grad_up,
        branch,
        query_rows,
        key_rows,
        value_rows,
        probs,
        mlp_low,
        hidden,
    )


def last_kernel(
    dp_size,
    sol_size,
    x_ref,
    gain_ref,
    early_ref,
    normed_hbm,
    branch_hbm,
    query_grad_hbm,
    kv_grad_hbm,
    mixed_hbm,
    own_low_hbm,
    prefix_half_hbm,
    grad_hidden_hbm,
    query_out,
    key_out,
    value_out,
    out_out,
    input_grad_out,
    sums_ref,
    normed_v,
    branch_v,
    query_grad_v,
    kv_grad_v,
    mixed_v,
    own_low_v,
    own_recv_v,
    half_v,
    half_recv_v,
    prefix_v,
    grad_hidden_v,
    out_v,
    table_v,
    table_recv_v,
    ring_send_v,
    ring_recv_v,
    stage_v,
    ring_send,
    ring_recv,
    ring_end,
    load_sem,
    tile_sem,
    cross_send,
    cross_recv,
    chain_send,
    chain_recv,
    table_send,
    table_recv,
):
    here = Place(dp_size, sol_size)
    rows, width = x_ref.shape
    shard = stage_v.shape[1]
    head_cols = query_grad_v.shape[1]
    tiles = rows // CHUNK
    blocks = here.blocks()
    loads = [
        pltpu.make_async_copy(src, dst, load_sem.at[i])
        for i, (src, dst) in enumerate(
            (
                (query_grad_hbm, query_grad_v),
                (kv_grad_hbm, kv_grad_v),
                (mixed_hbm, mixed_v),
                (prefix_half_hbm, half_v),
                (normed_hbm, normed_v),
                (branch_hbm, branch_v),
                (own_low_hbm, own_low_v),
            )
        )
    ]
    for copy in loads:
        copy.start()
    partners = here.partners()
    here.greet(partners[1:])
    own_cross = remote(own_low_hbm, own_recv_v, cross_send.at[0], cross_recv.at[0], here.across)
    own_cross.start()

    def chunk(j, which):
        at = pl.ds(pl.multiple_of((2 * j + which) * shard, shard), shard)
        return jnp.concatenate(
            [
                dot_left_t(normed_v[: 2 * rows, at], query_grad_v[...]),
                dot_left_t(normed_v[:, at], kv_grad_v[...]),
                dot_left_t(branch_v[:, at], mixed_v[...]),
            ],
            axis=1,
        )

    ring = RingSum(
        here,
        chunk,
        ring_send_v,
        ring_recv_v,
        stage_v,
        (ring_send, ring_recv, ring_end),
        tuple(
            (ref, i * head_cols, head_cols)
            for i, ref in enumerate((query_out, key_out, value_out, out_out))
        ),
        upward=True,
    )

    parts = chain_send.shape[0]
    part = CHUNK // parts

    def chain_copy(i):
        at = pl.ds(i * part, part)
        return remote(
            half_v.at[at], half_recv_v.at[at], chain_send.at[i], chain_recv.at[i], here.along(-1)
        )

    def mine(i):
        return pl.ds(pl.multiple_of(here.y * CHUNK + i * part, part), part)

    def half_cross(i):
        return remote(
            half_recv_v.at[pl.ds(i * part, part)],
            prefix_v.at[mine(i)],
            cross_send.at[1 + i],
            cross_recv.at[1 + i],
            here.across,
        )

    def chain(stage, i):
        at = pl.ds(i * part, part)

        @pl.when(here.z == stage)
        def _():
            if stage < sol_size - 1:
                chain_copy(i).wait_recv()
            if 0 < stage < sol_size - 1:
                half_v[at, :] = (
                    half_v[at, :].astype(WIDE) + half_recv_v[at, :].astype(WIDE)
                ).astype(LOW)
            if stage > 0:
                chain_copy(i).start()
            else:
                half_cross(i).start()
                prefix_v[mine(i), :] = half_recv_v[at, :]

    loads[3].wait()
    for i in range(parts):
        chain(sol_size - 1, i)

    @pl.when(here.z > 0)
    def _():
        prefix_v[...] = jnp.zeros_like(prefix_v)

    for i in (0, 1, 2, 4, 5):
        loads[i].wait()
    ring.to(2)
    for step in range(1, sol_size + parts - 1):
        for i in range(parts):
            if 1 <= step - i < sol_size:
                chain(sol_size - 1 - (step - i), i)
        ring.to(1 + step)
        if step == 4:
            ring.prepare()

    loads[6].wait()
    own_cross.wait()

    @pl.when(here.z == 0)
    def _():
        for i in range(parts):
            half_cross(i).wait()

    gain = read_ordered(gain_ref, pl.ds(0, 1), blocks, shard)

    def tile_load(t):
        return pltpu.make_async_copy(
            grad_hidden_hbm.at[tile_rows(t)], grad_hidden_v, tile_sem.at[0]
        )

    def tile_store(t):
        return pltpu.make_async_copy(out_v, input_grad_out.at[tile_rows(t)], tile_sem.at[1])

    tile_load(0).start()
    totals = [jnp.zeros((1, width), WIDE)] * 2
    small = CHUNK // 2
    for t in range(tiles):
        tile_load(t).wait()
        if t > 0:
            tile_store(t - 1).wait()
        for piece in range(2):
            at = pl.ds(t * CHUNK + piece * small, small)
            inner = pl.ds(piece * small, small)
            grad = (
                own_low_v[at, :].astype(WIDE)
                + own_recv_v[at, :].astype(WIDE)
                + read_ordered(prefix_v, at, blocks, shard)
            )
            back, gain_terms, shift_terms = norm_back(
                read_ordered(x_ref, at, blocks, shard), gain, grad
            )
            totals = [totals[0] + gain_terms, totals[1] + shift_terms]
            write_ordered(out_v, inner, blocks, shard, back + grad_hidden_v[inner, :])
        tile_store(t).start()
        if t + 1 < tiles:
            tile_load(t + 1).start()

    for row in range(2):
        write_ordered(table_v.at[0], pl.ds(row, 1), blocks, shard, totals[row])
    for row in range(3):
        write_ordered(
            table_v.at[0], pl.ds(2 + row, 1), blocks, shard, early_ref[row : row + 1, :]
        )
    bias = early_ref[3:4, :]
    table_v[0, 5:6, :] = jnp.where(here.core == 0, bias, 0.0)
    table_v[0, 6:7, :] = jnp.where(here.core == 0, 0.0, bias)
    table_v[0, 7:8, :] = jnp.zeros((1, width), WIDE)

    def table_copy(k):
        return remote(
            table_v.at[k], table_recv_v.at[k], table_send.at[k], table_recv.at[k], partners[k]
        )

    for k in range(len(partners)):
        table_copy(k).start()
        ring.to(9 + k)
        table_copy(k).wait_recv()
        if k + 1 < len(partners):
            table_v[k + 1] = table_v[k] + table_recv_v[k]
        else:
            sums_ref[...] = table_v[k] + table_recv_v[k]
    tile_store(tiles - 1).wait()
    ring.finish()
    for k in range(len(partners)):
        table_copy(k).wait_send()
    for i in range(parts):

        @pl.when(here.z > 0)
        def _():
            chain_copy(i).wait_send()


def run_last(
    dp_size,
    sol_size,
    shard,
    x,
    gain,
    early,
    normed,
    branch,
    query_grad,
    kv_grad,
    mixed,
    own_low,
    prefix_half,
    grad_hidden,
):
    rows, width = x.shape
    head_cols = query_grad.shape[1]
    count = dp_size // 2 * sol_size
    bits = (dp_size * sol_size).bit_length() - 1
    dma = pltpu.SemaphoreType.DMA

    def shape(*dims, dtype=LOW):
        return jax.ShapeDtypeStruct(dims, dtype)

    def low(*dims):
        return pltpu.VMEM(dims, LOW)

    outs = [shape(shard, 2 * head_cols, dtype=WIDE)] * 4 + [
        shape(rows, width),
        shape(8, width, dtype=WIDE),
    ]
    return pl.pallas_call(
        functools.partial(last_kernel, dp_size, sol_size),
        out_shape=outs,
        in_specs=[vmem_spec()] * 3 + [any_spec()] * 8,
        out_specs=[any_spec()] * 5 + [vmem_spec()],
        scratch_shapes=[
            low(4 * rows, width),
            low(2 * rows, width),
            low(2 * rows, head_cols),
            low(4 * rows, 2 * head_cols),
            low(2 * rows, head_cols),
            low(rows, width),
            low(rows, width),
            low(CHUNK, width),
            low(CHUNK, width),
            low(rows, width),
            pltpu.VMEM((CHUNK, width), WIDE),
            low(CHUNK, width),
            pltpu.VMEM((bits, 8, width), WIDE),
            pltpu.VMEM((bits, 8, width), WIDE),
        ]
        + ring_sum_scratch(count // 2, shard, 4 * head_cols, 4)
        + [
            dma((7,)),
            dma((2,)),
            dma((5,)),
            dma((5,)),
            dma((4,)),
            dma((4,)),
            dma((bits,)),
            dma((bits,)),
        ],
        compiler_params=pltpu.CompilerParams(
            collective_id=3, has_side_effects=True, vmem_limit_bytes=60 * 2**20
        ),
    )(
        x,
        gain,
        early,
        normed,
        branch,
        query_grad,
        kv_grad,
        mixed,
        own_low,
        prefix_half,
        grad_hidden,
    )


FINISH_PARTS = 4


def finish_kernel(*refs):
    count = (len(refs) - 2) // 3
    ins, outs, rooms = refs[:count], refs[count : 2 * count], refs[2 * count : 3 * count]
    in_sem, out_sem = refs[3 * count :]
    loads, stores = [], []
    for i, (src, dst, room) in enumerate(zip(ins, outs, rooms)):
        part = src.shape[0] // FINISH_PARTS
        for k in range(FINISH_PARTS):
            at = pl.ds(k * part, part)
            loads.append(pltpu.make_async_copy(src.at[at], room.at[at], in_sem.at[i, k]))
            stores.append(pltpu.make_async_copy(room.at[at], dst.at[at], out_sem.at[i, k]))
    for copy in loads:
        copy.start()
    for load, store in zip(loads, stores):
        load.wait()
        store.start()
    for copy in stores:
        copy.wait()


def run_finish(arrays):
    dma = pltpu.SemaphoreType.DMA
    return pl.pallas_call(
        finish_kernel,
        out_shape=[jax.ShapeDtypeStruct(a.shape, a.dtype) for a in arrays],
        in_specs=[any_spec()] * len(arrays),
        out_specs=[any_spec()] * len(arrays),
        scratch_shapes=[pltpu.VMEM(a.shape, a.dtype) for a in arrays]
        + [dma((len(arrays), FINISH_PARTS))] * 2,
        compiler_params=pltpu.CompilerParams(vmem_limit_bytes=60 * 2**20),
    )(*arrays)


def ring_program(
    inputs,
    cotangent,
    attn_gain,
    attn_shift,
    query_weight,
    key_weight,
    value_weight,
    out_weight,
    mlp_gain,
    mlp_shift,
    up_weight,
    up_bias,
    down_weight,
    down_bias,
    live_rows,
):
    block_rows, width = inputs.shape
    shard_rows = query_weight.shape[0]
    head_cols = query_weight.shape[1] // 2
    ff_cols = up_weight.shape[1] // 2
    ff_part = ff_cols // 2
    local_heads = head_cols // HEAD_DIM
    score_scale = 1.0 / math.sqrt(HEAD_DIM)
    dp_size, sol_size = lax.axis_size("dp"), lax.axis_size("sol")
    count, ahead, back, cores = ring_pairs(dp_size, sol_size)
    dp_place, sol_place = lax.axis_index("dp"), lax.axis_index("sol")
    x_place, core = dp_place // 2, dp_place % 2
    first_core = core == 0
    along = jnp.where(x_place % 2 == 0, sol_place, sol_size - 1 - sol_place)
    ring_here = x_place * sol_size + along

    order_list = []
    for j in range(count):
        q = (ring_here + j) % count
        qx, qa = q // sol_size, q % sol_size
        qz = jnp.where(qx % 2 == 0, qa, sol_size - 1 - qa)
        order_list += [(qx * 2) * sol_size + qz, (qx * 2 + 1) * sol_size + qz]
    order = jnp.stack(order_list).astype(jnp.int32)
    back_order = jnp.argsort(order).astype(jnp.int32)

    def to_core(value):
        return lax.ppermute(value, ROWS_AXES, cores)

    def to_tensor(value):
        return lax.ppermute(value, "tensor", [(0, 1), (1, 0)])

    def reorder_vector(vector, by):
        return jnp.take(vector.reshape(by.shape[0], -1), by, axis=0).reshape(vector.shape)

    def gather_ring(piece, flip):
        hops_ahead = count // 2 - (1 if flip else 0)
        hops_back = count - 1 - hops_ahead
        got = {0: piece}
        moving_a, moving_b = piece, piece
        for k in range(1, count // 2 + 1):
            if k <= hops_ahead:
                moving_a = lax.ppermute(moving_a, ROWS_AXES, ahead)
                got[count - k] = moving_a
            if k <= hops_back:
                moving_b = lax.ppermute(moving_b, ROWS_AXES, back)
                got[k] = moving_b
        return jnp.concatenate([got[j] for j in range(count)], axis=0)

    def scatter_ring(chunk, flip):
        hops_ahead = count // 2 - (1 if flip else 0)
        hops_back = count - 1 - hops_ahead
        carried_a = carried_b = None
        for k in range(count // 2, 0, -1):
            if k <= hops_ahead:
                value = chunk(k)
                if carried_a is not None:
                    value = value + carried_a.astype(WIDE)
                carried_a = lax.ppermute(value.astype(LOW), ROWS_AXES, ahead)
            if k <= hops_back:
                value = chunk(count - k)
                if carried_b is not None:
                    value = value + carried_b.astype(WIDE)
                carried_b = lax.ppermute(value.astype(LOW), ROWS_AXES, back)
        return chunk(0) + carried_a.astype(WIDE) + carried_b.astype(WIDE)

    def own_part(shards):
        firsts, seconds = [], []
        for shard, start, size in shards:
            half = shard.shape[1] // 2
            firsts.append(shard[:, start : start + size])
            seconds.append(shard[:, half + start : half + start + size])
        low_half = jnp.concatenate(firsts, axis=1) if len(firsts) > 1 else firsts[0]
        high_half = jnp.concatenate(seconds, axis=1) if len(seconds) > 1 else seconds[0]
        mine = jnp.where(first_core, low_half, high_half)
        other = to_core(jnp.where(first_core, high_half, low_half))
        return jnp.concatenate(
            [jnp.where(first_core, mine, other), jnp.where(first_core, other, mine)], axis=0
        )

    def split_rows(full):
        upper, lower = full[:shard_rows], full[shard_rows:]
        mine = jnp.where(first_core, upper, lower)
        other = to_core(jnp.where(first_core, lower, upper))
        return jnp.where(first_core, mine, other), jnp.where(first_core, other, mine)

    def sum_partials(partial):
        mine = partial[:block_rows] + to_core(partial[block_rows:].astype(LOW)).astype(WIDE)
        low = mine.astype(LOW)
        return low.astype(WIDE) + to_tensor(low).astype(WIDE)

    def pair_rows(own):
        return jnp.concatenate([own, to_core(own)], axis=0)

    qk_piece = own_part([(query_weight, 0, head_cols), (key_weight, 0, head_cols)])
    vo_piece = own_part([(value_weight, 0, head_cols), (out_weight, 0, head_cols)])
    up_pieces = [own_part([(up_weight, s, ff_part)]) for s in (0, ff_part)]
    down_pieces = [own_part([(down_weight, s, ff_part)]) for s in (0, ff_part)]
    qk_full = gather_ring(qk_piece, False)
    vo_full = gather_ring(vo_piece, True)
    up_full = [gather_ring(up_pieces[0], False), gather_ring(up_pieces[1], True)]
    down_full = [gather_ring(down_pieces[0], False), gather_ring(down_pieces[1], True)]
    query_full, key_full = qk_full[:, :head_cols], qk_full[:, head_cols:]
    value_full, out_full = vo_full[:, :head_cols], vo_full[:, head_cols:]

    tensor_place = lax.axis_index("tensor")
    half_rows = block_rows // 2
    half = jnp.where(tensor_place == 0, inputs[:half_rows], inputs[half_rows:])
    prefix_half = half
    hop = half
    for k in range(1, sol_size):
        hop = lax.ppermute(hop, "sol", [(k - 1, k)])
        prefix_half = jnp.where(sol_place == k, hop, prefix_half)
    other_half = to_tensor(prefix_half)
    prefix_inputs = jnp.concatenate(
        [
            jnp.where(tensor_place == 0, prefix_half, other_half),
            jnp.where(tensor_place == 0, other_half, prefix_half),
        ],
        axis=0,
    )

    own_low = reorder(inputs, order)
    prefix_low = reorder(prefix_inputs, order)
    cot_low = reorder(cotangent, order)
    attn_gain_o, attn_shift_o, mlp_gain_o, mlp_shift_o, down_bias_o = [
        reorder_vector(v, order) for v in (attn_gain, attn_shift, mlp_gain, mlp_shift, down_bias)
    ]
    up_bias_c = jnp.where(first_core, up_bias[:ff_cols], up_bias[ff_cols:])
    up_bias_parts = [up_bias_c[:ff_part], up_bias_c[ff_part:]]

    features = own_low.astype(WIDE)
    normed = pair_rows(layer_norm(features, attn_gain_o, attn_shift_o).astype(LOW))
    normed_prefix = pair_rows(
        layer_norm(prefix_low.astype(WIDE), attn_gain_o, attn_shift_o).astype(LOW)
    )
    cot_pair = pair_rows(cot_low)

    query_rows = dot_plain(normed, query_full).astype(LOW)
    key_rows = dot_plain(normed, key_full).astype(LOW)
    value_rows = dot_plain(normed, value_full).astype(LOW)
    key_prefix = dot_plain(normed_prefix, key_full).astype(LOW)
    value_prefix = dot_plain(normed_prefix, value_full).astype(LOW)

    def heads_of(rows):
        return rows.reshape(2, -1, local_heads, HEAD_DIM)

    head_queries = heads_of(query_rows)
    all_keys = jnp.concatenate([heads_of(key_prefix), heads_of(key_rows)], axis=1)
    all_values = jnp.concatenate([heads_of(value_prefix), heads_of(value_rows)], axis=1)

    row_ids = jnp.arange(block_rows)[:, None]
    col_ids = jnp.arange(block_rows)[None, :]
    masks = []
    for place in (dp_place, dp_place + 1 - 2 * core):
        own_live = live_rows[place * sol_size + sol_place]
        prefix_live = live_rows[place * sol_size]
        prefix_ok = jnp.logical_and(col_ids < prefix_live, sol_place != 0)
        own_ok = jnp.logical_and(col_ids <= row_ids, col_ids < own_live)
        masks.append(
            jnp.concatenate(
                [jnp.broadcast_to(prefix_ok, (block_rows, block_rows)), own_ok], axis=1
            )
        )
    allowed = jnp.stack(masks)[:, None]

    def masked_scores():
        raw = jnp.einsum("bqhd,bkhd->bhqk", head_queries, all_keys, preferred_element_type=WIDE)
        return jnp.where(allowed, raw * score_scale, NEG_FILL)

    scores = masked_scores()
    row_peak = jnp.max(scores, axis=-1, keepdims=True)
    exp_scores = jnp.exp(scores - row_peak)
    totals = jnp.sum(exp_scores, axis=-1, keepdims=True)
    attn_probs = exp_scores / totals
    log_total = row_peak + jnp.log(totals)
    mixed = jnp.einsum(
        "bhqk,bkhd->bqhd", attn_probs.astype(LOW), all_values, preferred_element_type=WIDE
    )
    mixed_low = mixed.reshape(2 * block_rows, head_cols).astype(LOW)

    hidden = features + sum_partials(dot_right_t(mixed_low, out_full))
    normed_two = pair_rows(layer_norm(hidden, mlp_gain_o, mlp_shift_o).astype(LOW))
    upward = [dot_plain(normed_two, up_full[i]) + up_bias_parts[i] for i in range(2)]
    active = [gelu_tanh(u).astype(LOW) for u in upward]
    down_grads = [
        scatter_ring(
            lambda j, i=i: dot_left_t(
                cot_pair[:, j * 2 * shard_rows : (j + 1) * 2 * shard_rows], active[i]
            ),
            i == 1,
        )
        for i in range(2)
    ]
    grad_up = []
    for i in range(2):
        grad_active = dot_plain(cot_pair, down_full[i])
        unused_gelu, gelu_pull = jax.vjp(gelu_tanh, upward[i])
        grad_up.append(gelu_pull(grad_active)[0].astype(LOW))
    grad_normed_two = sum_partials(
        dot_right_t(grad_up[0], up_full[0]) + dot_right_t(grad_up[1], up_full[1])
    )
    up_grads = [
        scatter_ring(
            lambda j, i=i: dot_left_t(
                normed_two[:, j * 2 * shard_rows : (j + 1) * 2 * shard_rows], grad_up[i]
            ),
            i == 1,
        )
        for i in range(2)
    ]
    mlp_total = sum_partials(
        dot_right_t(active[0], down_full[0]) + dot_right_t(active[1], down_full[1])
    )
    outputs = reorder((hidden + mlp_total + down_bias_o).astype(LOW), back_order)

    grad_out = cot_low.astype(WIDE)
    down_bias_grad = jnp.sum(grad_out, axis=0)
    grad_hidden_norm, mlp_gain_grad, mlp_shift_grad = layer_norm_back(
        hidden, mlp_gain_o, grad_normed_two
    )
    grad_hidden = grad_out + grad_hidden_norm
    grad_branch = pair_rows(grad_hidden.astype(LOW))
    grad_mixed_low = dot_plain(grad_branch, out_full).astype(LOW)

    grad_head_mixed = heads_of(grad_mixed_low)
    attn_probs = jnp.exp(masked_scores() - log_total)
    grad_probs = jnp.einsum(
        "bqhd,bkhd->bhqk", grad_head_mixed, all_values, preferred_element_type=WIDE
    )
    row_delta = jnp.sum(attn_probs * grad_probs, axis=-1, keepdims=True)
    grad_scores = (attn_probs * (grad_probs - row_delta)).astype(LOW)
    grad_queries = (
        jnp.einsum("bhqk,bkhd->bqhd", grad_scores, all_keys, preferred_element_type=WIDE)
        * score_scale
    )
    grad_keys = (
        jnp.einsum("bhqk,bqhd->bkhd", grad_scores, head_queries, preferred_element_type=WIDE)
        * score_scale
    )
    grad_values = jnp.einsum(
        "bhqk,bqhd->bkhd", attn_probs.astype(LOW), grad_head_mixed, preferred_element_type=WIDE
    )

    def rows_of(heads):
        return heads.reshape(2 * block_rows, head_cols).astype(LOW)

    query_grad_low = rows_of(grad_queries)
    key_own = rows_of(grad_keys[:, block_rows:])
    value_own = rows_of(grad_values[:, block_rows:])
    key_pre = rows_of(grad_keys[:, :block_rows])
    value_pre = rows_of(grad_values[:, :block_rows])

    kv_pre = jnp.concatenate([key_pre, value_pre], axis=1)
    carried = kv_pre
    for k in range(sol_size - 1, 0, -1):
        came = lax.ppermute(carried, "sol", [(k, k - 1)])
        if k > 1:
            carried = (kv_pre.astype(WIDE) + came.astype(WIDE)).astype(LOW)
    key_all = (key_own.astype(WIDE) + came[:, :head_cols].astype(WIDE)).astype(LOW)
    value_all = (value_own.astype(WIDE) + came[:, head_cols:].astype(WIDE)).astype(LOW)

    normed_all = jnp.concatenate([normed, normed_prefix], axis=0)
    key_rows_grad = jnp.concatenate([key_own, key_pre], axis=0)
    value_rows_grad = jnp.concatenate([value_own, value_pre], axis=0)

    def qk_chunk(j):
        at = slice(j * 2 * shard_rows, (j + 1) * 2 * shard_rows)
        return jnp.concatenate(
            [
                dot_left_t(normed[:, at], query_grad_low),
                dot_left_t(normed_all[:, at], key_rows_grad),
            ],
            axis=1,
        )

    def vo_chunk(j):
        at = slice(j * 2 * shard_rows, (j + 1) * 2 * shard_rows)
        return jnp.concatenate(
            [
                dot_left_t(normed_all[:, at], value_rows_grad),
                dot_left_t(grad_branch[:, at], mixed_low),
            ],
            axis=1,
        )

    qk_grad = scatter_ring(qk_chunk, False)
    vo_grad = scatter_ring(vo_chunk, True)

    grad_normed = sum_partials(
        dot_right_t(query_grad_low, query_full)
        + dot_right_t(key_all, key_full)
        + dot_right_t(value_all, value_full)
    )
    grad_features, attn_gain_grad, attn_shift_grad = layer_norm_back(
        features, attn_gain_o, grad_normed
    )
    input_grad = reorder((grad_hidden + grad_features).astype(LOW), back_order)

    up_bias_grad = jnp.concatenate([jnp.sum(g.astype(WIDE), axis=0) for g in grad_up])
    up_bias_both = jnp.concatenate(
        [
            jnp.where(first_core, up_bias_grad, 0.0),
            jnp.where(first_core, 0.0, up_bias_grad),
        ]
    )

    def sum_rows_axes(vector):
        vector = vector + to_core(vector)
        step = 1
        while step < sol_size:
            vector = vector + lax.ppermute(vector, "sol", [(i, i ^ step) for i in range(sol_size)])
            step *= 2
        step = 2
        while step < dp_size:
            vector = vector + lax.ppermute(vector, "dp", [(i, i ^ step) for i in range(dp_size)])
            step *= 2
        return vector

    early = sum_rows_axes(
        jnp.concatenate(
            [reorder_vector(v, back_order) for v in (mlp_gain_grad, mlp_shift_grad, down_bias_grad)]
            + [up_bias_both]
        )
    )
    late = sum_rows_axes(
        jnp.concatenate([reorder_vector(v, back_order) for v in (attn_gain_grad, attn_shift_grad)])
    )

    qk_low, qk_high = split_rows(qk_grad)
    vo_low, vo_high = split_rows(vo_grad)
    up_low, up_high = zip(*[split_rows(g) for g in up_grads])
    down_low, down_high = zip(*[split_rows(g) for g in down_grads])

    def both(low_cols, high_cols):
        return jnp.concatenate([low_cols, high_cols], axis=1)

    return (
        outputs,
        input_grad,
        late[:width],
        late[width:],
        both(qk_low[:, :head_cols], qk_high[:, :head_cols]),
        both(qk_low[:, head_cols:], qk_high[:, head_cols:]),
        both(vo_low[:, :head_cols], vo_high[:, :head_cols]),
        both(vo_low[:, head_cols:], vo_high[:, head_cols:]),
        early[:width],
        early[width : 2 * width],
        jnp.concatenate(up_low + up_high, axis=1),
        early[3 * width :],
        jnp.concatenate(down_low + down_high, axis=1),
        early[2 * width : 3 * width],
    )


def per_device(*arrays):
    inputs, query_weight, up_weight = arrays[0], arrays[4], arrays[10]
    width = inputs.shape[1]
    fits = (
        query_weight.shape[0] % 128 == 0
        and inputs.shape[0] == 2 * CHUNK
        and up_weight.shape[1] == 2 * width
        and query_weight.shape[1] * 2 == width
        and lax.axis_size("dp") % 2 == 0
        and lax.axis_size("dp") * lax.axis_size("sol") == 16
        and lax.axis_size("tensor") == 2
    )
    return kernel_program(*arrays) if fits else ring_program(*arrays)


def kernel_program(
    inputs,
    cotangent,
    attn_gain,
    attn_shift,
    query_weight,
    key_weight,
    value_weight,
    out_weight,
    mlp_gain,
    mlp_shift,
    up_weight,
    up_bias,
    down_weight,
    down_bias,
    live_rows,
):
    width = inputs.shape[1]
    shard_rows = query_weight.shape[0]
    dp_size, sol_size = lax.axis_size("dp"), lax.axis_size("sol")
    attn_gain, attn_shift, mlp_gain, mlp_shift, up_bias, down_bias = [
        v.reshape(1, -1) for v in (attn_gain, attn_shift, mlp_gain, mlp_shift, up_bias, down_bias)
    ]
    (
        weights,
        normed_all,
        cot_pair,
        query_rows,
        key_rows,
        value_rows,
        probs,
        mixed_low,
        hidden,
        normed_two,
        slope,
        active,
    ) = run_forward(
        dp_size,
        sol_size,
        inputs,
        (attn_gain, attn_shift, mlp_gain, mlp_shift, up_bias),
        live_rows,
        cotangent,
        (query_weight, key_weight, value_weight, out_weight, up_weight, down_weight),
    )
    grad_up, grad_branch, grad_hidden, mlp_low, down_grad, early_sums = run_down(
        dp_size, sol_size, shard_rows, mlp_gain, weights, cot_pair, active, slope, hidden
    )
    query_grad, kv_grad, own_low, prefix_half, up_grad, outputs, _ = run_attend_back(
        dp_size,
        sol_size,
        shard_rows,
        down_bias,
        weights,
        normed_two,
        grad_up,
        grad_branch,
        query_rows,
        key_rows,
        value_rows,
        probs,
        mlp_low,
        hidden,
    )
    query_grads, key_grads, value_grads, out_grads, input_grad, sums = run_last(
        dp_size,
        sol_size,
        shard_rows,
        inputs,
        attn_gain,
        early_sums,
        normed_all,
        grad_branch,
        query_grad,
        kv_grad,
        mixed_low,
        own_low,
        prefix_half,
        grad_hidden,
    )

    (
        outputs,
        input_grad,
        query_grads,
        key_grads,
        value_grads,
        out_grads,
        up_grad,
        down_grad,
    ) = run_finish(
        [
            outputs,
            input_grad,
            query_grads,
            key_grads,
            value_grads,
            out_grads,
            up_grad,
            down_grad,
        ]
    )
    return (
        outputs,
        input_grad,
        sums[0],
        sums[1],
        query_grads,
        key_grads,
        value_grads,
        out_grads,
        sums[2],
        sums[3],
        up_grad,
        sums[5:7].reshape(-1),
        down_grad,
        sums[4],
    )


def solution(mesh):
    rows = P(("dp", "sol"), None)
    matrix = P(("dp", "sol"), "tensor")
    return jax.shard_map(
        per_device,
        mesh=mesh,
        in_specs=(
            rows,
            rows,
            P(),
            P(),
            matrix,
            matrix,
            matrix,
            matrix,
            P(),
            P(),
            matrix,
            P("tensor"),
            matrix,
            P(),
            P(),
        ),
        out_specs=(
            rows,
            rows,
            P(),
            P(),
            matrix,
            matrix,
            matrix,
            matrix,
            P(),
            P(),
            matrix,
            P("tensor"),
            matrix,
            P(),
        ),
        check_vma=False,
    )
```
